32 devices in a mesh: ctx: 8 (over z, y), fsdp: 4 (over x, core).
Axes of the slice: x: 2, y: 2, z: 4, core: 2. Of those that a mesh axis runs over, the one named last changes fastest.
Arguments:
- tokens: bfloat16 [4, 1280, 1024], P('fsdp', 'ctx')
- lengths: int32 [4, 4], P('fsdp'), may hold values from 1 to 1024, 1280 in all within a row
- deal: int32 [4, 8, 8], P('fsdp'), may hold values from 0 to 7, each once within a row
- attn_gain: bfloat16 [1024], P('fsdp'), may hold values from 0.25 to 1.75
- w_q: bfloat16 [1024, 2048], P('fsdp'), may hold values from -0.1875 to 0.1875
- key_weight: bfloat16 [1024, 1024], P('fsdp'), may hold values from -0.1875 to 0.1875
- value_weight: bfloat16 [1024, 1024], P('fsdp'), may hold values from -0.1875 to 0.1875
- query_norm_gain: bfloat16 [128], P('fsdp'), may hold values from 0.25 to 1.75
- k_gain: bfloat16 [128], P('fsdp'), may hold values from 0.25 to 1.75
- w_o: bfloat16 [2048, 1024], P('fsdp'), may hold values from -0.5 to 0.5
- mlp_gain: bfloat16 [1024], P('fsdp'), may hold values from 0.25 to 1.75
- w_gate: bfloat16 [1024, 3072], P('fsdp'), may hold values from -0.1875 to 0.1875
- w_up: bfloat16 [1024, 3072], P('fsdp'), may hold values from -0.1875 to 0.1875
- w_down: bfloat16 [3072, 1024], P('fsdp'), may hold values from -0.109375 to 0.109375
- out_cotangent: bfloat16 [4, 1280, 1024], P('fsdp', 'ctx'), may hold values from -6 to 6
Outputs:
- output: bfloat16 [4, 1280, 1024], P('fsdp', 'ctx')
- input_grad: float32 [4, 1280, 1024], P('fsdp', 'ctx')
- attn_gain_grad: float32 [1024], P('fsdp')
- q_gain_grad: float32 [128], P('fsdp')
- k_gain_grad: float32 [128], P('fsdp')
- mlp_gain_grad: float32 [1024], P('fsdp')
- w_q_grad: float32 [1024, 2048], P('fsdp')
- w_k_grad: float32 [1024, 1024], P('fsdp')
- w_v_grad: float32 [1024, 1024], P('fsdp')
- w_o_grad: float32 [2048, 1024], P('fsdp')
- w_gate_grad: float32 [1024, 3072], P('fsdp')
- w_up_grad: float32 [1024, 3072], P('fsdp')
- w_down_grad: float32 [3072, 1024], P('fsdp')
The draws below stay inside these ranges and needn't reach their ends.
Inputs may be any that keep to these rules, and one draw needn't show every extreme that they name: Each group's 4 lengths sum to 1280; the longest is exactly 1024. Each row deal[g, s] names every device of a group once.
All inputs are finite; a program needn't handle non-finite values.
Results may differ from the reference program's by a relative error of at most 0.034.
Values may be sent and summed in bfloat16 or wider, within the bound.
A program may use at most 320 MiB of HBM per device.

```python
import math
import jax
import jax.numpy as jnp
import numpy as np
from jax import lax

MODEL_WIDTH = 1024
QUERY_HEADS = 16
KEY_VALUE_HEADS = 8
HEAD_SIZE = 128
FF = 3072
TOK_DEV = 160
GROUPS = 4
GROUP_TOK = 1280
SEQ_MOST = 1024
NSEQ = 4
PIECES = 8


def draw_tokens(key, part):
    key = jax.random.fold_in(key, 11)
    key_base, key_row_block, key_cols = jax.random.split(key, 3)
    shape = (GROUPS, GROUP_TOK, MODEL_WIDTH)
    base = jax.random.normal(key_base, shape, jnp.float32)
    row_scale = jnp.exp(jax.random.uniform(key_row_block, (GROUPS, GROUP_TOK, 1), jnp.float32, math.log(1.0 / 3.0), math.log(10.0 / 3.0)))
    col_scale = jnp.exp(jax.random.uniform(key_cols, (1, 1, MODEL_WIDTH), jnp.float32, math.log(0.5), math.log(2.0)))
    return (base * row_scale * col_scale).astype(jnp.bfloat16)


def levels(stream_key, shape, cuts, low, largest):
    loudness = 1.0
    for axis_at, shards_of in cuts:
        steps = jax.random.uniform(jax.random.fold_in(jax.random.fold_in(stream_key, 6), axis_at), (shards_of,), jnp.float32, low / len(cuts), largest / len(cuts))
        loudness = loudness * jnp.repeat(jnp.exp(steps), shape[axis_at] // shards_of).reshape((-1,) + (1,) * (len(shape) - 1 - axis_at))
    return loudness


def profile(count, total, most, lean):
    loads = [(1 << 20) // math.isqrt(rank ** lean) + 1 for rank in range(2, count + 1)]
    rest, holding = total - most - (count - 1), [1] * (count - 1)
    while rest > 0:
        free = [i for i in range(count - 1) if holding[i] < most]
        pool, remaining = sum([loads[i] for i in free]), rest
        for i in free:
            extra = min(most - holding[i], max(1, remaining * loads[i] // pool), rest)
            holding[i] = holding[i] + extra
            rest = rest - extra
    return np.array([most] + holding)


def uneven_parts(key, number_of, total, reach, slope):
    if number_of == 2:
        one = jax.random.randint(key, (), max(1, total - reach), min(reach, total - 1) + 1)
        return jnp.stack([one, total - one])
    tallies = jnp.asarray(profile(number_of, total, reach, slope), jnp.int32)
    couples = (number_of - 1) // 2
    source_of, taker = tallies[1:1 + 2 * couples:2], tallies[2:2 + 2 * couples:2]
    margin = jnp.minimum(source_of - 1, reach - taker)
    passed = jax.random.randint(jax.random.fold_in(key, 1), (couples,), 0, 1 << 20) % (margin + 1)
    tallies = tallies.at[1:1 + 2 * couples:2].set(source_of - passed).at[2:2 + 2 * couples:2].set(taker + passed)
    return tallies[jax.random.permutation(jax.random.fold_in(key, 2), number_of)]


def scatter_about(rng, extent, scale, most, cuts=(), kind=jnp.bfloat16):
    array = scale * jax.random.normal(rng, extent, jnp.float32)
    if cuts:
        array = array * levels(rng, extent, cuts, -0.22, 0.18)
    return jnp.clip(array, -most, most).astype(kind)


def setup_inputs(seed: int = 0) -> dict:
    keys = jax.random.split(jax.random.key(seed), 16)
    return {
        "tokens": draw_tokens(jax.random.fold_in(keys[15], 71), 0),
        "lengths": jax.vmap(lambda own: uneven_parts(own, NSEQ, GROUP_TOK, SEQ_MOST, 2))(jax.random.split(keys[1], GROUPS)).reshape((GROUPS, NSEQ)).astype(jnp.int32),
        "deal": jax.vmap(lambda own: jax.random.permutation(own, PIECES))(jax.random.split(keys[2], GROUPS * PIECES)).reshape((GROUPS, PIECES, PIECES)).astype(jnp.int32),
        "attn_gain": jnp.clip(1.0 + 0.15 * jax.random.normal(keys[3], (MODEL_WIDTH,), jnp.float32), 0.25, 1.75).astype(jnp.bfloat16),
        "w_q": scatter_about(keys[4], (MODEL_WIDTH, QUERY_HEADS * HEAD_SIZE), MODEL_WIDTH ** -0.5, 0.1875, ((0, 4),)),
        "key_weight": scatter_about(keys[5], (MODEL_WIDTH, KEY_VALUE_HEADS * HEAD_SIZE), MODEL_WIDTH ** -0.5, 0.1875, ((0, 4),)),
        "value_weight": scatter_about(keys[6], (MODEL_WIDTH, KEY_VALUE_HEADS * HEAD_SIZE), MODEL_WIDTH ** -0.5, 0.1875, ((0, 4),)),
        "query_norm_gain": jnp.clip(1.0 + 0.15 * jax.random.normal(keys[7], (HEAD_SIZE,), jnp.float32), 0.25, 1.75).astype(jnp.bfloat16),
        "k_gain": jnp.clip(1.0 + 0.15 * jax.random.normal(keys[8], (HEAD_SIZE,), jnp.float32), 0.25, 1.75).astype(jnp.bfloat16),
        "w_o": scatter_about(keys[9], (QUERY_HEADS * HEAD_SIZE, MODEL_WIDTH), (QUERY_HEADS * HEAD_SIZE // 16) ** -0.5, 0.5, ((0, 4),)),
        "mlp_gain": jnp.clip(1.0 + 0.15 * jax.random.normal(keys[10], (MODEL_WIDTH,), jnp.float32), 0.25, 1.75).astype(jnp.bfloat16),
        "w_gate": scatter_about(keys[11], (MODEL_WIDTH, FF), MODEL_WIDTH ** -0.5, 0.1875, ((0, 4),)),
        "w_up": scatter_about(keys[12], (MODEL_WIDTH, FF), MODEL_WIDTH ** -0.5, 0.1875, ((0, 4),)),
        "w_down": scatter_about(keys[13], (FF, MODEL_WIDTH), FF ** -0.5, 0.109375, ((0, 4),)),
        "out_cotangent": scatter_about(keys[14], (GROUPS, GROUP_TOK, MODEL_WIDTH), 1.0, 6.0, ((0, 4), (1, 8))),
    }


@jax.custom_vjp
def narrow_precision(v):
    return lax.optimization_barrier(v.astype(jnp.bfloat16)).astype(jnp.float32)

@jax.custom_vjp
def narrow_backward(v):
    return v

def low_keep(v):
    return (narrow_precision(v), None)

def low_pass(kept, grad):
    return (grad,)

def back_keep(v):
    return (v, None)

def back_low(kept, grad):
    return (narrow_precision(grad),)
narrow_precision.defvjp(low_keep, low_pass)
narrow_backward.defvjp(back_keep, back_low)
eps = 1e-06
theta_base = 1000000.0
negative_filler = -1e+30
exact_result = lax.Precision.HIGHEST

def root_mean_norm(values, gain_vec):
    return values * lax.rsqrt(lax.optimization_barrier(jnp.mean(values * values, axis=-1, keepdims=True)) + eps) * gain_vec

def rotary_embedding(values, token_position):
    half_width = values.shape[-1] // 2
    frequency = theta_base ** (-(jnp.arange(half_width, dtype=jnp.float32) * 2.0) / values.shape[-1])
    angles = token_position.astype(jnp.float32)[:, None] * frequency[None, :]
    cosine = jnp.concatenate([jnp.cos(angles), jnp.cos(angles)], axis=-1)[:, None, :]
    sine_part = jnp.concatenate([jnp.sin(angles), jnp.sin(angles)], axis=-1)[:, None, :]
    turned = jnp.concatenate([-values[..., half_width:], values[..., :half_width]], axis=-1)
    return values * cosine + turned * sine_part

def dealt_rows(plan):
    piece_count = plan.shape[0]
    piece_rows = TOK_DEV // piece_count
    devices = jnp.arange(piece_count, dtype=jnp.int32)
    hits = plan[:, :, None] == devices[None, None, :]
    slot_of = lax.optimization_barrier(jnp.sum(jnp.where(hits, devices[None, :, None], 0), axis=1)).astype(jnp.int32)
    inner = jnp.arange(piece_rows, dtype=jnp.int32)
    rows = devices[None, :, None] * TOK_DEV + jnp.transpose(slot_of)[:, :, None] * piece_rows + inner[None, None, :]
    return rows.reshape(GROUP_TOK).astype(jnp.int32)

def group_layer(params, token_group, segment_initial, token_position):
    attn_gain, w_q, key_weight, value_weight, query_norm_gain, k_gain, w_o, mlp_gain, w_gate, w_up, w_down = params
    token_count = token_group.shape[0]
    group_width = QUERY_HEADS // KEY_VALUE_HEADS
    normalized_input = narrow_precision(root_mean_norm(token_group, attn_gain))
    query_prenorm = narrow_backward(jnp.dot(normalized_input, w_q, precision=exact_result)).reshape(token_count, QUERY_HEADS, HEAD_SIZE)
    key_prenorm = narrow_backward(jnp.dot(normalized_input, key_weight, precision=exact_result)).reshape(token_count, KEY_VALUE_HEADS, HEAD_SIZE)
    value_narrow = narrow_precision(narrow_backward(jnp.dot(normalized_input, value_weight, precision=exact_result))).reshape(token_count, KEY_VALUE_HEADS, HEAD_SIZE)
    query_narrow = narrow_precision(rotary_embedding(root_mean_norm(query_prenorm, query_norm_gain), token_position)).reshape(token_count, KEY_VALUE_HEADS, group_width, HEAD_SIZE)
    key_narrow = narrow_precision(rotary_embedding(root_mean_norm(key_prenorm, k_gain), token_position))
    rows_per_block = 512 if token_count % 512 == 0 else token_count
    count_of_blocks = token_count // rows_per_block
    key_identifiers = jnp.arange(token_count, dtype=jnp.int32)

    def attend_over_block(block_args):
        q_block, id_block, first_block = block_args
        scores = narrow_backward(jnp.einsum('rkgh,ckh->kgrc', q_block, key_narrow, precision=exact_result) * HEAD_SIZE ** (-0.5))
        allowed = (key_identifiers[None, :] >= first_block[:, None]) & (key_identifiers[None, :] <= id_block[:, None])
        scores = jnp.where(allowed, scores, negative_filler)
        weights = narrow_precision(jax.nn.softmax(scores, axis=-1))
        return jnp.einsum('kgrc,ckh->rkgh', weights, value_narrow, precision=exact_result)
    attended_rows = lax.map(jax.checkpoint(attend_over_block), (query_narrow.reshape(count_of_blocks, rows_per_block, KEY_VALUE_HEADS, group_width, HEAD_SIZE), key_identifiers.reshape(count_of_blocks, rows_per_block), segment_initial.reshape(count_of_blocks, rows_per_block)))
    attention_mixed = narrow_precision(narrow_backward(attended_rows.reshape(token_count, QUERY_HEADS * HEAD_SIZE)))
    middle = token_group + narrow_backward(jnp.dot(attention_mixed, w_o, precision=exact_result))
    normed2 = narrow_precision(root_mean_norm(middle, mlp_gain))
    gate_pre = narrow_backward(jnp.dot(normed2, w_gate, precision=exact_result))
    up_pre = narrow_backward(jnp.dot(normed2, w_up, precision=exact_result))
    hidden = narrow_precision(jax.nn.silu(gate_pre) * up_pre)
    return middle + narrow_backward(jnp.dot(hidden, w_down, precision=exact_result))

def reference(tokens, lengths, deal, attn_gain, w_q, key_weight, value_weight, query_norm_gain, k_gain, w_o, mlp_gain, w_gate, w_up, w_down, out_cotangent):
    tok_ids = jnp.arange(GROUP_TOK, dtype=jnp.int32)
    starts = (jnp.cumsum(lengths, axis=1) - lengths).astype(jnp.int32)
    segment_initial = lax.optimization_barrier(jnp.max(jnp.where(tok_ids[None, :, None] >= starts[:, None, :], starts[:, None, :], 0), axis=2)).astype(jnp.int32)
    token_position = (tok_ids[None, :] - segment_initial).astype(jnp.int32)
    dealt_index = jax.vmap(dealt_rows)(deal)
    params = tuple((member.astype(jnp.float32) for member in (attn_gain, w_q, key_weight, value_weight, query_norm_gain, k_gain, w_o, mlp_gain, w_gate, w_up, w_down)))

    def whole_layer(token_values, weight_values):
        return lax.map(lambda group_args: jnp.take(group_layer(weight_values, group_args[0], group_args[1], group_args[2]), group_args[3], axis=0), (token_values, segment_initial, token_position, dealt_index))
    output, pull_back = jax.vjp(whole_layer, tokens.astype(jnp.float32), params)
    input_grad, weight_grads = pull_back(out_cotangent.astype(jnp.float32))
    return (output.astype(jnp.bfloat16), input_grad, weight_grads[0], weight_grads[4], weight_grads[5], weight_grads[7], weight_grads[1], weight_grads[2], weight_grads[3], weight_grads[6], weight_grads[8], weight_grads[9], weight_grads[10])
```

```python
import math

import jax
import jax.numpy as jnp
from jax import lax
from jax.sharding import Mesh
from jax.sharding import PartitionSpec as P

MODEL_WIDTH = 1024
QUERY_HEADS = 16
KEY_VALUE_HEADS = 8
HEAD_SIZE = 128


eps = 1e-06
theta_base = 1000000.0
negative_filler = -1e30


def root_mean_norm(values, gain_vec):
    return values * lax.rsqrt(jnp.mean(values * values, axis=-1, keepdims=True) + eps) * gain_vec


def rotary_embedding(values, token_position):
    half_width = values.shape[-1] // 2
    frequency = theta_base ** (
        -(jnp.arange(half_width, dtype=jnp.float32) * 2.0) / values.shape[-1]
    )
    angles = token_position.astype(jnp.float32)[:, None] * frequency[None, :]
    cosine = jnp.concatenate([jnp.cos(angles), jnp.cos(angles)], axis=-1)[:, None, :]
    sine_part = jnp.concatenate([jnp.sin(angles), jnp.sin(angles)], axis=-1)[:, None, :]
    turned = jnp.concatenate([-values[..., half_width:], values[..., :half_width]], axis=-1)
    return values * cosine + turned * sine_part


def dot_trans(left_side, right_side):
    return lax.dot_general(
        left_side, right_side, (((1,), (1,)), ((), ())), preferred_element_type=jnp.float32
    )


def outer_rows(left_side, right_side):
    return lax.dot_general(
        left_side, right_side, (((0,), (0,)), ((), ())), preferred_element_type=jnp.float32
    )


def block_plan(piece_rows, local_rows):
    shards = piece_rows // local_rows
    per_block = math.gcd(shards, max(1, 1024 // local_rows))
    return (per_block * local_rows, shards // per_block)


def over_blocks(carried, arrays, local_rows, block_work):
    rows_per_block, count_of_blocks = block_plan(arrays[0].shape[0], local_rows)

    def one_block(turn_index, state_now):
        offset = turn_index * rows_per_block
        parts = tuple(
            (lax.dynamic_slice_in_dim(member, offset, rows_per_block, 0) for member in arrays)
        )
        return block_work(state_now, parts, offset)

    return lax.fori_loop(0, count_of_blocks, one_block, carried)


def segment_begin(tok_ids, starts):
    return jnp.max(jnp.where(tok_ids[:, None] >= starts[None, :], starts[None, :], 0), axis=1)


def general_layer(
    tokens,
    lengths,
    deal,
    attn_gain,
    w_q,
    key_weight,
    value_weight,
    query_norm_gain,
    k_gain,
    w_o,
    mlp_gain,
    w_gate,
    w_up,
    w_down,
    out_cotangent,
):
    local_rows = tokens.shape[1]
    piece_count = lax.axis_size("ctx")
    piece_rows = local_rows // piece_count
    here = lax.axis_index("ctx")
    group_width = QUERY_HEADS // KEY_VALUE_HEADS
    score_scale = HEAD_SIZE ** (-0.5)
    seq_lengths = lengths[0]
    starts = jnp.cumsum(seq_lengths) - seq_lengths
    plan = deal[0]
    devices = jnp.arange(piece_count, dtype=jnp.int32)
    hits = plan[:, :, None] == devices[None, None, :]
    slot_of = jnp.sum(jnp.where(hits, devices[None, :, None], 0), axis=1)
    inner = jnp.arange(piece_rows, dtype=jnp.int32)
    dealt_index = (
        devices[None, :, None] * local_rows
        + jnp.transpose(slot_of)[:, :, None] * piece_rows
        + inner[None, None, :]
    ).reshape(piece_count * local_rows)
    dealt_first = segment_begin(dealt_index, starts)
    tok_index = lax.dynamic_slice_in_dim(dealt_index, here * local_rows, local_rows)
    segment_initial = lax.dynamic_slice_in_dim(dealt_first, here * local_rows, local_rows)
    token_position = tok_index - segment_initial
    own_slots = lax.dynamic_index_in_dim(slot_of, here, 0, keepdims=False)
    own_plan = lax.dynamic_index_in_dim(plan, here, 0, keepdims=False)
    token_pieces = jnp.take(
        tokens[0].reshape(piece_count, piece_rows, MODEL_WIDTH), own_slots, axis=0
    )
    dealt_tok = lax.all_to_all(
        token_pieces, "ctx", split_axis=0, concat_axis=0, tiled=True
    ).reshape(local_rows, MODEL_WIDTH)

    def key_mask(start_row, local_row_count):
        key_identifiers = lax.dynamic_slice_in_dim(dealt_index, start_row, local_row_count)
        return (key_identifiers[None, :] >= segment_initial[:, None]) & (
            key_identifiers[None, :] <= tok_index[:, None]
        )

    def query_mask(start_row, local_row_count):
        query_ids = lax.dynamic_slice_in_dim(dealt_index, start_row, local_row_count)
        first_key = lax.dynamic_slice_in_dim(dealt_first, start_row, local_row_count)
        return (tok_index[None, :] >= first_key[:, None]) & (
            tok_index[None, :] <= query_ids[:, None]
        )

    def fetch_weights():
        attn_set = (
            lax.all_gather(attn_gain, "fsdp", axis=0, tiled=True),
            lax.all_gather(query_norm_gain, "fsdp", axis=0, tiled=True),
            lax.all_gather(k_gain, "fsdp", axis=0, tiled=True),
            lax.all_gather(w_q, "fsdp", axis=0, tiled=True),
            lax.all_gather(key_weight, "fsdp", axis=0, tiled=True),
            lax.all_gather(value_weight, "fsdp", axis=0, tiled=True),
            lax.all_gather(w_o, "fsdp", axis=0, tiled=True),
        )
        mlp_set = (
            lax.all_gather(mlp_gain, "fsdp", axis=0, tiled=True),
            lax.all_gather(w_gate, "fsdp", axis=0, tiled=True),
            lax.all_gather(w_up, "fsdp", axis=0, tiled=True),
            lax.all_gather(w_down, "fsdp", axis=0, tiled=True),
        )
        return (attn_set, mlp_set)

    def forward(attn_set, mlp_set, token_rows):
        a_gain, qn_gain, kn_gain, proj_q, proj_k, proj_v, proj_o = attn_set
        m_gain, proj_gate, proj_up, proj_down = mlp_set
        residual = token_rows.astype(jnp.float32)
        normalized_input = root_mean_norm(residual, a_gain.astype(jnp.float32)).astype(jnp.bfloat16)
        query_prenorm = jnp.dot(
            normalized_input, proj_q, preferred_element_type=jnp.float32
        ).reshape(local_rows, QUERY_HEADS, HEAD_SIZE)
        key_prenorm = jnp.dot(normalized_input, proj_k, preferred_element_type=jnp.float32).reshape(
            local_rows, KEY_VALUE_HEADS, HEAD_SIZE
        )
        value_narrow = jnp.dot(normalized_input, proj_v, preferred_element_type=jnp.float32).astype(
            jnp.bfloat16
        )
        q_heads = (
            rotary_embedding(
                root_mean_norm(query_prenorm, qn_gain.astype(jnp.float32)), token_position
            )
            .astype(jnp.bfloat16)
            .reshape(local_rows, KEY_VALUE_HEADS, group_width, HEAD_SIZE)
        )
        key_narrow = (
            rotary_embedding(
                root_mean_norm(key_prenorm, kn_gain.astype(jnp.float32)), token_position
            )
            .astype(jnp.bfloat16)
            .reshape(local_rows, KEY_VALUE_HEADS * HEAD_SIZE)
        )

        def attend_over_block(state_now, shard_piece, start_row):
            key_segment, value_segment = shard_piece
            local_row_count = key_segment.shape[0]
            allowed = key_mask(start_row, local_row_count)
            row_top, row_total, weighted = state_now
            scores = (
                jnp.einsum(
                    "rkgh,ckh->kgrc",
                    q_heads,
                    key_segment.reshape(local_row_count, KEY_VALUE_HEADS, HEAD_SIZE),
                    preferred_element_type=jnp.float32,
                )
                * score_scale
            )
            scores = jnp.where(allowed, scores, negative_filler)
            new_top = jnp.maximum(row_top, jnp.max(scores, axis=-1))
            rescale = jnp.exp(row_top - new_top)
            weights = jnp.where(allowed, jnp.exp(scores - new_top[..., None]), 0.0)
            row_total = row_total * rescale + jnp.sum(weights, axis=-1)
            weighted = weighted * rescale[..., None] + jnp.einsum(
                "kgrc,ckh->kgrh",
                weights.astype(jnp.bfloat16),
                value_segment.reshape(local_row_count, KEY_VALUE_HEADS, HEAD_SIZE),
                preferred_element_type=jnp.float32,
            )
            return (new_top, row_total, weighted)

        initial = (
            jnp.full((KEY_VALUE_HEADS, group_width, local_rows), negative_filler, jnp.float32),
            jnp.zeros((KEY_VALUE_HEADS, group_width, local_rows), jnp.float32),
            jnp.zeros((KEY_VALUE_HEADS, group_width, local_rows, HEAD_SIZE), jnp.float32),
        )
        row_top, row_total, weighted = over_blocks(
            initial,
            (
                lax.all_gather(key_narrow, "ctx", axis=0, tiled=True),
                lax.all_gather(value_narrow, "ctx", axis=0, tiled=True),
            ),
            local_rows,
            attend_over_block,
        )
        attention_mixed = jnp.transpose(weighted / row_total[..., None], (2, 0, 1, 3)).reshape(
            local_rows, QUERY_HEADS * HEAD_SIZE
        )
        log_total = row_top + jnp.log(row_total)
        mixed_low = attention_mixed.astype(jnp.bfloat16)
        middle = residual + jnp.dot(mixed_low, proj_o, preferred_element_type=jnp.float32)
        normed2 = root_mean_norm(middle, m_gain.astype(jnp.float32)).astype(jnp.bfloat16)
        gate_pre = jnp.dot(normed2, proj_gate, preferred_element_type=jnp.float32)
        up_pre = jnp.dot(normed2, proj_up, preferred_element_type=jnp.float32)
        hidden = (jax.nn.silu(gate_pre) * up_pre).astype(jnp.bfloat16)
        result = middle + jnp.dot(hidden, proj_down, preferred_element_type=jnp.float32)
        return (
            result,
            residual,
            normalized_input,
            query_prenorm,
            key_prenorm,
            value_narrow,
            q_heads,
            key_narrow,
            attention_mixed,
            mixed_low,
            log_total,
            middle,
            normed2,
            gate_pre,
            up_pre,
            hidden,
            attn_set,
            mlp_set,
        )

    first_sets = fetch_weights()
    first_pass = forward(first_sets[0], first_sets[1], dealt_tok)
    again_tok = lax.all_to_all(
        token_pieces, "ctx", split_axis=0, concat_axis=0, tiled=True
    ).reshape(local_rows, MODEL_WIDTH)
    second_sets = fetch_weights()
    kept_pass = forward(second_sets[0], second_sets[1], again_tok)
    (
        unused,
        residual,
        normalized_input,
        query_prenorm,
        key_prenorm,
        value_narrow,
        q_heads,
        key_narrow,
        attention_mixed,
        mixed_low,
        log_total,
        middle,
        normed2,
        gate_pre,
        up_pre,
        hidden,
        attn_set,
        mlp_set,
    ) = kept_pass
    a_gain, qn_gain, kn_gain, proj_q, proj_k, proj_v, proj_o = attn_set
    m_gain, proj_gate, proj_up, proj_down = mlp_set
    grad_low = out_cotangent[0]
    grad_out = grad_low.astype(jnp.float32)
    d_hidden = dot_trans(grad_low, proj_down)
    down_grad = lax.psum_scatter(
        outer_rows(hidden, grad_low).astype(jnp.bfloat16), "fsdp", scatter_dimension=0, tiled=True
    )
    unused, swiglu_back = jax.vjp(
        lambda gate_in, up_in: jax.nn.silu(gate_in) * up_in, gate_pre, up_pre
    )
    d_gate, d_up = swiglu_back(d_hidden)
    d_gate_low = d_gate.astype(jnp.bfloat16)
    d_up_low = d_up.astype(jnp.bfloat16)
    d_normed2 = dot_trans(d_gate_low, proj_gate) + dot_trans(d_up_low, proj_up)
    both_low = jnp.concatenate([d_gate_low, d_up_low], axis=1)
    gate_up_grad = lax.psum_scatter(
        outer_rows(normed2, both_low).astype(jnp.bfloat16), "fsdp", scatter_dimension=0, tiled=True
    )
    unused, norm2_back = jax.vjp(root_mean_norm, middle, m_gain.astype(jnp.float32))
    d_middle_norm, d_m_gain = norm2_back(d_normed2)
    d_middle = grad_out + d_middle_norm
    middle_low = d_middle.astype(jnp.bfloat16)
    mixed_gradient = dot_trans(middle_low, proj_o).astype(jnp.bfloat16)
    out_proj_grad = lax.psum_scatter(
        outer_rows(mixed_low, middle_low).astype(jnp.bfloat16),
        "fsdp",
        scatter_dimension=0,
        tiled=True,
    )
    heads_gradient = mixed_gradient.reshape(local_rows, KEY_VALUE_HEADS, group_width, HEAD_SIZE)
    delta_rows = jnp.sum(
        heads_gradient.astype(jnp.float32)
        * attention_mixed.reshape(local_rows, KEY_VALUE_HEADS, group_width, HEAD_SIZE),
        axis=-1,
    )
    delta_t = jnp.transpose(delta_rows, (1, 2, 0))
    local_keys = key_narrow.reshape(local_rows, KEY_VALUE_HEADS, HEAD_SIZE)
    local_values = value_narrow.reshape(local_rows, KEY_VALUE_HEADS, HEAD_SIZE)

    def query_block(state_now, shard_piece, start_row):
        key_segment, value_segment = shard_piece
        local_row_count = key_segment.shape[0]
        allowed = key_mask(start_row, local_row_count)
        key_row_block = key_segment.reshape(local_row_count, KEY_VALUE_HEADS, HEAD_SIZE)
        scores = (
            jnp.einsum("rkgh,ckh->kgrc", q_heads, key_row_block, preferred_element_type=jnp.float32)
            * score_scale
        )
        probability = jnp.where(allowed, jnp.exp(scores - log_total[..., None]), 0.0)
        d_probs = jnp.einsum(
            "rkgh,ckh->kgrc",
            heads_gradient,
            value_segment.reshape(local_row_count, KEY_VALUE_HEADS, HEAD_SIZE),
            preferred_element_type=jnp.float32,
        )
        d_scores = (probability * (d_probs - delta_t[..., None])).astype(jnp.bfloat16)
        return (
            state_now
            + jnp.einsum(
                "kgrc,ckh->kgrh", d_scores, key_row_block, preferred_element_type=jnp.float32
            )
            * score_scale
        )

    query_grad = over_blocks(
        jnp.zeros((KEY_VALUE_HEADS, group_width, local_rows, HEAD_SIZE), jnp.float32),
        (
            lax.all_gather(key_narrow, "ctx", axis=0, tiled=True),
            lax.all_gather(value_narrow, "ctx", axis=0, tiled=True),
        ),
        local_rows,
        query_block,
    )
    lse_rows = jnp.transpose(log_total, (2, 0, 1)).reshape(local_rows, QUERY_HEADS)
    delta_send = delta_rows.reshape(local_rows, QUERY_HEADS)

    def key_block(state_now, shard_piece, start_row):
        query_segment, output_gradient_segment, logsumexp_segment, delta_segment = shard_piece
        local_row_count = query_segment.shape[0]
        allowed = query_mask(start_row, local_row_count)
        key_grad, value_gradient = state_now
        query_matrix = query_segment.reshape(
            local_row_count, KEY_VALUE_HEADS, group_width, HEAD_SIZE
        )
        gradient_rows = output_gradient_segment.reshape(
            local_row_count, KEY_VALUE_HEADS, group_width, HEAD_SIZE
        )
        scores = (
            jnp.einsum(
                "ckgh,rkh->kgcr", query_matrix, local_keys, preferred_element_type=jnp.float32
            )
            * score_scale
        )
        logsumexp_portion = jnp.transpose(
            logsumexp_segment.reshape(local_row_count, KEY_VALUE_HEADS, group_width), (1, 2, 0)
        )
        delta_portion = jnp.transpose(
            delta_segment.reshape(local_row_count, KEY_VALUE_HEADS, group_width), (1, 2, 0)
        )
        probability = jnp.where(allowed, jnp.exp(scores - logsumexp_portion[..., None]), 0.0)
        value_gradient = value_gradient + jnp.einsum(
            "kgcr,ckgh->rkh",
            probability.astype(jnp.bfloat16),
            gradient_rows,
            preferred_element_type=jnp.float32,
        )
        d_probs = jnp.einsum(
            "ckgh,rkh->kgcr", gradient_rows, local_values, preferred_element_type=jnp.float32
        )
        d_scores = (probability * (d_probs - delta_portion[..., None])).astype(jnp.bfloat16)
        key_grad = (
            key_grad
            + jnp.einsum(
                "kgcr,ckgh->rkh", d_scores, query_matrix, preferred_element_type=jnp.float32
            )
            * score_scale
        )
        return (key_grad, value_gradient)

    key_grad, value_gradient = over_blocks(
        (
            jnp.zeros((local_rows, KEY_VALUE_HEADS, HEAD_SIZE), jnp.float32),
            jnp.zeros((local_rows, KEY_VALUE_HEADS, HEAD_SIZE), jnp.float32),
        ),
        (
            lax.all_gather(
                q_heads.reshape(local_rows, QUERY_HEADS * HEAD_SIZE), "ctx", axis=0, tiled=True
            ),
            lax.all_gather(mixed_gradient, "ctx", axis=0, tiled=True),
            lax.all_gather(lse_rows.astype(jnp.bfloat16), "ctx", axis=0, tiled=True).astype(
                jnp.float32
            ),
            lax.all_gather(delta_send.astype(jnp.bfloat16), "ctx", axis=0, tiled=True).astype(
                jnp.float32
            ),
        ),
        local_rows,
        key_block,
    )
    query_rows = jnp.transpose(query_grad, (2, 0, 1, 3)).reshape(local_rows, QUERY_HEADS, HEAD_SIZE)
    unused, q_back = jax.vjp(
        lambda head_in, gain_in: rotary_embedding(root_mean_norm(head_in, gain_in), token_position),
        query_prenorm,
        qn_gain.astype(jnp.float32),
    )
    d_q_pre, d_qn_gain = q_back(query_rows)
    unused, k_back = jax.vjp(
        lambda head_in, gain_in: rotary_embedding(root_mean_norm(head_in, gain_in), token_position),
        key_prenorm,
        kn_gain.astype(jnp.float32),
    )
    key_prenorm_gradient, d_kn_gain = k_back(key_grad)
    dq_low = d_q_pre.reshape(local_rows, QUERY_HEADS * HEAD_SIZE).astype(jnp.bfloat16)
    key_gradient_narrow = key_prenorm_gradient.reshape(
        local_rows, KEY_VALUE_HEADS * HEAD_SIZE
    ).astype(jnp.bfloat16)
    value_gradient_narrow = value_gradient.reshape(local_rows, KEY_VALUE_HEADS * HEAD_SIZE).astype(
        jnp.bfloat16
    )
    d_normed = (
        dot_trans(dq_low, proj_q)
        + dot_trans(key_gradient_narrow, proj_k)
        + dot_trans(value_gradient_narrow, proj_v)
    )
    qkv_low = jnp.concatenate([dq_low, key_gradient_narrow, value_gradient_narrow], axis=1)
    qkv_grad = lax.psum_scatter(
        outer_rows(normalized_input, qkv_low).astype(jnp.bfloat16),
        "fsdp",
        scatter_dimension=0,
        tiled=True,
    )
    unused, norm1_back = jax.vjp(root_mean_norm, residual, a_gain.astype(jnp.float32))
    d_resid_norm, d_a_gain = norm1_back(d_normed)
    input_dealt = d_middle + d_resid_norm
    back_pieces = lax.all_to_all(
        input_dealt.reshape(piece_count, piece_rows, MODEL_WIDTH).astype(jnp.bfloat16),
        "ctx",
        split_axis=0,
        concat_axis=0,
        tiled=True,
    ).astype(jnp.float32)
    input_grad = jnp.take(back_pieces, own_plan, axis=0).reshape(local_rows, MODEL_WIDTH)
    gain_parts = (
        lax.psum_scatter(d_a_gain, "fsdp", scatter_dimension=0, tiled=True),
        lax.psum_scatter(d_qn_gain, "fsdp", scatter_dimension=0, tiled=True),
        lax.psum_scatter(d_kn_gain, "fsdp", scatter_dimension=0, tiled=True),
        lax.psum_scatter(d_m_gain, "fsdp", scatter_dimension=0, tiled=True),
    )
    totals = (
        lax.psum(gain_parts[0].astype(jnp.bfloat16), "ctx").astype(jnp.float32),
        lax.psum(gain_parts[1].astype(jnp.bfloat16), "ctx").astype(jnp.float32),
        lax.psum(gain_parts[2].astype(jnp.bfloat16), "ctx").astype(jnp.float32),
        lax.psum(gain_parts[3].astype(jnp.bfloat16), "ctx").astype(jnp.float32),
        lax.psum(qkv_grad, "ctx").astype(jnp.float32),
        lax.psum(out_proj_grad, "ctx").astype(jnp.float32),
        lax.psum(gate_up_grad, "ctx").astype(jnp.float32),
        lax.psum(down_grad, "ctx").astype(jnp.float32),
    )
    q_width = QUERY_HEADS * HEAD_SIZE
    key_value_width = KEY_VALUE_HEADS * HEAD_SIZE
    qkv_total = totals[4]
    gate_up_total = totals[6]
    ff_width = w_gate.shape[1]
    return (
        first_pass[0].astype(jnp.bfloat16)[None],
        input_grad[None],
        totals[0],
        totals[1],
        totals[2],
        totals[3],
        qkv_total[:, :q_width],
        qkv_total[:, q_width : q_width + key_value_width],
        qkv_total[:, q_width + key_value_width :],
        totals[5],
        gate_up_total[:, :ff_width],
        gate_up_total[:, ff_width:],
        totals[7],
    )


CTX = ("z", "y")
FSDP = ("x", "core")


def norm_back(values, gain_vec, grad):
    scale = lax.rsqrt(jnp.mean(values * values, axis=-1, keepdims=True) + eps)
    inner = gain_vec * grad
    d_values = scale * inner - values * (scale * scale * scale) * jnp.mean(
        values * inner, axis=-1, keepdims=True
    )
    return d_values, grad * values * scale


def half_turn(values):
    half = values.shape[-1] // 2
    return jnp.concatenate([-values[..., half:], values[..., :half]], axis=-1)


def rope_tables(token_position):
    half = HEAD_SIZE // 2
    frequency = theta_base ** (-(jnp.arange(half, dtype=jnp.float32) * 2.0) / HEAD_SIZE)
    angles = token_position.astype(jnp.float32)[:, None] * frequency[None, :]
    cosine, sine = jnp.cos(angles), jnp.sin(angles)
    return jnp.concatenate([cosine, cosine], axis=1), jnp.concatenate([sine, sine], axis=1)


def dot(a, b):
    return jnp.dot(a, b, preferred_element_type=jnp.float32)


def low(a):
    return a.astype(jnp.bfloat16)


def gather_ctx(block):
    return lax.all_gather(block, CTX, axis=0, tiled=True)


def gather_fsdp(block):
    return lax.all_gather(block, FSDP, axis=0, tiled=True)


def gather_quad(block):
    return lax.all_gather(block, ("y", "core"), axis=0, tiled=True)


def fast_layer(
    tokens,
    lengths,
    deal,
    attn_gain,
    w_q,
    key_weight,
    value_weight,
    query_norm_gain,
    k_gain,
    w_o,
    mlp_gain,
    w_gate,
    w_up,
    w_down,
    out_cotangent,
):
    rows = tokens.shape[1]
    slots = lax.axis_size(CTX)
    piece = rows // slots
    count = rows * slots
    here = lax.axis_index(CTX)
    y, core = lax.axis_index("y"), lax.axis_index("core")
    x = lax.axis_index("x")
    ff_shard = w_down.shape[0]
    ff_half = ff_shard // 2
    width = HEAD_SIZE * 2

    starts = jnp.cumsum(lengths[0]) - lengths[0]
    ids = jnp.arange(count, dtype=jnp.int32)
    first = segment_begin(ids, starts)
    cosine, sine = rope_tables(ids - first)
    plan = deal[0]
    devices = jnp.arange(slots, dtype=jnp.int32)
    slot_of = jnp.sum(
        jnp.where(plan[:, :, None] == devices[None, None, :], devices[None, :, None], 0), axis=1
    )
    dealt_index = (
        devices[None, :, None] * rows
        + jnp.transpose(slot_of)[:, :, None] * piece
        + jnp.arange(piece, dtype=jnp.int32)[None, None, :]
    ).reshape(count)
    to_dealt = low(dealt_index[:, None] == ids[None, :])

    packed_gain = jnp.concatenate([attn_gain, mlp_gain, query_norm_gain, k_gain])[None]
    gains = gather_fsdp(packed_gain).astype(jnp.float32)
    a_gain = gains[:, :256].reshape(-1)
    m_gain = gains[:, 256:512].reshape(-1)
    q_gain = gains[:, 512:544].reshape(-1)
    k_gain_all = gains[:, 544:576].reshape(-1)
    qkv_own = jnp.concatenate(
        [
            lax.dynamic_slice_in_dim(w_q, here * width, width, 1),
            lax.dynamic_slice_in_dim(key_weight, here * HEAD_SIZE, HEAD_SIZE, 1),
            lax.dynamic_slice_in_dim(value_weight, here * HEAD_SIZE, HEAD_SIZE, 1),
        ],
        axis=1,
    )
    all_tokens = gather_ctx(tokens[0])
    w_qkv = gather_fsdp(qkv_own)
    values = all_tokens.astype(jnp.float32)
    normed = low(root_mean_norm(values, a_gain))
    qkv = dot(normed, w_qkv)
    q_pre = qkv[:, :width].reshape(count, 2, HEAD_SIZE)
    k_pre = qkv[:, width : width + HEAD_SIZE]
    v_low = low(qkv[:, width + HEAD_SIZE :])

    def rope(v, cos, sin):
        return v * cos + half_turn(v) * sin

    q_low = low(rope(root_mean_norm(q_pre, q_gain), cosine[:, None], sine[:, None]))
    k_low = low(rope(root_mean_norm(k_pre, k_gain_all), cosine, sine))
    allowed = (ids[None, :] >= first[:, None]) & (ids[None, :] <= ids[:, None])
    scale = HEAD_SIZE**-0.5
    scores = jnp.einsum("tgh,uh->gtu", q_low, k_low, preferred_element_type=jnp.float32) * scale
    scores = jnp.where(allowed, scores, negative_filler)
    top = jnp.max(scores, axis=-1, keepdims=True)
    weights = jnp.exp(scores - top)
    total = jnp.sum(weights, axis=-1, keepdims=True)
    log_total = top + jnp.log(total)
    mixed = (
        jnp.einsum("gtu,uh->gth", low(weights), v_low, preferred_element_type=jnp.float32) / total
    )
    mixed_heads = low(jnp.transpose(mixed, (1, 0, 2)).reshape(count, width))
    mixed_out = low(dot(to_dealt, mixed_heads)).reshape(slots, rows, width)
    mixed_in = lax.all_to_all(mixed_out, CTX, 0, 0, tiled=True)
    mixed_low = jnp.transpose(mixed_in, (1, 0, 2)).reshape(rows, slots * width)

    own_rows = lax.dynamic_slice_in_dim(to_dealt, here * rows, rows, 0)
    residual = dot(own_rows, all_tokens)
    full_o = gather_fsdp(w_o)
    middle = residual + dot(mixed_low, full_o)
    normed2 = low(root_mean_norm(middle, m_gain))

    def quarter_cols(w, c):
        return jnp.concatenate(
            [
                lax.dynamic_slice_in_dim(w, (2 * xs + c) * ff_shard + y * ff_half, ff_half, 1)
                for xs in range(2)
            ],
            axis=1,
        )

    sides = jnp.stack(
        [
            jnp.concatenate([quarter_cols(w_gate, c), quarter_cols(w_up, c)], axis=1)
            for c in range(2)
        ]
    )
    sides = lax.all_to_all(sides, "core", 0, 0, tiled=True)
    w_gu = lax.all_gather(sides, "x", axis=0, tiled=True).reshape(-1, 4 * ff_half)
    down_own = lax.dynamic_slice_in_dim(w_down, y * ff_half, ff_half, 0)
    w_dn = lax.all_gather(down_own, "x", axis=0, tiled=True)
    quad_n = gather_quad(normed2)
    quad_g = gather_quad(out_cotangent[0])
    gate_up = dot(quad_n, w_gu)
    gate, up = gate_up[:, : 2 * ff_half], gate_up[:, 2 * ff_half :]
    sig = 1.0 / (1.0 + jnp.exp(-gate))
    silu = gate * sig
    hidden = low(silu * up)
    partial_out = low(dot(hidden, w_dn))
    out_sum = lax.psum_scatter(partial_out, ("y", "core"), scatter_dimension=0, tiled=True)
    output = low(middle + out_sum.astype(jnp.float32))

    d_hidden = dot_trans(quad_g, w_dn)
    d_gate = low(d_hidden * up * (sig * (1.0 + gate * (1.0 - sig))))
    d_up = low(d_hidden * silu)
    d_gu = jnp.concatenate([d_gate, d_up], axis=1)
    dn2_part = low(dot_trans(d_gu, w_gu))
    d_normed2 = lax.psum_scatter(
        dn2_part, ("y", "core"), scatter_dimension=0, tiled=True
    ).astype(jnp.float32)
    grad_gu = low(outer_rows(quad_n, d_gu))
    grad_dn = low(outer_rows(hidden, quad_g))
    dx2, dg2 = norm_back(middle, m_gain, d_normed2)
    d_middle = out_cotangent[0].astype(jnp.float32) + dx2
    middle_low = low(d_middle)
    d_mixed_tok = low(dot_trans(middle_low, full_o))
    dm_out = jnp.transpose(d_mixed_tok.reshape(rows, slots, width), (1, 0, 2))
    dm_in = lax.all_to_all(dm_out, CTX, 0, 0, tiled=True).reshape(count, width)
    d_mixed = low(
        lax.dot_general(
            to_dealt, dm_in, (((0,), (0,)), ((), ())), preferred_element_type=jnp.float32
        )
    )
    grad_o = low(outer_rows(mixed_low, middle_low))
    d_heads = d_mixed.reshape(count, 2, HEAD_SIZE)
    delta = jnp.sum(
        jnp.transpose(d_heads, (1, 0, 2)).astype(jnp.float32) * mixed, axis=-1, keepdims=True
    )
    probs = jnp.where(allowed, jnp.exp(scores - log_total), 0.0)
    d_probs = jnp.einsum("tgh,uh->gtu", d_heads, v_low, preferred_element_type=jnp.float32)
    d_scores = low(probs * (d_probs - delta))
    d_v = jnp.einsum("gtu,tgh->uh", low(probs), d_heads, preferred_element_type=jnp.float32)
    d_q = jnp.einsum("gtu,uh->tgh", d_scores, k_low, preferred_element_type=jnp.float32) * scale
    d_k = jnp.einsum("gtu,tgh->uh", d_scores, q_low, preferred_element_type=jnp.float32) * scale

    def rope_back(v, cos, sin):
        return v * cos - half_turn(v * sin)

    d_q_pre, dg_q = norm_back(q_pre, q_gain, rope_back(d_q, cosine[:, None], sine[:, None]))
    d_k_pre, dg_k = norm_back(k_pre, k_gain_all, rope_back(d_k, cosine, sine))
    d_qkv = jnp.concatenate([low(d_q_pre.reshape(count, width)), low(d_k_pre), low(d_v)], axis=1)
    dn_part = low(dot_trans(d_qkv, w_qkv))
    d_normed = lax.psum_scatter(dn_part, CTX, scatter_dimension=0, tiled=True).astype(jnp.float32)
    grad_qkv = low(outer_rows(normed, d_qkv))

    back = lax.all_to_all(middle_low.reshape(slots, piece, MODEL_WIDTH), CTX, 0, 0, tiled=True)
    own_plan = lax.dynamic_index_in_dim(plan, here, 0, keepdims=False)
    d_middle_given = jnp.take(back, own_plan, axis=0).reshape(rows, MODEL_WIDTH)
    dx1, dg1 = norm_back(tokens[0].astype(jnp.float32), a_gain, d_normed)
    input_grad = d_middle_given.astype(jnp.float32) + dx1

    gain_sums = lax.psum(
        jnp.concatenate(
            [
                jnp.sum(dg1, axis=0).reshape(4, 256),
                jnp.sum(dg2, axis=0).reshape(4, 256),
                jnp.sum(dg_q, axis=(0, 1)).reshape(4, 32),
                jnp.sum(dg_k, axis=0).reshape(4, 32),
            ],
            axis=1,
        ),
        ("z", "y", "x", "core"),
    )
    own_gain = lax.dynamic_index_in_dim(gain_sums, 2 * x + core, 0, keepdims=False)

    qkv_sum = lax.psum_scatter(grad_qkv, FSDP, scatter_dimension=0, tiled=True)
    qkv_all = lax.all_gather(qkv_sum, CTX, axis=0)
    q_all = jnp.transpose(qkv_all[:, :, :width], (1, 0, 2)).reshape(-1, slots * width)
    k_all = jnp.transpose(qkv_all[:, :, width : width + HEAD_SIZE], (1, 0, 2))
    v_all = jnp.transpose(qkv_all[:, :, width + HEAD_SIZE :], (1, 0, 2))
    o_sum = lax.psum(
        lax.psum_scatter(grad_o, FSDP, scatter_dimension=0, tiled=True), CTX
    )
    gu_sum = lax.psum(lax.psum_scatter(grad_gu, "x", scatter_dimension=0, tiled=True), "z")
    gu_pair = lax.all_to_all(
        gu_sum.reshape(2, -1, 4 * ff_half), "core", 0, 0, tiled=True
    )
    gu_all = lax.all_gather(gu_pair, "y", axis=0)
    gu_all = gu_all.reshape(2, 2, -1, 2, 2, ff_half)
    gu_all = jnp.transpose(gu_all, (3, 2, 4, 1, 0, 5)).reshape(2, -1, 8 * ff_half)
    dn_sum = lax.psum(lax.psum_scatter(grad_dn, "x", scatter_dimension=0, tiled=True), "z")
    dn_all = lax.all_gather(dn_sum, "y", axis=0, tiled=True)

    def wide(a):
        return a.astype(jnp.float32)

    return (
        output[None],
        input_grad[None],
        own_gain[:256],
        own_gain[512:544],
        own_gain[544:576],
        own_gain[256:512],
        wide(q_all),
        wide(k_all.reshape(-1, slots * HEAD_SIZE)),
        wide(v_all.reshape(-1, slots * HEAD_SIZE)),
        wide(o_sum),
        wide(gu_all[0]),
        wide(gu_all[1]),
        wide(dn_all),
    )


def solution(mesh):
    devices = mesh.devices
    if devices.shape == (8, 4):
        mesh = Mesh(devices.reshape(4, 2, 2, 2), CTX + FSDP)
        layer, ctx, fsdp = fast_layer, CTX, FSDP
    else:
        layer, ctx, fsdp = general_layer, "ctx", "fsdp"
    wide_rows = P(fsdp, ctx, None)
    return jax.shard_map(
        layer,
        mesh=mesh,
        in_specs=(
            wide_rows,
            P(fsdp, None),
            P(fsdp, None, None),
            P(fsdp),
            P(fsdp, None),
            P(fsdp, None),
            P(fsdp, None),
            P(fsdp),
            P(fsdp),
            P(fsdp, None),
            P(fsdp),
            P(fsdp, None),
            P(fsdp, None),
            P(fsdp, None),
            wide_rows,
        ),
        out_specs=(wide_rows, wide_rows) + (P(fsdp),) * 4 + (P(fsdp, None),) * 7,
        check_vma=False,
    )
```

```python
import math

import jax
import jax.numpy as jnp
from jax import lax
from jax.experimental import pallas as pl
from jax.experimental.pallas import tpu as pltpu
from jax.sharding import Mesh
from jax.sharding import PartitionSpec as P

MODEL_WIDTH = 1024
QUERY_HEADS = 16
KEY_VALUE_HEADS = 8
HEAD_SIZE = 128


eps = 1e-06
theta_base = 1000000.0
negative_filler = -1e30


def root_mean_norm(values, gain_vec):
    return values * lax.rsqrt(jnp.mean(values * values, axis=-1, keepdims=True) + eps) * gain_vec


def rotary_embedding(values, token_position):
    half_width = values.shape[-1] // 2
    frequency = theta_base ** (
        -(jnp.arange(half_width, dtype=jnp.float32) * 2.0) / values.shape[-1]
    )
    angles = token_position.astype(jnp.float32)[:, None] * frequency[None, :]
    cosine = jnp.concatenate([jnp.cos(angles), jnp.cos(angles)], axis=-1)[:, None, :]
    sine_part = jnp.concatenate([jnp.sin(angles), jnp.sin(angles)], axis=-1)[:, None, :]
    turned = jnp.concatenate([-values[..., half_width:], values[..., :half_width]], axis=-1)
    return values * cosine + turned * sine_part


def dot_trans(left_side, right_side):
    return lax.dot_general(
        left_side, right_side, (((1,), (1,)), ((), ())), preferred_element_type=jnp.float32
    )


def outer_rows(left_side, right_side):
    return lax.dot_general(
        left_side, right_side, (((0,), (0,)), ((), ())), preferred_element_type=jnp.float32
    )


def block_plan(piece_rows, local_rows):
    shards = piece_rows // local_rows
    per_block = math.gcd(shards, max(1, 1024 // local_rows))
    return (per_block * local_rows, shards // per_block)


def over_blocks(carried, arrays, local_rows, block_work):
    rows_per_block, count_of_blocks = block_plan(arrays[0].shape[0], local_rows)

    def one_block(turn_index, state_now):
        offset = turn_index * rows_per_block
        parts = tuple(
            (lax.dynamic_slice_in_dim(member, offset, rows_per_block, 0) for member in arrays)
        )
        return block_work(state_now, parts, offset)

    return lax.fori_loop(0, count_of_blocks, one_block, carried)


def segment_begin(tok_ids, starts):
    return jnp.max(jnp.where(tok_ids[:, None] >= starts[None, :], starts[None, :], 0), axis=1)


def general_layer(
    tokens,
    lengths,
    deal,
    attn_gain,
    w_q,
    key_weight,
    value_weight,
    query_norm_gain,
    k_gain,
    w_o,
    mlp_gain,
    w_gate,
    w_up,
    w_down,
    out_cotangent,
):
    local_rows = tokens.shape[1]
    piece_count = lax.axis_size("ctx")
    piece_rows = local_rows // piece_count
    here = lax.axis_index("ctx")
    group_width = QUERY_HEADS // KEY_VALUE_HEADS
    score_scale = HEAD_SIZE ** (-0.5)
    seq_lengths = lengths[0]
    starts = jnp.cumsum(seq_lengths) - seq_lengths
    plan = deal[0]
    devices = jnp.arange(piece_count, dtype=jnp.int32)
    hits = plan[:, :, None] == devices[None, None, :]
    slot_of = jnp.sum(jnp.where(hits, devices[None, :, None], 0), axis=1)
    inner = jnp.arange(piece_rows, dtype=jnp.int32)
    dealt_index = (
        devices[None, :, None] * local_rows
        + jnp.transpose(slot_of)[:, :, None] * piece_rows
        + inner[None, None, :]
    ).reshape(piece_count * local_rows)
    dealt_first = segment_begin(dealt_index, starts)
    tok_index = lax.dynamic_slice_in_dim(dealt_index, here * local_rows, local_rows)
    segment_initial = lax.dynamic_slice_in_dim(dealt_first, here * local_rows, local_rows)
    token_position = tok_index - segment_initial
    own_slots = lax.dynamic_index_in_dim(slot_of, here, 0, keepdims=False)
    own_plan = lax.dynamic_index_in_dim(plan, here, 0, keepdims=False)
    token_pieces = jnp.take(
        tokens[0].reshape(piece_count, piece_rows, MODEL_WIDTH), own_slots, axis=0
    )
    dealt_tok = lax.all_to_all(
        token_pieces, "ctx", split_axis=0, concat_axis=0, tiled=True
    ).reshape(local_rows, MODEL_WIDTH)

    def key_mask(start_row, local_row_count):
        key_identifiers = lax.dynamic_slice_in_dim(dealt_index, start_row, local_row_count)
        return (key_identifiers[None, :] >= segment_initial[:, None]) & (
            key_identifiers[None, :] <= tok_index[:, None]
        )

    def query_mask(start_row, local_row_count):
        query_ids = lax.dynamic_slice_in_dim(dealt_index, start_row, local_row_count)
        first_key = lax.dynamic_slice_in_dim(dealt_first, start_row, local_row_count)
        return (tok_index[None, :] >= first_key[:, None]) & (
            tok_index[None, :] <= query_ids[:, None]
        )

    def fetch_weights():
        attn_set = (
            lax.all_gather(attn_gain, "fsdp", axis=0, tiled=True),
            lax.all_gather(query_norm_gain, "fsdp", axis=0, tiled=True),
            lax.all_gather(k_gain, "fsdp", axis=0, tiled=True),
            lax.all_gather(w_q, "fsdp", axis=0, tiled=True),
            lax.all_gather(key_weight, "fsdp", axis=0, tiled=True),
            lax.all_gather(value_weight, "fsdp", axis=0, tiled=True),
            lax.all_gather(w_o, "fsdp", axis=0, tiled=True),
        )
        mlp_set = (
            lax.all_gather(mlp_gain, "fsdp", axis=0, tiled=True),
            lax.all_gather(w_gate, "fsdp", axis=0, tiled=True),
            lax.all_gather(w_up, "fsdp", axis=0, tiled=True),
            lax.all_gather(w_down, "fsdp", axis=0, tiled=True),
        )
        return (attn_set, mlp_set)

    def forward(attn_set, mlp_set, token_rows):
        a_gain, qn_gain, kn_gain, proj_q, proj_k, proj_v, proj_o = attn_set
        m_gain, proj_gate, proj_up, proj_down = mlp_set
        residual = token_rows.astype(jnp.float32)
        normalized_input = root_mean_norm(residual, a_gain.astype(jnp.float32)).astype(jnp.bfloat16)
        query_prenorm = jnp.dot(
            normalized_input, proj_q, preferred_element_type=jnp.float32
        ).reshape(local_rows, QUERY_HEADS, HEAD_SIZE)
        key_prenorm = jnp.dot(normalized_input, proj_k, preferred_element_type=jnp.float32).reshape(
            local_rows, KEY_VALUE_HEADS, HEAD_SIZE
        )
        value_narrow = jnp.dot(normalized_input, proj_v, preferred_element_type=jnp.float32).astype(
            jnp.bfloat16
        )
        q_heads = (
            rotary_embedding(
                root_mean_norm(query_prenorm, qn_gain.astype(jnp.float32)), token_position
            )
            .astype(jnp.bfloat16)
            .reshape(local_rows, KEY_VALUE_HEADS, group_width, HEAD_SIZE)
        )
        key_narrow = (
            rotary_embedding(
                root_mean_norm(key_prenorm, kn_gain.astype(jnp.float32)), token_position
            )
            .astype(jnp.bfloat16)
            .reshape(local_rows, KEY_VALUE_HEADS * HEAD_SIZE)
        )

        def attend_over_block(state_now, shard_piece, start_row):
            key_segment, value_segment = shard_piece
            local_row_count = key_segment.shape[0]
            allowed = key_mask(start_row, local_row_count)
            row_top, row_total, weighted = state_now
            scores = (
                jnp.einsum(
                    "rkgh,ckh->kgrc",
                    q_heads,
                    key_segment.reshape(local_row_count, KEY_VALUE_HEADS, HEAD_SIZE),
                    preferred_element_type=jnp.float32,
                )
                * score_scale
            )
            scores = jnp.where(allowed, scores, negative_filler)
            new_top = jnp.maximum(row_top, jnp.max(scores, axis=-1))
            rescale = jnp.exp(row_top - new_top)
            weights = jnp.where(allowed, jnp.exp(scores - new_top[..., None]), 0.0)
            row_total = row_total * rescale + jnp.sum(weights, axis=-1)
            weighted = weighted * rescale[..., None] + jnp.einsum(
                "kgrc,ckh->kgrh",
                weights.astype(jnp.bfloat16),
                value_segment.reshape(local_row_count, KEY_VALUE_HEADS, HEAD_SIZE),
                preferred_element_type=jnp.float32,
            )
            return (new_top, row_total, weighted)

        initial = (
            jnp.full((KEY_VALUE_HEADS, group_width, local_rows), negative_filler, jnp.float32),
            jnp.zeros((KEY_VALUE_HEADS, group_width, local_rows), jnp.float32),
            jnp.zeros((KEY_VALUE_HEADS, group_width, local_rows, HEAD_SIZE), jnp.float32),
        )
        row_top, row_total, weighted = over_blocks(
            initial,
            (
                lax.all_gather(key_narrow, "ctx", axis=0, tiled=True),
                lax.all_gather(value_narrow, "ctx", axis=0, tiled=True),
            ),
            local_rows,
            attend_over_block,
        )
        attention_mixed = jnp.transpose(weighted / row_total[..., None], (2, 0, 1, 3)).reshape(
            local_rows, QUERY_HEADS * HEAD_SIZE
        )
        log_total = row_top + jnp.log(row_total)
        mixed_low = attention_mixed.astype(jnp.bfloat16)
        middle = residual + jnp.dot(mixed_low, proj_o, preferred_element_type=jnp.float32)
        normed2 = root_mean_norm(middle, m_gain.astype(jnp.float32)).astype(jnp.bfloat16)
        gate_pre = jnp.dot(normed2, proj_gate, preferred_element_type=jnp.float32)
        up_pre = jnp.dot(normed2, proj_up, preferred_element_type=jnp.float32)
        hidden = (jax.nn.silu(gate_pre) * up_pre).astype(jnp.bfloat16)
        result = middle + jnp.dot(hidden, proj_down, preferred_element_type=jnp.float32)
        return (
            result,
            residual,
            normalized_input,
            query_prenorm,
            key_prenorm,
            value_narrow,
            q_heads,
            key_narrow,
            attention_mixed,
            mixed_low,
            log_total,
            middle,
            normed2,
            gate_pre,
            up_pre,
            hidden,
            attn_set,
            mlp_set,
        )

    first_sets = fetch_weights()
    first_pass = forward(first_sets[0], first_sets[1], dealt_tok)
    again_tok = lax.all_to_all(
        token_pieces, "ctx", split_axis=0, concat_axis=0, tiled=True
    ).reshape(local_rows, MODEL_WIDTH)
    second_sets = fetch_weights()
    kept_pass = forward(second_sets[0], second_sets[1], again_tok)
    (
        unused,
        residual,
        normalized_input,
        query_prenorm,
        key_prenorm,
        value_narrow,
        q_heads,
        key_narrow,
        attention_mixed,
        mixed_low,
        log_total,
        middle,
        normed2,
        gate_pre,
        up_pre,
        hidden,
        attn_set,
        mlp_set,
    ) = kept_pass
    a_gain, qn_gain, kn_gain, proj_q, proj_k, proj_v, proj_o = attn_set
    m_gain, proj_gate, proj_up, proj_down = mlp_set
    grad_low = out_cotangent[0]
    grad_out = grad_low.astype(jnp.float32)
    d_hidden = dot_trans(grad_low, proj_down)
    down_grad = lax.psum_scatter(
        outer_rows(hidden, grad_low).astype(jnp.bfloat16), "fsdp", scatter_dimension=0, tiled=True
    )
    unused, swiglu_back = jax.vjp(
        lambda gate_in, up_in: jax.nn.silu(gate_in) * up_in, gate_pre, up_pre
    )
    d_gate, d_up = swiglu_back(d_hidden)
    d_gate_low = d_gate.astype(jnp.bfloat16)
    d_up_low = d_up.astype(jnp.bfloat16)
    d_normed2 = dot_trans(d_gate_low, proj_gate) + dot_trans(d_up_low, proj_up)
    both_low = jnp.concatenate([d_gate_low, d_up_low], axis=1)
    gate_up_grad = lax.psum_scatter(
        outer_rows(normed2, both_low).astype(jnp.bfloat16), "fsdp", scatter_dimension=0, tiled=True
    )
    unused, norm2_back = jax.vjp(root_mean_norm, middle, m_gain.astype(jnp.float32))
    d_middle_norm, d_m_gain = norm2_back(d_normed2)
    d_middle = grad_out + d_middle_norm
    middle_low = d_middle.astype(jnp.bfloat16)
    mixed_gradient = dot_trans(middle_low, proj_o).astype(jnp.bfloat16)
    out_proj_grad = lax.psum_scatter(
        outer_rows(mixed_low, middle_low).astype(jnp.bfloat16),
        "fsdp",
        scatter_dimension=0,
        tiled=True,
    )
    heads_gradient = mixed_gradient.reshape(local_rows, KEY_VALUE_HEADS, group_width, HEAD_SIZE)
    delta_rows = jnp.sum(
        heads_gradient.astype(jnp.float32)
        * attention_mixed.reshape(local_rows, KEY_VALUE_HEADS, group_width, HEAD_SIZE),
        axis=-1,
    )
    delta_t = jnp.transpose(delta_rows, (1, 2, 0))
    local_keys = key_narrow.reshape(local_rows, KEY_VALUE_HEADS, HEAD_SIZE)
    local_values = value_narrow.reshape(local_rows, KEY_VALUE_HEADS, HEAD_SIZE)

    def query_block(state_now, shard_piece, start_row):
        key_segment, value_segment = shard_piece
        local_row_count = key_segment.shape[0]
        allowed = key_mask(start_row, local_row_count)
        key_row_block = key_segment.reshape(local_row_count, KEY_VALUE_HEADS, HEAD_SIZE)
        scores = (
            jnp.einsum("rkgh,ckh->kgrc", q_heads, key_row_block, preferred_element_type=jnp.float32)
            * score_scale
        )
        probability = jnp.where(allowed, jnp.exp(scores - log_total[..., None]), 0.0)
        d_probs = jnp.einsum(
            "rkgh,ckh->kgrc",
            heads_gradient,
            value_segment.reshape(local_row_count, KEY_VALUE_HEADS, HEAD_SIZE),
            preferred_element_type=jnp.float32,
        )
        d_scores = (probability * (d_probs - delta_t[..., None])).astype(jnp.bfloat16)
        return (
            state_now
            + jnp.einsum(
                "kgrc,ckh->kgrh", d_scores, key_row_block, preferred_element_type=jnp.float32
            )
            * score_scale
        )

    query_grad = over_blocks(
        jnp.zeros((KEY_VALUE_HEADS, group_width, local_rows, HEAD_SIZE), jnp.float32),
        (
            lax.all_gather(key_narrow, "ctx", axis=0, tiled=True),
            lax.all_gather(value_narrow, "ctx", axis=0, tiled=True),
        ),
        local_rows,
        query_block,
    )
    lse_rows = jnp.transpose(log_total, (2, 0, 1)).reshape(local_rows, QUERY_HEADS)
    delta_send = delta_rows.reshape(local_rows, QUERY_HEADS)

    def key_block(state_now, shard_piece, start_row):
        query_segment, output_gradient_segment, logsumexp_segment, delta_segment = shard_piece
        local_row_count = query_segment.shape[0]
        allowed = query_mask(start_row, local_row_count)
        key_grad, value_gradient = state_now
        query_matrix = query_segment.reshape(
            local_row_count, KEY_VALUE_HEADS, group_width, HEAD_SIZE
        )
        gradient_rows = output_gradient_segment.reshape(
            local_row_count, KEY_VALUE_HEADS, group_width, HEAD_SIZE
        )
        scores = (
            jnp.einsum(
                "ckgh,rkh->kgcr", query_matrix, local_keys, preferred_element_type=jnp.float32
            )
            * score_scale
        )
        logsumexp_portion = jnp.transpose(
            logsumexp_segment.reshape(local_row_count, KEY_VALUE_HEADS, group_width), (1, 2, 0)
        )
        delta_portion = jnp.transpose(
            delta_segment.reshape(local_row_count, KEY_VALUE_HEADS, group_width), (1, 2, 0)
        )
        probability = jnp.where(allowed, jnp.exp(scores - logsumexp_portion[..., None]), 0.0)
        value_gradient = value_gradient + jnp.einsum(
            "kgcr,ckgh->rkh",
            probability.astype(jnp.bfloat16),
            gradient_rows,
            preferred_element_type=jnp.float32,
        )
        d_probs = jnp.einsum(
            "ckgh,rkh->kgcr", gradient_rows, local_values, preferred_element_type=jnp.float32
        )
        d_scores = (probability * (d_probs - delta_portion[..., None])).astype(jnp.bfloat16)
        key_grad = (
            key_grad
            + jnp.einsum(
                "kgcr,ckgh->rkh", d_scores, query_matrix, preferred_element_type=jnp.float32
            )
            * score_scale
        )
        return (key_grad, value_gradient)

    key_grad, value_gradient = over_blocks(
        (
            jnp.zeros((local_rows, KEY_VALUE_HEADS, HEAD_SIZE), jnp.float32),
            jnp.zeros((local_rows, KEY_VALUE_HEADS, HEAD_SIZE), jnp.float32),
        ),
        (
            lax.all_gather(
                q_heads.reshape(local_rows, QUERY_HEADS * HEAD_SIZE), "ctx", axis=0, tiled=True
            ),
            lax.all_gather(mixed_gradient, "ctx", axis=0, tiled=True),
            lax.all_gather(lse_rows.astype(jnp.bfloat16), "ctx", axis=0, tiled=True).astype(
                jnp.float32
            ),
            lax.all_gather(delta_send.astype(jnp.bfloat16), "ctx", axis=0, tiled=True).astype(
                jnp.float32
            ),
        ),
        local_rows,
        key_block,
    )
    query_rows = jnp.transpose(query_grad, (2, 0, 1, 3)).reshape(local_rows, QUERY_HEADS, HEAD_SIZE)
    unused, q_back = jax.vjp(
        lambda head_in, gain_in: rotary_embedding(root_mean_norm(head_in, gain_in), token_position),
        query_prenorm,
        qn_gain.astype(jnp.float32),
    )
    d_q_pre, d_qn_gain = q_back(query_rows)
    unused, k_back = jax.vjp(
        lambda head_in, gain_in: rotary_embedding(root_mean_norm(head_in, gain_in), token_position),
        key_prenorm,
        kn_gain.astype(jnp.float32),
    )
    key_prenorm_gradient, d_kn_gain = k_back(key_grad)
    dq_low = d_q_pre.reshape(local_rows, QUERY_HEADS * HEAD_SIZE).astype(jnp.bfloat16)
    key_gradient_narrow = key_prenorm_gradient.reshape(
        local_rows, KEY_VALUE_HEADS * HEAD_SIZE
    ).astype(jnp.bfloat16)
    value_gradient_narrow = value_gradient.reshape(local_rows, KEY_VALUE_HEADS * HEAD_SIZE).astype(
        jnp.bfloat16
    )
    d_normed = (
        dot_trans(dq_low, proj_q)
        + dot_trans(key_gradient_narrow, proj_k)
        + dot_trans(value_gradient_narrow, proj_v)
    )
    qkv_low = jnp.concatenate([dq_low, key_gradient_narrow, value_gradient_narrow], axis=1)
    qkv_grad = lax.psum_scatter(
        outer_rows(normalized_input, qkv_low).astype(jnp.bfloat16),
        "fsdp",
        scatter_dimension=0,
        tiled=True,
    )
    unused, norm1_back = jax.vjp(root_mean_norm, residual, a_gain.astype(jnp.float32))
    d_resid_norm, d_a_gain = norm1_back(d_normed)
    input_dealt = d_middle + d_resid_norm
    back_pieces = lax.all_to_all(
        input_dealt.reshape(piece_count, piece_rows, MODEL_WIDTH).astype(jnp.bfloat16),
        "ctx",
        split_axis=0,
        concat_axis=0,
        tiled=True,
    ).astype(jnp.float32)
    input_grad = jnp.take(back_pieces, own_plan, axis=0).reshape(local_rows, MODEL_WIDTH)
    gain_parts = (
        lax.psum_scatter(d_a_gain, "fsdp", scatter_dimension=0, tiled=True),
        lax.psum_scatter(d_qn_gain, "fsdp", scatter_dimension=0, tiled=True),
        lax.psum_scatter(d_kn_gain, "fsdp", scatter_dimension=0, tiled=True),
        lax.psum_scatter(d_m_gain, "fsdp", scatter_dimension=0, tiled=True),
    )
    totals = (
        lax.psum(gain_parts[0].astype(jnp.bfloat16), "ctx").astype(jnp.float32),
        lax.psum(gain_parts[1].astype(jnp.bfloat16), "ctx").astype(jnp.float32),
        lax.psum(gain_parts[2].astype(jnp.bfloat16), "ctx").astype(jnp.float32),
        lax.psum(gain_parts[3].astype(jnp.bfloat16), "ctx").astype(jnp.float32),
        lax.psum(qkv_grad, "ctx").astype(jnp.float32),
        lax.psum(out_proj_grad, "ctx").astype(jnp.float32),
        lax.psum(gate_up_grad, "ctx").astype(jnp.float32),
        lax.psum(down_grad, "ctx").astype(jnp.float32),
    )
    q_width = QUERY_HEADS * HEAD_SIZE
    key_value_width = KEY_VALUE_HEADS * HEAD_SIZE
    qkv_total = totals[4]
    gate_up_total = totals[6]
    ff_width = w_gate.shape[1]
    return (
        first_pass[0].astype(jnp.bfloat16)[None],
        input_grad[None],
        totals[0],
        totals[1],
        totals[2],
        totals[3],
        qkv_total[:, :q_width],
        qkv_total[:, q_width : q_width + key_value_width],
        qkv_total[:, q_width + key_value_width :],
        totals[5],
        gate_up_total[:, :ff_width],
        gate_up_total[:, ff_width:],
        totals[7],
    )


CTX = ("z", "y")
FSDP = ("x", "core")
VMEM_BYTES = 56 << 20


def norm_back(values, gain_vec, grad):
    scale = lax.rsqrt(jnp.mean(values * values, axis=-1, keepdims=True) + eps)
    inner = gain_vec * grad
    d_values = scale * inner - values * (scale * scale * scale) * jnp.mean(
        values * inner, axis=-1, keepdims=True
    )
    return d_values, grad * values * scale


def half_turn(values):
    half = values.shape[-1] // 2
    return jnp.concatenate([-values[..., half:], values[..., :half]], axis=-1)


def rope_tables(token_position):
    half = HEAD_SIZE // 2
    frequency = theta_base ** (-(jnp.arange(half, dtype=jnp.float32) * 2.0) / HEAD_SIZE)
    angles = token_position.astype(jnp.float32)[:, None] * frequency[None, :]
    cosine, sine = jnp.cos(angles), jnp.sin(angles)
    return jnp.concatenate([cosine, cosine], axis=1), jnp.concatenate([sine, sine], axis=1)


def dot(a, b):
    return jnp.dot(a, b, preferred_element_type=jnp.float32)


def low(a):
    return a.astype(jnp.bfloat16)


def gather_fsdp_plain(block):
    return lax.all_gather(block, FSDP, axis=0, tiled=True)


def over(block, axis):
    return lax.ppermute(block, axis, [(0, 1), (1, 0)])


def half_sum(block, axis):
    place = lax.axis_index(axis)
    got = over(lax.dynamic_index_in_dim(block, 1 - place, 0, keepdims=False), axis)
    own = lax.dynamic_index_in_dim(block, place, 0, keepdims=False)
    return low(own.astype(jnp.float32) + got.astype(jnp.float32))


MESH_ID = pl.DeviceIdType.MESH
LINE = 4


class Net:
    def __init__(self, send, recv):
        self.send, self.recv, self.used = send, recv, 0
        self.z, self.y, self.x, self.core = (lax.axis_index(a) for a in CTX + FSDP)
        self.me = 2 * self.z + self.y
        self.open = []

    def at(self, dz=0, dy=0, dx=0, dc=0):
        return (
            self.z + dz,
            1 - self.y if dy else self.y,
            1 - self.x if dx else self.x,
            1 - self.core if dc else self.core,
        )

    def put(self, src, dst, target, sends=None, recvs=None):
        copy = Copy(self, src, dst, target, sends, recvs)
        self.open.append(copy)
        return copy

    def close(self):
        for copy in self.open:
            copy.arrived()
        for copy in self.open:
            copy.left()


def guarded(condition, action):
    if condition is None:
        action()
    else:
        pl.when(condition)(action)


class Copy:
    def __init__(self, net, src, dst, target, sends, recvs):
        i = net.used
        net.used += 1
        self.sends, self.recvs, self.waited = sends, recvs, False
        self.copy = pltpu.make_async_remote_copy(
            src, dst, net.send.at[i], net.recv.at[i], device_id=target, device_id_type=MESH_ID
        )
        guarded(sends, self.copy.start)

    def arrived(self):
        if not self.waited:
            self.waited = True
            guarded(self.recvs, self.copy.wait_recv)

    def left(self):
        guarded(self.sends, self.copy.wait_send)


def greet(net, kinds):
    barrier = pltpu.get_barrier_semaphore()
    partners = []
    if "z" in kinds:
        partners += [(net.at(dz=1), net.z < LINE - 1), (net.at(dz=-1), net.z > 0)]
    if "y" in kinds:
        partners.append((net.at(dy=1), None))
    if "x" in kinds:
        partners.append((net.at(dx=1), None))
    if "core" in kinds:
        partners.append((net.at(dc=1), None))
    if "ctx" in kinds:
        for k in range(1, 2 * LINE):
            other = lax.rem(net.me + k, 2 * LINE)
            partners.append(((other // 2, lax.rem(other, 2), net.x, net.core), None))
    for target, there in partners:
        guarded(
            there,
            lambda target=target: pl.semaphore_signal(
                barrier, inc=1, device_id=target, device_id_type=MESH_ID
            ),
        )
    ends = 0
    if "z" in kinds:
        ends = (net.z == 0).astype(jnp.int32) + (net.z == LINE - 1).astype(jnp.int32)
    pl.semaphore_wait(barrier, len(partners) - ends)


def drive(*programs):
    live = list(programs)
    while live:
        for program in list(live):
            if next(program, "end") == "end":
                live.remove(program)


def along_line(net, own, view, sides, slot):
    z = net.z
    up = net.put(own, view(slot(z)), net.at(dz=1), z < LINE - 1, z > 0)
    down = net.put(own, view(slot(z)), net.at(dz=-1), z > 0, z < LINE - 1)
    for s in range(1, LINE):
        from_low, from_high = z >= s, z + s <= LINE - 1
        up.arrived()
        low_block, high_block = view(slot(z - s)), view(slot(z + s))
        if s < LINE - 1:
            up = net.put(low_block, low_block, net.at(dz=1), from_low & (z < LINE - 1), z >= s + 1)
        if sides:
            net.put(low_block, low_block, net.at(dy=1), from_low, from_low)
        down.arrived()
        if s < LINE - 1:
            down = net.put(
                high_block, high_block, net.at(dz=-1), from_high & (z > 0), z + s + 1 <= LINE - 1
            )
        if sides:
            net.put(high_block, high_block, net.at(dy=1), from_high, from_high)
        yield


def gather_line_first(net, own, view):
    net.put(own, view(net.me), net.at(dy=1))
    yield from along_line(net, own, view, True, lambda z: 2 * z + net.y)


def gather_side_first(net, own, view):
    side = net.put(own, view(net.me), net.at(dy=1))
    first = along_line(net, own, view, False, lambda z: 2 * z + net.y)
    yield next(first)
    side.arrived()
    other = view(net.me + 1 - 2 * net.y)
    second = along_line(net, other, view, False, lambda z: 2 * z + 1 - net.y)
    for _ in second:
        next(first, None)
        yield


def gather_ctx_programs(net, own, out, cut):
    rows = own.shape[0]
    programs = [
        gather_line_first(
            net, own.at[pl.ds(0, cut)], lambda slot: out.at[slot, pl.ds(0, cut)]
        )
    ]
    if cut < rows:
        rest = pl.ds(cut, rows - cut)
        programs.append(gather_side_first(net, own.at[rest], lambda slot: out.at[slot, rest]))
    return programs


def gather_fsdp(net, own, out):
    f = 2 * net.x + net.core
    net.put(own, out.at[f], net.at(dc=1))
    over = net.put(own, out.at[f], net.at(dx=1))
    yield
    yield
    yield
    over.arrived()
    far = out.at[2 * (1 - net.x) + net.core]
    net.put(far, far, net.at(dc=1))
    yield


def gather_quad(net, own, out):
    q = 2 * net.y + net.core
    net.put(own, out.at[q], net.at(dc=1))
    over = net.put(own, out.at[q], net.at(dy=1))
    yield
    over.arrived()
    far = out.at[2 * (1 - net.y) + net.core]
    net.put(far, far, net.at(dc=1))
    yield


def swap_ctx(net, blocks, out):
    for k in range(1, 2 * LINE):
        other = lax.rem(net.me + k, 2 * LINE)
        net.put(
            blocks.at[other], out.at[net.me], (other // 2, lax.rem(other, 2), net.x, net.core)
        )
    yield


def own_copies(pairs, sem):
    copies = [pltpu.make_async_copy(src, dst, sem.at[i]) for i, (src, dst) in enumerate(pairs)]
    for copy in copies:
        copy.start()
    return copies


def net_call(body, outs, args, copies, locals_, number, scratch=(), vmem=()):
    def kernel(*refs):
        *rest, send, recv, local = refs
        net = Net(send, recv)
        body(net, local, *rest)
        assert net.used <= copies, net.used

    any_space = pl.BlockSpec(memory_space=pl.ANY)
    in_vmem = pl.BlockSpec(memory_space=pltpu.VMEM)
    count = len(args)
    return pl.pallas_call(
        kernel,
        out_shape=outs,
        in_specs=[in_vmem if i in vmem else any_space for i in range(count)],
        out_specs=[in_vmem if count + i in vmem else any_space for i in range(len(outs))],
        scratch_shapes=list(scratch)
        + [
            pltpu.SemaphoreType.DMA((copies,)),
            pltpu.SemaphoreType.DMA((copies,)),
            pltpu.SemaphoreType.DMA((max(1, locals_),)),
        ],
        compiler_params=pltpu.CompilerParams(
            collective_id=number, has_side_effects=True, vmem_limit_bytes=VMEM_BYTES
        ),
    )(*args)


def shape_of(*dims, kind=jnp.bfloat16):
    return jax.ShapeDtypeStruct(dims, kind)


def gather_first(tokens, w_qkv, gains):
    rows = tokens.shape[0]

    def body(net, local, tok, wts, gns, tok_all, wts_all, gns_all):
        greet(net, ("z", "y", "x", "core"))
        f = 2 * net.x + net.core
        mine = own_copies(
            [(tok, tok_all.at[net.me]), (wts, wts_all.at[f]), (gns, gns_all.at[f])], local
        )
        drive(
            *gather_ctx_programs(net, tok, tok_all, rows * 4 // 5),
            gather_fsdp(net, wts, wts_all),
            gather_fsdp(net, gns, gns_all),
        )
        for copy in mine:
            copy.wait()
        net.close()

    return net_call(
        body,
        [
            shape_of(2 * LINE, *tokens.shape),
            shape_of(4, *w_qkv.shape),
            shape_of(4, *gains.shape),
        ],
        [tokens, w_qkv, gains],
        40,
        3,
        0,
    )


def swap_heads(blocks, number):
    def body(net, local, src, out):
        greet(net, ("ctx",))
        mine = own_copies([(src.at[net.me], out.at[net.me])], local)
        drive(swap_ctx(net, src, out))
        mine[0].wait()
        net.close()

    return net_call(body, [shape_of(*blocks.shape)], [blocks], 8, 1, number)[0]


def swap_two(first, second, number):
    def body(net, local, a, b, a_out, b_out):
        greet(net, ("ctx",))
        mine = own_copies(
            [(a.at[net.me], a_out.at[net.me]), (b.at[net.me], b_out.at[net.me])], local
        )
        drive(swap_ctx(net, a, a_out), swap_ctx(net, b, b_out))
        for copy in mine:
            copy.wait()
        net.close()

    return net_call(
        body, [shape_of(*first.shape), shape_of(*second.shape)], [first, second], 16, 2, number
    )


def gather_four(block, number):
    def body(net, local, own, out):
        greet(net, ("y", "core"))
        mine = own_copies([(own, out.at[2 * net.y + net.core])], local)
        drive(gather_quad(net, own, out))
        mine[0].wait()
        net.close()

    return net_call(body, [shape_of(4, *block.shape)], [block], 8, 1, number)[0]


def scatter_four(parts, number):
    _, rows, cols = parts.shape

    def body(net, local, src, out, from_core, near, from_side):
        greet(net, ("y", "core"))
        own, beside = 2 * net.y + net.core, 2 * net.y + 1 - net.core
        far, far_beside = 2 * (1 - net.y) + net.core, 2 * (1 - net.y) + 1 - net.core
        one = net.put(src.at[far_beside], from_core.at[0], net.at(dc=1))
        two = net.put(src.at[beside], from_core.at[1], net.at(dc=1))
        one.arrived()
        near[...] = low(src[far].astype(jnp.float32) + from_core[0].astype(jnp.float32))
        side = net.put(near, from_side, net.at(dy=1))
        two.arrived()
        out[...] = src[own].astype(jnp.float32) + from_core[1].astype(jnp.float32)
        side.arrived()
        out[...] += from_side[...].astype(jnp.float32)
        net.close()

    block = (rows, cols)
    return net_call(
        body,
        [shape_of(*block, kind=jnp.float32)],
        [parts],
        4,
        0,
        number,
        scratch=[
            pltpu.VMEM((2, *block), jnp.bfloat16),
            pltpu.VMEM(block, jnp.bfloat16),
            pltpu.VMEM(block, jnp.bfloat16),
        ],
        vmem=(0, 1),
    )[0]


def sum_line(net, held, send_up, send_down, got_up, got_down, ready):
    z = net.z
    ups, downs = [], []

    def fill(send, got, block, t, first):
        def alone():
            send[t] = low(held[block])

        def added():
            send[t] = low(held[block] + got[t - 1].astype(jnp.float32))

        return alone if first else added

    for t in range(LINE - 1):
        ready(t)
        to_up, to_down = LINE - 1 - t + z, z - LINE + 1 + t
        up_on, down_on = (z <= t) & (z < LINE - 1), (z >= LINE - 1 - t) & (z > 0)
        pl.when(z == 0)(fill(send_up, got_up, to_up, t, True))
        pl.when(z == LINE - 1)(fill(send_down, got_down, to_down, t, True))
        if t:
            pl.when(up_on & (z >= 1))(fill(send_up, got_up, to_up, t, False))
            pl.when(down_on & (z <= LINE - 2))(fill(send_down, got_down, to_down, t, False))
        ups.append(
            net.put(
                send_up.at[t], got_up.at[t], net.at(dz=1), up_on, (z >= 1) & (z - 1 <= t)
            )
        )
        downs.append(
            net.put(
                send_down.at[t],
                got_down.at[t],
                net.at(dz=-1),
                down_on,
                (z <= LINE - 2) & (z + 1 >= LINE - 1 - t),
            )
        )
        yield
        ups[t].arrived()
        downs[t].arrived()
    ready(LINE - 1)
    last = LINE - 2

    def add_up():
        held[z] += got_up[last].astype(jnp.float32)

    def add_down():
        held[z] += got_down[last].astype(jnp.float32)

    pl.when(z >= 1)(add_up)
    pl.when(z <= LINE - 2)(add_down)
    yield


def far_first(z):
    return [
        jnp.where(z < 2, 3, 0),
        jnp.where(z < 2, 2, 1),
        z + 1 - 2 * lax.rem(z, 2),
        z,
    ]


def line_scratch(rows, cols):
    line = pltpu.VMEM((LINE - 1, rows, cols), jnp.bfloat16)
    return [pltpu.VMEM((LINE, rows, cols), jnp.float32), line, line, line, line]


def sum_sides(net, src, from_side, line):
    z, y = net.z, net.y
    held = line[0]
    order = far_first(z)
    sides = [net.put(src.at[2 * k + 1 - y], from_side.at[k], net.at(dy=1)) for k in order]

    def ready(t):
        k = order[t]
        sides[t].arrived()
        held[k] = src[2 * k + y].astype(jnp.float32) + from_side[k].astype(jnp.float32)

    yield from sum_line(net, *line, ready)


def scatter_ctx(parts, number):
    _, rows, cols = parts.shape

    def body(net, local, src, out, from_side, *line):
        greet(net, ("z", "y"))
        drive(sum_sides(net, src, from_side, line))
        out[...] = line[0][net.z]
        net.close()

    return net_call(
        body,
        [shape_of(rows, cols, kind=jnp.float32)],
        [parts],
        12,
        0,
        number,
        scratch=[pltpu.VMEM((LINE, rows, cols), jnp.bfloat16)] + line_scratch(rows, cols),
        vmem=(0, 1),
    )[0]


def sum_and_gather(gate_up, down, out_proj, heads, number):
    _, _, gu_rows, gu_cols = gate_up.shape
    dn_rows, dn_cols = down.shape[1:]
    o_rows, o_cols = out_proj.shape[1:]

    def body(net, local, gu, dn, op, hd, gu_all, dn_all, op_all, hd_all, *scratch):
        gu_line, dn_line, op_line = scratch[:5], scratch[5:10], scratch[10:15]
        op_side, gu_low, gu_pair, dn_low, op_low = scratch[15:]
        greet(net, ("z", "y", "core"))
        z, core = net.z, net.core
        mine = own_copies([(hd, hd_all.at[net.me])], local)

        def gu_ready(t):
            k = far_first(z)[t]
            for c in range(2):
                gu_line[0][k, pl.ds(c * gu_rows, gu_rows)] = gu[k, c].astype(jnp.float32)

        def dn_ready(t):
            k = far_first(z)[t]
            dn_line[0][k] = dn[k].astype(jnp.float32)

        drive(
            sum_line(net, *gu_line, gu_ready),
            sum_line(net, *dn_line, dn_ready),
            sum_sides(net, op, op_side, op_line),
        )
        dn_low[...] = low(dn_line[0][z])
        op_low[...] = low(op_line[0][z])
        for c in range(2):
            gu_low[c] = low(gu_line[0][z, pl.ds(c * gu_rows, gu_rows)])
        swap = net.put(gu_low.at[1 - core], gu_pair.at[core], net.at(dc=1))
        gu_pair[core] = gu_low[core]
        swap.arrived()
        rest = own_copies(
            [
                (gu_pair, gu_all.at[net.me]),
                (dn_low, dn_all.at[net.me]),
                (op_low, op_all.at[net.me]),
            ],
            local.at[pl.ds(1, 3)],
        )
        drive(
            gather_line_first(net, gu_pair, lambda slot: gu_all.at[slot]),
            gather_line_first(net, dn_low, lambda slot: dn_all.at[slot]),
            gather_line_first(net, op_low, lambda slot: op_all.at[slot]),
            gather_side_first(net, hd, lambda slot: hd_all.at[slot]),
        )
        for copy in mine + rest:
            copy.wait()
        net.close()

    return net_call(
        body,
        [
            shape_of(2 * LINE, 2, gu_rows, gu_cols),
            shape_of(2 * LINE, dn_rows, dn_cols),
            shape_of(2 * LINE, o_rows, o_cols),
            shape_of(2 * LINE, *heads.shape),
        ],
        [gate_up, down, out_proj, heads],
        96,
        4,
        number,
        scratch=line_scratch(2 * gu_rows, gu_cols)
        + line_scratch(dn_rows, dn_cols)
        + line_scratch(o_rows, o_cols)
        + [
            pltpu.VMEM((LINE, o_rows, o_cols), jnp.bfloat16),
            pltpu.VMEM((2, gu_rows, gu_cols), jnp.bfloat16),
            pltpu.VMEM((2, gu_rows, gu_cols), jnp.bfloat16),
            pltpu.VMEM((dn_rows, dn_cols), jnp.bfloat16),
            pltpu.VMEM((o_rows, o_cols), jnp.bfloat16),
        ],
        vmem=(0, 1, 2),
    )


def fast_layer(
    tokens,
    lengths,
    deal,
    attn_gain,
    w_q,
    key_weight,
    value_weight,
    query_norm_gain,
    k_gain,
    w_o,
    mlp_gain,
    w_gate,
    w_up,
    w_down,
    out_cotangent,
):
    rows = tokens.shape[1]
    slots = lax.axis_size(CTX)
    piece = rows // slots
    count = rows * slots
    here = lax.axis_index(CTX)
    y, core = lax.axis_index("y"), lax.axis_index("core")
    x = lax.axis_index("x")
    ff_shard = w_down.shape[0]
    ff_half = ff_shard // 2
    width = HEAD_SIZE * 2

    starts = jnp.cumsum(lengths[0]) - lengths[0]
    ids = jnp.arange(count, dtype=jnp.int32)
    first = segment_begin(ids, starts)
    cosine, sine = rope_tables(ids - first)
    plan = deal[0]
    devices = jnp.arange(slots, dtype=jnp.int32)
    slot_of = jnp.sum(
        jnp.where(plan[:, :, None] == devices[None, None, :], devices[None, :, None], 0), axis=1
    )
    dealt_index = (
        devices[None, :, None] * rows
        + jnp.transpose(slot_of)[:, :, None] * piece
        + jnp.arange(piece, dtype=jnp.int32)[None, None, :]
    ).reshape(count)
    to_dealt = low(dealt_index[:, None] == ids[None, :])

    packed_gain = jnp.concatenate([attn_gain, mlp_gain, query_norm_gain, k_gain])[None]
    qkv_own = jnp.concatenate(
        [
            lax.dynamic_slice_in_dim(w_q, here * width, width, 1),
            lax.dynamic_slice_in_dim(key_weight, here * HEAD_SIZE, HEAD_SIZE, 1),
            lax.dynamic_slice_in_dim(value_weight, here * HEAD_SIZE, HEAD_SIZE, 1),
        ],
        axis=1,
    )
    all_tokens, w_qkv, gains = gather_first(tokens[0], qkv_own, jnp.tile(packed_gain, (16, 1)))
    all_tokens = all_tokens.reshape(count, MODEL_WIDTH)
    w_qkv = w_qkv.reshape(MODEL_WIDTH, -1)
    gains = gains[:, 0].astype(jnp.float32)
    a_gain = gains[:, :256].reshape(-1)
    m_gain = gains[:, 256:512].reshape(-1)
    q_gain = gains[:, 512:544].reshape(-1)
    k_gain_all = gains[:, 544:576].reshape(-1)
    values = all_tokens.astype(jnp.float32)
    normed = low(root_mean_norm(values, a_gain))
    qkv = dot(normed, w_qkv)
    q_pre = qkv[:, :width].reshape(count, 2, HEAD_SIZE)
    k_pre = qkv[:, width : width + HEAD_SIZE]
    v_low = low(qkv[:, width + HEAD_SIZE :])

    def rope(v, cos, sin):
        return v * cos + half_turn(v) * sin

    q_low = low(rope(root_mean_norm(q_pre, q_gain), cosine[:, None], sine[:, None]))
    k_low = low(rope(root_mean_norm(k_pre, k_gain_all), cosine, sine))
    allowed = (ids[None, :] >= first[:, None]) & (ids[None, :] <= ids[:, None])
    scale = HEAD_SIZE**-0.5
    scores = jnp.einsum("tgh,uh->gtu", q_low, k_low, preferred_element_type=jnp.float32) * scale
    scores = jnp.where(allowed, scores, negative_filler)
    top = jnp.max(scores, axis=-1, keepdims=True)
    weights = jnp.exp(scores - top)
    total = jnp.sum(weights, axis=-1, keepdims=True)
    log_total = top + jnp.log(total)
    mixed = (
        jnp.einsum("gtu,uh->gth", low(weights), v_low, preferred_element_type=jnp.float32) / total
    )
    mixed_heads = low(jnp.transpose(mixed, (1, 0, 2)).reshape(count, width))
    mixed_out = low(dot(to_dealt, mixed_heads)).reshape(slots, rows, width)
    mixed_in = swap_heads(mixed_out, 1)
    mixed_low = jnp.transpose(mixed_in, (1, 0, 2)).reshape(rows, slots * width)

    own_rows = lax.dynamic_slice_in_dim(to_dealt, here * rows, rows, 0)
    residual = dot(own_rows, all_tokens)
    full_o = gather_fsdp_plain(w_o)
    middle = residual + dot(mixed_low, full_o)
    normed2 = low(root_mean_norm(middle, m_gain))

    def quarter_cols(w, c):
        return jnp.concatenate(
            [
                lax.dynamic_slice_in_dim(w, (2 * xs + c) * ff_shard + y * ff_half, ff_half, 1)
                for xs in range(2)
            ],
            axis=1,
        )

    sides = jnp.stack(
        [
            jnp.concatenate([quarter_cols(w_gate, c), quarter_cols(w_up, c)], axis=1)
            for c in range(2)
        ]
    )
    sides = lax.all_to_all(sides, "core", 0, 0, tiled=True)
    w_gu = lax.all_gather(sides, "x", axis=0, tiled=True).reshape(-1, 4 * ff_half)
    down_own = lax.dynamic_slice_in_dim(w_down, y * ff_half, ff_half, 0)
    w_dn = lax.all_gather(down_own, "x", axis=0, tiled=True)
    quad_n = gather_four(normed2, 2).reshape(4 * rows, -1)
    quad_g = gather_four(out_cotangent[0], 3).reshape(4 * rows, -1)
    gate_up = dot(quad_n, w_gu)
    gate, up = gate_up[:, : 2 * ff_half], gate_up[:, 2 * ff_half :]
    sig = 1.0 / (1.0 + jnp.exp(-gate))
    silu = gate * sig
    hidden = low(silu * up)
    partial_out = low(dot(hidden, w_dn))
    out_sum = scatter_four(partial_out.reshape(4, rows, -1), 4)
    output = low(middle + out_sum)

    d_hidden = dot_trans(quad_g, w_dn)
    d_gate = low(d_hidden * up * (sig * (1.0 + gate * (1.0 - sig))))
    d_up = low(d_hidden * silu)
    d_gu = jnp.concatenate([d_gate, d_up], axis=1)
    dn2_part = low(dot_trans(d_gu, w_gu))
    d_normed2 = scatter_four(dn2_part.reshape(4, rows, -1), 5)
    grad_gu = low(outer_rows(quad_n, d_gu))
    grad_dn = low(outer_rows(hidden, quad_g))
    dx2, dg2 = norm_back(middle, m_gain, d_normed2)
    d_middle = out_cotangent[0].astype(jnp.float32) + dx2
    middle_low = low(d_middle)
    d_mixed_tok = low(dot_trans(middle_low, full_o))
    dm_out = jnp.transpose(d_mixed_tok.reshape(rows, slots, width), (1, 0, 2))
    padded = jnp.pad(
        middle_low.reshape(slots, piece, MODEL_WIDTH), ((0, 0), (0, 32 - piece), (0, 0))
    )
    dm_in, back = swap_two(dm_out, padded, 6)
    dm_in = dm_in.reshape(count, width)
    d_mixed = low(
        lax.dot_general(
            to_dealt, dm_in, (((0,), (0,)), ((), ())), preferred_element_type=jnp.float32
        )
    )
    grad_o = low(outer_rows(mixed_low, middle_low))
    d_heads = d_mixed.reshape(count, 2, HEAD_SIZE)
    delta = jnp.sum(
        jnp.transpose(d_heads, (1, 0, 2)).astype(jnp.float32) * mixed, axis=-1, keepdims=True
    )
    probs = jnp.where(allowed, jnp.exp(scores - log_total), 0.0)
    d_probs = jnp.einsum("tgh,uh->gtu", d_heads, v_low, preferred_element_type=jnp.float32)
    d_scores = low(probs * (d_probs - delta))
    d_v = jnp.einsum("gtu,tgh->uh", low(probs), d_heads, preferred_element_type=jnp.float32)
    d_q = jnp.einsum("gtu,uh->tgh", d_scores, k_low, preferred_element_type=jnp.float32) * scale
    d_k = jnp.einsum("gtu,tgh->uh", d_scores, q_low, preferred_element_type=jnp.float32) * scale

    def rope_back(v, cos, sin):
        return v * cos - half_turn(v * sin)

    d_q_pre, dg_q = norm_back(q_pre, q_gain, rope_back(d_q, cosine[:, None], sine[:, None]))
    d_k_pre, dg_k = norm_back(k_pre, k_gain_all, rope_back(d_k, cosine, sine))
    d_qkv = jnp.concatenate([low(d_q_pre.reshape(count, width)), low(d_k_pre), low(d_v)], axis=1)
    dn_part = low(dot_trans(d_qkv, w_qkv))
    d_normed = scatter_ctx(dn_part.reshape(slots, rows, -1), 7)
    grad_qkv = low(outer_rows(normed, d_qkv))

    own_plan = lax.dynamic_index_in_dim(plan, here, 0, keepdims=False)
    d_middle_given = jnp.take(back[:, :piece], own_plan, axis=0).reshape(rows, MODEL_WIDTH)
    dx1, dg1 = norm_back(tokens[0].astype(jnp.float32), a_gain, d_normed)
    input_grad = d_middle_given.astype(jnp.float32) + dx1

    gain_sums = lax.psum(
        jnp.concatenate(
            [
                jnp.sum(dg1, axis=0).reshape(4, 256),
                jnp.sum(dg2, axis=0).reshape(4, 256),
                jnp.sum(dg_q, axis=(0, 1)).reshape(4, 32),
                jnp.sum(dg_k, axis=0).reshape(4, 32),
            ],
            axis=1,
        ),
        ("z", "y", "x", "core"),
    )
    own_gain = lax.dynamic_index_in_dim(gain_sums, 2 * x + core, 0, keepdims=False)

    def halves(a):
        return a.reshape(2, a.shape[0] // 2, *a.shape[1:])

    def by_core(a):
        return jnp.swapaxes(a.reshape(2, 2, -1, a.shape[-1]), 0, 1)

    gu_half = half_sum(halves(grad_gu), "x")
    gu_blocks = jnp.swapaxes(gu_half.reshape(2, LINE, -1, 4 * ff_half), 0, 1)
    dn_half = half_sum(halves(grad_dn), "x").reshape(LINE, -1, MODEL_WIDTH)
    o_half = half_sum(half_sum(by_core(grad_o), "core"), "x").reshape(slots, -1, MODEL_WIDTH)
    qkv_sum = half_sum(half_sum(by_core(grad_qkv), "core"), "x")
    gu_all, dn_all, o_all, qkv_all = sum_and_gather(gu_blocks, dn_half, o_half, qkv_sum, 8)
    q_all = jnp.transpose(qkv_all[:, :, :width], (1, 0, 2)).reshape(-1, slots * width)
    k_all = jnp.transpose(qkv_all[:, :, width : width + HEAD_SIZE], (1, 0, 2))
    v_all = jnp.transpose(qkv_all[:, :, width + HEAD_SIZE :], (1, 0, 2))
    o_sum = o_all.reshape(-1, MODEL_WIDTH)
    gu_all = gu_all.reshape(LINE, 2, 2, -1, 2, 2, ff_half)
    gu_all = jnp.transpose(gu_all, (4, 0, 3, 5, 2, 1, 6)).reshape(2, -1, 8 * ff_half)
    dn_all = jnp.swapaxes(dn_all.reshape(LINE, 2, -1, MODEL_WIDTH), 0, 1).reshape(-1, MODEL_WIDTH)

    def wide(a):
        return a.astype(jnp.float32)

    return (
        output[None],
        input_grad[None],
        own_gain[:256],
        own_gain[512:544],
        own_gain[544:576],
        own_gain[256:512],
        wide(q_all),
        wide(k_all.reshape(-1, slots * HEAD_SIZE)),
        wide(v_all.reshape(-1, slots * HEAD_SIZE)),
        wide(o_sum),
        wide(gu_all[0]),
        wide(gu_all[1]),
        wide(dn_all),
    )


def solution(mesh):
    devices = mesh.devices
    if devices.shape == (8, 4):
        mesh = Mesh(devices.reshape(4, 2, 2, 2), CTX + FSDP)
        layer, ctx, fsdp = fast_layer, CTX, FSDP
    else:
        layer, ctx, fsdp = general_layer, "ctx", "fsdp"
    wide_rows = P(fsdp, ctx, None)
    return jax.shard_map(
        layer,
        mesh=mesh,
        in_specs=(
            wide_rows,
            P(fsdp, None),
            P(fsdp, None, None),
            P(fsdp),
            P(fsdp, None),
            P(fsdp, None),
            P(fsdp, None),
            P(fsdp),
            P(fsdp),
            P(fsdp, None),
            P(fsdp),
            P(fsdp, None),
            P(fsdp, None),
            P(fsdp, None),
            wide_rows,
        ),
        out_specs=(wide_rows, wide_rows) + (P(fsdp),) * 4 + (P(fsdp, None),) * 7,
        check_vma=False,
    )
```

```python
import math

import jax
import jax.numpy as jnp
from jax import lax
from jax.experimental import pallas as pl
from jax.experimental.pallas import tpu as pltpu
from jax.sharding import Mesh
from jax.sharding import PartitionSpec as P

MODEL_WIDTH = 1024
QUERY_HEADS = 16
KEY_VALUE_HEADS = 8
HEAD_SIZE = 128


eps = 1e-06
theta_base = 1000000.0
negative_filler = -1e30


def root_mean_norm(values, gain_vec):
    return values * lax.rsqrt(jnp.mean(values * values, axis=-1, keepdims=True) + eps) * gain_vec


def rotary_embedding(values, token_position):
    half_width = values.shape[-1] // 2
    frequency = theta_base ** (
        -(jnp.arange(half_width, dtype=jnp.float32) * 2.0) / values.shape[-1]
    )
    angles = token_position.astype(jnp.float32)[:, None] * frequency[None, :]
    cosine = jnp.concatenate([jnp.cos(angles), jnp.cos(angles)], axis=-1)[:, None, :]
    sine_part = jnp.concatenate([jnp.sin(angles), jnp.sin(angles)], axis=-1)[:, None, :]
    turned = jnp.concatenate([-values[..., half_width:], values[..., :half_width]], axis=-1)
    return values * cosine + turned * sine_part


def dot_trans(left_side, right_side):
    return lax.dot_general(
        left_side, right_side, (((1,), (1,)), ((), ())), preferred_element_type=jnp.float32
    )


def outer_rows(left_side, right_side):
    return lax.dot_general(
        left_side, right_side, (((0,), (0,)), ((), ())), preferred_element_type=jnp.float32
    )


def block_plan(piece_rows, local_rows):
    shards = piece_rows // local_rows
    per_block = math.gcd(shards, max(1, 1024 // local_rows))
    return (per_block * local_rows, shards // per_block)


def over_blocks(carried, arrays, local_rows, block_work):
    rows_per_block, count_of_blocks = block_plan(arrays[0].shape[0], local_rows)

    def one_block(turn_index, state_now):
        offset = turn_index * rows_per_block
        parts = tuple(
            (lax.dynamic_slice_in_dim(member, offset, rows_per_block, 0) for member in arrays)
        )
        return block_work(state_now, parts, offset)

    return lax.fori_loop(0, count_of_blocks, one_block, carried)


def segment_begin(tok_ids, starts):
    return jnp.max(jnp.where(tok_ids[:, None] >= starts[None, :], starts[None, :], 0), axis=1)


def general_layer(
    tokens,
    lengths,
    deal,
    attn_gain,
    w_q,
    key_weight,
    value_weight,
    query_norm_gain,
    k_gain,
    w_o,
    mlp_gain,
    w_gate,
    w_up,
    w_down,
    out_cotangent,
):
    local_rows = tokens.shape[1]
    piece_count = lax.axis_size("ctx")
    piece_rows = local_rows // piece_count
    here = lax.axis_index("ctx")
    group_width = QUERY_HEADS // KEY_VALUE_HEADS
    score_scale = HEAD_SIZE ** (-0.5)
    seq_lengths = lengths[0]
    starts = jnp.cumsum(seq_lengths) - seq_lengths
    plan = deal[0]
    devices = jnp.arange(piece_count, dtype=jnp.int32)
    hits = plan[:, :, None] == devices[None, None, :]
    slot_of = jnp.sum(jnp.where(hits, devices[None, :, None], 0), axis=1)
    inner = jnp.arange(piece_rows, dtype=jnp.int32)
    dealt_index = (
        devices[None, :, None] * local_rows
        + jnp.transpose(slot_of)[:, :, None] * piece_rows
        + inner[None, None, :]
    ).reshape(piece_count * local_rows)
    dealt_first = segment_begin(dealt_index, starts)
    tok_index = lax.dynamic_slice_in_dim(dealt_index, here * local_rows, local_rows)
    segment_initial = lax.dynamic_slice_in_dim(dealt_first, here * local_rows, local_rows)
    token_position = tok_index - segment_initial
    own_slots = lax.dynamic_index_in_dim(slot_of, here, 0, keepdims=False)
    own_plan = lax.dynamic_index_in_dim(plan, here, 0, keepdims=False)
    token_pieces = jnp.take(
        tokens[0].reshape(piece_count, piece_rows, MODEL_WIDTH), own_slots, axis=0
    )
    dealt_tok = lax.all_to_all(
        token_pieces, "ctx", split_axis=0, concat_axis=0, tiled=True
    ).reshape(local_rows, MODEL_WIDTH)

    def key_mask(start_row, local_row_count):
        key_identifiers = lax.dynamic_slice_in_dim(dealt_index, start_row, local_row_count)
        return (key_identifiers[None, :] >= segment_initial[:, None]) & (
            key_identifiers[None, :] <= tok_index[:, None]
        )

    def query_mask(start_row, local_row_count):
        query_ids = lax.dynamic_slice_in_dim(dealt_index, start_row, local_row_count)
        first_key = lax.dynamic_slice_in_dim(dealt_first, start_row, local_row_count)
        return (tok_index[None, :] >= first_key[:, None]) & (
            tok_index[None, :] <= query_ids[:, None]
        )

    def fetch_weights():
        attn_set = (
            lax.all_gather(attn_gain, "fsdp", axis=0, tiled=True),
            lax.all_gather(query_norm_gain, "fsdp", axis=0, tiled=True),
            lax.all_gather(k_gain, "fsdp", axis=0, tiled=True),
            lax.all_gather(w_q, "fsdp", axis=0, tiled=True),
            lax.all_gather(key_weight, "fsdp", axis=0, tiled=True),
            lax.all_gather(value_weight, "fsdp", axis=0, tiled=True),
            lax.all_gather(w_o, "fsdp", axis=0, tiled=True),
        )
        mlp_set = (
            lax.all_gather(mlp_gain, "fsdp", axis=0, tiled=True),
            lax.all_gather(w_gate, "fsdp", axis=0, tiled=True),
            lax.all_gather(w_up, "fsdp", axis=0, tiled=True),
            lax.all_gather(w_down, "fsdp", axis=0, tiled=True),
        )
        return (attn_set, mlp_set)

    def forward(attn_set, mlp_set, token_rows):
        a_gain, qn_gain, kn_gain, proj_q, proj_k, proj_v, proj_o = attn_set
        m_gain, proj_gate, proj_up, proj_down = mlp_set
        residual = token_rows.astype(jnp.float32)
        normalized_input = root_mean_norm(residual, a_gain.astype(jnp.float32)).astype(jnp.bfloat16)
        query_prenorm = jnp.dot(
            normalized_input, proj_q, preferred_element_type=jnp.float32
        ).reshape(local_rows, QUERY_HEADS, HEAD_SIZE)
        key_prenorm = jnp.dot(normalized_input, proj_k, preferred_element_type=jnp.float32).reshape(
            local_rows, KEY_VALUE_HEADS, HEAD_SIZE
        )
        value_narrow = jnp.dot(normalized_input, proj_v, preferred_element_type=jnp.float32).astype(
            jnp.bfloat16
        )
        q_heads = (
            rotary_embedding(
                root_mean_norm(query_prenorm, qn_gain.astype(jnp.float32)), token_position
            )
            .astype(jnp.bfloat16)
            .reshape(local_rows, KEY_VALUE_HEADS, group_width, HEAD_SIZE)
        )
        key_narrow = (
            rotary_embedding(
                root_mean_norm(key_prenorm, kn_gain.astype(jnp.float32)), token_position
            )
            .astype(jnp.bfloat16)
            .reshape(local_rows, KEY_VALUE_HEADS * HEAD_SIZE)
        )

        def attend_over_block(state_now, shard_piece, start_row):
            key_segment, value_segment = shard_piece
            local_row_count = key_segment.shape[0]
            allowed = key_mask(start_row, local_row_count)
            row_top, row_total, weighted = state_now
            scores = (
                jnp.einsum(
                    "rkgh,ckh->kgrc",
                    q_heads,
                    key_segment.reshape(local_row_count, KEY_VALUE_HEADS, HEAD_SIZE),
                    preferred_element_type=jnp.float32,
                )
                * score_scale
            )
            scores = jnp.where(allowed, scores, negative_filler)
            new_top = jnp.maximum(row_top, jnp.max(scores, axis=-1))
            rescale = jnp.exp(row_top - new_top)
            weights = jnp.where(allowed, jnp.exp(scores - new_top[..., None]), 0.0)
            row_total = row_total * rescale + jnp.sum(weights, axis=-1)
            weighted = weighted * rescale[..., None] + jnp.einsum(
                "kgrc,ckh->kgrh",
                weights.astype(jnp.bfloat16),
                value_segment.reshape(local_row_count, KEY_VALUE_HEADS, HEAD_SIZE),
                preferred_element_type=jnp.float32,
            )
            return (new_top, row_total, weighted)

        initial = (
            jnp.full((KEY_VALUE_HEADS, group_width, local_rows), negative_filler, jnp.float32),
            jnp.zeros((KEY_VALUE_HEADS, group_width, local_rows), jnp.float32),
            jnp.zeros((KEY_VALUE_HEADS, group_width, local_rows, HEAD_SIZE), jnp.float32),
        )
        row_top, row_total, weighted = over_blocks(
            initial,
            (
                lax.all_gather(key_narrow, "ctx", axis=0, tiled=True),
                lax.all_gather(value_narrow, "ctx", axis=0, tiled=True),
            ),
            local_rows,
            attend_over_block,
        )
        attention_mixed = jnp.transpose(weighted / row_total[..., None], (2, 0, 1, 3)).reshape(
            local_rows, QUERY_HEADS * HEAD_SIZE
        )
        log_total = row_top + jnp.log(row_total)
        mixed_low = attention_mixed.astype(jnp.bfloat16)
        middle = residual + jnp.dot(mixed_low, proj_o, preferred_element_type=jnp.float32)
        normed2 = root_mean_norm(middle, m_gain.astype(jnp.float32)).astype(jnp.bfloat16)
        gate_pre = jnp.dot(normed2, proj_gate, preferred_element_type=jnp.float32)
        up_pre = jnp.dot(normed2, proj_up, preferred_element_type=jnp.float32)
        hidden = (jax.nn.silu(gate_pre) * up_pre).astype(jnp.bfloat16)
        result = middle + jnp.dot(hidden, proj_down, preferred_element_type=jnp.float32)
        return (
            result,
            residual,
            normalized_input,
            query_prenorm,
            key_prenorm,
            value_narrow,
            q_heads,
            key_narrow,
            attention_mixed,
            mixed_low,
            log_total,
            middle,
            normed2,
            gate_pre,
            up_pre,
            hidden,
            attn_set,
            mlp_set,
        )

    first_sets = fetch_weights()
    first_pass = forward(first_sets[0], first_sets[1], dealt_tok)
    again_tok = lax.all_to_all(
        token_pieces, "ctx", split_axis=0, concat_axis=0, tiled=True
    ).reshape(local_rows, MODEL_WIDTH)
    second_sets = fetch_weights()
    kept_pass = forward(second_sets[0], second_sets[1], again_tok)
    (
        unused,
        residual,
        normalized_input,
        query_prenorm,
        key_prenorm,
        value_narrow,
        q_heads,
        key_narrow,
        attention_mixed,
        mixed_low,
        log_total,
        middle,
        normed2,
        gate_pre,
        up_pre,
        hidden,
        attn_set,
        mlp_set,
    ) = kept_pass
    a_gain, qn_gain, kn_gain, proj_q, proj_k, proj_v, proj_o = attn_set
    m_gain, proj_gate, proj_up, proj_down = mlp_set
    grad_low = out_cotangent[0]
    grad_out = grad_low.astype(jnp.float32)
    d_hidden = dot_trans(grad_low, proj_down)
    down_grad = lax.psum_scatter(
        outer_rows(hidden, grad_low).astype(jnp.bfloat16), "fsdp", scatter_dimension=0, tiled=True
    )
    unused, swiglu_back = jax.vjp(
        lambda gate_in, up_in: jax.nn.silu(gate_in) * up_in, gate_pre, up_pre
    )
    d_gate, d_up = swiglu_back(d_hidden)
    d_gate_low = d_gate.astype(jnp.bfloat16)
    d_up_low = d_up.astype(jnp.bfloat16)
    d_normed2 = dot_trans(d_gate_low, proj_gate) + dot_trans(d_up_low, proj_up)
    both_low = jnp.concatenate([d_gate_low, d_up_low], axis=1)
    gate_up_grad = lax.psum_scatter(
        outer_rows(normed2, both_low).astype(jnp.bfloat16), "fsdp", scatter_dimension=0, tiled=True
    )
    unused, norm2_back = jax.vjp(root_mean_norm, middle, m_gain.astype(jnp.float32))
    d_middle_norm, d_m_gain = norm2_back(d_normed2)
    d_middle = grad_out + d_middle_norm
    middle_low = d_middle.astype(jnp.bfloat16)
    mixed_gradient = dot_trans(middle_low, proj_o).astype(jnp.bfloat16)
    out_proj_grad = lax.psum_scatter(
        outer_rows(mixed_low, middle_low).astype(jnp.bfloat16),
        "fsdp",
        scatter_dimension=0,
        tiled=True,
    )
    heads_gradient = mixed_gradient.reshape(local_rows, KEY_VALUE_HEADS, group_width, HEAD_SIZE)
    delta_rows = jnp.sum(
        heads_gradient.astype(jnp.float32)
        * attention_mixed.reshape(local_rows, KEY_VALUE_HEADS, group_width, HEAD_SIZE),
        axis=-1,
    )
    delta_t = jnp.transpose(delta_rows, (1, 2, 0))
    local_keys = key_narrow.reshape(local_rows, KEY_VALUE_HEADS, HEAD_SIZE)
    local_values = value_narrow.reshape(local_rows, KEY_VALUE_HEADS, HEAD_SIZE)

    def query_block(state_now, shard_piece, start_row):
        key_segment, value_segment = shard_piece
        local_row_count = key_segment.shape[0]
        allowed = key_mask(start_row, local_row_count)
        key_row_block = key_segment.reshape(local_row_count, KEY_VALUE_HEADS, HEAD_SIZE)
        scores = (
            jnp.einsum("rkgh,ckh->kgrc", q_heads, key_row_block, preferred_element_type=jnp.float32)
            * score_scale
        )
        probability = jnp.where(allowed, jnp.exp(scores - log_total[..., None]), 0.0)
        d_probs = jnp.einsum(
            "rkgh,ckh->kgrc",
            heads_gradient,
            value_segment.reshape(local_row_count, KEY_VALUE_HEADS, HEAD_SIZE),
            preferred_element_type=jnp.float32,
        )
        d_scores = (probability * (d_probs - delta_t[..., None])).astype(jnp.bfloat16)
        return (
            state_now
            + jnp.einsum(
                "kgrc,ckh->kgrh", d_scores, key_row_block, preferred_element_type=jnp.float32
            )
            * score_scale
        )

    query_grad = over_blocks(
        jnp.zeros((KEY_VALUE_HEADS, group_width, local_rows, HEAD_SIZE), jnp.float32),
        (
            lax.all_gather(key_narrow, "ctx", axis=0, tiled=True),
            lax.all_gather(value_narrow, "ctx", axis=0, tiled=True),
        ),
        local_rows,
        query_block,
    )
    lse_rows = jnp.transpose(log_total, (2, 0, 1)).reshape(local_rows, QUERY_HEADS)
    delta_send = delta_rows.reshape(local_rows, QUERY_HEADS)

    def key_block(state_now, shard_piece, start_row):
        query_segment, output_gradient_segment, logsumexp_segment, delta_segment = shard_piece
        local_row_count = query_segment.shape[0]
        allowed = query_mask(start_row, local_row_count)
        key_grad, value_gradient = state_now
        query_matrix = query_segment.reshape(
            local_row_count, KEY_VALUE_HEADS, group_width, HEAD_SIZE
        )
        gradient_rows = output_gradient_segment.reshape(
            local_row_count, KEY_VALUE_HEADS, group_width, HEAD_SIZE
        )
        scores = (
            jnp.einsum(
                "ckgh,rkh->kgcr", query_matrix, local_keys, preferred_element_type=jnp.float32
            )
            * score_scale
        )
        logsumexp_portion = jnp.transpose(
            logsumexp_segment.reshape(local_row_count, KEY_VALUE_HEADS, group_width), (1, 2, 0)
        )
        delta_portion = jnp.transpose(
            delta_segment.reshape(local_row_count, KEY_VALUE_HEADS, group_width), (1, 2, 0)
        )
        probability = jnp.where(allowed, jnp.exp(scores - logsumexp_portion[..., None]), 0.0)
        value_gradient = value_gradient + jnp.einsum(
            "kgcr,ckgh->rkh",
            probability.astype(jnp.bfloat16),
            gradient_rows,
            preferred_element_type=jnp.float32,
        )
        d_probs = jnp.einsum(
            "ckgh,rkh->kgcr", gradient_rows, local_values, preferred_element_type=jnp.float32
        )
        d_scores = (probability * (d_probs - delta_portion[..., None])).astype(jnp.bfloat16)
        key_grad = (
            key_grad
            + jnp.einsum(
                "kgcr,ckgh->rkh", d_scores, query_matrix, preferred_element_type=jnp.float32
            )
            * score_scale
        )
        return (key_grad, value_gradient)

    key_grad, value_gradient = over_blocks(
        (
            jnp.zeros((local_rows, KEY_VALUE_HEADS, HEAD_SIZE), jnp.float32),
            jnp.zeros((local_rows, KEY_VALUE_HEADS, HEAD_SIZE), jnp.float32),
        ),
        (
            lax.all_gather(
                q_heads.reshape(local_rows, QUERY_HEADS * HEAD_SIZE), "ctx", axis=0, tiled=True
            ),
            lax.all_gather(mixed_gradient, "ctx", axis=0, tiled=True),
            lax.all_gather(lse_rows.astype(jnp.bfloat16), "ctx", axis=0, tiled=True).astype(
                jnp.float32
            ),
            lax.all_gather(delta_send.astype(jnp.bfloat16), "ctx", axis=0, tiled=True).astype(
                jnp.float32
            ),
        ),
        local_rows,
        key_block,
    )
    query_rows = jnp.transpose(query_grad, (2, 0, 1, 3)).reshape(local_rows, QUERY_HEADS, HEAD_SIZE)
    unused, q_back = jax.vjp(
        lambda head_in, gain_in: rotary_embedding(root_mean_norm(head_in, gain_in), token_position),
        query_prenorm,
        qn_gain.astype(jnp.float32),
    )
    d_q_pre, d_qn_gain = q_back(query_rows)
    unused, k_back = jax.vjp(
        lambda head_in, gain_in: rotary_embedding(root_mean_norm(head_in, gain_in), token_position),
        key_prenorm,
        kn_gain.astype(jnp.float32),
    )
    key_prenorm_gradient, d_kn_gain = k_back(key_grad)
    dq_low = d_q_pre.reshape(local_rows, QUERY_HEADS * HEAD_SIZE).astype(jnp.bfloat16)
    key_gradient_narrow = key_prenorm_gradient.reshape(
        local_rows, KEY_VALUE_HEADS * HEAD_SIZE
    ).astype(jnp.bfloat16)
    value_gradient_narrow = value_gradient.reshape(local_rows, KEY_VALUE_HEADS * HEAD_SIZE).astype(
        jnp.bfloat16
    )
    d_normed = (
        dot_trans(dq_low, proj_q)
        + dot_trans(key_gradient_narrow, proj_k)
        + dot_trans(value_gradient_narrow, proj_v)
    )
    qkv_low = jnp.concatenate([dq_low, key_gradient_narrow, value_gradient_narrow], axis=1)
    qkv_grad = lax.psum_scatter(
        outer_rows(normalized_input, qkv_low).astype(jnp.bfloat16),
        "fsdp",
        scatter_dimension=0,
        tiled=True,
    )
    unused, norm1_back = jax.vjp(root_mean_norm, residual, a_gain.astype(jnp.float32))
    d_resid_norm, d_a_gain = norm1_back(d_normed)
    input_dealt = d_middle + d_resid_norm
    back_pieces = lax.all_to_all(
        input_dealt.reshape(piece_count, piece_rows, MODEL_WIDTH).astype(jnp.bfloat16),
        "ctx",
        split_axis=0,
        concat_axis=0,
        tiled=True,
    ).astype(jnp.float32)
    input_grad = jnp.take(back_pieces, own_plan, axis=0).reshape(local_rows, MODEL_WIDTH)
    gain_parts = (
        lax.psum_scatter(d_a_gain, "fsdp", scatter_dimension=0, tiled=True),
        lax.psum_scatter(d_qn_gain, "fsdp", scatter_dimension=0, tiled=True),
        lax.psum_scatter(d_kn_gain, "fsdp", scatter_dimension=0, tiled=True),
        lax.psum_scatter(d_m_gain, "fsdp", scatter_dimension=0, tiled=True),
    )
    totals = (
        lax.psum(gain_parts[0].astype(jnp.bfloat16), "ctx").astype(jnp.float32),
        lax.psum(gain_parts[1].astype(jnp.bfloat16), "ctx").astype(jnp.float32),
        lax.psum(gain_parts[2].astype(jnp.bfloat16), "ctx").astype(jnp.float32),
        lax.psum(gain_parts[3].astype(jnp.bfloat16), "ctx").astype(jnp.float32),
        lax.psum(qkv_grad, "ctx").astype(jnp.float32),
        lax.psum(out_proj_grad, "ctx").astype(jnp.float32),
        lax.psum(gate_up_grad, "ctx").astype(jnp.float32),
        lax.psum(down_grad, "ctx").astype(jnp.float32),
    )
    q_width = QUERY_HEADS * HEAD_SIZE
    key_value_width = KEY_VALUE_HEADS * HEAD_SIZE
    qkv_total = totals[4]
    gate_up_total = totals[6]
    ff_width = w_gate.shape[1]
    return (
        first_pass[0].astype(jnp.bfloat16)[None],
        input_grad[None],
        totals[0],
        totals[1],
        totals[2],
        totals[3],
        qkv_total[:, :q_width],
        qkv_total[:, q_width : q_width + key_value_width],
        qkv_total[:, q_width + key_value_width :],
        totals[5],
        gate_up_total[:, :ff_width],
        gate_up_total[:, ff_width:],
        totals[7],
    )


CTX = ("z", "y")
FSDP = ("x", "core")
VMEM_BYTES = 62 << 20


def norm_back(values, gain_vec, grad):
    scale = lax.rsqrt(jnp.mean(values * values, axis=-1, keepdims=True) + eps)
    inner = gain_vec * grad
    d_values = scale * inner - values * (scale * scale * scale) * jnp.mean(
        values * inner, axis=-1, keepdims=True
    )
    return d_values, grad * values * scale


def half_turn(values):
    half = values.shape[-1] // 2
    return jnp.concatenate([-values[..., half:], values[..., :half]], axis=-1)


def rope_tables(token_position):
    half = HEAD_SIZE // 2
    frequency = theta_base ** (-(jnp.arange(half, dtype=jnp.float32) * 2.0) / HEAD_SIZE)
    angles = token_position.astype(jnp.float32)[:, None] * frequency[None, :]
    cosine, sine = jnp.cos(angles), jnp.sin(angles)
    return jnp.concatenate([cosine, cosine], axis=1), jnp.concatenate([sine, sine], axis=1)


def dot(a, b):
    return jnp.dot(a, b, preferred_element_type=jnp.float32)


def low(a):
    return a.astype(jnp.bfloat16)


def gather_fsdp_plain(block):
    return lax.all_gather(block, FSDP, axis=0, tiled=True)


def over(block, axis):
    return lax.ppermute(block, axis, [(0, 1), (1, 0)])


def half_sum(block, axis):
    place = lax.axis_index(axis)
    got = over(lax.dynamic_index_in_dim(block, 1 - place, 0, keepdims=False), axis)
    own = lax.dynamic_index_in_dim(block, place, 0, keepdims=False)
    return low(own.astype(jnp.float32) + got.astype(jnp.float32))


MESH_ID = pl.DeviceIdType.MESH
LINE = 4


class Net:
    def __init__(self, send, recv):
        self.send, self.recv, self.used = send, recv, 0
        self.z, self.y, self.x, self.core = (lax.axis_index(a) for a in CTX + FSDP)
        self.me = 2 * self.z + self.y
        self.open = []

    def at(self, dz=0, dy=0, dx=0, dc=0):
        return (
            self.z + dz,
            1 - self.y if dy else self.y,
            1 - self.x if dx else self.x,
            1 - self.core if dc else self.core,
        )

    def put(self, src, dst, target, sends=None, recvs=None):
        copy = Copy(self, src, dst, target, sends, recvs)
        self.open.append(copy)
        return copy

    def close(self):
        for copy in self.open:
            copy.arrived()
        for copy in self.open:
            copy.left()


def guarded(condition, action):
    if condition is None:
        action()
    else:
        pl.when(condition)(action)


class Copy:
    def __init__(self, net, src, dst, target, sends, recvs):
        i = net.used
        net.used += 1
        self.sends, self.recvs, self.waited = sends, recvs, False
        self.copy = pltpu.make_async_remote_copy(
            src, dst, net.send.at[i], net.recv.at[i], device_id=target, device_id_type=MESH_ID
        )
        guarded(sends, self.copy.start)

    def arrived(self):
        if not self.waited:
            self.waited = True
            guarded(self.recvs, self.copy.wait_recv)

    def left(self):
        guarded(self.sends, self.copy.wait_send)


def greet(net, kinds):
    barrier = pltpu.get_barrier_semaphore()
    partners = []
    if "z" in kinds:
        partners += [(net.at(dz=1), net.z < LINE - 1), (net.at(dz=-1), net.z > 0)]
    if "y" in kinds:
        partners.append((net.at(dy=1), None))
    if "x" in kinds:
        partners.append((net.at(dx=1), None))
    if "core" in kinds:
        partners.append((net.at(dc=1), None))
    if "ctx" in kinds:
        for k in range(1, 2 * LINE):
            other = lax.rem(net.me + k, 2 * LINE)
            partners.append(((other // 2, lax.rem(other, 2), net.x, net.core), None))
    for target, there in partners:
        guarded(
            there,
            lambda target=target: pl.semaphore_signal(
                barrier, inc=1, device_id=target, device_id_type=MESH_ID
            ),
        )
    ends = 0
    if "z" in kinds:
        ends = (net.z == 0).astype(jnp.int32) + (net.z == LINE - 1).astype(jnp.int32)
    pl.semaphore_wait(barrier, len(partners) - ends)


def drive(*programs):
    live = list(programs)
    while live:
        for program in list(live):
            if next(program, "end") == "end":
                live.remove(program)


def along_line(net, own, view, sides, slot):
    z = net.z
    up = net.put(own, view(slot(z)), net.at(dz=1), z < LINE - 1, z > 0)
    down = net.put(own, view(slot(z)), net.at(dz=-1), z > 0, z < LINE - 1)
    for s in range(1, LINE):
        from_low, from_high = z >= s, z + s <= LINE - 1
        up.arrived()
        low_block, high_block = view(slot(z - s)), view(slot(z + s))
        if s < LINE - 1:
            up = net.put(low_block, low_block, net.at(dz=1), from_low & (z < LINE - 1), z >= s + 1)
        if sides:
            net.put(low_block, low_block, net.at(dy=1), from_low, from_low)
        down.arrived()
        if s < LINE - 1:
            down = net.put(
                high_block, high_block, net.at(dz=-1), from_high & (z > 0), z + s + 1 <= LINE - 1
            )
        if sides:
            net.put(high_block, high_block, net.at(dy=1), from_high, from_high)
        yield


def gather_line_first(net, own, view):
    net.put(own, view(net.me), net.at(dy=1))
    yield from along_line(net, own, view, True, lambda z: 2 * z + net.y)


def gather_side_first(net, own, view):
    side = net.put(own, view(net.me), net.at(dy=1))
    first = along_line(net, own, view, False, lambda z: 2 * z + net.y)
    yield next(first)
    side.arrived()
    other = view(net.me + 1 - 2 * net.y)
    second = along_line(net, other, view, False, lambda z: 2 * z + 1 - net.y)
    for _ in second:
        next(first, None)
        yield


def gather_ctx_programs(net, own, out, cut):
    rows = own.shape[0]
    programs = [
        gather_line_first(
            net, own.at[pl.ds(0, cut)], lambda slot: out.at[slot, pl.ds(0, cut)]
        )
    ]
    if cut < rows:
        rest = pl.ds(cut, rows - cut)
        programs.append(gather_side_first(net, own.at[rest], lambda slot: out.at[slot, rest]))
    return programs


def gather_fsdp(net, own, out):
    f = 2 * net.x + net.core
    net.put(own, out.at[f], net.at(dc=1))
    over = net.put(own, out.at[f], net.at(dx=1))
    yield
    yield
    yield
    over.arrived()
    far = out.at[2 * (1 - net.x) + net.core]
    net.put(far, far, net.at(dc=1))
    yield


def gather_quad(net, own, out):
    q = 2 * net.y + net.core
    net.put(own, out.at[q], net.at(dc=1))
    over = net.put(own, out.at[q], net.at(dy=1))
    yield
    over.arrived()
    far = out.at[2 * (1 - net.y) + net.core]
    net.put(far, far, net.at(dc=1))
    yield


def swap_ctx(net, blocks, out):
    for k in range(1, 2 * LINE):
        other = lax.rem(net.me + k, 2 * LINE)
        net.put(
            blocks.at[other], out.at[net.me], (other // 2, lax.rem(other, 2), net.x, net.core)
        )
    yield


def own_copies(pairs, sem):
    copies = [pltpu.make_async_copy(src, dst, sem.at[i]) for i, (src, dst) in enumerate(pairs)]
    for copy in copies:
        copy.start()
    return copies


def net_call(body, outs, args, copies, locals_, number, scratch=(), vmem=()):
    def kernel(*refs):
        *rest, send, recv, local = refs
        net = Net(send, recv)
        body(net, local, *rest)
        assert net.used <= copies, net.used

    any_space = pl.BlockSpec(memory_space=pl.ANY)
    in_vmem = pl.BlockSpec(memory_space=pltpu.VMEM)
    count = len(args)
    return pl.pallas_call(
        kernel,
        out_shape=outs,
        in_specs=[in_vmem if i in vmem else any_space for i in range(count)],
        out_specs=[in_vmem if count + i in vmem else any_space for i in range(len(outs))],
        scratch_shapes=list(scratch)
        + [
            pltpu.SemaphoreType.DMA((copies,)),
            pltpu.SemaphoreType.DMA((copies,)),
            pltpu.SemaphoreType.DMA((max(1, locals_),)),
        ],
        compiler_params=pltpu.CompilerParams(
            collective_id=number, has_side_effects=True, vmem_limit_bytes=VMEM_BYTES
        ),
    )(*args)


def shape_of(*dims, kind=jnp.bfloat16):
    return jax.ShapeDtypeStruct(dims, kind)


def gather_first(tokens, w_qkv, gains):
    rows = tokens.shape[0]

    def body(net, local, tok, wts, gns, tok_all, wts_all, gns_all):
        greet(net, ("z", "y", "x", "core"))
        f = 2 * net.x + net.core
        mine = own_copies(
            [(tok, tok_all.at[net.me]), (wts, wts_all.at[f]), (gns, gns_all.at[f])], local
        )
        drive(
            *gather_ctx_programs(net, tok, tok_all, rows * 4 // 5),
            gather_fsdp(net, wts, wts_all),
            gather_fsdp(net, gns, gns_all),
        )
        for copy in mine:
            copy.wait()
        net.close()

    return net_call(
        body,
        [
            shape_of(2 * LINE, *tokens.shape),
            shape_of(4, *w_qkv.shape),
            shape_of(4, *gains.shape),
        ],
        [tokens, w_qkv, gains],
        40,
        3,
        0,
    )


def swap_heads(blocks, number):
    def body(net, local, src, out):
        greet(net, ("ctx",))
        mine = own_copies([(src.at[net.me], out.at[net.me])], local)
        drive(swap_ctx(net, src, out))
        mine[0].wait()
        net.close()

    return net_call(body, [shape_of(*blocks.shape)], [blocks], 8, 1, number)[0]


def swap_two(first, second, number):
    def body(net, local, a, b, a_out, b_out):
        greet(net, ("ctx",))
        mine = own_copies(
            [(a.at[net.me], a_out.at[net.me]), (b.at[net.me], b_out.at[net.me])], local
        )
        drive(swap_ctx(net, a, a_out), swap_ctx(net, b, b_out))
        for copy in mine:
            copy.wait()
        net.close()

    return net_call(
        body, [shape_of(*first.shape), shape_of(*second.shape)], [first, second], 16, 2, number
    )


def gather_four(block, number):
    def body(net, local, own, out):
        greet(net, ("y", "core"))
        mine = own_copies([(own, out.at[2 * net.y + net.core])], local)
        drive(gather_quad(net, own, out))
        mine[0].wait()
        net.close()

    return net_call(body, [shape_of(4, *block.shape)], [block], 8, 1, number)[0]


def scatter_four(parts, number):
    _, rows, cols = parts.shape

    def body(net, local, src, out, from_core, near, from_side):
        greet(net, ("y", "core"))
        own, beside = 2 * net.y + net.core, 2 * net.y + 1 - net.core
        far, far_beside = 2 * (1 - net.y) + net.core, 2 * (1 - net.y) + 1 - net.core
        one = net.put(src.at[far_beside], from_core.at[0], net.at(dc=1))
        two = net.put(src.at[beside], from_core.at[1], net.at(dc=1))
        one.arrived()
        near[...] = low(src[far].astype(jnp.float32) + from_core[0].astype(jnp.float32))
        side = net.put(near, from_side, net.at(dy=1))
        two.arrived()
        out[...] = src[own].astype(jnp.float32) + from_core[1].astype(jnp.float32)
        side.arrived()
        out[...] += from_side[...].astype(jnp.float32)
        net.close()

    block = (rows, cols)
    return net_call(
        body,
        [shape_of(*block, kind=jnp.float32)],
        [parts],
        4,
        0,
        number,
        scratch=[
            pltpu.VMEM((2, *block), jnp.bfloat16),
            pltpu.VMEM(block, jnp.bfloat16),
            pltpu.VMEM(block, jnp.bfloat16),
        ],
        vmem=(0, 1),
    )[0]


def sum_line(net, held, send_up, send_down, got_up, got_down, ready):
    z = net.z
    ups, downs = [], []

    def fill(send, got, block, t, first):
        def alone():
            send[t] = low(held[block])

        def added():
            send[t] = low(held[block] + got[t - 1].astype(jnp.float32))

        return alone if first else added

    for t in range(LINE - 1):
        ready(t)
        to_up, to_down = LINE - 1 - t + z, z - LINE + 1 + t
        up_on, down_on = (z <= t) & (z < LINE - 1), (z >= LINE - 1 - t) & (z > 0)
        pl.when(z == 0)(fill(send_up, got_up, to_up, t, True))
        pl.when(z == LINE - 1)(fill(send_down, got_down, to_down, t, True))
        if t:
            pl.when(up_on & (z >= 1))(fill(send_up, got_up, to_up, t, False))
            pl.when(down_on & (z <= LINE - 2))(fill(send_down, got_down, to_down, t, False))
        ups.append(
            net.put(
                send_up.at[t], got_up.at[t], net.at(dz=1), up_on, (z >= 1) & (z - 1 <= t)
            )
        )
        downs.append(
            net.put(
                send_down.at[t],
                got_down.at[t],
                net.at(dz=-1),
                down_on,
                (z <= LINE - 2) & (z + 1 >= LINE - 1 - t),
            )
        )
        yield
        ups[t].arrived()
        downs[t].arrived()
    ready(LINE - 1)
    last = LINE - 2

    def add_up():
        held[z] += got_up[last].astype(jnp.float32)

    def add_down():
        held[z] += got_down[last].astype(jnp.float32)

    pl.when(z >= 1)(add_up)
    pl.when(z <= LINE - 2)(add_down)
    yield


def far_first(z):
    return [
        jnp.where(z < 2, 3, 0),
        jnp.where(z < 2, 2, 1),
        z + 1 - 2 * lax.rem(z, 2),
        z,
    ]


def line_scratch(rows, cols):
    line = pltpu.VMEM((LINE - 1, rows, cols), jnp.bfloat16)
    return [pltpu.VMEM((LINE, rows, cols), jnp.float32), line, line, line, line]


def sum_sides(net, src, from_side, line, make=None):
    z, y = net.z, net.y
    held = line[0]
    order = far_first(z)
    sides = []
    for k in order:
        if make is not None:
            make(2 * k + 1 - y)
        sides.append(net.put(src.at[2 * k + 1 - y], from_side.at[k], net.at(dy=1)))

    def ready(t):
        k = order[t]
        if make is not None:
            make(2 * k + y)
        sides[t].arrived()
        held[k] = src[2 * k + y].astype(jnp.float32) + from_side[k].astype(jnp.float32)

    yield from sum_line(net, *line, ready)


BLOCK = 256


def turn_lanes(v):
    return pltpu.roll(v, HEAD_SIZE // 2, 1)


def dot_last(a, b):
    return lax.dot_general(a, b, (((1,), (1,)), ((), ())), preferred_element_type=jnp.float32)


def resting(rounds):
    for _ in range(rounds):
        yield


class Bag:
    def __init__(self, **members):
        self.__dict__.update(members)


def bags(tree):
    return Bag(**{n: bags(v) for n, v in tree.items()}) if isinstance(tree, dict) else tree


def back_kernel(dims, number):
    rows, count, piece_rows = dims
    blocks = count // BLOCK
    scale = HEAD_SIZE**-0.5
    width = 2 * HEAD_SIZE
    d = MODEL_WIDTH

    def run(moved, loaded):
        a = Bag(**moved)
        gu_rows, gu_cols = a.gate.shape[1:]
        dn_rows = a.down.shape[1]
        o_rows = a.oproj.shape[1]
        bf, f32 = jnp.bfloat16, jnp.float32
        z_gu, z_dn, z_o = gu_rows // LINE, dn_rows // LINE, o_rows // (2 * LINE)
        gain_width = 2 * d + 2 * HEAD_SIZE

        def quarter():
            return dict(
                own=pltpu.VMEM((2, gu_rows, gu_cols), bf),
                got=pltpu.VMEM((2, gu_rows, gu_cols), bf),
                low=pltpu.VMEM((2, z_gu, gu_cols), bf),
                pair=pltpu.VMEM((2, z_gu, gu_cols), bf),
                line=line_scratch(2 * z_gu, gu_cols),
            )

        scratch = dict(
            held={n: pltpu.VMEM(v.shape, v.dtype) for n, v in loaded.items()},
            gate=quarter(),
            up=quarter(),
            down=dict(
                own=pltpu.VMEM((dn_rows, d), bf),
                got=pltpu.VMEM((dn_rows, d), bf),
                low=pltpu.VMEM((z_dn, d), bf),
                line=line_scratch(z_dn, d),
            ),
            o=dict(
                own=pltpu.VMEM((2, o_rows, d), bf),
                core=pltpu.VMEM((2, o_rows, d), bf),
                got=pltpu.VMEM((o_rows, d), bf),
                sum=pltpu.VMEM((2 * LINE, z_o, d), bf),
                side=pltpu.VMEM((LINE, z_o, d), bf),
                low=pltpu.VMEM((z_o, d), bf),
                line=line_scratch(z_o, d),
            ),
            h=dict(
                own=pltpu.VMEM((4, d // 4, 2 * width), bf),
                core=pltpu.VMEM((2, d // 4, 2 * width), bf),
                got=pltpu.VMEM((d // 4, 2 * width), bf),
                low=pltpu.VMEM((d // 4, 2 * width), bf),
            ),
            dm_all=pltpu.VMEM((2 * LINE, rows, width), bf),
            do=pltpu.VMEM((count, width), bf),
            dk=pltpu.VMEM((count, HEAD_SIZE), f32),
            dv=pltpu.VMEM((count, HEAD_SIZE), f32),
            dqkv=pltpu.VMEM((count, 2 * width), bf),
            dgq=pltpu.VMEM((1, HEAD_SIZE), f32),
            dgk=pltpu.VMEM((1, HEAD_SIZE), f32),
            part=dict(
                sum=pltpu.VMEM((2 * LINE, rows, d), bf),
                side=pltpu.VMEM((LINE, rows, d), bf),
                line=line_scratch(rows, d),
            ),
            g=dict(
                mine=pltpu.VMEM((1, gain_width), f32),
                pair=pltpu.VMEM((1, gain_width), f32),
                four=pltpu.VMEM((1, gain_width), f32),
                got=pltpu.VMEM((2, 1, gain_width), f32),
                all=pltpu.VMEM((2 * LINE, 1, gain_width), f32),
            ),
        )
        flat, tree = jax.tree.flatten(scratch)
        f_in, in_tree = jax.tree.flatten((moved, loaded))
        outs = dict(
            dx1=shape_of(rows, d, kind=f32),
            back=shape_of(*a.back.shape),
            gains=shape_of(1, gain_width, kind=f32),
            gate=shape_of(2 * LINE, 2, z_gu, gu_cols),
            up=shape_of(2 * LINE, 2, z_gu, gu_cols),
            down=shape_of(2 * LINE, z_dn, d),
            o=shape_of(2 * LINE, z_o, d),
            heads=shape_of(2 * LINE, d // 4, 2 * width),
        )
        f_out, out_tree = jax.tree.flatten(outs)

        def body(net, local, *refs):
            given, to_load = jax.tree.unflatten(in_tree, refs[: len(f_in)])
            given = Bag(**given)
            out = Bag(**jax.tree.unflatten(out_tree, refs[len(f_in) : len(f_in) + len(f_out)]))
            r = bags(jax.tree.unflatten(tree, refs[len(f_in) + len(f_out) :]))
            h = r.held
            z, y, x, core, me = net.z, net.y, net.x, net.core, net.me
            slots = 2 * LINE
            used = iter(range(64))

            def fetch(src, dst):
                copy = pltpu.make_async_copy(src, dst, local.at[next(used)])
                copy.start()
                return copy

            greet(net, ("ctx", "x", "core"))
            done = set()
            dm_own = fetch(given.dm.at[me], r.dm_all.at[me])
            for k in range(1, slots):
                other = lax.rem(me + k, slots)
                there = (other // 2, lax.rem(other, 2), x, core)
                net.put(given.dm.at[other], r.dm_all.at[me], there)
            dm_copies = list(net.open)
            loads = [fetch(to_load[n], getattr(h, n)) for n in to_load]

            def over_x(src, piece):
                own = [fetch(src.at[2 * x + c], piece.own.at[c]) for c in range(2)]
                sent = [
                    net.put(src.at[2 * (1 - x) + c], piece.got.at[c], net.at(dx=1))
                    for c in range(2)
                ]
                return own, sent

            o_own = [fetch(given.oproj.at[2 * s + core], r.o.own.at[s]) for s in range(2)]
            o_core = [
                net.put(given.oproj.at[2 * s + 1 - core], r.o.core.at[s], net.at(dc=1))
                for s in range(2)
            ]
            gate_over, up_over = over_x(given.gate, r.gate), over_x(given.up, r.up)
            down_over = (
                [fetch(given.down.at[x], r.down.own)],
                [net.put(given.down.at[1 - x], r.down.got, net.at(dx=1))],
            )

            def land(over):
                own, sent = over
                for c in own:
                    c.wait()
                for c in sent:
                    c.arrived()

            def main():
                for c in loads:
                    c.wait()
                dm_own.wait()
                for c in dm_copies:
                    c.arrived()
                yield
                for i in range(blocks):
                    t = i * BLOCK + lax.broadcasted_iota(jnp.int32, (BLOCK, count), 0)
                    hot = low(jnp.where(h.dealt[...] == t, 1.0, 0.0))
                    r.do[pl.ds(i * BLOCK, BLOCK)] = low(
                        dot(hot, r.dm_all[...].reshape(count, width))
                    )
                r.dk[...] = jnp.zeros_like(r.dk)
                r.dv[...] = jnp.zeros_like(r.dv)
                yield
                dgq = jnp.zeros((1, HEAD_SIZE), f32)
                for i in range(blocks):
                    here = pl.ds(i * BLOCK, BLOCK)
                    first = h.first[:, here]
                    t = i * BLOCK + lax.broadcasted_iota(jnp.int32, (BLOCK, BLOCK), 1)
                    heads = []
                    for g in range(2):
                        lanes = pl.ds(g * HEAD_SIZE, HEAD_SIZE)
                        q, do = h.q[here, lanes], r.do[here, lanes]
                        product = do.astype(f32) * h.mixed[here, lanes]
                        delta = jnp.sum(jnp.transpose(product), axis=0, keepdims=True)
                        heads.append((q, do, h.lse[g, :, here], delta))

                    def step(j, held, heads=heads, first=first, t=t):
                        at = pl.ds(pl.multiple_of(j * BLOCK, BLOCK), BLOCK)
                        k, v, kt = h.k[at], h.v[at], h.kt[:, at]
                        u = j * BLOCK + lax.broadcasted_iota(jnp.int32, (BLOCK, BLOCK), 0)
                        allowed = (u >= first) & (u <= t)
                        dk, dv, out = r.dk[at], r.dv[at], []
                        for (q, do, lse, delta), dq in zip(heads, held):
                            p = jnp.where(allowed, jnp.exp(dot_last(k, q) * scale - lse), 0.0)
                            ds = low(p * (dot_last(v, do) - delta))
                            dv = dv + dot(low(p), do)
                            dk = dk + dot(ds, q)
                            out.append(dq + dot(kt, ds))
                        r.dk[at] = dk
                        r.dv[at] = dv
                        return tuple(out)

                    zero = jnp.zeros((HEAD_SIZE, BLOCK), f32)
                    result = lax.fori_loop(0, i + 1, step, (zero, zero))
                    cos, sin = h.cos[here], h.sin[here]
                    for g in range(2):
                        lanes = pl.ds(g * HEAD_SIZE, HEAD_SIZE)
                        grad = jnp.transpose(result[g]) * scale
                        grad = grad * cos - turn_lanes(grad) * sin
                        dx, dg = norm_back(h.q_pre[here, lanes], h.q_gain[...], grad)
                        r.dqkv[here, lanes] = low(dx)
                        dgq = dgq + jnp.sum(dg, axis=0, keepdims=True)
                    yield
                dgk = jnp.zeros((1, HEAD_SIZE), f32)
                for i in range(blocks):
                    here = pl.ds(i * BLOCK, BLOCK)
                    grad = r.dk[here] * scale
                    grad = grad * h.cos[here] - turn_lanes(grad) * h.sin[here]
                    dx, dg = norm_back(h.k_pre[here], h.k_gain[...], grad)
                    r.dqkv[here, pl.ds(width, HEAD_SIZE)] = low(dx)
                    r.dqkv[here, pl.ds(width + HEAD_SIZE, HEAD_SIZE)] = low(r.dv[here])
                    dgk = dgk + jnp.sum(dg, axis=0, keepdims=True)
                r.dgq[...] = dgq
                r.dgk[...] = dgk
                done.add("dqkv")

                def make(slot):
                    at = pl.ds(pl.multiple_of(slot * rows, rows), rows)
                    r.part.sum[slot] = low(dot_last(r.dqkv[at], h.w_qkv[...]))

                yield from sum_sides(net, r.part.sum, r.part.side, r.part.line, make)
                dx1, dg1 = norm_back(
                    h.tok[...].astype(f32), h.a_gain[...], r.part.line[0][z]
                )
                out.dx1[...] = dx1
                r.g.mine[:, pl.ds(0, d)] = jnp.sum(dg1, axis=0, keepdims=True)
                r.g.mine[:, pl.ds(d, d)] = h.dg2[...]
                r.g.mine[:, pl.ds(2 * d, HEAD_SIZE)] = r.dgq[...]
                r.g.mine[:, pl.ds(2 * d + HEAD_SIZE, HEAD_SIZE)] = r.dgk[...]
                done.add("gains")
                yield

            def gains():
                while "gains" not in done:
                    yield
                pair = net.put(r.g.mine, r.g.got.at[0], net.at(dc=1))
                yield
                pair.arrived()
                r.g.pair[...] = r.g.mine[...] + r.g.got[0]
                four = net.put(r.g.pair, r.g.got.at[1], net.at(dx=1))
                yield
                four.arrived()
                r.g.four[...] = r.g.pair[...] + r.g.got[1]
                r.g.all[me] = r.g.four[...]
                copies = []
                for k in range(1, slots):
                    other = lax.rem(me + k, slots)
                    there = (other // 2, lax.rem(other, 2), x, core)
                    copies.append(net.put(r.g.four, r.g.all.at[me], there))
                yield
                yield
                for c in copies:
                    c.arrived()
                out.gains[...] = jnp.sum(r.g.all[...], axis=0)
                yield

            def back_rows():
                while "dqkv" not in done:
                    yield
                own = fetch(given.back.at[me], out.back.at[me])
                for k in range(1, slots):
                    other = lax.rem(me + k, slots)
                    there = (other // 2, lax.rem(other, 2), x, core)
                    net.put(given.back.at[other], out.back.at[me], there)
                yield
                own.wait()

            def gate_or_up(over, piece, gathered, rest):
                yield from resting(rest)
                land(over)
                line = piece.line

                def ready(t):
                    k = far_first(z)[t]
                    at = pl.ds(pl.multiple_of(k * z_gu, z_gu), z_gu)
                    for c in range(2):
                        line[0][k, pl.ds(c * z_gu, z_gu)] = piece.own[c, at].astype(
                            f32
                        ) + piece.got[c, at].astype(f32)

                yield from sum_line(net, *line, ready)
                for c in range(2):
                    piece.low[c] = low(line[0][z, pl.ds(c * z_gu, z_gu)])
                swap = net.put(piece.low.at[1 - core], piece.pair.at[core], net.at(dc=1))
                piece.pair[core] = piece.low[core]
                yield
                swap.arrived()
                own = fetch(piece.pair, gathered.at[me])
                yield from gather_line_first(net, piece.pair, lambda slot: gathered.at[slot])
                own.wait()

            def down(rest):
                yield from resting(rest)
                land(down_over)
                line = r.down.line

                def ready(t):
                    k = far_first(z)[t]
                    at = pl.ds(pl.multiple_of(k * z_dn, z_dn), z_dn)
                    line[0][k] = r.down.own[at].astype(f32) + r.down.got[at].astype(f32)

                yield from sum_line(net, *line, ready)
                r.down.low[...] = low(line[0][z])
                own = fetch(r.down.low, out.down.at[me])
                yield from gather_line_first(net, r.down.low, lambda slot: out.down.at[slot])
                own.wait()

            def out_proj(rest_core, rest_x):
                yield from resting(rest_core)
                for c in o_own:
                    c.wait()
                for c in o_core:
                    c.arrived()
                r.o.own[...] = low(r.o.own[...].astype(f32) + r.o.core[...].astype(f32))
                over = net.put(r.o.own.at[1 - x], r.o.got, net.at(dx=1))
                yield from resting(rest_x)
                over.arrived()
                for i in range(slots):
                    at = pl.ds(i * z_o, z_o)
                    r.o.sum[i] = low(r.o.own[x, at].astype(f32) + r.o.got[at].astype(f32))
                yield from sum_sides(net, r.o.sum, r.o.side, r.o.line)
                r.o.low[...] = low(r.o.line[0][z])
                own = fetch(r.o.low, out.o.at[me])
                yield from gather_line_first(net, r.o.low, lambda slot: out.o.at[slot])
                own.wait()

            def heads(rest):
                while "dqkv" not in done:
                    yield
                for f in range(4):
                    at = pl.ds(f * (d // 4), d // 4)
                    r.h.own[f] = low(outer_rows(h.normed[:, at], r.dqkv[...]))
                core_copies = [
                    net.put(r.h.own.at[2 * s + 1 - core], r.h.core.at[s], net.at(dc=1))
                    for s in range(2)
                ]
                yield
                for c in core_copies:
                    c.arrived()
                for s in range(2):
                    f = 2 * s + core
                    r.h.own[f] = low(r.h.own[f].astype(f32) + r.h.core[s].astype(f32))
                over = net.put(r.h.own.at[2 * (1 - x) + core], r.h.got, net.at(dx=1))
                yield from resting(rest)
                over.arrived()
                r.h.low[...] = low(
                    r.h.own[2 * x + core].astype(f32) + r.h.got[...].astype(f32)
                )
                own = fetch(r.h.low, out.heads.at[me])
                yield from gather_line_first(net, r.h.low, lambda slot: out.heads.at[slot])
                own.wait()

            drive(
                main(),
                gate_or_up(gate_over, r.gate, out.gate, 3),
                gate_or_up(up_over, r.up, out.up, 9),
                down(11),
                out_proj(1, 13),
                heads(3),
                back_rows(),
                gains(),
            )
            net.close()

        order = jax.tree.unflatten(out_tree, range(len(f_out)))
        result = net_call(
            body,
            f_out,
            f_in,
            200,
            64,
            number,
            scratch=flat,
            vmem=(len(f_in) + order.get("dx1"), len(f_in) + order.get("gains")),
        )
        return Bag(**jax.tree.unflatten(out_tree, result))

    return run


def widen(gate_all, up_all, down_all, o_all, heads_all):
    _, _, z_gu, gu_cols = gate_all.shape
    half = gu_cols // 2
    z_dn, z_o = down_all.shape[1], o_all.shape[1]
    h_rows = heads_all.shape[1] // LINE

    def kernel(gate, up, down, o, heads, gate_out, up_out, down_out, o_out, q_out, k_out, v_out):
        for src, out in ((gate, gate_out), (up, up_out)):
            for y in range(2):
                for c in range(2):
                    for xs in range(2):
                        to = (2 * xs + c) * 2 * half + y * half
                        out[:, pl.ds(to, half)] = src[y, c, :, pl.ds(xs * half, half)].astype(
                            jnp.float32
                        )
        for y in range(2):
            down_out[y] = down[y].astype(jnp.float32)
            o_out[pl.ds(y * z_o, z_o)] = o[y].astype(jnp.float32)
        for h in range(2 * LINE):
            q_out[:, pl.ds(h * 256, 256)] = heads[h, :, pl.ds(0, 256)].astype(jnp.float32)
            k_out[:, pl.ds(h * 128, 128)] = heads[h, :, pl.ds(256, 128)].astype(jnp.float32)
            v_out[:, pl.ds(h * 128, 128)] = heads[h, :, pl.ds(384, 128)].astype(jnp.float32)

    f32 = jnp.float32
    outs = pl.pallas_call(
        kernel,
        grid=(LINE,),
        in_specs=[
            pl.BlockSpec((2, 2, z_gu, gu_cols), lambda i: (i, 0, 0, 0)),
            pl.BlockSpec((2, 2, z_gu, gu_cols), lambda i: (i, 0, 0, 0)),
            pl.BlockSpec((2, z_dn, MODEL_WIDTH), lambda i: (i, 0, 0)),
            pl.BlockSpec((2, z_o, MODEL_WIDTH), lambda i: (i, 0, 0)),
            pl.BlockSpec((2 * LINE, h_rows, 512), lambda i: (0, i, 0)),
        ],
        out_specs=[
            pl.BlockSpec((z_gu, 8 * half), lambda i: (i, 0)),
            pl.BlockSpec((z_gu, 8 * half), lambda i: (i, 0)),
            pl.BlockSpec((2, z_dn, MODEL_WIDTH), lambda i: (0, i, 0)),
            pl.BlockSpec((2 * z_o, MODEL_WIDTH), lambda i: (i, 0)),
            pl.BlockSpec((h_rows, 2048), lambda i: (i, 0)),
            pl.BlockSpec((h_rows, 1024), lambda i: (i, 0)),
            pl.BlockSpec((h_rows, 1024), lambda i: (i, 0)),
        ],
        out_shape=[
            shape_of(LINE * z_gu, 8 * half, kind=f32),
            shape_of(LINE * z_gu, 8 * half, kind=f32),
            shape_of(2, LINE * z_dn, MODEL_WIDTH, kind=f32),
            shape_of(2 * LINE * z_o, MODEL_WIDTH, kind=f32),
            shape_of(LINE * h_rows, 2048, kind=f32),
            shape_of(LINE * h_rows, 1024, kind=f32),
            shape_of(LINE * h_rows, 1024, kind=f32),
        ],
        compiler_params=pltpu.CompilerParams(vmem_limit_bytes=VMEM_BYTES),
    )(gate_all, up_all, down_all, o_all, heads_all)
    outs = list(outs)
    outs[2] = outs[2].reshape(-1, MODEL_WIDTH)
    return outs


def fast_layer(
    tokens,
    lengths,
    deal,
    attn_gain,
    w_q,
    key_weight,
    value_weight,
    query_norm_gain,
    k_gain,
    w_o,
    mlp_gain,
    w_gate,
    w_up,
    w_down,
    out_cotangent,
):
    rows = tokens.shape[1]
    slots = lax.axis_size(CTX)
    piece = rows // slots
    count = rows * slots
    here = lax.axis_index(CTX)
    y, core = lax.axis_index("y"), lax.axis_index("core")
    x = lax.axis_index("x")
    ff_shard = w_down.shape[0]
    ff_half = ff_shard // 2
    width = HEAD_SIZE * 2

    starts = jnp.cumsum(lengths[0]) - lengths[0]
    ids = jnp.arange(count, dtype=jnp.int32)
    first = segment_begin(ids, starts)
    cosine, sine = rope_tables(ids - first)
    plan = deal[0]
    devices = jnp.arange(slots, dtype=jnp.int32)
    slot_of = jnp.sum(
        jnp.where(plan[:, :, None] == devices[None, None, :], devices[None, :, None], 0), axis=1
    )
    dealt_index = (
        devices[None, :, None] * rows
        + jnp.transpose(slot_of)[:, :, None] * piece
        + jnp.arange(piece, dtype=jnp.int32)[None, None, :]
    ).reshape(count)
    to_dealt = low(dealt_index[:, None] == ids[None, :])

    packed_gain = jnp.concatenate([attn_gain, mlp_gain, query_norm_gain, k_gain])[None]
    qkv_own = jnp.concatenate(
        [
            lax.dynamic_slice_in_dim(w_q, here * width, width, 1),
            lax.dynamic_slice_in_dim(key_weight, here * HEAD_SIZE, HEAD_SIZE, 1),
            lax.dynamic_slice_in_dim(value_weight, here * HEAD_SIZE, HEAD_SIZE, 1),
        ],
        axis=1,
    )
    all_tokens, w_qkv, gains = gather_first(tokens[0], qkv_own, jnp.tile(packed_gain, (16, 1)))
    all_tokens = all_tokens.reshape(count, MODEL_WIDTH)
    w_qkv = w_qkv.reshape(MODEL_WIDTH, -1)
    gains = gains[:, 0].astype(jnp.float32)
    a_gain = gains[:, :256].reshape(-1)
    m_gain = gains[:, 256:512].reshape(-1)
    q_gain = gains[:, 512:544].reshape(-1)
    k_gain_all = gains[:, 544:576].reshape(-1)
    values = all_tokens.astype(jnp.float32)
    normed = low(root_mean_norm(values, a_gain))
    qkv = dot(normed, w_qkv)
    q_pre = qkv[:, :width].reshape(count, 2, HEAD_SIZE)
    k_pre = qkv[:, width : width + HEAD_SIZE]
    v_low = low(qkv[:, width + HEAD_SIZE :])

    def rope(v, cos, sin):
        return v * cos + half_turn(v) * sin

    q_low = low(rope(root_mean_norm(q_pre, q_gain), cosine[:, None], sine[:, None]))
    k_low = low(rope(root_mean_norm(k_pre, k_gain_all), cosine, sine))
    allowed = (ids[None, :] >= first[:, None]) & (ids[None, :] <= ids[:, None])
    scale = HEAD_SIZE**-0.5
    scores = jnp.einsum("tgh,uh->gtu", q_low, k_low, preferred_element_type=jnp.float32) * scale
    scores = jnp.where(allowed, scores, negative_filler)
    top = jnp.max(scores, axis=-1, keepdims=True)
    weights = jnp.exp(scores - top)
    total = jnp.sum(weights, axis=-1, keepdims=True)
    log_total = top + jnp.log(total)
    mixed = (
        jnp.einsum("gtu,uh->gth", low(weights), v_low, preferred_element_type=jnp.float32) / total
    )
    mixed_heads = low(jnp.transpose(mixed, (1, 0, 2)).reshape(count, width))
    mixed_out = low(dot(to_dealt, mixed_heads)).reshape(slots, rows, width)
    mixed_in = swap_heads(mixed_out, 1)
    mixed_low = jnp.transpose(mixed_in, (1, 0, 2)).reshape(rows, slots * width)

    own_rows = lax.dynamic_slice_in_dim(to_dealt, here * rows, rows, 0)
    residual = dot(own_rows, all_tokens)
    full_o = gather_fsdp_plain(w_o)
    middle = residual + dot(mixed_low, full_o)
    normed2 = low(root_mean_norm(middle, m_gain))

    def quarter_cols(w, c):
        return jnp.concatenate(
            [
                lax.dynamic_slice_in_dim(w, (2 * xs + c) * ff_shard + y * ff_half, ff_half, 1)
                for xs in range(2)
            ],
            axis=1,
        )

    sides = jnp.stack(
        [
            jnp.concatenate([quarter_cols(w_gate, c), quarter_cols(w_up, c)], axis=1)
            for c in range(2)
        ]
    )
    sides = lax.all_to_all(sides, "core", 0, 0, tiled=True)
    w_gu = lax.all_gather(sides, "x", axis=0, tiled=True).reshape(-1, 4 * ff_half)
    down_own = lax.dynamic_slice_in_dim(w_down, y * ff_half, ff_half, 0)
    w_dn = lax.all_gather(down_own, "x", axis=0, tiled=True)
    quad_n = gather_four(normed2, 2).reshape(4 * rows, -1)
    quad_g = gather_four(out_cotangent[0], 3).reshape(4 * rows, -1)
    gate_up = dot(quad_n, w_gu)
    gate, up = gate_up[:, : 2 * ff_half], gate_up[:, 2 * ff_half :]
    sig = 1.0 / (1.0 + jnp.exp(-gate))
    silu = gate * sig
    hidden = low(silu * up)
    partial_out = low(dot(hidden, w_dn))
    out_sum = scatter_four(partial_out.reshape(4, rows, -1), 4)
    output = low(middle + out_sum)

    d_hidden = dot_trans(quad_g, w_dn)
    d_gate = low(d_hidden * up * (sig * (1.0 + gate * (1.0 - sig))))
    d_up = low(d_hidden * silu)
    d_gu = jnp.concatenate([d_gate, d_up], axis=1)
    dn2_part = low(dot_trans(d_gu, w_gu))
    d_normed2 = scatter_four(dn2_part.reshape(4, rows, -1), 5)
    grad_gate = low(outer_rows(quad_n, d_gate))
    grad_up = low(outer_rows(quad_n, d_up))
    grad_dn = low(outer_rows(hidden, quad_g))
    dx2, dg2 = norm_back(middle, m_gain, d_normed2)
    d_middle = out_cotangent[0].astype(jnp.float32) + dx2
    middle_low = low(d_middle)
    d_mixed_tok = low(dot_trans(middle_low, full_o))
    dm_out = jnp.transpose(d_mixed_tok.reshape(rows, slots, width), (1, 0, 2))
    grad_o = low(outer_rows(mixed_low, middle_low))
    moved = dict(
        dm=dm_out,
        back=middle_low.reshape(slots, -1, HEAD_SIZE),
        gate=grad_gate.reshape(4, -1, 2 * ff_half),
        up=grad_up.reshape(4, -1, 2 * ff_half),
        down=grad_dn.reshape(2, -1, MODEL_WIDTH),
        oproj=grad_o.reshape(4, -1, MODEL_WIDTH),
    )
    loaded = dict(
        tok=tokens[0],
        a_gain=a_gain[None],
        dg2=jnp.sum(dg2, axis=0)[None],
        q=q_low.reshape(count, width),
        k=k_low,
        kt=jnp.transpose(k_low),
        v=v_low,
        mixed=jnp.transpose(mixed, (1, 0, 2)).reshape(count, width),
        lse=log_total.reshape(2, 1, count),
        first=first[None],
        dealt=dealt_index[None],
        q_pre=qkv[:, :width],
        k_pre=k_pre,
        q_gain=q_gain[None],
        k_gain=k_gain_all[None],
        cos=cosine,
        sin=sine * jnp.where(jnp.arange(HEAD_SIZE) < HEAD_SIZE // 2, -1.0, 1.0),
        normed=normed,
        w_qkv=w_qkv,
    )
    sums = back_kernel((rows, count, piece), 6)(moved, loaded)

    own_plan = lax.dynamic_index_in_dim(plan, here, 0, keepdims=False)
    back = sums.back.reshape(slots, piece, MODEL_WIDTH)
    d_middle_given = jnp.take(back, own_plan, axis=0).reshape(rows, MODEL_WIDTH)
    input_grad = d_middle_given.astype(jnp.float32) + sums.dx1

    place = 2 * x + core

    def own_part(start, size):
        part = sums.gains[0, start : start + size]
        return lax.dynamic_slice_in_dim(part, place * (size // 4), size // 4)

    gate_sum, up_sum, down_sum, o_sum, q_sum, k_sum, v_sum = widen(
        sums.gate, sums.up, sums.down, sums.o, sums.heads
    )
    return (
        output[None],
        input_grad[None],
        own_part(0, MODEL_WIDTH),
        own_part(2 * MODEL_WIDTH, HEAD_SIZE),
        own_part(2 * MODEL_WIDTH + HEAD_SIZE, HEAD_SIZE),
        own_part(MODEL_WIDTH, MODEL_WIDTH),
        q_sum,
        k_sum,
        v_sum,
        o_sum,
        gate_sum,
        up_sum,
        down_sum,
    )


def solution(mesh):
    devices = mesh.devices
    if devices.shape == (8, 4):
        mesh = Mesh(devices.reshape(4, 2, 2, 2), CTX + FSDP)
        layer, ctx, fsdp = fast_layer, CTX, FSDP
    else:
        layer, ctx, fsdp = general_layer, "ctx", "fsdp"
    wide_rows = P(fsdp, ctx, None)
    return jax.shard_map(
        layer,
        mesh=mesh,
        in_specs=(
            wide_rows,
            P(fsdp, None),
            P(fsdp, None, None),
            P(fsdp),
            P(fsdp, None),
            P(fsdp, None),
            P(fsdp, None),
            P(fsdp),
            P(fsdp),
            P(fsdp, None),
            P(fsdp),
            P(fsdp, None),
            P(fsdp, None),
            P(fsdp, None),
            wide_rows,
        ),
        out_specs=(wide_rows, wide_rows) + (P(fsdp),) * 4 + (P(fsdp, None),) * 7,
        check_vma=False,
    )
```

```python
import math

import jax
import jax.numpy as jnp
from jax import lax
from jax.experimental import pallas as pl
from jax.experimental.pallas import tpu as pltpu
from jax.sharding import Mesh
from jax.sharding import PartitionSpec as P

MODEL_WIDTH = 1024
QUERY_HEADS = 16
KEY_VALUE_HEADS = 8
HEAD_SIZE = 128


eps = 1e-06
theta_base = 1000000.0
negative_filler = -1e30


def root_mean_norm(values, gain_vec):
    return values * lax.rsqrt(jnp.mean(values * values, axis=-1, keepdims=True) + eps) * gain_vec


def rotary_embedding(values, token_position):
    half_width = values.shape[-1] // 2
    frequency = theta_base ** (
        -(jnp.arange(half_width, dtype=jnp.float32) * 2.0) / values.shape[-1]
    )
    angles = token_position.astype(jnp.float32)[:, None] * frequency[None, :]
    cosine = jnp.concatenate([jnp.cos(angles), jnp.cos(angles)], axis=-1)[:, None, :]
    sine_part = jnp.concatenate([jnp.sin(angles), jnp.sin(angles)], axis=-1)[:, None, :]
    turned = jnp.concatenate([-values[..., half_width:], values[..., :half_width]], axis=-1)
    return values * cosine + turned * sine_part


def dot_trans(left_side, right_side):
    return lax.dot_general(
        left_side, right_side, (((1,), (1,)), ((), ())), preferred_element_type=jnp.float32
    )


def outer_rows(left_side, right_side):
    return lax.dot_general(
        left_side, right_side, (((0,), (0,)), ((), ())), preferred_element_type=jnp.float32
    )


def block_plan(piece_rows, local_rows):
    shards = piece_rows // local_rows
    per_block = math.gcd(shards, max(1, 1024 // local_rows))
    return (per_block * local_rows, shards // per_block)


def over_blocks(carried, arrays, local_rows, block_work):
    rows_per_block, count_of_blocks = block_plan(arrays[0].shape[0], local_rows)

    def one_block(turn_index, state_now):
        offset = turn_index * rows_per_block
        parts = tuple(
            (lax.dynamic_slice_in_dim(member, offset, rows_per_block, 0) for member in arrays)
        )
        return block_work(state_now, parts, offset)

    return lax.fori_loop(0, count_of_blocks, one_block, carried)


def segment_begin(tok_ids, starts):
    return jnp.max(jnp.where(tok_ids[:, None] >= starts[None, :], starts[None, :], 0), axis=1)


def general_layer(
    tokens,
    lengths,
    deal,
    attn_gain,
    w_q,
    key_weight,
    value_weight,
    query_norm_gain,
    k_gain,
    w_o,
    mlp_gain,
    w_gate,
    w_up,
    w_down,
    out_cotangent,
):
    local_rows = tokens.shape[1]
    piece_count = lax.axis_size("ctx")
    piece_rows = local_rows // piece_count
    here = lax.axis_index("ctx")
    group_width = QUERY_HEADS // KEY_VALUE_HEADS
    score_scale = HEAD_SIZE ** (-0.5)
    seq_lengths = lengths[0]
    starts = jnp.cumsum(seq_lengths) - seq_lengths
    plan = deal[0]
    devices = jnp.arange(piece_count, dtype=jnp.int32)
    hits = plan[:, :, None] == devices[None, None, :]
    slot_of = jnp.sum(jnp.where(hits, devices[None, :, None], 0), axis=1)
    inner = jnp.arange(piece_rows, dtype=jnp.int32)
    dealt_index = (
        devices[None, :, None] * local_rows
        + jnp.transpose(slot_of)[:, :, None] * piece_rows
        + inner[None, None, :]
    ).reshape(piece_count * local_rows)
    dealt_first = segment_begin(dealt_index, starts)
    tok_index = lax.dynamic_slice_in_dim(dealt_index, here * local_rows, local_rows)
    segment_initial = lax.dynamic_slice_in_dim(dealt_first, here * local_rows, local_rows)
    token_position = tok_index - segment_initial
    own_slots = lax.dynamic_index_in_dim(slot_of, here, 0, keepdims=False)
    own_plan = lax.dynamic_index_in_dim(plan, here, 0, keepdims=False)
    token_pieces = jnp.take(
        tokens[0].reshape(piece_count, piece_rows, MODEL_WIDTH), own_slots, axis=0
    )
    dealt_tok = lax.all_to_all(
        token_pieces, "ctx", split_axis=0, concat_axis=0, tiled=True
    ).reshape(local_rows, MODEL_WIDTH)

    def key_mask(start_row, local_row_count):
        key_identifiers = lax.dynamic_slice_in_dim(dealt_index, start_row, local_row_count)
        return (key_identifiers[None, :] >= segment_initial[:, None]) & (
            key_identifiers[None, :] <= tok_index[:, None]
        )

    def query_mask(start_row, local_row_count):
        query_ids = lax.dynamic_slice_in_dim(dealt_index, start_row, local_row_count)
        first_key = lax.dynamic_slice_in_dim(dealt_first, start_row, local_row_count)
        return (tok_index[None, :] >= first_key[:, None]) & (
            tok_index[None, :] <= query_ids[:, None]
        )

    def fetch_weights():
        attn_set = (
            lax.all_gather(attn_gain, "fsdp", axis=0, tiled=True),
            lax.all_gather(query_norm_gain, "fsdp", axis=0, tiled=True),
            lax.all_gather(k_gain, "fsdp", axis=0, tiled=True),
            lax.all_gather(w_q, "fsdp", axis=0, tiled=True),
            lax.all_gather(key_weight, "fsdp", axis=0, tiled=True),
            lax.all_gather(value_weight, "fsdp", axis=0, tiled=True),
            lax.all_gather(w_o, "fsdp", axis=0, tiled=True),
        )
        mlp_set = (
            lax.all_gather(mlp_gain, "fsdp", axis=0, tiled=True),
            lax.all_gather(w_gate, "fsdp", axis=0, tiled=True),
            lax.all_gather(w_up, "fsdp", axis=0, tiled=True),
            lax.all_gather(w_down, "fsdp", axis=0, tiled=True),
        )
        return (attn_set, mlp_set)

    def forward(attn_set, mlp_set, token_rows):
        a_gain, qn_gain, kn_gain, proj_q, proj_k, proj_v, proj_o = attn_set
        m_gain, proj_gate, proj_up, proj_down = mlp_set
        residual = token_rows.astype(jnp.float32)
        normalized_input = root_mean_norm(residual, a_gain.astype(jnp.float32)).astype(jnp.bfloat16)
        query_prenorm = jnp.dot(
            normalized_input, proj_q, preferred_element_type=jnp.float32
        ).reshape(local_rows, QUERY_HEADS, HEAD_SIZE)
        key_prenorm = jnp.dot(normalized_input, proj_k, preferred_element_type=jnp.float32).reshape(
            local_rows, KEY_VALUE_HEADS, HEAD_SIZE
        )
        value_narrow = jnp.dot(normalized_input, proj_v, preferred_element_type=jnp.float32).astype(
            jnp.bfloat16
        )
        q_heads = (
            rotary_embedding(
                root_mean_norm(query_prenorm, qn_gain.astype(jnp.float32)), token_position
            )
            .astype(jnp.bfloat16)
            .reshape(local_rows, KEY_VALUE_HEADS, group_width, HEAD_SIZE)
        )
        key_narrow = (
            rotary_embedding(
                root_mean_norm(key_prenorm, kn_gain.astype(jnp.float32)), token_position
            )
            .astype(jnp.bfloat16)
            .reshape(local_rows, KEY_VALUE_HEADS * HEAD_SIZE)
        )

        def attend_over_block(state_now, shard_piece, start_row):
            key_segment, value_segment = shard_piece
            local_row_count = key_segment.shape[0]
            allowed = key_mask(start_row, local_row_count)
            row_top, row_total, weighted = state_now
            scores = (
                jnp.einsum(
                    "rkgh,ckh->kgrc",
                    q_heads,
                    key_segment.reshape(local_row_count, KEY_VALUE_HEADS, HEAD_SIZE),
                    preferred_element_type=jnp.float32,
                )
                * score_scale
            )
            scores = jnp.where(allowed, scores, negative_filler)
            new_top = jnp.maximum(row_top, jnp.max(scores, axis=-1))
            rescale = jnp.exp(row_top - new_top)
            weights = jnp.where(allowed, jnp.exp(scores - new_top[..., None]), 0.0)
            row_total = row_total * rescale + jnp.sum(weights, axis=-1)
            weighted = weighted * rescale[..., None] + jnp.einsum(
                "kgrc,ckh->kgrh",
                weights.astype(jnp.bfloat16),
                value_segment.reshape(local_row_count, KEY_VALUE_HEADS, HEAD_SIZE),
                preferred_element_type=jnp.float32,
            )
            return (new_top, row_total, weighted)

        initial = (
            jnp.full((KEY_VALUE_HEADS, group_width, local_rows), negative_filler, jnp.float32),
            jnp.zeros((KEY_VALUE_HEADS, group_width, local_rows), jnp.float32),
            jnp.zeros((KEY_VALUE_HEADS, group_width, local_rows, HEAD_SIZE), jnp.float32),
        )
        row_top, row_total, weighted = over_blocks(
            initial,
            (
                lax.all_gather(key_narrow, "ctx", axis=0, tiled=True),
                lax.all_gather(value_narrow, "ctx", axis=0, tiled=True),
            ),
            local_rows,
            attend_over_block,
        )
        attention_mixed = jnp.transpose(weighted / row_total[..., None], (2, 0, 1, 3)).reshape(
            local_rows, QUERY_HEADS * HEAD_SIZE
        )
        log_total = row_top + jnp.log(row_total)
        mixed_low = attention_mixed.astype(jnp.bfloat16)
        middle = residual + jnp.dot(mixed_low, proj_o, preferred_element_type=jnp.float32)
        normed2 = root_mean_norm(middle, m_gain.astype(jnp.float32)).astype(jnp.bfloat16)
        gate_pre = jnp.dot(normed2, proj_gate, preferred_element_type=jnp.float32)
        up_pre = jnp.dot(normed2, proj_up, preferred_element_type=jnp.float32)
        hidden = (jax.nn.silu(gate_pre) * up_pre).astype(jnp.bfloat16)
        result = middle + jnp.dot(hidden, proj_down, preferred_element_type=jnp.float32)
        return (
            result,
            residual,
            normalized_input,
            query_prenorm,
            key_prenorm,
            value_narrow,
            q_heads,
            key_narrow,
            attention_mixed,
            mixed_low,
            log_total,
            middle,
            normed2,
            gate_pre,
            up_pre,
            hidden,
            attn_set,
            mlp_set,
        )

    first_sets = fetch_weights()
    first_pass = forward(first_sets[0], first_sets[1], dealt_tok)
    again_tok = lax.all_to_all(
        token_pieces, "ctx", split_axis=0, concat_axis=0, tiled=True
    ).reshape(local_rows, MODEL_WIDTH)
    second_sets = fetch_weights()
    kept_pass = forward(second_sets[0], second_sets[1], again_tok)
    (
        unused,
        residual,
        normalized_input,
        query_prenorm,
        key_prenorm,
        value_narrow,
        q_heads,
        key_narrow,
        attention_mixed,
        mixed_low,
        log_total,
        middle,
        normed2,
        gate_pre,
        up_pre,
        hidden,
        attn_set,
        mlp_set,
    ) = kept_pass
    a_gain, qn_gain, kn_gain, proj_q, proj_k, proj_v, proj_o = attn_set
    m_gain, proj_gate, proj_up, proj_down = mlp_set
    grad_low = out_cotangent[0]
    grad_out = grad_low.astype(jnp.float32)
    d_hidden = dot_trans(grad_low, proj_down)
    down_grad = lax.psum_scatter(
        outer_rows(hidden, grad_low).astype(jnp.bfloat16), "fsdp", scatter_dimension=0, tiled=True
    )
    unused, swiglu_back = jax.vjp(
        lambda gate_in, up_in: jax.nn.silu(gate_in) * up_in, gate_pre, up_pre
    )
    d_gate, d_up = swiglu_back(d_hidden)
    d_gate_low = d_gate.astype(jnp.bfloat16)
    d_up_low = d_up.astype(jnp.bfloat16)
    d_normed2 = dot_trans(d_gate_low, proj_gate) + dot_trans(d_up_low, proj_up)
    both_low = jnp.concatenate([d_gate_low, d_up_low], axis=1)
    gate_up_grad = lax.psum_scatter(
        outer_rows(normed2, both_low).astype(jnp.bfloat16), "fsdp", scatter_dimension=0, tiled=True
    )
    unused, norm2_back = jax.vjp(root_mean_norm, middle, m_gain.astype(jnp.float32))
    d_middle_norm, d_m_gain = norm2_back(d_normed2)
    d_middle = grad_out + d_middle_norm
    middle_low = d_middle.astype(jnp.bfloat16)
    mixed_gradient = dot_trans(middle_low, proj_o).astype(jnp.bfloat16)
    out_proj_grad = lax.psum_scatter(
        outer_rows(mixed_low, middle_low).astype(jnp.bfloat16),
        "fsdp",
        scatter_dimension=0,
        tiled=True,
    )
    heads_gradient = mixed_gradient.reshape(local_rows, KEY_VALUE_HEADS, group_width, HEAD_SIZE)
    delta_rows = jnp.sum(
        heads_gradient.astype(jnp.float32)
        * attention_mixed.reshape(local_rows, KEY_VALUE_HEADS, group_width, HEAD_SIZE),
        axis=-1,
    )
    delta_t = jnp.transpose(delta_rows, (1, 2, 0))
    local_keys = key_narrow.reshape(local_rows, KEY_VALUE_HEADS, HEAD_SIZE)
    local_values = value_narrow.reshape(local_rows, KEY_VALUE_HEADS, HEAD_SIZE)

    def query_block(state_now, shard_piece, start_row):
        key_segment, value_segment = shard_piece
        local_row_count = key_segment.shape[0]
        allowed = key_mask(start_row, local_row_count)
        key_row_block = key_segment.reshape(local_row_count, KEY_VALUE_HEADS, HEAD_SIZE)
        scores = (
            jnp.einsum("rkgh,ckh->kgrc", q_heads, key_row_block, preferred_element_type=jnp.float32)
            * score_scale
        )
        probability = jnp.where(allowed, jnp.exp(scores - log_total[..., None]), 0.0)
        d_probs = jnp.einsum(
            "rkgh,ckh->kgrc",
            heads_gradient,
            value_segment.reshape(local_row_count, KEY_VALUE_HEADS, HEAD_SIZE),
            preferred_element_type=jnp.float32,
        )
        d_scores = (probability * (d_probs - delta_t[..., None])).astype(jnp.bfloat16)
        return (
            state_now
            + jnp.einsum(
                "kgrc,ckh->kgrh", d_scores, key_row_block, preferred_element_type=jnp.float32
            )
            * score_scale
        )

    query_grad = over_blocks(
        jnp.zeros((KEY_VALUE_HEADS, group_width, local_rows, HEAD_SIZE), jnp.float32),
        (
            lax.all_gather(key_narrow, "ctx", axis=0, tiled=True),
            lax.all_gather(value_narrow, "ctx", axis=0, tiled=True),
        ),
        local_rows,
        query_block,
    )
    lse_rows = jnp.transpose(log_total, (2, 0, 1)).reshape(local_rows, QUERY_HEADS)
    delta_send = delta_rows.reshape(local_rows, QUERY_HEADS)

    def key_block(state_now, shard_piece, start_row):
        query_segment, output_gradient_segment, logsumexp_segment, delta_segment = shard_piece
        local_row_count = query_segment.shape[0]
        allowed = query_mask(start_row, local_row_count)
        key_grad, value_gradient = state_now
        query_matrix = query_segment.reshape(
            local_row_count, KEY_VALUE_HEADS, group_width, HEAD_SIZE
        )
        gradient_rows = output_gradient_segment.reshape(
            local_row_count, KEY_VALUE_HEADS, group_width, HEAD_SIZE
        )
        scores = (
            jnp.einsum(
                "ckgh,rkh->kgcr", query_matrix, local_keys, preferred_element_type=jnp.float32
            )
            * score_scale
        )
        logsumexp_portion = jnp.transpose(
            logsumexp_segment.reshape(local_row_count, KEY_VALUE_HEADS, group_width), (1, 2, 0)
        )
        delta_portion = jnp.transpose(
            delta_segment.reshape(local_row_count, KEY_VALUE_HEADS, group_width), (1, 2, 0)
        )
        probability = jnp.where(allowed, jnp.exp(scores - logsumexp_portion[..., None]), 0.0)
        value_gradient = value_gradient + jnp.einsum(
            "kgcr,ckgh->rkh",
            probability.astype(jnp.bfloat16),
            gradient_rows,
            preferred_element_type=jnp.float32,
        )
        d_probs = jnp.einsum(
            "ckgh,rkh->kgcr", gradient_rows, local_values, preferred_element_type=jnp.float32
        )
        d_scores = (probability * (d_probs - delta_portion[..., None])).astype(jnp.bfloat16)
        key_grad = (
            key_grad
            + jnp.einsum(
                "kgcr,ckgh->rkh", d_scores, query_matrix, preferred_element_type=jnp.float32
            )
            * score_scale
        )
        return (key_grad, value_gradient)

    key_grad, value_gradient = over_blocks(
        (
            jnp.zeros((local_rows, KEY_VALUE_HEADS, HEAD_SIZE), jnp.float32),
            jnp.zeros((local_rows, KEY_VALUE_HEADS, HEAD_SIZE), jnp.float32),
        ),
        (
            lax.all_gather(
                q_heads.reshape(local_rows, QUERY_HEADS * HEAD_SIZE), "ctx", axis=0, tiled=True
            ),
            lax.all_gather(mixed_gradient, "ctx", axis=0, tiled=True),
            lax.all_gather(lse_rows.astype(jnp.bfloat16), "ctx", axis=0, tiled=True).astype(
                jnp.float32
            ),
            lax.all_gather(delta_send.astype(jnp.bfloat16), "ctx", axis=0, tiled=True).astype(
                jnp.float32
            ),
        ),
        local_rows,
        key_block,
    )
    query_rows = jnp.transpose(query_grad, (2, 0, 1, 3)).reshape(local_rows, QUERY_HEADS, HEAD_SIZE)
    unused, q_back = jax.vjp(
        lambda head_in, gain_in: rotary_embedding(root_mean_norm(head_in, gain_in), token_position),
        query_prenorm,
        qn_gain.astype(jnp.float32),
    )
    d_q_pre, d_qn_gain = q_back(query_rows)
    unused, k_back = jax.vjp(
        lambda head_in, gain_in: rotary_embedding(root_mean_norm(head_in, gain_in), token_position),
        key_prenorm,
        kn_gain.astype(jnp.float32),
    )
    key_prenorm_gradient, d_kn_gain = k_back(key_grad)
    dq_low = d_q_pre.reshape(local_rows, QUERY_HEADS * HEAD_SIZE).astype(jnp.bfloat16)
    key_gradient_narrow = key_prenorm_gradient.reshape(
        local_rows, KEY_VALUE_HEADS * HEAD_SIZE
    ).astype(jnp.bfloat16)
    value_gradient_narrow = value_gradient.reshape(local_rows, KEY_VALUE_HEADS * HEAD_SIZE).astype(
        jnp.bfloat16
    )
    d_normed = (
        dot_trans(dq_low, proj_q)
        + dot_trans(key_gradient_narrow, proj_k)
        + dot_trans(value_gradient_narrow, proj_v)
    )
    qkv_low = jnp.concatenate([dq_low, key_gradient_narrow, value_gradient_narrow], axis=1)
    qkv_grad = lax.psum_scatter(
        outer_rows(normalized_input, qkv_low).astype(jnp.bfloat16),
        "fsdp",
        scatter_dimension=0,
        tiled=True,
    )
    unused, norm1_back = jax.vjp(root_mean_norm, residual, a_gain.astype(jnp.float32))
    d_resid_norm, d_a_gain = norm1_back(d_normed)
    input_dealt = d_middle + d_resid_norm
    back_pieces = lax.all_to_all(
        input_dealt.reshape(piece_count, piece_rows, MODEL_WIDTH).astype(jnp.bfloat16),
        "ctx",
        split_axis=0,
        concat_axis=0,
        tiled=True,
    ).astype(jnp.float32)
    input_grad = jnp.take(back_pieces, own_plan, axis=0).reshape(local_rows, MODEL_WIDTH)
    gain_parts = (
        lax.psum_scatter(d_a_gain, "fsdp", scatter_dimension=0, tiled=True),
        lax.psum_scatter(d_qn_gain, "fsdp", scatter_dimension=0, tiled=True),
        lax.psum_scatter(d_kn_gain, "fsdp", scatter_dimension=0, tiled=True),
        lax.psum_scatter(d_m_gain, "fsdp", scatter_dimension=0, tiled=True),
    )
    totals = (
        lax.psum(gain_parts[0].astype(jnp.bfloat16), "ctx").astype(jnp.float32),
        lax.psum(gain_parts[1].astype(jnp.bfloat16), "ctx").astype(jnp.float32),
        lax.psum(gain_parts[2].astype(jnp.bfloat16), "ctx").astype(jnp.float32),
        lax.psum(gain_parts[3].astype(jnp.bfloat16), "ctx").astype(jnp.float32),
        lax.psum(qkv_grad, "ctx").astype(jnp.float32),
        lax.psum(out_proj_grad, "ctx").astype(jnp.float32),
        lax.psum(gate_up_grad, "ctx").astype(jnp.float32),
        lax.psum(down_grad, "ctx").astype(jnp.float32),
    )
    q_width = QUERY_HEADS * HEAD_SIZE
    key_value_width = KEY_VALUE_HEADS * HEAD_SIZE
    qkv_total = totals[4]
    gate_up_total = totals[6]
    ff_width = w_gate.shape[1]
    return (
        first_pass[0].astype(jnp.bfloat16)[None],
        input_grad[None],
        totals[0],
        totals[1],
        totals[2],
        totals[3],
        qkv_total[:, :q_width],
        qkv_total[:, q_width : q_width + key_value_width],
        qkv_total[:, q_width + key_value_width :],
        totals[5],
        gate_up_total[:, :ff_width],
        gate_up_total[:, ff_width:],
        totals[7],
    )


CTX = ("z", "y")
FSDP = ("x", "core")
VMEM_BYTES = 62 << 20


def norm_back(values, gain_vec, grad):
    scale = lax.rsqrt(jnp.mean(values * values, axis=-1, keepdims=True) + eps)
    inner = gain_vec * grad
    d_values = scale * inner - values * (scale * scale * scale) * jnp.mean(
        values * inner, axis=-1, keepdims=True
    )
    return d_values, grad * values * scale


def half_turn(values):
    half = values.shape[-1] // 2
    return jnp.concatenate([-values[..., half:], values[..., :half]], axis=-1)


def rope_tables(token_position):
    half = HEAD_SIZE // 2
    frequency = theta_base ** (-(jnp.arange(half, dtype=jnp.float32) * 2.0) / HEAD_SIZE)
    angles = token_position.astype(jnp.float32)[:, None] * frequency[None, :]
    cosine, sine = jnp.cos(angles), jnp.sin(angles)
    return jnp.concatenate([cosine, cosine], axis=1), jnp.concatenate([sine, sine], axis=1)


def dot(a, b):
    return jnp.dot(a, b, preferred_element_type=jnp.float32)


def low(a):
    return a.astype(jnp.bfloat16)


def gather_fsdp_plain(block):
    return lax.all_gather(block, FSDP, axis=0, tiled=True)


def over(block, axis):
    return lax.ppermute(block, axis, [(0, 1), (1, 0)])


def half_sum(block, axis):
    place = lax.axis_index(axis)
    got = over(lax.dynamic_index_in_dim(block, 1 - place, 0, keepdims=False), axis)
    own = lax.dynamic_index_in_dim(block, place, 0, keepdims=False)
    return low(own.astype(jnp.float32) + got.astype(jnp.float32))


MESH_ID = pl.DeviceIdType.MESH
LINE = 4


class Net:
    def __init__(self, send, recv):
        self.send, self.recv, self.used = send, recv, 0
        self.z, self.y, self.x, self.core = (lax.axis_index(a) for a in CTX + FSDP)
        self.me = 2 * self.z + self.y
        self.open = []

    def at(self, dz=0, dy=0, dx=0, dc=0):
        return (
            self.z + dz,
            1 - self.y if dy else self.y,
            1 - self.x if dx else self.x,
            1 - self.core if dc else self.core,
        )

    def put(self, src, dst, target, sends=None, recvs=None):
        copy = Copy(self, src, dst, target, sends, recvs)
        self.open.append(copy)
        return copy

    def close(self):
        for copy in self.open:
            copy.arrived()
        for copy in self.open:
            copy.left()


def guarded(condition, action):
    if condition is None:
        action()
    else:
        pl.when(condition)(action)


class Copy:
    def __init__(self, net, src, dst, target, sends, recvs):
        i = net.used
        net.used += 1
        self.sends, self.recvs, self.waited = sends, recvs, False
        self.copy = pltpu.make_async_remote_copy(
            src, dst, net.send.at[i], net.recv.at[i], device_id=target, device_id_type=MESH_ID
        )
        guarded(sends, self.copy.start)

    def arrived(self):
        if not self.waited:
            self.waited = True
            guarded(self.recvs, self.copy.wait_recv)

    def left(self):
        guarded(self.sends, self.copy.wait_send)


def greet(net, kinds):
    barrier = pltpu.get_barrier_semaphore()
    partners = []
    if "z" in kinds:
        partners += [(net.at(dz=1), net.z < LINE - 1), (net.at(dz=-1), net.z > 0)]
    if "y" in kinds:
        partners.append((net.at(dy=1), None))
    if "x" in kinds:
        partners.append((net.at(dx=1), None))
    if "core" in kinds:
        partners.append((net.at(dc=1), None))
    if "far" in kinds:
        partners.append((net.at(dx=1, dc=1), None))
    if "ctx" in kinds:
        for k in range(1, 2 * LINE):
            other = lax.rem(net.me + k, 2 * LINE)
            partners.append(((other // 2, lax.rem(other, 2), net.x, net.core), None))
    for target, there in partners:
        guarded(
            there,
            lambda target=target: pl.semaphore_signal(
                barrier, inc=1, device_id=target, device_id_type=MESH_ID
            ),
        )
    ends = 0
    if "z" in kinds:
        ends = (net.z == 0).astype(jnp.int32) + (net.z == LINE - 1).astype(jnp.int32)
    pl.semaphore_wait(barrier, len(partners) - ends)


def drive(*programs):
    live = list(programs)
    while live:
        for program in list(live):
            if next(program, "end") == "end":
                live.remove(program)


def along_line(net, own, view, slot, log=None):
    z = net.z
    up = net.put(own, view(slot(z)), net.at(dz=1), z < LINE - 1, z > 0)
    down = net.put(own, view(slot(z)), net.at(dz=-1), z > 0, z < LINE - 1)
    yield
    for s in range(1, LINE):
        from_low, from_high = z >= s, z + s <= LINE - 1
        up.arrived()
        low_block, high_block = view(slot(z - s)), view(slot(z + s))
        if s < LINE - 1:
            up = net.put(low_block, low_block, net.at(dz=1), from_low & (z < LINE - 1), z >= s + 1)
        if log is not None:
            log[s].append(net.put(low_block, low_block, net.at(dy=1), from_low, from_low))
        down.arrived()
        if s < LINE - 1:
            down = net.put(
                high_block, high_block, net.at(dz=-1), from_high & (z > 0), z + s + 1 <= LINE - 1
            )
        if log is not None:
            log[s].append(net.put(high_block, high_block, net.at(dy=1), from_high, from_high))
        yield


def gather_line_first(net, own, view, log=None):
    log = {s: [] for s in range(LINE)} if log is None else log
    log[0].append(net.put(own, view(net.me), net.at(dy=1)))
    yield from along_line(net, own, view, lambda z: 2 * z + net.y, log)


def gather_side_first(net, own, view):
    side = net.put(own, view(net.me), net.at(dy=1))
    first = along_line(net, own, view, lambda z: 2 * z + net.y)
    yield next(first)
    side.arrived()
    other = view(net.me + 1 - 2 * net.y)
    second = along_line(net, other, view, lambda z: 2 * z + 1 - net.y)
    for _ in second:
        next(first, None)
        yield


def gather_ctx_programs(net, own, out, cut):
    rows = own.shape[0]
    programs = [
        gather_line_first(
            net, own.at[pl.ds(0, cut)], lambda slot: out.at[slot, pl.ds(0, cut)]
        )
    ]
    if cut < rows:
        rest = pl.ds(cut, rows - cut)
        programs.append(gather_side_first(net, own.at[rest], lambda slot: out.at[slot, rest]))
    return programs


def gather_fsdp(net, own, out):
    f = 2 * net.x + net.core
    net.put(own, out.at[f], net.at(dc=1))
    over = net.put(own, out.at[f], net.at(dx=1))
    yield
    yield
    yield
    over.arrived()
    far = out.at[2 * (1 - net.x) + net.core]
    net.put(far, far, net.at(dc=1))
    yield


def gather_quad(net, own, out):
    q = 2 * net.y + net.core
    net.put(own, out.at[q], net.at(dc=1))
    over = net.put(own, out.at[q], net.at(dy=1))
    yield
    over.arrived()
    far = out.at[2 * (1 - net.y) + net.core]
    net.put(far, far, net.at(dc=1))
    yield


def swap_ctx(net, blocks, out):
    for k in range(1, 2 * LINE):
        other = lax.rem(net.me + k, 2 * LINE)
        net.put(
            blocks.at[other], out.at[net.me], (other // 2, lax.rem(other, 2), net.x, net.core)
        )
    yield


def own_copies(pairs, sem):
    copies = [pltpu.make_async_copy(src, dst, sem.at[i]) for i, (src, dst) in enumerate(pairs)]
    for copy in copies:
        copy.start()
    return copies


def net_call(body, outs, args, copies, locals_, number, scratch=(), vmem=()):
    def kernel(*refs):
        *rest, send, recv, local = refs
        net = Net(send, recv)
        body(net, local, *rest)
        assert net.used <= copies, net.used

    any_space = pl.BlockSpec(memory_space=pl.ANY)
    in_vmem = pl.BlockSpec(memory_space=pltpu.VMEM)
    count = len(args)
    return pl.pallas_call(
        kernel,
        out_shape=outs,
        in_specs=[in_vmem if i in vmem else any_space for i in range(count)],
        out_specs=[in_vmem if count + i in vmem else any_space for i in range(len(outs))],
        scratch_shapes=list(scratch)
        + [
            pltpu.SemaphoreType.DMA((copies,)),
            pltpu.SemaphoreType.DMA((copies,)),
            pltpu.SemaphoreType.DMA((max(1, locals_),)),
        ],
        compiler_params=pltpu.CompilerParams(
            collective_id=number, has_side_effects=True, vmem_limit_bytes=VMEM_BYTES
        ),
    )(*args)


def shape_of(*dims, kind=jnp.bfloat16):
    return jax.ShapeDtypeStruct(dims, kind)


def sum_line(net, held, send_up, send_down, got_up, got_down, ready):
    z = net.z
    ups, downs = [], []

    def fill(send, got, block, t, first):
        def alone():
            send[t] = low(held[block])

        def added():
            send[t] = low(held[block] + got[t - 1].astype(jnp.float32))

        return alone if first else added

    for t in range(LINE - 1):
        ready(t)
        to_up, to_down = LINE - 1 - t + z, z - LINE + 1 + t
        up_on, down_on = (z <= t) & (z < LINE - 1), (z >= LINE - 1 - t) & (z > 0)
        pl.when(z == 0)(fill(send_up, got_up, to_up, t, True))
        pl.when(z == LINE - 1)(fill(send_down, got_down, to_down, t, True))
        if t:
            pl.when(up_on & (z >= 1))(fill(send_up, got_up, to_up, t, False))
            pl.when(down_on & (z <= LINE - 2))(fill(send_down, got_down, to_down, t, False))
        ups.append(
            net.put(
                send_up.at[t], got_up.at[t], net.at(dz=1), up_on, (z >= 1) & (z - 1 <= t)
            )
        )
        downs.append(
            net.put(
                send_down.at[t],
                got_down.at[t],
                net.at(dz=-1),
                down_on,
                (z <= LINE - 2) & (z + 1 >= LINE - 1 - t),
            )
        )
        yield
        ups[t].arrived()
        downs[t].arrived()
    ready(LINE - 1)
    last = LINE - 2

    def add_up():
        held[z] += got_up[last].astype(jnp.float32)

    def add_down():
        held[z] += got_down[last].astype(jnp.float32)

    pl.when(z >= 1)(add_up)
    pl.when(z <= LINE - 2)(add_down)
    yield


def far_first(z):
    return [
        jnp.where(z < 2, 3, 0),
        jnp.where(z < 2, 2, 1),
        z + 1 - 2 * lax.rem(z, 2),
        z,
    ]


def line_scratch(rows, cols):
    line = pltpu.VMEM((LINE - 1, rows, cols), jnp.bfloat16)
    return [pltpu.VMEM((LINE, rows, cols), jnp.float32), line, line, line, line]


def sum_sides(net, src, from_side, line, make=None):
    z, y = net.z, net.y
    held = line[0]
    order = far_first(z)
    sides = []
    for k in order:
        if make is not None:
            make(2 * k + 1 - y)
        sides.append(net.put(src.at[2 * k + 1 - y], from_side.at[k], net.at(dy=1)))

    def ready(t):
        k = order[t]
        if make is not None:
            make(2 * k + y)
        sides[t].arrived()
        held[k] = src[2 * k + y].astype(jnp.float32) + from_side[k].astype(jnp.float32)

    yield from sum_line(net, *line, ready)


BLOCK = 256


def turn_lanes(v):
    return pltpu.roll(v, HEAD_SIZE // 2, 1)


def dot_last(a, b):
    return lax.dot_general(a, b, (((1,), (1,)), ((), ())), preferred_element_type=jnp.float32)


def resting(rounds):
    for _ in range(rounds):
        yield


class Bag:
    def __init__(self, **members):
        self.__dict__.update(members)


def bags(tree):
    return Bag(**{n: bags(v) for n, v in tree.items()}) if isinstance(tree, dict) else tree


def near_first(z):
    return far_first(z)[::-1]


def kernel_with(body, moved, loaded, outs, scratch, copies, number, in_vmem=()):
    scratch = dict(
        scratch, held={n: pltpu.VMEM(v.shape, v.dtype) for n, v in loaded.items()}
    )
    flat, tree = jax.tree.flatten(scratch)
    f_in, in_tree = jax.tree.flatten((moved, loaded))
    f_out, out_tree = jax.tree.flatten(outs)

    def whole(net, local, *refs):
        given, to_load = jax.tree.unflatten(in_tree, refs[: len(f_in)])
        out = Bag(**jax.tree.unflatten(out_tree, refs[len(f_in) : len(f_in) + len(f_out)]))
        r = bags(jax.tree.unflatten(tree, refs[len(f_in) + len(f_out) :]))
        used = iter(range(96))

        def fetch(src, dst):
            copy = pltpu.make_async_copy(src, dst, local.at[next(used)])
            copy.start()
            return copy

        def load():
            return [fetch(to_load[n], getattr(r.held, n)) for n in to_load]

        body(net, fetch, load, Bag(**given), out, r)
        net.close()

    order = jax.tree.unflatten(out_tree, range(len(f_out)))
    result = net_call(
        whole,
        f_out,
        f_in,
        copies,
        96,
        number,
        scratch=flat,
        vmem=[len(f_in) + order.get(n) for n in in_vmem],
    )
    return Bag(**jax.tree.unflatten(out_tree, result))


def front_kernel(moved, loaded, number):
    a = Bag(**moved)
    rows, d = a.tok.shape
    slots = 2 * LINE
    count = rows * slots
    blocks = count // BLOCK
    width = 2 * HEAD_SIZE
    shard = a.w_q.shape[0]
    half = a.w_gate.shape[1] // 8
    o_rows = a.w_o.shape[0]
    scale = HEAD_SIZE**-0.5
    bf, f32 = jnp.bfloat16, jnp.float32
    gain_cols = a.gains.shape[1]

    scratch = dict(
        tok=pltpu.VMEM((slots, rows, d), bf),
        w_qkv=pltpu.VMEM((4, shard, 2 * width), bf),
        gains=pltpu.VMEM((4, 16, gain_cols), bf),
        normed=pltpu.VMEM((count, d), bf),
        qkv=pltpu.VMEM((count, 2 * width), f32),
        q=pltpu.VMEM((count, width), bf),
        k=pltpu.VMEM((count, HEAD_SIZE), bf),
        v=pltpu.VMEM((count, HEAD_SIZE), bf),
        kt=pltpu.VMEM((HEAD_SIZE, count), bf),
        vt=pltpu.VMEM((HEAD_SIZE, count), bf),
        cos=pltpu.VMEM((count, HEAD_SIZE), f32),
        sin=pltpu.VMEM((count, HEAD_SIZE), f32),
        mixed=pltpu.VMEM((count, width), f32),
        mixed_low=pltpu.VMEM((count, width), bf),
        sent=pltpu.VMEM((slots, rows, width), bf),
        w_o=pltpu.VMEM((o_rows, d), bf),
        w_gu=pltpu.VMEM((shard, 4 * half), bf),
        grad=pltpu.VMEM((rows, d), bf),
    )
    outs = dict(
        mixed_in=shape_of(slots, rows, width),
        residual=shape_of(rows, d),
        normed=shape_of(count, d),
        qkv=shape_of(count, 2 * width, kind=f32),
        q=shape_of(count, width),
        k=shape_of(count, HEAD_SIZE),
        v=shape_of(count, HEAD_SIZE),
        kt=shape_of(HEAD_SIZE, count),
        cos=shape_of(count, HEAD_SIZE, kind=f32),
        sin=shape_of(count, HEAD_SIZE, kind=f32),
        mixed=shape_of(count, width, kind=f32),
        lse=shape_of(2, 1, count, kind=f32),
        w_qkv=shape_of(4, shard, 2 * width),
        a_gain=shape_of(1, d, kind=f32),
        m_gain=shape_of(1, d, kind=f32),
        q_gain=shape_of(1, HEAD_SIZE, kind=f32),
        k_gain=shape_of(1, HEAD_SIZE, kind=f32),
        grad=shape_of(4, rows, d),
        w_o=shape_of(4, o_rows, d),
        w_gu=shape_of(4, shard, 4 * half),
    )

    def body(net, fetch, load, given, out, r):
        z, y, x, core, me = net.z, net.y, net.x, net.core, net.me
        f = 2 * x + core
        done = set()
        loads = load()
        tok_own = fetch(given.tok, r.tok.at[me])
        gains_own = fetch(given.gains, r.gains.at[f])

        def lanes(start, size):
            return pl.ds(pl.multiple_of(start, HEAD_SIZE), size)

        head_parts = [
            (given.w_q.at[:, lanes(me * width, width)], pl.ds(0, width)),
            (given.w_k.at[:, lanes(me * HEAD_SIZE, HEAD_SIZE)], pl.ds(width, HEAD_SIZE)),
            (
                given.w_v.at[:, lanes(me * HEAD_SIZE, HEAD_SIZE)],
                pl.ds(width + HEAD_SIZE, HEAD_SIZE),
            ),
        ]
        w_own = [fetch(src, r.w_qkv.at[f, :, to]) for src, to in head_parts]
        greet(net, ("ctx", "x", "core", "far"))
        log = {s: [] for s in range(LINE)}
        waits = list(w_own) + [gains_own]

        def head_weights():
            beside = [net.put(src, r.w_qkv.at[f, :, to], net.at(dc=1)) for src, to in head_parts]
            beside.append(net.put(given.gains, r.gains.at[f], net.at(dc=1)))
            across = [net.put(src, r.w_qkv.at[f, :, to], net.at(dx=1)) for src, to in head_parts]
            across.append(net.put(given.gains, r.gains.at[f], net.at(dx=1)))
            yield
            for c in across:
                c.arrived()
            far = 2 * (1 - x) + core
            beside += [
                net.put(r.w_qkv.at[far], r.w_qkv.at[far], net.at(dc=1)),
                net.put(r.gains.at[far], r.gains.at[far], net.at(dc=1)),
            ]
            for c in waits:
                c.wait()
            for c in beside:
                c.arrived()
            r.own = fetch(r.w_qkv, out.w_qkv)
            done.add("head")
            yield

        def other_weights():
            yield
            own = [fetch(given.w_o, r.w_o)]
            over = net.put(given.w_o, out.w_o.at[f], net.at(dx=1))
            net.put(given.w_o, out.w_o.at[f], net.at(dc=1))

            def quarter(c):
                return [
                    (
                        w.at[:, lanes((2 * xs + c) * 2 * half + y * half, half)],
                        out.w_gu.at[f, :, pl.ds((2 * i + xs) * half, half)],
                    )
                    for i, w in enumerate((given.w_gate, given.w_up))
                    for xs in range(2)
                ]

            own += [
                fetch(src, r.w_gu.at[:, pl.ds(i * half, half)])
                for i, (src, _) in enumerate(quarter(core))
            ]
            for src, to in quarter(1 - core):
                net.put(src, to, net.at(dc=1))
            for src, to in quarter(core):
                net.put(src, to, net.at(dx=1))
            for src, to in quarter(1 - core):
                net.put(src, to, net.at(dx=1, dc=1))
            own.append(fetch(given.grad, r.grad))
            yield
            for c in own:
                c.wait()
            own = [
                fetch(r.w_o, out.w_o.at[f]),
                fetch(r.w_gu, out.w_gu.at[f]),
                fetch(r.grad, out.grad.at[2 * y + core]),
            ]
            yield from resting(6)
            over.arrived()
            far = out.w_o.at[2 * (1 - x) + core]
            net.put(far, far, net.at(dc=1))
            for c in own:
                c.wait()

        def output_grad():
            yield from resting(5)
            yield from gather_quad(net, given.grad, out.grad)

        def project(slot):
            at = pl.ds(pl.multiple_of(slot * rows, rows), rows)
            normed = low(root_mean_norm(r.tok[slot].astype(f32), out.a_gain[...]))
            r.normed[at] = normed
            qkv = dot(normed, r.w_qkv[...].reshape(4 * shard, 2 * width))
            r.qkv[at] = qkv
            cos, sin = r.cos[at], r.sin[at]

            def turned(part, gain):
                v = root_mean_norm(part, gain)
                return low(v * cos + turn_lanes(v) * sin)

            for g in range(2):
                cols = pl.ds(g * HEAD_SIZE, HEAD_SIZE)
                r.q[at, cols] = turned(
                    qkv[:, g * HEAD_SIZE : (g + 1) * HEAD_SIZE], out.q_gain[...]
                )
            r.k[at] = turned(qkv[:, width : width + HEAD_SIZE], out.k_gain[...])
            r.v[at] = low(qkv[:, width + HEAD_SIZE :])

        def main():
            for c in loads:
                c.wait()
            for i in range(slots):
                at = pl.ds(i * rows, rows)
                angle = r.held.pos[at] * r.held.freq[...]
                r.cos[at] = jnp.cos(angle)
                r.sin[at] = jnp.sin(angle) * r.held.sign[...]
            yield
            while "head" not in done:
                yield
            gains = [r.gains[i, pl.ds(0, 1)].astype(f32) for i in range(4)]
            part = d // 4
            for i in range(4):
                out.a_gain[:, pl.ds(i * part, part)] = gains[i][:, :part]
                out.m_gain[:, pl.ds(i * part, part)] = gains[i][:, part : 2 * part]
            total = gains[0] + gains[1] + gains[2] + gains[3]
            out.q_gain[...] = total[:, 2 * part : 2 * part + HEAD_SIZE]
            out.k_gain[...] = total[:, 2 * part + HEAD_SIZE :]
            tok_own.wait()
            near = near_first(z)
            for k in range(LINE):
                project(2 * near[k] + y)
                if k:
                    for c in log[k - 1]:
                        c.arrived()
                    project(2 * near[k - 1] + 1 - y)
                yield
            for c in log[LINE - 1]:
                c.arrived()
            project(2 * near[LINE - 1] + 1 - y)
            results = [
                fetch(r.normed, out.normed),
                fetch(r.qkv, out.qkv),
                fetch(r.q, out.q),
                fetch(r.k, out.k),
                fetch(r.v, out.v),
                fetch(r.cos, out.cos),
                fetch(r.sin, out.sin),
                r.own,
            ]
            for i in range(blocks):
                at = pl.ds(i * BLOCK, BLOCK)
                r.kt[:, at] = jnp.transpose(r.k[at])
                r.vt[:, at] = jnp.transpose(r.v[at])
            results.append(fetch(r.kt, out.kt))
            for i in range(blocks):
                here = pl.ds(i * BLOCK, BLOCK)
                first = r.held.first[:, here]
                t = i * BLOCK + lax.broadcasted_iota(jnp.int32, (BLOCK, BLOCK), 1)
                q = [r.q[here, pl.ds(g * HEAD_SIZE, HEAD_SIZE)] for g in range(2)]

                def step(n, held, i=i, q=q, first=first, t=t):
                    j = i - n
                    at = pl.ds(pl.multiple_of(j * BLOCK, BLOCK), BLOCK)
                    k, vt = r.k[at], r.vt[:, at]
                    u = j * BLOCK + lax.broadcasted_iota(jnp.int32, (BLOCK, BLOCK), 0)
                    allowed = (u >= first) & (u <= t)
                    result = []
                    for g in range(2):
                        top, total, mixed = held[g]
                        scores = jnp.where(allowed, dot_last(k, q[g]) * scale, negative_filler)
                        new = jnp.maximum(top, jnp.max(scores, axis=0, keepdims=True))
                        fade = jnp.exp(top - new)
                        p = jnp.exp(scores - new)
                        total = total * fade + jnp.sum(p, axis=0, keepdims=True)
                        result.append((new, total, mixed * fade + dot(vt, low(p))))
                    return tuple(result)

                row = jnp.full((1, BLOCK), negative_filler, f32)
                none = (row, jnp.zeros((1, BLOCK), f32), jnp.zeros((HEAD_SIZE, BLOCK), f32))
                held = lax.fori_loop(0, i + 1, step, (none, none))
                for g in range(2):
                    top, total, mixed = held[g]
                    cols = pl.ds(g * HEAD_SIZE, HEAD_SIZE)
                    out.lse[g, :, here] = top + jnp.log(total)
                    mixed = jnp.transpose(mixed / total)
                    r.mixed[here, cols] = mixed
                    r.mixed_low[here, cols] = low(mixed)
                yield
            results.append(fetch(r.mixed, out.mixed))
            ids = lax.broadcasted_iota(jnp.int32, (rows, count), 1)

            def hot(slot):
                at = pl.ds(pl.multiple_of(slot * rows, rows), rows)
                return low(jnp.where(r.held.dealt[at] == ids, 1.0, 0.0))

            for k in range(1, slots):
                other = lax.rem(me + k, slots)
                r.sent[other] = low(dot(hot(other), r.mixed_low[...]))
                there = (other // 2, lax.rem(other, 2), x, core)
                net.put(r.sent.at[other], out.mixed_in.at[me], there)
            mine = hot(me)
            r.sent[me] = low(dot(mine, r.mixed_low[...]))
            results.append(fetch(r.sent.at[me], out.mixed_in.at[me]))
            out.residual[...] = low(dot(mine, r.tok[...].reshape(count, d)))
            for c in results:
                c.wait()
            yield

        drive(
            head_weights(),
            gather_line_first(net, given.tok, lambda slot: r.tok.at[slot], log),
            main(),
            other_weights(),
            output_grad(),
        )

    return kernel_with(
        body,
        moved,
        loaded,
        outs,
        scratch,
        80,
        number,
        ("residual", "lse", "a_gain", "m_gain", "q_gain", "k_gain"),
    )


def middle_kernel(moved, loaded, number):
    a, b = Bag(**moved), Bag(**loaded)
    rows, d = b.residual.shape
    slots, _, width = b.mixed.shape
    half = a.w_down.shape[0] // 2
    shard = b.w_gu.shape[1]
    piece = rows // slots
    pad = 32
    bf, f32 = jnp.bfloat16, jnp.float32
    ff = 2 * half

    def block(*dims, kind=bf):
        return pltpu.VMEM(dims, kind)

    scratch = dict(
        w_dn=block(2, half, d),
        middle=block(rows, d, kind=f32),
        quad=block(4, rows, d),
        hidden=block(2, 2 * rows, ff),
        d_gu=block(2, 2 * rows, 2 * ff),
        near_part=block(2, rows, d, kind=f32),
        far_part=block(2, rows, d),
        near_out=block(2, rows, d, kind=f32),
        far_out=block(2, rows, d),
        beside=block(rows, d),
        beside_out=block(rows, d),
        got=block(6, rows, d),
        to_side=block(2, rows, d),
        g_gate=block(d, ff),
        g_up=block(d, ff),
        g_dn=block(ff, d),
        dm=block(slots, rows, width),
    )
    outs = dict(
        output=shape_of(rows, d),
        back=shape_of(slots, pad, d),
        dm=shape_of(slots, rows, width),
        gate=shape_of(d, ff),
        up=shape_of(d, ff),
        down=shape_of(ff, d),
        oproj=shape_of(slots * width, d),
        dg2=shape_of(1, d, kind=f32),
    )

    def body(net, fetch, load, given, out, r):
        z, y, x, core = net.z, net.y, net.x, net.core
        h = r.held
        half_rows = pl.ds(pl.multiple_of(y * half, half), half)
        loads = load()
        dn_own = fetch(given.w_down.at[half_rows], r.w_dn.at[x])
        greet(net, ("y", "x", "core"))
        dn_over = net.put(given.w_down.at[half_rows], r.w_dn.at[x], net.at(dx=1))
        for c in loads:
            c.wait()
        total = h.residual[...].astype(f32)
        for i in range(slots):
            total = total + dot(h.mixed[i], h.w_o[pl.ds(i * width, width)])
        r.middle[...] = total
        own = 2 * y + core
        r.quad[own] = low(root_mean_norm(total, h.m_gain[...]))
        net.put(r.quad.at[own], r.quad.at[own], net.at(dc=1))
        near = net.open[-1]
        net.put(r.quad.at[own], r.quad.at[own], net.at(dy=1))
        over = net.open[-1]
        near.arrived()
        dn_own.wait()

        def forward(side):
            n2 = r.quad[pl.ds(2 * side, 2)].reshape(2 * rows, d)
            g = h.grad[pl.ds(2 * side, 2)].reshape(2 * rows, d)
            w_gu = h.w_gu[...].reshape(4 * shard, 2 * ff)
            gate_up = dot(n2, w_gu)
            return g, gate_up[:, :ff], gate_up[:, ff:]

        def backward(side, g, gate, up):
            w_dn = r.w_dn[...].reshape(ff, d)
            d_hidden = dot_last(g, w_dn)
            sig = 1.0 / (1.0 + jnp.exp(-gate))
            silu = gate * sig
            r.hidden[side] = low(silu * up)
            r.d_gu[side, :, pl.ds(0, ff)] = low(d_hidden * up * (sig * (1.0 + gate * (1.0 - sig))))
            r.d_gu[side, :, pl.ds(ff, ff)] = low(d_hidden * silu)

        def part(side):
            w_gu = h.w_gu[...].reshape(4 * shard, 2 * ff)
            return dot_last(r.d_gu[side], w_gu).reshape(2, rows, d)

        def out_part(side):
            return dot(r.hidden[side], r.w_dn[...].reshape(ff, d)).reshape(2, rows, d)

        near_values = forward(y)
        over.arrived()
        far = 2 * (1 - y) + core
        net.put(r.quad.at[far], r.quad.at[far], net.at(dc=1))
        last = net.open[-1]
        dn_over.arrived()
        backward(y, *near_values)
        last.arrived()
        backward(1 - y, *forward(1 - y))
        r.far_part[...] = low(part(1 - y))
        one = net.put(r.far_part.at[1 - core], r.got.at[0], net.at(dc=1))
        r.near_part[...] = part(y)
        r.beside[...] = low(r.near_part[1 - core])
        two = net.put(r.beside, r.got.at[1], net.at(dc=1))
        one.arrived()
        r.to_side[0] = low(r.far_part[core].astype(f32) + r.got[0].astype(f32))
        side = net.put(r.to_side.at[0], r.got.at[2], net.at(dy=1))
        r.far_out[...] = low(out_part(1 - y))
        one_out = net.put(r.far_out.at[1 - core], r.got.at[3], net.at(dc=1))
        r.near_out[...] = out_part(y)
        r.beside_out[...] = low(r.near_out[1 - core])
        two_out = net.put(r.beside_out, r.got.at[4], net.at(dc=1))
        n2 = r.quad[...].reshape(4 * rows, d)
        g = h.grad[...].reshape(4 * rows, d)
        d_gu = r.d_gu[...].reshape(4 * rows, 2 * ff)
        r.g_gate[...] = low(outer_rows(n2, d_gu[:, :ff]))
        sent = [fetch(r.g_gate, out.gate)]
        one_out.arrived()
        r.to_side[1] = low(r.far_out[core].astype(f32) + r.got[3].astype(f32))
        side_out = net.put(r.to_side.at[1], r.got.at[5], net.at(dy=1))
        r.g_up[...] = low(outer_rows(n2, d_gu[:, ff:]))
        sent.append(fetch(r.g_up, out.up))
        r.g_dn[...] = low(outer_rows(r.hidden[...].reshape(4 * rows, ff), g))
        sent.append(fetch(r.g_dn, out.down))
        two.arrived()
        side.arrived()
        d_normed = (
            r.near_part[core] + r.got[1].astype(f32) + r.got[2].astype(f32)
        )
        dx2, dg2 = norm_back(r.middle[...], h.m_gain[...], d_normed)
        out.dg2[...] = jnp.sum(dg2, axis=0, keepdims=True)
        middle_low = low(h.grad[own].astype(f32) + dx2)
        for i in range(slots):
            r.dm[i] = low(dot_last(middle_low, h.w_o[pl.ds(i * width, width)]))
        sent.append(fetch(r.dm, out.dm))
        for i in range(slots):
            out.back[i, pl.ds(0, piece)] = middle_low[i * piece : (i + 1) * piece]
            out.back[i, pl.ds(piece, pad - piece)] = jnp.zeros((pad - piece, d), bf)
        for i in range(slots):
            out.oproj[pl.ds(i * width, width)] = low(outer_rows(h.mixed[i], middle_low))
        two_out.arrived()
        side_out.arrived()
        out.output[...] = low(
            r.middle[...]
            + r.near_out[core]
            + r.got[4].astype(f32)
            + r.got[5].astype(f32)
        )
        for c in sent:
            c.wait()

    return kernel_with(
        body, moved, loaded, outs, scratch, 24, number, ("output", "back", "oproj", "dg2")
    )


def back_kernel(dims, number):
    rows, count = dims
    blocks = count // BLOCK
    scale = HEAD_SIZE**-0.5
    width = 2 * HEAD_SIZE
    d = MODEL_WIDTH

    def run(moved, loaded):
        a = Bag(**moved)
        gu_rows, gu_cols = a.gate.shape[1:]
        dn_rows = a.down.shape[1]
        o_rows = a.oproj.shape[1]
        bf, f32 = jnp.bfloat16, jnp.float32
        z_gu, z_dn, z_o = gu_rows // LINE, dn_rows // LINE, o_rows // (2 * LINE)
        gain_width = 2 * d + 2 * HEAD_SIZE

        def quarter():
            return dict(
                own=pltpu.VMEM((2, gu_rows, gu_cols), bf),
                got=pltpu.VMEM((2, gu_rows, gu_cols), bf),
                low=pltpu.VMEM((2, z_gu, gu_cols), bf),
                pair=pltpu.VMEM((2, z_gu, gu_cols), bf),
                line=line_scratch(2 * z_gu, gu_cols),
            )

        scratch = dict(
            held={n: pltpu.VMEM(v.shape, v.dtype) for n, v in loaded.items()},
            gate=quarter(),
            up=quarter(),
            down=dict(
                own=pltpu.VMEM((dn_rows, d), bf),
                got=pltpu.VMEM((dn_rows, d), bf),
                low=pltpu.VMEM((z_dn, d), bf),
                line=line_scratch(z_dn, d),
            ),
            o=dict(
                own=pltpu.VMEM((2, o_rows, d), bf),
                core=pltpu.VMEM((2, o_rows, d), bf),
                got=pltpu.VMEM((o_rows, d), bf),
                sum=pltpu.VMEM((2 * LINE, z_o, d), bf),
                side=pltpu.VMEM((LINE, z_o, d), bf),
                low=pltpu.VMEM((z_o, d), bf),
                line=line_scratch(z_o, d),
            ),
            h=dict(
                own=pltpu.VMEM((4, d // 4, 2 * width), bf),
                core=pltpu.VMEM((2, d // 4, 2 * width), bf),
                got=pltpu.VMEM((d // 4, 2 * width), bf),
                low=pltpu.VMEM((d // 4, 2 * width), bf),
            ),
            dm_all=pltpu.VMEM((2 * LINE, rows, width), bf),
            back=pltpu.VMEM(a.back.shape, bf),
            do=pltpu.VMEM((count, width), bf),
            dk=pltpu.VMEM((count, HEAD_SIZE), f32),
            dv=pltpu.VMEM((count, HEAD_SIZE), f32),
            dqkv=pltpu.VMEM((count, 2 * width), bf),
            dgq=pltpu.VMEM((1, HEAD_SIZE), f32),
            dgk=pltpu.VMEM((1, HEAD_SIZE), f32),
            part=dict(
                sum=pltpu.VMEM((2 * LINE, rows, d), bf),
                side=pltpu.VMEM((LINE, rows, d), bf),
                line=line_scratch(rows, d),
            ),
            g=dict(
                mine=pltpu.VMEM((1, gain_width), f32),
                pair=pltpu.VMEM((1, gain_width), f32),
                four=pltpu.VMEM((1, gain_width), f32),
                got=pltpu.VMEM((2, 1, gain_width), f32),
                all=pltpu.VMEM((2 * LINE, 1, gain_width), f32),
            ),
        )
        flat, tree = jax.tree.flatten(scratch)
        f_in, in_tree = jax.tree.flatten((moved, loaded))
        outs = dict(
            input_grad=shape_of(rows, d, kind=f32),
            gains=shape_of(1, gain_width, kind=f32),
            gate=shape_of(2 * LINE, 2, z_gu, gu_cols),
            up=shape_of(2 * LINE, 2, z_gu, gu_cols),
            down=shape_of(2 * LINE, z_dn, d),
            o=shape_of(2 * LINE, z_o, d),
            heads=shape_of(2 * LINE, d // 4, 2 * width),
        )
        f_out, out_tree = jax.tree.flatten(outs)

        def body(net, local, *refs):
            given, to_load = jax.tree.unflatten(in_tree, refs[: len(f_in)])
            given = Bag(**given)
            out = Bag(**jax.tree.unflatten(out_tree, refs[len(f_in) : len(f_in) + len(f_out)]))
            r = bags(jax.tree.unflatten(tree, refs[len(f_in) + len(f_out) :]))
            h = r.held
            z, y, x, core, me = net.z, net.y, net.x, net.core, net.me
            slots = 2 * LINE
            used = iter(range(64))

            def fetch(src, dst):
                copy = pltpu.make_async_copy(src, dst, local.at[next(used)])
                copy.start()
                return copy

            greet(net, ("ctx", "x", "core"))
            done = set()
            dm_own = fetch(given.dm.at[me], r.dm_all.at[me])
            for k in range(1, slots):
                other = lax.rem(me + k, slots)
                there = (other // 2, lax.rem(other, 2), x, core)
                net.put(given.dm.at[other], r.dm_all.at[me], there)
            dm_copies = list(net.open)
            back_own = fetch(given.back.at[me], r.back.at[me])
            back_copies = []
            loads = [fetch(to_load[n], getattr(h, n)) for n in to_load]

            def over_x(src, piece):
                own = [fetch(src.at[2 * x + c], piece.own.at[c]) for c in range(2)]
                sent = [
                    net.put(src.at[2 * (1 - x) + c], piece.got.at[c], net.at(dx=1))
                    for c in range(2)
                ]
                return own, sent

            o_own = [fetch(given.oproj.at[2 * s + core], r.o.own.at[s]) for s in range(2)]
            o_core = [
                net.put(given.oproj.at[2 * s + 1 - core], r.o.core.at[s], net.at(dc=1))
                for s in range(2)
            ]
            gate_over, up_over = over_x(given.gate, r.gate), over_x(given.up, r.up)
            down_over = (
                [fetch(given.down.at[x], r.down.own)],
                [net.put(given.down.at[1 - x], r.down.got, net.at(dx=1))],
            )

            def land(over):
                own, sent = over
                for c in own:
                    c.wait()
                for c in sent:
                    c.arrived()

            def main():
                for c in loads:
                    c.wait()
                dm_own.wait()
                for c in dm_copies:
                    c.arrived()
                yield
                for i in range(blocks):
                    t = i * BLOCK + lax.broadcasted_iota(jnp.int32, (BLOCK, count), 0)
                    hot = low(jnp.where(h.dealt[...] == t, 1.0, 0.0))
                    r.do[pl.ds(i * BLOCK, BLOCK)] = low(
                        dot(hot, r.dm_all[...].reshape(count, width))
                    )
                r.dk[...] = jnp.zeros_like(r.dk)
                r.dv[...] = jnp.zeros_like(r.dv)
                yield
                dgq = jnp.zeros((1, HEAD_SIZE), f32)
                for i in range(blocks):
                    here = pl.ds(i * BLOCK, BLOCK)
                    first = h.first[:, here]
                    t = i * BLOCK + lax.broadcasted_iota(jnp.int32, (BLOCK, BLOCK), 1)
                    heads = []
                    for g in range(2):
                        lanes = pl.ds(g * HEAD_SIZE, HEAD_SIZE)
                        q, do = h.q[here, lanes], r.do[here, lanes]
                        product = do.astype(f32) * h.mixed[here, lanes]
                        delta = jnp.sum(jnp.transpose(product), axis=0, keepdims=True)
                        heads.append((q, do, h.lse[g, :, here], delta))

                    def step(j, held, heads=heads, first=first, t=t):
                        at = pl.ds(pl.multiple_of(j * BLOCK, BLOCK), BLOCK)
                        k, v, kt = h.k[at], h.v[at], h.kt[:, at]
                        u = j * BLOCK + lax.broadcasted_iota(jnp.int32, (BLOCK, BLOCK), 0)
                        allowed = (u >= first) & (u <= t)
                        dk, dv, out = r.dk[at], r.dv[at], []
                        for (q, do, lse, delta), dq in zip(heads, held):
                            p = jnp.where(allowed, jnp.exp(dot_last(k, q) * scale - lse), 0.0)
                            ds = low(p * (dot_last(v, do) - delta))
                            dv = dv + dot(low(p), do)
                            dk = dk + dot(ds, q)
                            out.append(dq + dot(kt, ds))
                        r.dk[at] = dk
                        r.dv[at] = dv
                        return tuple(out)

                    zero = jnp.zeros((HEAD_SIZE, BLOCK), f32)
                    result = lax.fori_loop(0, i + 1, step, (zero, zero))
                    cos, sin = h.cos[here], h.sin[here]
                    for g in range(2):
                        lanes = pl.ds(g * HEAD_SIZE, HEAD_SIZE)
                        grad = jnp.transpose(result[g]) * scale
                        grad = grad * cos - turn_lanes(grad) * sin
                        dx, dg = norm_back(h.qkv[here, lanes], h.q_gain[...], grad)
                        r.dqkv[here, lanes] = low(dx)
                        dgq = dgq + jnp.sum(dg, axis=0, keepdims=True)
                    yield
                dgk = jnp.zeros((1, HEAD_SIZE), f32)
                for i in range(blocks):
                    here = pl.ds(i * BLOCK, BLOCK)
                    grad = r.dk[here] * scale
                    grad = grad * h.cos[here] - turn_lanes(grad) * h.sin[here]
                    dx, dg = norm_back(
                        h.qkv[here, pl.ds(width, HEAD_SIZE)], h.k_gain[...], grad
                    )
                    r.dqkv[here, pl.ds(width, HEAD_SIZE)] = low(dx)
                    r.dqkv[here, pl.ds(width + HEAD_SIZE, HEAD_SIZE)] = low(r.dv[here])
                    dgk = dgk + jnp.sum(dg, axis=0, keepdims=True)
                r.dgq[...] = dgq
                r.dgk[...] = dgk
                done.add("dqkv")
                for k in range(1, slots):
                    other = lax.rem(me + k, slots)
                    there = (other // 2, lax.rem(other, 2), x, core)
                    back_copies.append(net.put(given.back.at[other], r.back.at[me], there))

                def make(slot):
                    at = pl.ds(pl.multiple_of(slot * rows, rows), rows)
                    r.part.sum[slot] = low(dot_last(r.dqkv[at], h.w_qkv[...].reshape(d, 2 * width)))

                yield from sum_sides(net, r.part.sum, r.part.side, r.part.line, make)
                dx1, dg1 = norm_back(
                    h.tok[...].astype(f32), h.a_gain[...], r.part.line[0][z]
                )
                for c in back_copies:
                    c.arrived()
                back_own.wait()
                ids = lax.broadcasted_iota(jnp.int32, (rows, slots * a.back.shape[1]), 1)
                hot = low(jnp.where(h.back_from[...] == ids, 1.0, 0.0))
                out.input_grad[...] = dx1 + dot(hot, r.back[...].reshape(-1, d))
                r.g.mine[:, pl.ds(0, d)] = jnp.sum(dg1, axis=0, keepdims=True)
                r.g.mine[:, pl.ds(d, d)] = h.dg2[...]
                r.g.mine[:, pl.ds(2 * d, HEAD_SIZE)] = r.dgq[...]
                r.g.mine[:, pl.ds(2 * d + HEAD_SIZE, HEAD_SIZE)] = r.dgk[...]
                done.add("gains")
                yield

            def gains():
                while "gains" not in done:
                    yield
                pair = net.put(r.g.mine, r.g.got.at[0], net.at(dc=1))
                yield
                pair.arrived()
                r.g.pair[...] = r.g.mine[...] + r.g.got[0]
                four = net.put(r.g.pair, r.g.got.at[1], net.at(dx=1))
                yield
                four.arrived()
                r.g.four[...] = r.g.pair[...] + r.g.got[1]
                r.g.all[me] = r.g.four[...]
                copies = []
                for k in range(1, slots):
                    other = lax.rem(me + k, slots)
                    there = (other // 2, lax.rem(other, 2), x, core)
                    copies.append(net.put(r.g.four, r.g.all.at[me], there))
                yield
                yield
                for c in copies:
                    c.arrived()
                out.gains[...] = jnp.sum(r.g.all[...], axis=0)
                yield

            def gate_or_up(over, piece, gathered, rest):
                yield from resting(rest)
                land(over)
                line = piece.line

                def ready(t):
                    k = far_first(z)[t]
                    at = pl.ds(pl.multiple_of(k * z_gu, z_gu), z_gu)
                    for c in range(2):
                        line[0][k, pl.ds(c * z_gu, z_gu)] = piece.own[c, at].astype(
                            f32
                        ) + piece.got[c, at].astype(f32)

                yield from sum_line(net, *line, ready)
                for c in range(2):
                    piece.low[c] = low(line[0][z, pl.ds(c * z_gu, z_gu)])
                swap = net.put(piece.low.at[1 - core], piece.pair.at[core], net.at(dc=1))
                piece.pair[core] = piece.low[core]
                yield
                swap.arrived()
                own = fetch(piece.pair, gathered.at[me])
                yield from gather_line_first(net, piece.pair, lambda slot: gathered.at[slot])
                own.wait()

            def down(rest):
                yield from resting(rest)
                land(down_over)
                line = r.down.line

                def ready(t):
                    k = far_first(z)[t]
                    at = pl.ds(pl.multiple_of(k * z_dn, z_dn), z_dn)
                    line[0][k] = r.down.own[at].astype(f32) + r.down.got[at].astype(f32)

                yield from sum_line(net, *line, ready)
                r.down.low[...] = low(line[0][z])
                own = fetch(r.down.low, out.down.at[me])
                yield from gather_line_first(net, r.down.low, lambda slot: out.down.at[slot])
                own.wait()

            def out_proj(rest_core, rest_x):
                yield from resting(rest_core)
                for c in o_own:
                    c.wait()
                for c in o_core:
                    c.arrived()
                r.o.own[...] = low(r.o.own[...].astype(f32) + r.o.core[...].astype(f32))
                over = net.put(r.o.own.at[1 - x], r.o.got, net.at(dx=1))
                yield from resting(rest_x)
                over.arrived()
                for i in range(slots):
                    at = pl.ds(i * z_o, z_o)
                    r.o.sum[i] = low(r.o.own[x, at].astype(f32) + r.o.got[at].astype(f32))
                yield from sum_sides(net, r.o.sum, r.o.side, r.o.line)
                r.o.low[...] = low(r.o.line[0][z])
                own = fetch(r.o.low, out.o.at[me])
                yield from gather_line_first(net, r.o.low, lambda slot: out.o.at[slot])
                own.wait()

            def heads(rest):
                while "dqkv" not in done:
                    yield
                for f in range(4):
                    at = pl.ds(f * (d // 4), d // 4)
                    r.h.own[f] = low(outer_rows(h.normed[:, at], r.dqkv[...]))
                core_copies = [
                    net.put(r.h.own.at[2 * s + 1 - core], r.h.core.at[s], net.at(dc=1))
                    for s in range(2)
                ]
                yield
                for c in core_copies:
                    c.arrived()
                for s in range(2):
                    f = 2 * s + core
                    r.h.own[f] = low(r.h.own[f].astype(f32) + r.h.core[s].astype(f32))
                over = net.put(r.h.own.at[2 * (1 - x) + core], r.h.got, net.at(dx=1))
                yield from resting(rest)
                over.arrived()
                r.h.low[...] = low(
                    r.h.own[2 * x + core].astype(f32) + r.h.got[...].astype(f32)
                )
                own = fetch(r.h.low, out.heads.at[me])
                yield from gather_line_first(net, r.h.low, lambda slot: out.heads.at[slot])
                own.wait()

            drive(
                main(),
                gate_or_up(gate_over, r.gate, out.gate, 3),
                gate_or_up(up_over, r.up, out.up, 9),
                down(11),
                out_proj(1, 13),
                heads(3),
                gains(),
            )
            net.close()

        order = jax.tree.unflatten(out_tree, range(len(f_out)))
        result = net_call(
            body,
            f_out,
            f_in,
            200,
            64,
            number,
            scratch=flat,
            vmem=(len(f_in) + order.get("input_grad"), len(f_in) + order.get("gains")),
        )
        return Bag(**jax.tree.unflatten(out_tree, result))

    return run


def widen(gate_all, up_all, down_all, o_all, heads_all):
    _, _, z_gu, gu_cols = gate_all.shape
    half = gu_cols // 2
    z_dn, z_o = down_all.shape[1], o_all.shape[1]
    h_rows = heads_all.shape[1] // LINE

    def kernel(gate, up, down, o, heads, gate_out, up_out, down_out, o_out, q_out, k_out, v_out):
        for src, out in ((gate, gate_out), (up, up_out)):
            for y in range(2):
                for c in range(2):
                    for xs in range(2):
                        to = (2 * xs + c) * 2 * half + y * half
                        out[:, pl.ds(to, half)] = src[y, c, :, pl.ds(xs * half, half)].astype(
                            jnp.float32
                        )
        for y in range(2):
            down_out[y] = down[y].astype(jnp.float32)
            o_out[pl.ds(y * z_o, z_o)] = o[y].astype(jnp.float32)
        for h in range(2 * LINE):
            q_out[:, pl.ds(h * 256, 256)] = heads[h, :, pl.ds(0, 256)].astype(jnp.float32)
            k_out[:, pl.ds(h * 128, 128)] = heads[h, :, pl.ds(256, 128)].astype(jnp.float32)
            v_out[:, pl.ds(h * 128, 128)] = heads[h, :, pl.ds(384, 128)].astype(jnp.float32)

    f32 = jnp.float32
    outs = pl.pallas_call(
        kernel,
        grid=(LINE,),
        in_specs=[
            pl.BlockSpec((2, 2, z_gu, gu_cols), lambda i: (i, 0, 0, 0)),
            pl.BlockSpec((2, 2, z_gu, gu_cols), lambda i: (i, 0, 0, 0)),
            pl.BlockSpec((2, z_dn, MODEL_WIDTH), lambda i: (i, 0, 0)),
            pl.BlockSpec((2, z_o, MODEL_WIDTH), lambda i: (i, 0, 0)),
            pl.BlockSpec((2 * LINE, h_rows, 512), lambda i: (0, i, 0)),
        ],
        out_specs=[
            pl.BlockSpec((z_gu, 8 * half), lambda i: (i, 0)),
            pl.BlockSpec((z_gu, 8 * half), lambda i: (i, 0)),
            pl.BlockSpec((2, z_dn, MODEL_WIDTH), lambda i: (0, i, 0)),
            pl.BlockSpec((2 * z_o, MODEL_WIDTH), lambda i: (i, 0)),
            pl.BlockSpec((h_rows, 2048), lambda i: (i, 0)),
            pl.BlockSpec((h_rows, 1024), lambda i: (i, 0)),
            pl.BlockSpec((h_rows, 1024), lambda i: (i, 0)),
        ],
        out_shape=[
            shape_of(LINE * z_gu, 8 * half, kind=f32),
            shape_of(LINE * z_gu, 8 * half, kind=f32),
            shape_of(2, LINE * z_dn, MODEL_WIDTH, kind=f32),
            shape_of(2 * LINE * z_o, MODEL_WIDTH, kind=f32),
            shape_of(LINE * h_rows, 2048, kind=f32),
            shape_of(LINE * h_rows, 1024, kind=f32),
            shape_of(LINE * h_rows, 1024, kind=f32),
        ],
        compiler_params=pltpu.CompilerParams(vmem_limit_bytes=VMEM_BYTES),
    )(gate_all, up_all, down_all, o_all, heads_all)
    outs = list(outs)
    outs[2] = outs[2].reshape(-1, MODEL_WIDTH)
    return outs


def fast_layer(
    tokens,
    lengths,
    deal,
    attn_gain,
    w_q,
    key_weight,
    value_weight,
    query_norm_gain,
    k_gain,
    w_o,
    mlp_gain,
    w_gate,
    w_up,
    w_down,
    out_cotangent,
):
    rows = tokens.shape[1]
    slots = lax.axis_size(CTX)
    piece = rows // slots
    count = rows * slots
    here = lax.axis_index(CTX)
    y, core = lax.axis_index("y"), lax.axis_index("core")
    x = lax.axis_index("x")
    ff_half = w_down.shape[0] // 2
    width = HEAD_SIZE * 2

    starts = jnp.cumsum(lengths[0]) - lengths[0]
    ids = jnp.arange(count, dtype=jnp.int32)
    first = segment_begin(ids, starts)
    plan = deal[0]
    devices = jnp.arange(slots, dtype=jnp.int32)
    slot_of = jnp.sum(
        jnp.where(plan[:, :, None] == devices[None, None, :], devices[None, :, None], 0), axis=1
    )
    dealt_index = (
        devices[None, :, None] * rows
        + jnp.transpose(slot_of)[:, :, None] * piece
        + jnp.arange(piece, dtype=jnp.int32)[None, None, :]
    ).reshape(count)

    lane = jnp.arange(HEAD_SIZE)
    zone = lane // (HEAD_SIZE // 4) == 2 * x + core
    packed_gain = jnp.concatenate(
        [
            attn_gain,
            mlp_gain,
            jnp.where(zone, jnp.tile(query_norm_gain, 4), 0),
            jnp.where(zone, jnp.tile(k_gain, 4), 0),
        ]
    )
    frequency = theta_base ** (
        -(jnp.arange(HEAD_SIZE // 2, dtype=jnp.float32) * 2.0) / HEAD_SIZE
    )
    front = front_kernel(
        dict(
            tok=tokens[0],
            gains=jnp.tile(packed_gain[None], (16, 1)),
            w_q=w_q,
            w_k=key_weight,
            w_v=value_weight,
            w_o=w_o,
            w_gate=w_gate,
            w_up=w_up,
            grad=out_cotangent[0],
        ),
        dict(
            first=first[None],
            dealt=dealt_index[:, None],
            pos=(ids - first).astype(jnp.float32)[:, None],
            freq=jnp.tile(frequency, 2)[None],
            sign=jnp.where(lane < HEAD_SIZE // 2, -1.0, 1.0)[None],
        ),
        0,
    )
    mid = middle_kernel(
        dict(w_down=w_down),
        dict(
            mixed=front.mixed_in,
            residual=front.residual,
            w_o=front.w_o.reshape(slots * width, MODEL_WIDTH),
            w_gu=front.w_gu,
            grad=front.grad,
            m_gain=front.m_gain,
        ),
        1,
    )
    own_plan = lax.dynamic_index_in_dim(plan, here, 0, keepdims=False)
    back_from = own_plan[:, None] * 32 + jnp.arange(piece, dtype=jnp.int32)[None, :]
    moved = dict(
        dm=mid.dm,
        back=mid.back,
        gate=mid.gate.reshape(4, -1, 2 * ff_half),
        up=mid.up.reshape(4, -1, 2 * ff_half),
        down=mid.down.reshape(2, -1, MODEL_WIDTH),
        oproj=mid.oproj.reshape(4, -1, MODEL_WIDTH),
    )
    loaded = dict(
        tok=tokens[0],
        back_from=back_from.reshape(rows, 1),
        a_gain=front.a_gain,
        dg2=mid.dg2,
        q=front.q,
        k=front.k,
        kt=front.kt,
        v=front.v,
        mixed=front.mixed,
        lse=front.lse,
        first=first[None],
        dealt=dealt_index[None],
        qkv=front.qkv,
        q_gain=front.q_gain,
        k_gain=front.k_gain,
        cos=front.cos,
        sin=front.sin,
        normed=front.normed,
        w_qkv=front.w_qkv,
    )
    sums = back_kernel((rows, count), 2)(moved, loaded)

    place = 2 * x + core

    def own_part(start, size):
        part = sums.gains[0, start : start + size]
        return lax.dynamic_slice_in_dim(part, place * (size // 4), size // 4)

    gate_sum, up_sum, down_sum, o_sum, q_sum, k_sum, v_sum = widen(
        sums.gate, sums.up, sums.down, sums.o, sums.heads
    )
    return (
        mid.output[None],
        sums.input_grad[None],
        own_part(0, MODEL_WIDTH),
        own_part(2 * MODEL_WIDTH, HEAD_SIZE),
        own_part(2 * MODEL_WIDTH + HEAD_SIZE, HEAD_SIZE),
        own_part(MODEL_WIDTH, MODEL_WIDTH),
        q_sum,
        k_sum,
        v_sum,
        o_sum,
        gate_sum,
        up_sum,
        down_sum,
    )


def solution(mesh):
    devices = mesh.devices
    if devices.shape == (8, 4):
        mesh = Mesh(devices.reshape(4, 2, 2, 2), CTX + FSDP)
        layer, ctx, fsdp = fast_layer, CTX, FSDP
    else:
        layer, ctx, fsdp = general_layer, "ctx", "fsdp"
    wide_rows = P(fsdp, ctx, None)
    return jax.shard_map(
        layer,
        mesh=mesh,
        in_specs=(
            wide_rows,
            P(fsdp, None),
            P(fsdp, None, None),
            P(fsdp),
            P(fsdp, None),
            P(fsdp, None),
            P(fsdp, None),
            P(fsdp),
            P(fsdp),
            P(fsdp, None),
            P(fsdp),
            P(fsdp, None),
            P(fsdp, None),
            P(fsdp, None),
            wide_rows,
        ),
        out_specs=(wide_rows, wide_rows) + (P(fsdp),) * 4 + (P(fsdp, None),) * 7,
        check_vma=False,
    )
```

```python
import math

import jax
import jax.numpy as jnp
import numpy as np
from jax import lax
from jax.experimental import pallas as pl
from jax.experimental.pallas import tpu as pltpu
from jax.sharding import Mesh
from jax.sharding import PartitionSpec as P

MODEL_WIDTH = 1024
QUERY_HEADS = 16
KEY_VALUE_HEADS = 8
HEAD_SIZE = 128


eps = 1e-06
theta_base = 1000000.0
negative_filler = -1e30


def root_mean_norm(values, gain_vec):
    return values * lax.rsqrt(jnp.mean(values * values, axis=-1, keepdims=True) + eps) * gain_vec


def rotary_embedding(values, token_position):
    half_width = values.shape[-1] // 2
    frequency = theta_base ** (
        -(jnp.arange(half_width, dtype=jnp.float32) * 2.0) / values.shape[-1]
    )
    angles = token_position.astype(jnp.float32)[:, None] * frequency[None, :]
    cosine = jnp.concatenate([jnp.cos(angles), jnp.cos(angles)], axis=-1)[:, None, :]
    sine_part = jnp.concatenate([jnp.sin(angles), jnp.sin(angles)], axis=-1)[:, None, :]
    turned = jnp.concatenate([-values[..., half_width:], values[..., :half_width]], axis=-1)
    return values * cosine + turned * sine_part


def dot_trans(left_side, right_side):
    return lax.dot_general(
        left_side, right_side, (((1,), (1,)), ((), ())), preferred_element_type=jnp.float32
    )


def outer_rows(left_side, right_side):
    return lax.dot_general(
        left_side, right_side, (((0,), (0,)), ((), ())), preferred_element_type=jnp.float32
    )


def block_plan(piece_rows, local_rows):
    shards = piece_rows // local_rows
    per_block = math.gcd(shards, max(1, 1024 // local_rows))
    return (per_block * local_rows, shards // per_block)


def over_blocks(carried, arrays, local_rows, block_work):
    rows_per_block, count_of_blocks = block_plan(arrays[0].shape[0], local_rows)

    def one_block(turn_index, state_now):
        offset = turn_index * rows_per_block
        parts = tuple(
            (lax.dynamic_slice_in_dim(member, offset, rows_per_block, 0) for member in arrays)
        )
        return block_work(state_now, parts, offset)

    return lax.fori_loop(0, count_of_blocks, one_block, carried)


def segment_begin(tok_ids, starts):
    return jnp.max(jnp.where(tok_ids[:, None] >= starts[None, :], starts[None, :], 0), axis=1)


def general_layer(
    tokens,
    lengths,
    deal,
    attn_gain,
    w_q,
    key_weight,
    value_weight,
    query_norm_gain,
    k_gain,
    w_o,
    mlp_gain,
    w_gate,
    w_up,
    w_down,
    out_cotangent,
):
    local_rows = tokens.shape[1]
    piece_count = lax.axis_size("ctx")
    piece_rows = local_rows // piece_count
    here = lax.axis_index("ctx")
    group_width = QUERY_HEADS // KEY_VALUE_HEADS
    score_scale = HEAD_SIZE ** (-0.5)
    seq_lengths = lengths[0]
    starts = jnp.cumsum(seq_lengths) - seq_lengths
    plan = deal[0]
    devices = jnp.arange(piece_count, dtype=jnp.int32)
    hits = plan[:, :, None] == devices[None, None, :]
    slot_of = jnp.sum(jnp.where(hits, devices[None, :, None], 0), axis=1)
    inner = jnp.arange(piece_rows, dtype=jnp.int32)
    dealt_index = (
        devices[None, :, None] * local_rows
        + jnp.transpose(slot_of)[:, :, None] * piece_rows
        + inner[None, None, :]
    ).reshape(piece_count * local_rows)
    dealt_first = segment_begin(dealt_index, starts)
    tok_index = lax.dynamic_slice_in_dim(dealt_index, here * local_rows, local_rows)
    segment_initial = lax.dynamic_slice_in_dim(dealt_first, here * local_rows, local_rows)
    token_position = tok_index - segment_initial
    own_slots = lax.dynamic_index_in_dim(slot_of, here, 0, keepdims=False)
    own_plan = lax.dynamic_index_in_dim(plan, here, 0, keepdims=False)
    token_pieces = jnp.take(
        tokens[0].reshape(piece_count, piece_rows, MODEL_WIDTH), own_slots, axis=0
    )
    dealt_tok = lax.all_to_all(
        token_pieces, "ctx", split_axis=0, concat_axis=0, tiled=True
    ).reshape(local_rows, MODEL_WIDTH)

    def key_mask(start_row, local_row_count):
        key_identifiers = lax.dynamic_slice_in_dim(dealt_index, start_row, local_row_count)
        return (key_identifiers[None, :] >= segment_initial[:, None]) & (
            key_identifiers[None, :] <= tok_index[:, None]
        )

    def query_mask(start_row, local_row_count):
        query_ids = lax.dynamic_slice_in_dim(dealt_index, start_row, local_row_count)
        first_key = lax.dynamic_slice_in_dim(dealt_first, start_row, local_row_count)
        return (tok_index[None, :] >= first_key[:, None]) & (
            tok_index[None, :] <= query_ids[:, None]
        )

    def fetch_weights():
        attn_set = (
            lax.all_gather(attn_gain, "fsdp", axis=0, tiled=True),
            lax.all_gather(query_norm_gain, "fsdp", axis=0, tiled=True),
            lax.all_gather(k_gain, "fsdp", axis=0, tiled=True),
            lax.all_gather(w_q, "fsdp", axis=0, tiled=True),
            lax.all_gather(key_weight, "fsdp", axis=0, tiled=True),
            lax.all_gather(value_weight, "fsdp", axis=0, tiled=True),
            lax.all_gather(w_o, "fsdp", axis=0, tiled=True),
        )
        mlp_set = (
            lax.all_gather(mlp_gain, "fsdp", axis=0, tiled=True),
            lax.all_gather(w_gate, "fsdp", axis=0, tiled=True),
            lax.all_gather(w_up, "fsdp", axis=0, tiled=True),
            lax.all_gather(w_down, "fsdp", axis=0, tiled=True),
        )
        return (attn_set, mlp_set)

    def forward(attn_set, mlp_set, token_rows):
        a_gain, qn_gain, kn_gain, proj_q, proj_k, proj_v, proj_o = attn_set
        m_gain, proj_gate, proj_up, proj_down = mlp_set
        residual = token_rows.astype(jnp.float32)
        normalized_input = root_mean_norm(residual, a_gain.astype(jnp.float32)).astype(jnp.bfloat16)
        query_prenorm = jnp.dot(
            normalized_input, proj_q, preferred_element_type=jnp.float32
        ).reshape(local_rows, QUERY_HEADS, HEAD_SIZE)
        key_prenorm = jnp.dot(normalized_input, proj_k, preferred_element_type=jnp.float32).reshape(
            local_rows, KEY_VALUE_HEADS, HEAD_SIZE
        )
        value_narrow = jnp.dot(normalized_input, proj_v, preferred_element_type=jnp.float32).astype(
            jnp.bfloat16
        )
        q_heads = (
            rotary_embedding(
                root_mean_norm(query_prenorm, qn_gain.astype(jnp.float32)), token_position
            )
            .astype(jnp.bfloat16)
            .reshape(local_rows, KEY_VALUE_HEADS, group_width, HEAD_SIZE)
        )
        key_narrow = (
            rotary_embedding(
                root_mean_norm(key_prenorm, kn_gain.astype(jnp.float32)), token_position
            )
            .astype(jnp.bfloat16)
            .reshape(local_rows, KEY_VALUE_HEADS * HEAD_SIZE)
        )

        def attend_over_block(state_now, shard_piece, start_row):
            key_segment, value_segment = shard_piece
            local_row_count = key_segment.shape[0]
            allowed = key_mask(start_row, local_row_count)
            row_top, row_total, weighted = state_now
            scores = (
                jnp.einsum(
                    "rkgh,ckh->kgrc",
                    q_heads,
                    key_segment.reshape(local_row_count, KEY_VALUE_HEADS, HEAD_SIZE),
                    preferred_element_type=jnp.float32,
                )
                * score_scale
            )
            scores = jnp.where(allowed, scores, negative_filler)
            new_top = jnp.maximum(row_top, jnp.max(scores, axis=-1))
            rescale = jnp.exp(row_top - new_top)
            weights = jnp.where(allowed, jnp.exp(scores - new_top[..., None]), 0.0)
            row_total = row_total * rescale + jnp.sum(weights, axis=-1)
            weighted = weighted * rescale[..., None] + jnp.einsum(
                "kgrc,ckh->kgrh",
                weights.astype(jnp.bfloat16),
                value_segment.reshape(local_row_count, KEY_VALUE_HEADS, HEAD_SIZE),
                preferred_element_type=jnp.float32,
            )
            return (new_top, row_total, weighted)

        initial = (
            jnp.full((KEY_VALUE_HEADS, group_width, local_rows), negative_filler, jnp.float32),
            jnp.zeros((KEY_VALUE_HEADS, group_width, local_rows), jnp.float32),
            jnp.zeros((KEY_VALUE_HEADS, group_width, local_rows, HEAD_SIZE), jnp.float32),
        )
        row_top, row_total, weighted = over_blocks(
            initial,
            (
                lax.all_gather(key_narrow, "ctx", axis=0, tiled=True),
                lax.all_gather(value_narrow, "ctx", axis=0, tiled=True),
            ),
            local_rows,
            attend_over_block,
        )
        attention_mixed = jnp.transpose(weighted / row_total[..., None], (2, 0, 1, 3)).reshape(
            local_rows, QUERY_HEADS * HEAD_SIZE
        )
        log_total = row_top + jnp.log(row_total)
        mixed_low = attention_mixed.astype(jnp.bfloat16)
        middle = residual + jnp.dot(mixed_low, proj_o, preferred_element_type=jnp.float32)
        normed2 = root_mean_norm(middle, m_gain.astype(jnp.float32)).astype(jnp.bfloat16)
        gate_pre = jnp.dot(normed2, proj_gate, preferred_element_type=jnp.float32)
        up_pre = jnp.dot(normed2, proj_up, preferred_element_type=jnp.float32)
        hidden = (jax.nn.silu(gate_pre) * up_pre).astype(jnp.bfloat16)
        result = middle + jnp.dot(hidden, proj_down, preferred_element_type=jnp.float32)
        return (
            result,
            residual,
            normalized_input,
            query_prenorm,
            key_prenorm,
            value_narrow,
            q_heads,
            key_narrow,
            attention_mixed,
            mixed_low,
            log_total,
            middle,
            normed2,
            gate_pre,
            up_pre,
            hidden,
            attn_set,
            mlp_set,
        )

    first_sets = fetch_weights()
    first_pass = forward(first_sets[0], first_sets[1], dealt_tok)
    again_tok = lax.all_to_all(
        token_pieces, "ctx", split_axis=0, concat_axis=0, tiled=True
    ).reshape(local_rows, MODEL_WIDTH)
    second_sets = fetch_weights()
    kept_pass = forward(second_sets[0], second_sets[1], again_tok)
    (
        unused,
        residual,
        normalized_input,
        query_prenorm,
        key_prenorm,
        value_narrow,
        q_heads,
        key_narrow,
        attention_mixed,
        mixed_low,
        log_total,
        middle,
        normed2,
        gate_pre,
        up_pre,
        hidden,
        attn_set,
        mlp_set,
    ) = kept_pass
    a_gain, qn_gain, kn_gain, proj_q, proj_k, proj_v, proj_o = attn_set
    m_gain, proj_gate, proj_up, proj_down = mlp_set
    grad_low = out_cotangent[0]
    grad_out = grad_low.astype(jnp.float32)
    d_hidden = dot_trans(grad_low, proj_down)
    down_grad = lax.psum_scatter(
        outer_rows(hidden, grad_low).astype(jnp.bfloat16), "fsdp", scatter_dimension=0, tiled=True
    )
    unused, swiglu_back = jax.vjp(
        lambda gate_in, up_in: jax.nn.silu(gate_in) * up_in, gate_pre, up_pre
    )
    d_gate, d_up = swiglu_back(d_hidden)
    d_gate_low = d_gate.astype(jnp.bfloat16)
    d_up_low = d_up.astype(jnp.bfloat16)
    d_normed2 = dot_trans(d_gate_low, proj_gate) + dot_trans(d_up_low, proj_up)
    both_low = jnp.concatenate([d_gate_low, d_up_low], axis=1)
    gate_up_grad = lax.psum_scatter(
        outer_rows(normed2, both_low).astype(jnp.bfloat16), "fsdp", scatter_dimension=0, tiled=True
    )
    unused, norm2_back = jax.vjp(root_mean_norm, middle, m_gain.astype(jnp.float32))
    d_middle_norm, d_m_gain = norm2_back(d_normed2)
    d_middle = grad_out + d_middle_norm
    middle_low = d_middle.astype(jnp.bfloat16)
    mixed_gradient = dot_trans(middle_low, proj_o).astype(jnp.bfloat16)
    out_proj_grad = lax.psum_scatter(
        outer_rows(mixed_low, middle_low).astype(jnp.bfloat16),
        "fsdp",
        scatter_dimension=0,
        tiled=True,
    )
    heads_gradient = mixed_gradient.reshape(local_rows, KEY_VALUE_HEADS, group_width, HEAD_SIZE)
    delta_rows = jnp.sum(
        heads_gradient.astype(jnp.float32)
        * attention_mixed.reshape(local_rows, KEY_VALUE_HEADS, group_width, HEAD_SIZE),
        axis=-1,
    )
    delta_t = jnp.transpose(delta_rows, (1, 2, 0))
    local_keys = key_narrow.reshape(local_rows, KEY_VALUE_HEADS, HEAD_SIZE)
    local_values = value_narrow.reshape(local_rows, KEY_VALUE_HEADS, HEAD_SIZE)

    def query_block(state_now, shard_piece, start_row):
        key_segment, value_segment = shard_piece
        local_row_count = key_segment.shape[0]
        allowed = key_mask(start_row, local_row_count)
        key_row_block = key_segment.reshape(local_row_count, KEY_VALUE_HEADS, HEAD_SIZE)
        scores = (
            jnp.einsum("rkgh,ckh->kgrc", q_heads, key_row_block, preferred_element_type=jnp.float32)
            * score_scale
        )
        probability = jnp.where(allowed, jnp.exp(scores - log_total[..., None]), 0.0)
        d_probs = jnp.einsum(
            "rkgh,ckh->kgrc",
            heads_gradient,
            value_segment.reshape(local_row_count, KEY_VALUE_HEADS, HEAD_SIZE),
            preferred_element_type=jnp.float32,
        )
        d_scores = (probability * (d_probs - delta_t[..., None])).astype(jnp.bfloat16)
        return (
            state_now
            + jnp.einsum(
                "kgrc,ckh->kgrh", d_scores, key_row_block, preferred_element_type=jnp.float32
            )
            * score_scale
        )

    query_grad = over_blocks(
        jnp.zeros((KEY_VALUE_HEADS, group_width, local_rows, HEAD_SIZE), jnp.float32),
        (
            lax.all_gather(key_narrow, "ctx", axis=0, tiled=True),
            lax.all_gather(value_narrow, "ctx", axis=0, tiled=True),
        ),
        local_rows,
        query_block,
    )
    lse_rows = jnp.transpose(log_total, (2, 0, 1)).reshape(local_rows, QUERY_HEADS)
    delta_send = delta_rows.reshape(local_rows, QUERY_HEADS)

    def key_block(state_now, shard_piece, start_row):
        query_segment, output_gradient_segment, logsumexp_segment, delta_segment = shard_piece
        local_row_count = query_segment.shape[0]
        allowed = query_mask(start_row, local_row_count)
        key_grad, value_gradient = state_now
        query_matrix = query_segment.reshape(
            local_row_count, KEY_VALUE_HEADS, group_width, HEAD_SIZE
        )
        gradient_rows = output_gradient_segment.reshape(
            local_row_count, KEY_VALUE_HEADS, group_width, HEAD_SIZE
        )
        scores = (
            jnp.einsum(
                "ckgh,rkh->kgcr", query_matrix, local_keys, preferred_element_type=jnp.float32
            )
            * score_scale
        )
        logsumexp_portion = jnp.transpose(
            logsumexp_segment.reshape(local_row_count, KEY_VALUE_HEADS, group_width), (1, 2, 0)
        )
        delta_portion = jnp.transpose(
            delta_segment.reshape(local_row_count, KEY_VALUE_HEADS, group_width), (1, 2, 0)
        )
        probability = jnp.where(allowed, jnp.exp(scores - logsumexp_portion[..., None]), 0.0)
        value_gradient = value_gradient + jnp.einsum(
            "kgcr,ckgh->rkh",
            probability.astype(jnp.bfloat16),
            gradient_rows,
            preferred_element_type=jnp.float32,
        )
        d_probs = jnp.einsum(
            "ckgh,rkh->kgcr", gradient_rows, local_values, preferred_element_type=jnp.float32
        )
        d_scores = (probability * (d_probs - delta_portion[..., None])).astype(jnp.bfloat16)
        key_grad = (
            key_grad
            + jnp.einsum(
                "kgcr,ckgh->rkh", d_scores, query_matrix, preferred_element_type=jnp.float32
            )
            * score_scale
        )
        return (key_grad, value_gradient)

    key_grad, value_gradient = over_blocks(
        (
            jnp.zeros((local_rows, KEY_VALUE_HEADS, HEAD_SIZE), jnp.float32),
            jnp.zeros((local_rows, KEY_VALUE_HEADS, HEAD_SIZE), jnp.float32),
        ),
        (
            lax.all_gather(
                q_heads.reshape(local_rows, QUERY_HEADS * HEAD_SIZE), "ctx", axis=0, tiled=True
            ),
            lax.all_gather(mixed_gradient, "ctx", axis=0, tiled=True),
            lax.all_gather(lse_rows.astype(jnp.bfloat16), "ctx", axis=0, tiled=True).astype(
                jnp.float32
            ),
            lax.all_gather(delta_send.astype(jnp.bfloat16), "ctx", axis=0, tiled=True).astype(
                jnp.float32
            ),
        ),
        local_rows,
        key_block,
    )
    query_rows = jnp.transpose(query_grad, (2, 0, 1, 3)).reshape(local_rows, QUERY_HEADS, HEAD_SIZE)
    unused, q_back = jax.vjp(
        lambda head_in, gain_in: rotary_embedding(root_mean_norm(head_in, gain_in), token_position),
        query_prenorm,
        qn_gain.astype(jnp.float32),
    )
    d_q_pre, d_qn_gain = q_back(query_rows)
    unused, k_back = jax.vjp(
        lambda head_in, gain_in: rotary_embedding(root_mean_norm(head_in, gain_in), token_position),
        key_prenorm,
        kn_gain.astype(jnp.float32),
    )
    key_prenorm_gradient, d_kn_gain = k_back(key_grad)
    dq_low = d_q_pre.reshape(local_rows, QUERY_HEADS * HEAD_SIZE).astype(jnp.bfloat16)
    key_gradient_narrow = key_prenorm_gradient.reshape(
        local_rows, KEY_VALUE_HEADS * HEAD_SIZE
    ).astype(jnp.bfloat16)
    value_gradient_narrow = value_gradient.reshape(local_rows, KEY_VALUE_HEADS * HEAD_SIZE).astype(
        jnp.bfloat16
    )
    d_normed = (
        dot_trans(dq_low, proj_q)
        + dot_trans(key_gradient_narrow, proj_k)
        + dot_trans(value_gradient_narrow, proj_v)
    )
    qkv_low = jnp.concatenate([dq_low, key_gradient_narrow, value_gradient_narrow], axis=1)
    qkv_grad = lax.psum_scatter(
        outer_rows(normalized_input, qkv_low).astype(jnp.bfloat16),
        "fsdp",
        scatter_dimension=0,
        tiled=True,
    )
    unused, norm1_back = jax.vjp(root_mean_norm, residual, a_gain.astype(jnp.float32))
    d_resid_norm, d_a_gain = norm1_back(d_normed)
    input_dealt = d_middle + d_resid_norm
    back_pieces = lax.all_to_all(
        input_dealt.reshape(piece_count, piece_rows, MODEL_WIDTH).astype(jnp.bfloat16),
        "ctx",
        split_axis=0,
        concat_axis=0,
        tiled=True,
    ).astype(jnp.float32)
    input_grad = jnp.take(back_pieces, own_plan, axis=0).reshape(local_rows, MODEL_WIDTH)
    gain_parts = (
        lax.psum_scatter(d_a_gain, "fsdp", scatter_dimension=0, tiled=True),
        lax.psum_scatter(d_qn_gain, "fsdp", scatter_dimension=0, tiled=True),
        lax.psum_scatter(d_kn_gain, "fsdp", scatter_dimension=0, tiled=True),
        lax.psum_scatter(d_m_gain, "fsdp", scatter_dimension=0, tiled=True),
    )
    totals = (
        lax.psum(gain_parts[0].astype(jnp.bfloat16), "ctx").astype(jnp.float32),
        lax.psum(gain_parts[1].astype(jnp.bfloat16), "ctx").astype(jnp.float32),
        lax.psum(gain_parts[2].astype(jnp.bfloat16), "ctx").astype(jnp.float32),
        lax.psum(gain_parts[3].astype(jnp.bfloat16), "ctx").astype(jnp.float32),
        lax.psum(qkv_grad, "ctx").astype(jnp.float32),
        lax.psum(out_proj_grad, "ctx").astype(jnp.float32),
        lax.psum(gate_up_grad, "ctx").astype(jnp.float32),
        lax.psum(down_grad, "ctx").astype(jnp.float32),
    )
    q_width = QUERY_HEADS * HEAD_SIZE
    key_value_width = KEY_VALUE_HEADS * HEAD_SIZE
    qkv_total = totals[4]
    gate_up_total = totals[6]
    ff_width = w_gate.shape[1]
    return (
        first_pass[0].astype(jnp.bfloat16)[None],
        input_grad[None],
        totals[0],
        totals[1],
        totals[2],
        totals[3],
        qkv_total[:, :q_width],
        qkv_total[:, q_width : q_width + key_value_width],
        qkv_total[:, q_width + key_value_width :],
        totals[5],
        gate_up_total[:, :ff_width],
        gate_up_total[:, ff_width:],
        totals[7],
    )


CTX = ("z", "y")
FSDP = ("x", "core")
VMEM_BYTES = 62 << 20


def norm_back(values, gain_vec, grad):
    scale = lax.rsqrt(jnp.mean(values * values, axis=-1, keepdims=True) + eps)
    inner = gain_vec * grad
    d_values = scale * inner - values * (scale * scale * scale) * jnp.mean(
        values * inner, axis=-1, keepdims=True
    )
    return d_values, grad * values * scale


def half_turn(values):
    half = values.shape[-1] // 2
    return jnp.concatenate([-values[..., half:], values[..., :half]], axis=-1)


def rope_tables(token_position):
    half = HEAD_SIZE // 2
    frequency = theta_base ** (-(jnp.arange(half, dtype=jnp.float32) * 2.0) / HEAD_SIZE)
    angles = token_position.astype(jnp.float32)[:, None] * frequency[None, :]
    cosine, sine = jnp.cos(angles), jnp.sin(angles)
    return jnp.concatenate([cosine, cosine], axis=1), jnp.concatenate([sine, sine], axis=1)


def dot(a, b):
    return jnp.dot(a, b, preferred_element_type=jnp.float32)


def low(a):
    return a.astype(jnp.bfloat16)


def gather_fsdp_plain(block):
    return lax.all_gather(block, FSDP, axis=0, tiled=True)


def over(block, axis):
    return lax.ppermute(block, axis, [(0, 1), (1, 0)])


def half_sum(block, axis):
    place = lax.axis_index(axis)
    got = over(lax.dynamic_index_in_dim(block, 1 - place, 0, keepdims=False), axis)
    own = lax.dynamic_index_in_dim(block, place, 0, keepdims=False)
    return low(own.astype(jnp.float32) + got.astype(jnp.float32))


MESH_ID = pl.DeviceIdType.MESH
LINE = 4


class Net:
    def __init__(self, send, recv):
        self.send, self.recv, self.used = send, recv, 0
        self.z, self.y, self.x, self.core = (lax.axis_index(a) for a in CTX + FSDP)
        self.me = 2 * self.z + self.y
        self.open = []

    def at(self, dz=0, dy=0, dx=0, dc=0):
        return (
            self.z + dz,
            1 - self.y if dy else self.y,
            1 - self.x if dx else self.x,
            1 - self.core if dc else self.core,
        )

    def put(self, src, dst, target, sends=None, recvs=None):
        copy = Copy(self, src, dst, target, sends, recvs)
        self.open.append(copy)
        return copy

    def close(self):
        for copy in self.open:
            copy.arrived()
        for copy in self.open:
            copy.left()


def guarded(condition, action):
    if condition is None:
        action()
    else:
        pl.when(condition)(action)


class Copy:
    def __init__(self, net, src, dst, target, sends, recvs):
        i = net.used
        net.used += 1
        self.sends, self.recvs, self.waited = sends, recvs, False
        self.copy = pltpu.make_async_remote_copy(
            src, dst, net.send.at[i], net.recv.at[i], device_id=target, device_id_type=MESH_ID
        )
        guarded(sends, self.copy.start)

    def arrived(self):
        if not self.waited:
            self.waited = True
            guarded(self.recvs, self.copy.wait_recv)

    def left(self):
        guarded(self.sends, self.copy.wait_send)


class Local:
    def __init__(self, copy):
        self.copy, self.waited = copy, False
        copy.start()

    def arrived(self):
        if not self.waited:
            self.waited = True
            self.copy.wait()

    wait = arrived


def greet(net, kinds):
    barrier = pltpu.get_barrier_semaphore()
    partners = []
    if "z" in kinds:
        partners += [(net.at(dz=1), net.z < LINE - 1), (net.at(dz=-1), net.z > 0)]
    if "y" in kinds:
        partners.append((net.at(dy=1), None))
    if "x" in kinds:
        partners.append((net.at(dx=1), None))
    if "core" in kinds:
        partners.append((net.at(dc=1), None))
    if "far" in kinds:
        partners.append((net.at(dx=1, dc=1), None))
    if "ctx" in kinds:
        for k in range(1, 2 * LINE):
            other = lax.rem(net.me + k, 2 * LINE)
            partners.append(((other // 2, lax.rem(other, 2), net.x, net.core), None))
    for target, there in partners:
        guarded(
            there,
            lambda target=target: pl.semaphore_signal(
                barrier, inc=1, device_id=target, device_id_type=MESH_ID
            ),
        )
    ends = 0
    if "z" in kinds:
        ends = (net.z == 0).astype(jnp.int32) + (net.z == LINE - 1).astype(jnp.int32)
    pl.semaphore_wait(barrier, len(partners) - ends)


def drive(*programs):
    live = list(programs)
    while live:
        for program in list(live):
            if next(program, "end") == "end":
                live.remove(program)


def in_order(order, programs):
    for i in order:
        next(programs[i], None)
    for program in programs:
        for _ in program:
            pass


def by_steps(program):
    yield next(program)
    while next(program, "end") != "end":
        if next(program, "end") == "end":
            return
        yield


def along_line(net, own, view, slot, log=None):
    z = net.z
    up = net.put(own, view(slot(z)), net.at(dz=1), z < LINE - 1, z > 0)
    down = net.put(own, view(slot(z)), net.at(dz=-1), z > 0, z < LINE - 1)
    yield
    for s in range(1, LINE):
        from_low, from_high = z >= s, z + s <= LINE - 1
        up.arrived()
        low_block, high_block = view(slot(z - s)), view(slot(z + s))
        if s < LINE - 1:
            up = net.put(low_block, low_block, net.at(dz=1), from_low & (z < LINE - 1), z >= s + 1)
        if log is not None:
            log[s].append(net.put(low_block, low_block, net.at(dy=1), from_low, from_low))
        yield
        down.arrived()
        if s < LINE - 1:
            down = net.put(
                high_block, high_block, net.at(dz=-1), from_high & (z > 0), z + s + 1 <= LINE - 1
            )
        if log is not None:
            log[s].append(net.put(high_block, high_block, net.at(dy=1), from_high, from_high))
        yield


def gather_line_first(net, own, view, log=None):
    log = {s: [] for s in range(LINE)} if log is None else log
    log[0].append(net.put(own, view(net.me), net.at(dy=1)))
    yield from along_line(net, own, view, lambda z: 2 * z + net.y, log)


def gather_side_first(net, own, view):
    side = net.put(own, view(net.me), net.at(dy=1))
    first = along_line(net, own, view, lambda z: 2 * z + net.y)
    yield next(first)
    side.arrived()
    other = view(net.me + 1 - 2 * net.y)
    second = along_line(net, other, view, lambda z: 2 * z + 1 - net.y)
    for _ in second:
        next(first, None)
        yield


def gather_ctx_programs(net, own, out, cut):
    rows = own.shape[0]
    programs = [
        gather_line_first(
            net, own.at[pl.ds(0, cut)], lambda slot: out.at[slot, pl.ds(0, cut)]
        )
    ]
    if cut < rows:
        rest = pl.ds(cut, rows - cut)
        programs.append(gather_side_first(net, own.at[rest], lambda slot: out.at[slot, rest]))
    return programs


def gather_fsdp(net, own, out):
    f = 2 * net.x + net.core
    net.put(own, out.at[f], net.at(dc=1))
    over = net.put(own, out.at[f], net.at(dx=1))
    yield
    yield
    yield
    over.arrived()
    far = out.at[2 * (1 - net.x) + net.core]
    net.put(far, far, net.at(dc=1))
    yield


def gather_quad(net, own, out):
    q = 2 * net.y + net.core
    net.put(own, out.at[q], net.at(dc=1))
    over = net.put(own, out.at[q], net.at(dy=1))
    yield
    over.arrived()
    far = out.at[2 * (1 - net.y) + net.core]
    net.put(far, far, net.at(dc=1))
    yield


def swap_ctx(net, blocks, out):
    for k in range(1, 2 * LINE):
        other = lax.rem(net.me + k, 2 * LINE)
        net.put(
            blocks.at[other], out.at[net.me], (other // 2, lax.rem(other, 2), net.x, net.core)
        )
    yield


def own_copies(pairs, sem):
    copies = [pltpu.make_async_copy(src, dst, sem.at[i]) for i, (src, dst) in enumerate(pairs)]
    for copy in copies:
        copy.start()
    return copies


def net_call(body, outs, args, copies, locals_, number, scratch=(), vmem=(), smem=()):
    def kernel(*refs):
        *rest, send, recv, local = refs
        net = Net(send, recv)
        body(net, local, *rest)
        assert net.used <= copies, net.used

    any_space = pl.BlockSpec(memory_space=pl.ANY)
    in_vmem = pl.BlockSpec(memory_space=pltpu.VMEM)
    in_smem = pl.BlockSpec(memory_space=pltpu.SMEM)
    count = len(args)

    def place(i):
        return in_vmem if i in vmem else in_smem if i in smem else any_space

    return pl.pallas_call(
        kernel,
        out_shape=outs,
        in_specs=[place(i) for i in range(count)],
        out_specs=[place(count + i) for i in range(len(outs))],
        scratch_shapes=list(scratch)
        + [
            pltpu.SemaphoreType.DMA((copies,)),
            pltpu.SemaphoreType.DMA((copies,)),
            pltpu.SemaphoreType.DMA((max(1, locals_),)),
        ],
        compiler_params=pltpu.CompilerParams(
            collective_id=number, has_side_effects=True, vmem_limit_bytes=VMEM_BYTES
        ),
    )(*args)


def shape_of(*dims, kind=jnp.bfloat16):
    return jax.ShapeDtypeStruct(dims, kind)


def sum_line(net, held, send_up, send_down, got_up, got_down, ready):
    z = net.z
    ups, downs = [], []

    def fill(send, got, block, t, first):
        def alone():
            send[t] = low(held[block])

        def added():
            send[t] = low(held[block] + got[t - 1].astype(jnp.float32))

        return alone if first else added

    for t in range(LINE - 1):
        if t:
            ups[t - 1].arrived()
        ready(t)
        to_up, to_down = LINE - 1 - t + z, z - LINE + 1 + t
        up_on, down_on = (z <= t) & (z < LINE - 1), (z >= LINE - 1 - t) & (z > 0)
        pl.when(z == 0)(fill(send_up, got_up, to_up, t, True))
        if t:
            pl.when(up_on & (z >= 1))(fill(send_up, got_up, to_up, t, False))
        ups.append(
            net.put(
                send_up.at[t], got_up.at[t], net.at(dz=1), up_on, (z >= 1) & (z - 1 <= t)
            )
        )
        yield
        if t:
            downs[t - 1].arrived()
        pl.when(z == LINE - 1)(fill(send_down, got_down, to_down, t, True))
        if t:
            pl.when(down_on & (z <= LINE - 2))(fill(send_down, got_down, to_down, t, False))
        downs.append(
            net.put(
                send_down.at[t],
                got_down.at[t],
                net.at(dz=-1),
                down_on,
                (z <= LINE - 2) & (z + 1 >= LINE - 1 - t),
            )
        )
        yield
    last = LINE - 2

    def add_up():
        held[z] += got_up[last].astype(jnp.float32)

    def add_down():
        held[z] += got_down[last].astype(jnp.float32)

    ups[last].arrived()
    ready(LINE - 1)
    pl.when(z >= 1)(add_up)
    yield
    downs[last].arrived()
    pl.when(z <= LINE - 2)(add_down)


def far_first(z):
    return [
        jnp.where(z < 2, 3, 0),
        jnp.where(z < 2, 2, 1),
        z + 1 - 2 * lax.rem(z, 2),
        z,
    ]


def line_scratch(rows, cols):
    line = pltpu.VMEM((LINE - 1, rows, cols), jnp.bfloat16)
    return [pltpu.VMEM((LINE, rows, cols), jnp.float32), line, line, line, line]


def sum_sides(net, src, from_side, line, make=None):
    z, y = net.z, net.y
    held = line[0]
    order = far_first(z)
    sides = []
    for k in order:
        if make is not None:
            make(2 * k + 1 - y)
        sides.append(net.put(src.at[2 * k + 1 - y], from_side.at[k], net.at(dy=1)))
        if make is not None and len(sides) == 2:
            yield
    yield

    def ready(t):
        k = order[t]
        if make is not None:
            make(2 * k + y)
        sides[t].arrived()
        held[k] = src[2 * k + y].astype(jnp.float32) + from_side[k].astype(jnp.float32)

    yield from sum_line(net, *line, ready)


BLOCK = 256
BACK_ORDER = (
    0, 3, 7, 4, 2, 3, 0, 7, 1, 3, 2, 3, 0, 7, 4, 7, 4, 5, 4, 7, 0, 5, 0, 7, 4, 3, 7, 3, 7, 7,
    7, 1, 1, 0, 6, 7, 4, 1, 6, 1, 4, 7, 4, 7, 0, 3, 2, 1, 1, 6, 1, 4, 7, 2, 7, 1, 6, 6, 7, 7,
    4, 1, 2, 0, 3, 7, 6, 4, 2, 3, 7, 7, 0, 4, 4, 1, 2, 8, 4, 7, 3, 2, 0, 1, 3, 2, 8, 2, 6, 3,
    2, 1, 1, 2, 0, 0, 0, 1, 6, 1, 4, 2, 3, 2, 3, 2, 2, 0, 6, 0, 3, 8, 0, 3, 4, 2, 8, 2, 6, 1,
)


def turn_lanes(v):
    return pltpu.roll(v, HEAD_SIZE // 2, 1)


def dot_last(a, b):
    return lax.dot_general(a, b, (((1,), (1,)), ((), ())), preferred_element_type=jnp.float32)


def resting(rounds):
    for _ in range(rounds):
        yield


class Bag:
    def __init__(self, **members):
        self.__dict__.update(members)


def bags(tree):
    if isinstance(tree, list):
        return [bags(v) for v in tree]
    return Bag(**{n: bags(v) for n, v in tree.items()}) if isinstance(tree, dict) else tree


def near_first(z):
    return far_first(z)[::-1]


def kernel_with(
    body, moved, loaded, outs, scratch, copies, number, in_vmem=(), near=(), scalar=()
):
    scratch = dict(
        scratch, held={n: pltpu.VMEM(v.shape, v.dtype) for n, v in loaded.items()}
    )
    flat, tree = jax.tree.flatten(scratch)
    f_in, in_tree = jax.tree.flatten((moved, loaded))
    f_out, out_tree = jax.tree.flatten(outs)

    def whole(net, local, *refs):
        given, to_load = jax.tree.unflatten(in_tree, refs[: len(f_in)])
        out = Bag(**jax.tree.unflatten(out_tree, refs[len(f_in) : len(f_in) + len(f_out)]))
        r = bags(jax.tree.unflatten(tree, refs[len(f_in) + len(f_out) :]))
        used = iter(range(96))

        def fetch(src, dst):
            return Local(pltpu.make_async_copy(src, dst, local.at[next(used)]))

        def load():
            return {n: fetch(to_load[n], getattr(r.held, n)) for n in to_load}

        body(net, fetch, load, Bag(**given), out, r)
        net.close()

    order = jax.tree.unflatten(out_tree, range(len(f_out)))
    in_order, _ = jax.tree.unflatten(in_tree, range(len(f_in)))
    result = net_call(
        whole,
        f_out,
        f_in,
        copies,
        96,
        number,
        scratch=flat,
        vmem=[len(f_in) + order.get(n) for n in in_vmem] + [in_order.get(n) for n in near],
        smem=[in_order.get(n) for n in scalar],
    )
    return Bag(**jax.tree.unflatten(out_tree, result))


def middle(net, fetch, arriving, out, r):
    y, x, core = net.y, net.x, net.core
    slots, rows, width = r.mixed_in.shape
    _, shard, wide = r.w_gu.shape
    ff, d = wide // 2, r.residual.shape[1]
    piece, pad = rows // slots, 32
    f32, bf = jnp.float32, jnp.bfloat16

    def land(copies):
        for c in copies:
            c.arrived()

    land(arriving.o)
    total = r.residual[...].astype(f32)
    for i in range(slots):
        total = total + dot(r.mixed_in[i], r.w_o[i // 2, pl.ds(i % 2 * width, width)])
    r.middle[...] = total
    own = 2 * y + core
    r.quad[own] = low(root_mean_norm(total, r.m_gain[...]))
    net.put(r.quad.at[own], r.quad.at[own], net.at(dc=1))
    near = net.open[-1]
    net.put(r.quad.at[own], r.quad.at[own], net.at(dy=1))
    over = net.open[-1]
    near.arrived()
    land(arriving.gu)
    land(arriving.grad)

    def forward(side):
        n2 = r.quad[pl.ds(2 * side, 2)].reshape(2 * rows, d)
        g = r.grad[pl.ds(2 * side, 2)].reshape(2 * rows, d)
        w_gu = r.w_gu[...].reshape(4 * shard, 2 * ff)
        gate_up = dot(n2, w_gu)
        return g, gate_up[:, :ff], gate_up[:, ff:]

    def backward(side, g, gate, up):
        w_dn = r.w_dn[...].reshape(ff, d)
        d_hidden = dot_last(g, w_dn)
        sig = 1.0 / (1.0 + jnp.exp(-gate))
        silu = gate * sig
        r.hidden[side] = low(silu * up)
        r.d_gu[side, :, pl.ds(0, ff)] = low(d_hidden * up * (sig * (1.0 + gate * (1.0 - sig))))
        r.d_gu[side, :, pl.ds(ff, ff)] = low(d_hidden * silu)

    def part(side):
        w_gu = r.w_gu[...].reshape(4 * shard, 2 * ff)
        return dot_last(r.d_gu[side], w_gu).reshape(2, rows, d)

    def out_part(side):
        return dot(r.hidden[side], r.w_dn[...].reshape(ff, d)).reshape(2, rows, d)

    near_values = forward(y)
    over.arrived()
    far = 2 * (1 - y) + core
    net.put(r.quad.at[far], r.quad.at[far], net.at(dc=1))
    last = net.open[-1]
    land(arriving.dn)
    backward(y, *near_values)
    last.arrived()
    backward(1 - y, *forward(1 - y))
    r.far_part[...] = low(part(1 - y))
    one = net.put(r.far_part.at[1 - core], r.got.at[0], net.at(dc=1))
    r.near_part[...] = part(y)
    r.beside[...] = low(r.near_part[1 - core])
    two = net.put(r.beside, r.got.at[1], net.at(dc=1))
    one.arrived()
    r.to_side[0] = low(r.far_part[core].astype(f32) + r.got[0].astype(f32))
    side = net.put(r.to_side.at[0], r.got.at[2], net.at(dy=1))
    r.far_out[...] = low(out_part(1 - y))
    one_out = net.put(r.far_out.at[1 - core], r.got.at[3], net.at(dc=1))
    r.near_out[...] = out_part(y)
    r.beside_out[...] = low(r.near_out[1 - core])
    two_out = net.put(r.beside_out, r.got.at[4], net.at(dc=1))
    n2 = r.quad[...].reshape(4 * rows, d)
    g = r.grad[...].reshape(4 * rows, d)
    d_gu = r.d_gu[...].reshape(4 * rows, 2 * ff)
    r.g_gate[...] = low(outer_rows(n2, d_gu[:, :ff])).reshape(4, shard, ff)
    gate_over = [
        net.put(r.g_gate.at[2 * (1 - x) + c], r.gate_got.at[c], net.at(dx=1))
        for c in range(2)
    ]
    one_out.arrived()
    r.to_side[1] = low(r.far_out[core].astype(f32) + r.got[3].astype(f32))
    side_out = net.put(r.to_side.at[1], r.got.at[5], net.at(dy=1))
    r.g_up[...] = low(outer_rows(n2, d_gu[:, ff:]))
    sent = [fetch(r.g_up, out.up)]
    r.g_dn[...] = low(outer_rows(r.hidden[...].reshape(4 * rows, ff), g))
    sent.append(fetch(r.g_dn, out.down))
    two.arrived()
    side.arrived()
    d_normed = (
        r.near_part[core] + r.got[1].astype(f32) + r.got[2].astype(f32)
    )
    dx2, dg2 = norm_back(r.middle[...], r.m_gain[...], d_normed)
    out.dg2[...] = jnp.sum(dg2, axis=0, keepdims=True)
    middle_low = low(r.grad[own].astype(f32) + dx2)
    for i in range(slots):
        r.dm[i] = low(dot_last(middle_low, r.w_o[i // 2, pl.ds(i % 2 * width, width)]))
    sent.append(fetch(r.dm, out.dm))
    for i in range(slots):
        out.back[i, pl.ds(0, piece)] = middle_low[i * piece : (i + 1) * piece]
        out.back[i, pl.ds(piece, pad - piece)] = jnp.zeros((pad - piece, d), bf)
    out.middle_low[...] = middle_low
    two_out.arrived()
    side_out.arrived()
    out.output[...] = low(
        r.middle[...]
        + r.near_out[core]
        + r.got[4].astype(f32)
        + r.got[5].astype(f32)
    )
    for c in range(2):
        gate_over[c].arrived()
        out.gate[c] = low(r.g_gate[2 * x + c].astype(f32) + r.gate_got[c].astype(f32))
    for c in sent:
        c.wait()


def front_kernel(moved, loaded, number):
    a = Bag(**moved)
    _, rows, d = a.tok.shape
    slots = 2 * LINE
    count = rows * slots
    blocks = count // BLOCK
    width = 2 * HEAD_SIZE
    shard = a.w_q.shape[0]
    half = a.w_gate.shape[1] // 8
    o_rows = a.w_o.shape[0]
    scale = HEAD_SIZE**-0.5
    bf, f32 = jnp.bfloat16, jnp.float32
    piece = rows // slots
    ff = 2 * half
    gain_cols = 2 * a.attn_gain.shape[0] + 2 * HEAD_SIZE

    scratch = dict(
        tok=pltpu.VMEM((slots, rows, d), bf),
        w_qkv=pltpu.VMEM((4, shard, 2 * width), bf),
        gains=pltpu.VMEM((4, 1, gain_cols), f32),
        columns=pltpu.VMEM((count, 8), f32),
        normed=pltpu.VMEM((count, d), bf),
        qkv=pltpu.VMEM((count, 2 * width), f32),
        q=pltpu.VMEM((count, width), bf),
        k=pltpu.VMEM((count, HEAD_SIZE), bf),
        v=pltpu.VMEM((count, HEAD_SIZE), bf),
        kt=pltpu.VMEM((HEAD_SIZE, count), bf),
        vt=pltpu.VMEM((HEAD_SIZE, count), bf),
        cos=pltpu.VMEM((count, HEAD_SIZE), f32),
        sin=pltpu.VMEM((count, HEAD_SIZE), f32),
        mixed=pltpu.VMEM((count, width), f32),
        mixed_low=pltpu.VMEM((count, width), bf),
        sent=pltpu.VMEM((slots, rows, width), bf),
        w_o=pltpu.VMEM((4, o_rows, d), bf),
        w_gu=pltpu.VMEM((4, shard, 4 * half), bf),
        grad=pltpu.VMEM((4, rows, d), bf),
        mixed_in=pltpu.VMEM((slots, rows, width), bf),
        residual=pltpu.VMEM((rows, d), bf),
        m_gain=pltpu.VMEM((1, d), f32),
        w_dn=pltpu.VMEM((2, half, d), bf),
        middle=pltpu.VMEM((rows, d), f32),
        quad=pltpu.VMEM((4, rows, d), bf),
        hidden=pltpu.VMEM((2, 2 * rows, ff), bf),
        d_gu=pltpu.VMEM((2, 2 * rows, 2 * ff), bf),
        near_part=pltpu.VMEM((2, rows, d), f32),
        far_part=pltpu.VMEM((2, rows, d), bf),
        near_out=pltpu.VMEM((2, rows, d), f32),
        far_out=pltpu.VMEM((2, rows, d), bf),
        beside=pltpu.VMEM((rows, d), bf),
        beside_out=pltpu.VMEM((rows, d), bf),
        got=pltpu.VMEM((6, rows, d), bf),
        to_side=pltpu.VMEM((2, rows, d), bf),
        g_gate=pltpu.VMEM((4, shard, ff), bf),
        gate_got=pltpu.VMEM((2, shard, ff), bf),
        g_up=pltpu.VMEM((d, ff), bf),
        g_dn=pltpu.VMEM((ff, d), bf),
        dm=pltpu.VMEM((slots, rows, width), bf),
    )
    outs = dict(
        first=shape_of(1, count, kind=jnp.int32),
        dealt=shape_of(1, count, kind=jnp.int32),
        back_from=shape_of(rows, 1, kind=jnp.int32),
        mixed_in=shape_of(slots, rows, width),
        normed=shape_of(count, d),
        qkv=shape_of(count, 2 * width, kind=f32),
        q=shape_of(count, width),
        k=shape_of(count, HEAD_SIZE),
        v=shape_of(count, HEAD_SIZE),
        kt=shape_of(HEAD_SIZE, count),
        cos=shape_of(count, HEAD_SIZE, kind=f32),
        sin=shape_of(count, HEAD_SIZE, kind=f32),
        mixed=shape_of(count, width, kind=f32),
        lse=shape_of(2, 1, count, kind=f32),
        w_qkv=shape_of(4, shard, 2 * width),
        a_gain=shape_of(1, d, kind=f32),
        q_gain=shape_of(1, HEAD_SIZE, kind=f32),
        k_gain=shape_of(1, HEAD_SIZE, kind=f32),
        output=shape_of(rows, d),
        back=shape_of(slots, 32, d),
        dm=shape_of(slots, rows, width),
        gate=shape_of(2, shard, ff),
        up=shape_of(d, ff),
        down=shape_of(ff, d),
        middle_low=shape_of(rows, d),
        dg2=shape_of(1, d, kind=f32),
    )

    def body(net, fetch, load, given, out, r):
        z, y, x, core, me = net.z, net.y, net.x, net.core, net.me
        f = 2 * x + core
        done = set()
        tok = given.tok.at[0]
        tok_own = fetch(tok, r.tok.at[me])

        def lanes(start, size):
            return pl.ds(pl.multiple_of(start, HEAD_SIZE), size)

        head_parts = [
            (given.w_q.at[:, lanes(me * width, width)], pl.ds(0, width)),
            (given.w_k.at[:, lanes(me * HEAD_SIZE, HEAD_SIZE)], pl.ds(width, HEAD_SIZE)),
            (
                given.w_v.at[:, lanes(me * HEAD_SIZE, HEAD_SIZE)],
                pl.ds(width + HEAD_SIZE, HEAD_SIZE),
            ),
        ]
        w_own = [fetch(src, r.w_qkv.at[f, :, to]) for src, to in head_parts]
        greet(net, ("ctx", "x", "core", "far"))
        log = {s: [] for s in range(LINE)}
        waits = list(w_own)
        zone = lax.broadcasted_iota(jnp.int32, (1, HEAD_SIZE), 1) // (HEAD_SIZE // 4) == f

        def zoned(ref):
            return jnp.where(zone, jnp.concatenate([ref[...].astype(f32)] * 4, axis=1), 0.0)

        r.gains[f] = jnp.concatenate(
            [
                given.attn_gain[...].astype(f32).reshape(1, -1),
                given.mlp_gain[...].astype(f32).reshape(1, -1),
                zoned(given.q_gain),
                zoned(given.k_gain),
            ],
            axis=1,
        )

        def head_weights():
            beside = [net.put(src, r.w_qkv.at[f, :, to], net.at(dc=1)) for src, to in head_parts]
            beside.append(net.put(r.gains.at[f], r.gains.at[f], net.at(dc=1)))
            across = [net.put(src, r.w_qkv.at[f, :, to], net.at(dx=1)) for src, to in head_parts]
            across.append(net.put(r.gains.at[f], r.gains.at[f], net.at(dx=1)))
            yield
            for c in across:
                c.arrived()
            far = 2 * (1 - x) + core
            beside += [
                net.put(r.w_qkv.at[far], r.w_qkv.at[far], net.at(dc=1)),
                net.put(r.gains.at[far], r.gains.at[far], net.at(dc=1)),
            ]
            for c in waits:
                c.wait()
            for c in beside:
                c.arrived()
            r.own = fetch(r.w_qkv, out.w_qkv)
            done.add("head")
            yield

        arriving = Bag(o=[], gu=[], dn=[], grad=[], heads=[])

        def other_weights():
            yield
            arriving.o += [
                fetch(given.w_o, r.w_o.at[f]),
                net.put(given.w_o, r.w_o.at[f], net.at(dx=1)),
                net.put(given.w_o, r.w_o.at[f], net.at(dc=1)),
            ]

            def quarter(c):
                return [
                    (
                        w.at[:, lanes((2 * xs + c) * 2 * half + y * half, half)],
                        r.w_gu.at[f, :, pl.ds((2 * i + xs) * half, half)],
                    )
                    for i, w in enumerate((given.w_gate, given.w_up))
                    for xs in range(2)
                ]

            arriving.gu += [fetch(src, to) for src, to in quarter(core)]
            arriving.gu += [net.put(src, to, net.at(dc=1)) for src, to in quarter(1 - core)]
            arriving.gu += [net.put(src, to, net.at(dx=1)) for src, to in quarter(core)]
            arriving.gu += [net.put(src, to, net.at(dx=1, dc=1)) for src, to in quarter(1 - core)]
            part = given.w_down.at[pl.ds(pl.multiple_of(y * half, half), half)]
            arriving.dn += [
                fetch(part, r.w_dn.at[x]),
                net.put(part, r.w_dn.at[x], net.at(dx=1)),
            ]
            yield from resting(7)
            arriving.o[1].arrived()
            far = r.w_o.at[2 * (1 - x) + core]
            arriving.o.append(net.put(far, far, net.at(dc=1)))

        def output_grad():
            yield from resting(5)
            own = r.grad.at[2 * y + core]
            grad = given.grad.at[0]
            arriving.grad += [
                fetch(grad, own),
                net.put(grad, own, net.at(dc=1)),
                net.put(grad, own, net.at(dy=1)),
            ]
            yield
            arriving.grad[2].arrived()
            far = r.grad.at[2 * (1 - y) + core]
            arriving.grad.append(net.put(far, far, net.at(dc=1)))

        def project(slot):
            at = pl.ds(pl.multiple_of(slot * rows, rows), rows)
            normed = low(root_mean_norm(r.tok[slot].astype(f32), out.a_gain[...]))
            r.normed[at] = normed
            qkv = dot(normed, r.w_qkv[...].reshape(4 * shard, 2 * width))
            r.qkv[at] = qkv
            cos, sin = r.cos[at], r.sin[at]

            def turned(part, gain):
                v = root_mean_norm(part, gain)
                return low(v * cos + turn_lanes(v) * sin)

            for g in range(2):
                cols = pl.ds(g * HEAD_SIZE, HEAD_SIZE)
                r.q[at, cols] = turned(
                    qkv[:, g * HEAD_SIZE : (g + 1) * HEAD_SIZE], out.q_gain[...]
                )
            r.k[at] = turned(qkv[:, width : width + HEAD_SIZE], out.k_gain[...])
            r.v[at] = low(qkv[:, width + HEAD_SIZE :])

        def main():
            ids = lax.broadcasted_iota(jnp.int32, (1, count), 1)
            first, dealt, back, start = jnp.zeros_like(ids), ids, ids, 0
            for i in range(1, given.lengths.shape[1]):
                start = start + given.lengths[0, i - 1]
                first = jnp.where(ids >= start, start, first)
            for s in range(slots):
                for j in range(slots):
                    begin = given.deal[0, s, j] * rows + s * piece
                    dealt = jnp.where(
                        (ids >= begin) & (ids < begin + piece),
                        ids - begin + (s * rows + j * piece),
                        dealt,
                    )
            for j in range(slots):
                begin = given.deal[0, me, j] * 32
                back = jnp.where(
                    (ids >= j * piece) & (ids < (j + 1) * piece), ids - j * piece + begin, back
                )
            out.first[...] = first
            out.dealt[...] = dealt
            row = lax.broadcasted_iota(jnp.int32, (8, count), 0)
            stack = jnp.where(row == 0, ids - first, jnp.where(row == 1, dealt, back))
            r.columns[...] = jnp.transpose(stack.astype(f32))
            out.back_from[...] = r.columns[pl.ds(0, rows), 2:3].astype(jnp.int32)
            for i in range(slots):
                at = pl.ds(i * rows, rows)
                angle = r.columns[at, 0:1] * given.freq[0:1]
                r.cos[at] = jnp.cos(angle)
                r.sin[at] = jnp.sin(angle) * given.freq[1:2]
            yield
            while "head" not in done:
                yield
            gains = [r.gains[i] for i in range(4)]
            part = d // 4
            for i in range(4):
                out.a_gain[:, pl.ds(i * part, part)] = gains[i][:, :part]
                r.m_gain[:, pl.ds(i * part, part)] = gains[i][:, part : 2 * part]
            total = gains[0] + gains[1] + gains[2] + gains[3]
            out.q_gain[...] = total[:, 2 * part : 2 * part + HEAD_SIZE]
            out.k_gain[...] = total[:, 2 * part + HEAD_SIZE :]
            tok_own.wait()
            near = near_first(z)
            for k in range(LINE):
                project(2 * near[k] + y)
                if k:
                    for c in log[k - 1]:
                        c.arrived()
                    project(2 * near[k - 1] + 1 - y)
                yield
            for c in log[LINE - 1]:
                c.arrived()
            project(2 * near[LINE - 1] + 1 - y)
            results = [
                fetch(r.normed, out.normed),
                fetch(r.qkv, out.qkv),
                fetch(r.q, out.q),
                fetch(r.k, out.k),
                fetch(r.v, out.v),
                fetch(r.cos, out.cos),
                fetch(r.sin, out.sin),
                r.own,
            ]
            for i in range(blocks):
                at = pl.ds(i * BLOCK, BLOCK)
                r.kt[:, at] = jnp.transpose(r.k[at])
                r.vt[:, at] = jnp.transpose(r.v[at])
            results.append(fetch(r.kt, out.kt))
            for i in range(blocks):
                here = pl.ds(i * BLOCK, BLOCK)
                first = out.first[:, here]
                t = i * BLOCK + lax.broadcasted_iota(jnp.int32, (BLOCK, BLOCK), 1)
                q = [r.q[here, pl.ds(g * HEAD_SIZE, HEAD_SIZE)] for g in range(2)]

                def step(n, held, i=i, q=q, first=first, t=t):
                    j = i - n
                    at = pl.ds(pl.multiple_of(j * BLOCK, BLOCK), BLOCK)
                    k, vt = r.k[at], r.vt[:, at]
                    u = j * BLOCK + lax.broadcasted_iota(jnp.int32, (BLOCK, BLOCK), 0)
                    allowed = (u >= first) & (u <= t)
                    result = []
                    for g in range(2):
                        top, total, mixed = held[g]
                        scores = jnp.where(allowed, dot_last(k, q[g]) * scale, negative_filler)
                        new = jnp.maximum(top, jnp.max(scores, axis=0, keepdims=True))
                        fade = jnp.exp(top - new)
                        p = jnp.exp(scores - new)
                        total = total * fade + jnp.sum(p, axis=0, keepdims=True)
                        result.append((new, total, mixed * fade + dot(vt, low(p))))
                    return tuple(result)

                row = jnp.full((1, BLOCK), negative_filler, f32)
                none = (row, jnp.zeros((1, BLOCK), f32), jnp.zeros((HEAD_SIZE, BLOCK), f32))
                held = lax.fori_loop(0, i + 1, step, (none, none))
                for g in range(2):
                    top, total, mixed = held[g]
                    cols = pl.ds(g * HEAD_SIZE, HEAD_SIZE)
                    out.lse[g, :, here] = top + jnp.log(total)
                    mixed = jnp.transpose(mixed / total)
                    r.mixed[here, cols] = mixed
                    r.mixed_low[here, cols] = low(mixed)
                yield
            results.append(fetch(r.mixed, out.mixed))
            ids = lax.broadcasted_iota(jnp.int32, (rows, count), 1)

            def hot(slot):
                at = pl.ds(pl.multiple_of(slot * rows, rows), rows)
                return low(jnp.where(r.columns[at, 1:2].astype(jnp.int32) == ids, 1.0, 0.0))

            for k in range(1, slots):
                other = lax.rem(me + k, slots)
                r.sent[other] = low(dot(hot(other), r.mixed_low[...]))
                there = (other // 2, lax.rem(other, 2), x, core)
                arriving.heads.append(net.put(r.sent.at[other], r.mixed_in.at[me], there))
            mine = hot(me)
            r.sent[me] = low(dot(mine, r.mixed_low[...]))
            arriving.heads.append(fetch(r.sent.at[me], r.mixed_in.at[me]))
            r.residual[...] = low(dot(mine, r.tok[...].reshape(count, d)))
            for c in arriving.heads:
                c.arrived()
            results.append(fetch(r.mixed_in, out.mixed_in))
            for c in results:
                c.wait()
            yield

        drive(
            head_weights(),
            by_steps(gather_line_first(net, tok, lambda slot: r.tok.at[slot], log)),
            main(),
            other_weights(),
            output_grad(),
        )
        middle(net, fetch, arriving, out, r)

    return kernel_with(
        body,
        moved,
        loaded,
        outs,
        scratch,
        110,
        number,
        (
            "lse",
            "a_gain",
            "q_gain",
            "k_gain",
            "first",
            "dealt",
            "back_from",
            "output",
            "back",
            "middle_low",
            "dg2",
            "gate",
        ),
        ("attn_gain", "mlp_gain", "q_gain", "k_gain", "freq"),
        ("lengths", "deal"),
    )


def back_kernel(dims, number):
    rows, count = dims
    blocks = count // BLOCK
    scale = HEAD_SIZE**-0.5
    width = 2 * HEAD_SIZE
    d = MODEL_WIDTH

    def run(moved, loaded):
        a = Bag(**moved)
        gu_rows, gu_cols = a.gate.shape[1:]
        dn_rows = a.down.shape[1]
        o_rows = 2 * width
        bf, f32 = jnp.bfloat16, jnp.float32
        z_gu, z_dn, z_o = gu_rows // LINE, dn_rows // LINE, o_rows // (2 * LINE)
        gain_width = 2 * d + 2 * HEAD_SIZE

        def quarter(**more):
            return dict(
                **more,
                own=pltpu.VMEM((2, gu_rows, gu_cols), bf),
                low=pltpu.VMEM((2, z_gu, gu_cols), bf),
                pair=pltpu.VMEM((2, z_gu, gu_cols), bf),
                line=line_scratch(2 * z_gu, gu_cols),
            )

        scratch = dict(
            held={n: pltpu.VMEM(v.shape, v.dtype) for n, v in loaded.items()},
            gate=quarter(),
            up=quarter(got=pltpu.VMEM((2, gu_rows, gu_cols), bf)),
            down=[
                dict(
                    own=pltpu.VMEM((dn_rows, d // 2), bf),
                    got=pltpu.VMEM((dn_rows, d // 2), bf),
                    low=pltpu.VMEM((z_dn, d // 2), bf),
                    line=line_scratch(z_dn, d // 2),
                )
                for _ in range(2)
            ],
            o=dict(
                own=pltpu.VMEM((4, o_rows, d), bf),
                core=pltpu.VMEM((2, o_rows, d), bf),
                got=pltpu.VMEM((o_rows, d), bf),
                sum=pltpu.VMEM((2 * LINE, z_o, d), bf),
                side=pltpu.VMEM((LINE, z_o, d), bf),
                low=pltpu.VMEM((z_o, d), bf),
                line=line_scratch(z_o, d),
            ),
            h=dict(
                own=pltpu.VMEM((4, d // 4, 2 * width), bf),
                core=pltpu.VMEM((2, d // 4, 2 * width), bf),
                got=pltpu.VMEM((d // 4, 2 * width), bf),
                low=pltpu.VMEM((d // 4, 2 * width), bf),
            ),
            dm_all=pltpu.VMEM((2 * LINE, rows, width), bf),
            back=pltpu.VMEM(a.back.shape, bf),
            do=pltpu.VMEM((count, width), bf),
            dk=pltpu.VMEM((count, HEAD_SIZE), f32),
            dv=pltpu.VMEM((count, HEAD_SIZE), f32),
            dqkv=pltpu.VMEM((count, 2 * width), bf),
            dgq=pltpu.VMEM((1, HEAD_SIZE), f32),
            dgk=pltpu.VMEM((1, HEAD_SIZE), f32),
            part=dict(
                sum=pltpu.VMEM((2 * LINE, rows, d), bf),
                side=pltpu.VMEM((LINE, rows, d), bf),
                line=line_scratch(rows, d),
            ),
            g=dict(
                mine=pltpu.VMEM((1, gain_width), f32),
                four=pltpu.VMEM((1, gain_width), f32),
                got=pltpu.VMEM((3, 1, gain_width), f32),
                all=pltpu.VMEM((2 * LINE, 1, gain_width), f32),
            ),
        )
        flat, tree = jax.tree.flatten(scratch)
        f_in, in_tree = jax.tree.flatten((moved, loaded))
        outs = dict(
            input_grad=shape_of(rows, d, kind=f32),
            a_grad=shape_of(1, d // 4, kind=f32),
            m_grad=shape_of(1, d // 4, kind=f32),
            q_grad=shape_of(1, HEAD_SIZE // 4, kind=f32),
            k_grad=shape_of(1, HEAD_SIZE // 4, kind=f32),
            gate=shape_of(2 * LINE, 2, z_gu, gu_cols),
            up=shape_of(2 * LINE, 2, z_gu, gu_cols),
            down=shape_of(2 * LINE, z_dn, d),
            o=shape_of(2 * LINE, z_o, d),
            heads=shape_of(2 * LINE, d // 4, 2 * width),
        )
        f_out, out_tree = jax.tree.flatten(outs)

        def body(net, local, *refs):
            given, to_load = jax.tree.unflatten(in_tree, refs[: len(f_in)])
            given = Bag(**given)
            out = Bag(**jax.tree.unflatten(out_tree, refs[len(f_in) : len(f_in) + len(f_out)]))
            r = bags(jax.tree.unflatten(tree, refs[len(f_in) + len(f_out) :]))
            h = r.held
            z, y, x, core, me = net.z, net.y, net.x, net.core, net.me
            slots = 2 * LINE
            used = iter(range(64))

            def fetch(src, dst):
                copy = pltpu.make_async_copy(src, dst, local.at[next(used)])
                copy.start()
                return copy

            greet(net, ("ctx", "x", "core", "far"))
            loads = {n: fetch(to_load[n], getattr(h, n)) for n in to_load}
            dm_own = fetch(given.dm.at[me], r.dm_all.at[me])
            back_own = fetch(given.back.at[me], r.back.at[me])
            gate_own = [fetch(given.gate.at[c], r.gate.own.at[c]) for c in range(2)]
            up_own = [fetch(given.up.at[2 * x + c], r.up.own.at[c]) for c in range(2)]
            columns = [pl.ds(0, d // 2), pl.ds(d // 2, d // 2)]
            down_own = [fetch(given.down.at[x, :, columns[i]], r.down[i].own) for i in range(2)]
            back_copies = []

            def need(*which):
                for n in which:
                    if n in loads:
                        loads.pop(n).wait()

            def to_all(src, out):
                copies = []
                for k in range(1, slots):
                    other = lax.rem(me + k, slots)
                    there = (other // 2, lax.rem(other, 2), x, core)
                    copies.append(net.put(src(other), out.at[me], there))
                return copies

            def back_rows():
                back_copies.extend(to_all(lambda other: given.back.at[other], r.back))
                yield

            def main():
                dm_copies = to_all(lambda other: given.dm.at[other], r.dm_all)
                yield
                need(*list(loads))
                dm_own.wait()
                for c in dm_copies:
                    c.arrived()
                yield
                for i in range(blocks):
                    t = i * BLOCK + lax.broadcasted_iota(jnp.int32, (BLOCK, count), 0)
                    hot = low(jnp.where(h.dealt[...] == t, 1.0, 0.0))
                    r.do[pl.ds(i * BLOCK, BLOCK)] = low(
                        dot(hot, r.dm_all[...].reshape(count, width))
                    )
                r.dk[...] = jnp.zeros_like(r.dk)
                r.dv[...] = jnp.zeros_like(r.dv)
                yield
                dgq = jnp.zeros((1, HEAD_SIZE), f32)
                for i in range(blocks):
                    here = pl.ds(i * BLOCK, BLOCK)
                    first = h.first[:, here]
                    t = i * BLOCK + lax.broadcasted_iota(jnp.int32, (BLOCK, BLOCK), 1)
                    heads = []
                    for g in range(2):
                        lanes = pl.ds(g * HEAD_SIZE, HEAD_SIZE)
                        q, do = h.q[here, lanes], r.do[here, lanes]
                        product = do.astype(f32) * h.mixed[here, lanes]
                        delta = jnp.sum(jnp.transpose(product), axis=0, keepdims=True)
                        heads.append((q, do, h.lse[g, :, here], delta))

                    def step(j, held, heads=heads, first=first, t=t):
                        at = pl.ds(pl.multiple_of(j * BLOCK, BLOCK), BLOCK)
                        k, v, kt = h.k[at], h.v[at], h.kt[:, at]
                        u = j * BLOCK + lax.broadcasted_iota(jnp.int32, (BLOCK, BLOCK), 0)
                        allowed = (u >= first) & (u <= t)
                        dk, dv, out = r.dk[at], r.dv[at], []
                        for (q, do, lse, delta), dq in zip(heads, held):
                            p = jnp.where(allowed, jnp.exp(dot_last(k, q) * scale - lse), 0.0)
                            ds = low(p * (dot_last(v, do) - delta))
                            dv = dv + dot(low(p), do)
                            dk = dk + dot(ds, q)
                            out.append(dq + dot(kt, ds))
                        r.dk[at] = dk
                        r.dv[at] = dv
                        return tuple(out)

                    zero = jnp.zeros((HEAD_SIZE, BLOCK), f32)
                    result = lax.fori_loop(0, i + 1, step, (zero, zero))
                    cos, sin = h.cos[here], h.sin[here]
                    for g in range(2):
                        lanes = pl.ds(g * HEAD_SIZE, HEAD_SIZE)
                        grad = jnp.transpose(result[g]) * scale
                        grad = grad * cos - turn_lanes(grad) * sin
                        dx, dg = norm_back(h.qkv[here, lanes], h.q_gain[...], grad)
                        r.dqkv[here, lanes] = low(dx)
                        dgq = dgq + jnp.sum(dg, axis=0, keepdims=True)
                    yield
                dgk = jnp.zeros((1, HEAD_SIZE), f32)
                for i in range(blocks):
                    here = pl.ds(i * BLOCK, BLOCK)
                    grad = r.dk[here] * scale
                    grad = grad * h.cos[here] - turn_lanes(grad) * h.sin[here]
                    dx, dg = norm_back(
                        h.qkv[here, pl.ds(width, HEAD_SIZE)], h.k_gain[...], grad
                    )
                    r.dqkv[here, pl.ds(width, HEAD_SIZE)] = low(dx)
                    r.dqkv[here, pl.ds(width + HEAD_SIZE, HEAD_SIZE)] = low(r.dv[here])
                    dgk = dgk + jnp.sum(dg, axis=0, keepdims=True)
                r.dgq[...] = dgq
                r.dgk[...] = dgk
                yield

                def make(slot):
                    at = pl.ds(pl.multiple_of(slot * rows, rows), rows)
                    r.part.sum[slot] = low(dot_last(r.dqkv[at], h.w_qkv[...].reshape(d, 2 * width)))

                yield from sum_sides(net, r.part.sum, r.part.side, r.part.line, make)
                yield
                dx1, dg1 = norm_back(
                    h.tok[0].astype(f32), h.a_gain[...], r.part.line[0][z]
                )
                for c in back_copies:
                    c.arrived()
                back_own.wait()
                ids = lax.broadcasted_iota(jnp.int32, (rows, slots * a.back.shape[1]), 1)
                hot = low(jnp.where(h.back_from[...] == ids, 1.0, 0.0))
                out.input_grad[...] = dx1 + dot(hot, r.back[...].reshape(-1, d))
                r.g.mine[:, pl.ds(0, d)] = jnp.sum(dg1, axis=0, keepdims=True)
                r.g.mine[:, pl.ds(d, d)] = h.dg2[...]
                r.g.mine[:, pl.ds(2 * d, HEAD_SIZE)] = r.dgq[...]
                r.g.mine[:, pl.ds(2 * d + HEAD_SIZE, HEAD_SIZE)] = r.dgk[...]
                yield

            def gains():
                sides = [net.at(dc=1), net.at(dx=1), net.at(dx=1, dc=1)]
                pair = [net.put(r.g.mine, r.g.got.at[i], to) for i, to in enumerate(sides)]
                yield
                for c in pair:
                    c.arrived()
                along = r.g.mine[...] + r.g.got[0]
                across = r.g.got[1] + r.g.got[2]
                r.g.four[...] = along + across
                r.g.all[me] = r.g.four[...]
                copies = to_all(lambda other: r.g.four, r.g.all)
                yield
                for c in copies:
                    c.arrived()
                total = jnp.sum(r.g.all[...], axis=0)

                def own_part(start, size):
                    part = total[:, start : start + size]
                    for i in range(1, 4):
                        at = start + i * size
                        part = jnp.where(2 * x + core == i, total[:, at : at + size], part)
                    return part

                out.a_grad[...] = own_part(0, d // 4)
                out.m_grad[...] = own_part(d, d // 4)
                out.q_grad[...] = own_part(2 * d, HEAD_SIZE // 4)
                out.k_grad[...] = own_part(2 * d + HEAD_SIZE, HEAD_SIZE // 4)
                yield

            def gate_or_up(piece, gathered):
                line = piece.line

                def ready(t):
                    k = far_first(z)[t]
                    at = pl.ds(pl.multiple_of(k * z_gu, z_gu), z_gu)
                    for c in range(2):
                        block = piece.own[c, at].astype(f32)
                        if hasattr(piece, "got"):
                            block = block + piece.got[c, at].astype(f32)
                        line[0][k, pl.ds(c * z_gu, z_gu)] = block

                yield from sum_line(net, *line, ready)
                for c in range(2):
                    piece.low[c] = low(line[0][z, pl.ds(c * z_gu, z_gu)])
                swap = net.put(piece.low.at[1 - core], piece.pair.at[core], net.at(dc=1))
                piece.pair[core] = piece.low[core]
                yield
                swap.arrived()
                own = fetch(piece.pair, gathered.at[me])
                yield from gather_line_first(net, piece.pair, lambda slot: gathered.at[slot])
                own.wait()

            def gate():
                for c in gate_own:
                    c.wait()
                yield from gate_or_up(r.gate, out.gate)

            def up():
                over = [
                    net.put(given.up.at[2 * (1 - x) + c], r.up.got.at[c], net.at(dx=1))
                    for c in range(2)
                ]
                yield
                for c in up_own:
                    c.wait()
                for c in over:
                    c.arrived()
                yield from gate_or_up(r.up, out.up)

            def down(i):
                piece, line = r.down[i], r.down[i].line
                over = net.put(given.down.at[1 - x, :, columns[i]], piece.got, net.at(dx=1))
                yield
                down_own[i].wait()
                over.arrived()

                def ready(t):
                    k = far_first(z)[t]
                    at = pl.ds(pl.multiple_of(k * z_dn, z_dn), z_dn)
                    line[0][k] = piece.own[at].astype(f32) + piece.got[at].astype(f32)

                yield from sum_line(net, *line, ready)
                piece.low[...] = low(line[0][z])
                own = fetch(piece.low, out.down.at[me, :, columns[i]])
                yield from gather_line_first(
                    net, piece.low, lambda slot: out.down.at[slot, :, columns[i]]
                )
                own.wait()

            def out_proj():
                need("heads_in", "middle_low")
                for i in range(slots):
                    r.o.own[i // 2, pl.ds(i % 2 * width, width)] = low(
                        outer_rows(h.heads_in[i], h.middle_low[...])
                    )
                o_core = [
                    net.put(r.o.own.at[2 * s + 1 - core], r.o.core.at[s], net.at(dc=1))
                    for s in range(2)
                ]
                yield
                for c in o_core:
                    c.arrived()
                for s in range(2):
                    f = 2 * s + core
                    r.o.own[f] = low(r.o.own[f].astype(f32) + r.o.core[s].astype(f32))
                over = net.put(r.o.own.at[2 * (1 - x) + core], r.o.got, net.at(dx=1))
                yield
                over.arrived()
                for i in range(slots):
                    at = pl.ds(i * z_o, z_o)
                    r.o.sum[i] = low(r.o.own[2 * x + core, at].astype(f32) + r.o.got[at].astype(f32))
                yield from sum_sides(net, r.o.sum, r.o.side, r.o.line)
                r.o.low[...] = low(r.o.line[0][z])
                own = fetch(r.o.low, out.o.at[me])
                yield from gather_line_first(net, r.o.low, lambda slot: out.o.at[slot])
                own.wait()

            def heads():
                for f in range(4):
                    at = pl.ds(f * (d // 4), d // 4)
                    r.h.own[f] = low(outer_rows(h.normed[:, at], r.dqkv[...]))
                core_copies = [
                    net.put(r.h.own.at[2 * s + 1 - core], r.h.core.at[s], net.at(dc=1))
                    for s in range(2)
                ]
                yield
                for c in core_copies:
                    c.arrived()
                for s in range(2):
                    f = 2 * s + core
                    r.h.own[f] = low(r.h.own[f].astype(f32) + r.h.core[s].astype(f32))
                over = net.put(r.h.own.at[2 * (1 - x) + core], r.h.got, net.at(dx=1))
                yield
                over.arrived()
                r.h.low[...] = low(
                    r.h.own[2 * x + core].astype(f32) + r.h.got[...].astype(f32)
                )
                own = fetch(r.h.low, out.heads.at[me])
                yield from gather_line_first(net, r.h.low, lambda slot: out.heads.at[slot])
                own.wait()

            in_order(
                BACK_ORDER,
                [
                    gate(),
                    up(),
                    out_proj(),
                    down(0),
                    down(1),
                    back_rows(),
                    heads(),
                    main(),
                    gains(),
                ],
            )
            net.close()

        order = jax.tree.unflatten(out_tree, range(len(f_out)))
        result = net_call(
            body,
            f_out,
            f_in,
            200,
            64,
            number,
            scratch=flat,
            vmem=[
                len(f_in) + order.get(n)
                for n in ("input_grad", "a_grad", "m_grad", "q_grad", "k_grad")
            ],
        )
        return Bag(**jax.tree.unflatten(out_tree, result))

    return run


def widen(gate_all, up_all, down_all, o_all, heads_all, *small):
    _, _, z_gu, gu_cols = gate_all.shape
    half = gu_cols // 2
    z_dn, z_o = down_all.shape[1], o_all.shape[1]
    h_rows = heads_all.shape[1] // LINE

    def kernel(gate, up, down, o, heads, *refs):
        passed, outs = refs[: len(small)], refs[len(small) :]
        gate_out, up_out, down_out, o_out, q_out, k_out, v_out = outs[:7]
        for src, out in zip(passed, outs[7:]):
            out[...] = src[...].reshape(out.shape)
        for src, out in ((gate, gate_out), (up, up_out)):
            for y in range(2):
                for c in range(2):
                    for xs in range(2):
                        to = (2 * xs + c) * 2 * half + y * half
                        out[:, pl.ds(to, half)] = src[y, c, :, pl.ds(xs * half, half)].astype(
                            jnp.float32
                        )
        for y in range(2):
            down_out[y] = down[y].astype(jnp.float32)
            o_out[pl.ds(y * z_o, z_o)] = o[y].astype(jnp.float32)
        for h in range(2 * LINE):
            q_out[:, pl.ds(h * 256, 256)] = heads[h, :, pl.ds(0, 256)].astype(jnp.float32)
            k_out[:, pl.ds(h * 128, 128)] = heads[h, :, pl.ds(256, 128)].astype(jnp.float32)
            v_out[:, pl.ds(h * 128, 128)] = heads[h, :, pl.ds(384, 128)].astype(jnp.float32)

    f32 = jnp.float32
    outs = pl.pallas_call(
        kernel,
        grid=(LINE,),
        in_specs=[
            pl.BlockSpec((2, 2, z_gu, gu_cols), lambda i: (i, 0, 0, 0)),
            pl.BlockSpec((2, 2, z_gu, gu_cols), lambda i: (i, 0, 0, 0)),
            pl.BlockSpec((2, z_dn, MODEL_WIDTH), lambda i: (i, 0, 0)),
            pl.BlockSpec((2, z_o, MODEL_WIDTH), lambda i: (i, 0, 0)),
            pl.BlockSpec((2 * LINE, h_rows, 512), lambda i: (0, i, 0)),
        ]
        + [pl.BlockSpec(v.shape, lambda i: (0, 0)) for v in small],
        out_specs=[
            pl.BlockSpec((z_gu, 8 * half), lambda i: (i, 0)),
            pl.BlockSpec((z_gu, 8 * half), lambda i: (i, 0)),
            pl.BlockSpec((2, z_dn, MODEL_WIDTH), lambda i: (0, i, 0)),
            pl.BlockSpec((2 * z_o, MODEL_WIDTH), lambda i: (i, 0)),
            pl.BlockSpec((h_rows, 2048), lambda i: (i, 0)),
            pl.BlockSpec((h_rows, 1024), lambda i: (i, 0)),
            pl.BlockSpec((h_rows, 1024), lambda i: (i, 0)),
        ]
        + [pl.BlockSpec((1, *v.shape), lambda i: (0, 0, 0)) for v in small],
        out_shape=[
            shape_of(LINE * z_gu, 8 * half, kind=f32),
            shape_of(LINE * z_gu, 8 * half, kind=f32),
            shape_of(2, LINE * z_dn, MODEL_WIDTH, kind=f32),
            shape_of(2 * LINE * z_o, MODEL_WIDTH, kind=f32),
            shape_of(LINE * h_rows, 2048, kind=f32),
            shape_of(LINE * h_rows, 1024, kind=f32),
            shape_of(LINE * h_rows, 1024, kind=f32),
        ]
        + [shape_of(1, *v.shape, kind=v.dtype) for v in small],
        compiler_params=pltpu.CompilerParams(vmem_limit_bytes=VMEM_BYTES),
    )(gate_all, up_all, down_all, o_all, heads_all, *small)
    outs = list(outs)
    outs[2] = outs[2].reshape(-1, MODEL_WIDTH)
    return outs


def fast_layer(
    tokens,
    lengths,
    deal,
    attn_gain,
    w_q,
    key_weight,
    value_weight,
    query_norm_gain,
    k_gain,
    w_o,
    mlp_gain,
    w_gate,
    w_up,
    w_down,
    out_cotangent,
):
    rows = tokens.shape[1]
    slots = lax.axis_size(CTX)
    count = rows * slots
    ff_half = w_down.shape[0] // 2
    width = HEAD_SIZE * 2

    frequency = theta_base ** (-(np.arange(HEAD_SIZE // 2) * 2.0) / HEAD_SIZE)
    sign = np.where(np.arange(HEAD_SIZE) < HEAD_SIZE // 2, -1.0, 1.0)
    tables = np.stack([np.tile(frequency, 2), sign]).astype(np.float32)

    front = front_kernel(
        dict(
            tok=tokens,
            lengths=lengths,
            deal=deal,
            attn_gain=attn_gain,
            mlp_gain=mlp_gain,
            q_gain=query_norm_gain[None],
            k_gain=k_gain[None],
            freq=tables,
            w_q=w_q,
            w_k=key_weight,
            w_v=value_weight,
            w_o=w_o,
            w_gate=w_gate,
            w_up=w_up,
            w_down=w_down,
            grad=out_cotangent,
        ),
        {},
        0,
    )
    moved = dict(
        dm=front.dm,
        back=front.back,
        gate=front.gate,
        up=front.up.reshape(4, -1, 2 * ff_half),
        down=front.down.reshape(2, -1, MODEL_WIDTH),
    )
    loaded = dict(
        tok=tokens,
        back_from=front.back_from,
        a_gain=front.a_gain,
        dg2=front.dg2,
        heads_in=front.mixed_in,
        middle_low=front.middle_low,
        q=front.q,
        k=front.k,
        kt=front.kt,
        v=front.v,
        mixed=front.mixed,
        lse=front.lse,
        first=front.first,
        dealt=front.dealt,
        qkv=front.qkv,
        q_gain=front.q_gain,
        k_gain=front.k_gain,
        cos=front.cos,
        sin=front.sin,
        normed=front.normed,
        w_qkv=front.w_qkv,
    )
    sums = back_kernel((rows, count), 2)(moved, loaded)

    gate_sum, up_sum, down_sum, o_sum, q_sum, k_sum, v_sum, *small = widen(
        sums.gate,
        sums.up,
        sums.down,
        sums.o,
        sums.heads,
        front.output,
        sums.input_grad,
        sums.a_grad,
        sums.q_grad,
        sums.k_grad,
        sums.m_grad,
    )
    output, input_grad, *gains = small
    return (
        output,
        input_grad,
        *(gain[0, 0] for gain in gains),
        q_sum,
        k_sum,
        v_sum,
        o_sum,
        gate_sum,
        up_sum,
        down_sum,
    )


def solution(mesh):
    devices = mesh.devices
    if devices.shape == (8, 4):
        mesh = Mesh(devices.reshape(4, 2, 2, 2), CTX + FSDP)
        layer, ctx, fsdp = fast_layer, CTX, FSDP
    else:
        layer, ctx, fsdp = general_layer, "ctx", "fsdp"
    wide_rows = P(fsdp, ctx, None)
    return jax.shard_map(
        layer,
        mesh=mesh,
        in_specs=(
            wide_rows,
            P(fsdp, None),
            P(fsdp, None, None),
            P(fsdp),
            P(fsdp, None),
            P(fsdp, None),
            P(fsdp, None),
            P(fsdp),
            P(fsdp),
            P(fsdp, None),
            P(fsdp),
            P(fsdp, None),
            P(fsdp, None),
            P(fsdp, None),
            wide_rows,
        ),
        out_specs=(wide_rows, wide_rows) + (P(fsdp),) * 4 + (P(fsdp, None),) * 7,
        check_vma=False,
    )
```

```python
import math

import jax
import jax.numpy as jnp
import numpy as np
from jax import lax
from jax.experimental import pallas as pl
from jax.experimental.pallas import tpu as pltpu
from jax.sharding import Mesh
from jax.sharding import PartitionSpec as P

MODEL_WIDTH = 1024
QUERY_HEADS = 16
KEY_VALUE_HEADS = 8
HEAD_SIZE = 128


eps = 1e-06
theta_base = 1000000.0
negative_filler = -1e30


def root_mean_norm(values, gain_vec):
    return values * lax.rsqrt(jnp.mean(values * values, axis=-1, keepdims=True) + eps) * gain_vec


def rotary_embedding(values, token_position):
    half_width = values.shape[-1] // 2
    frequency = theta_base ** (
        -(jnp.arange(half_width, dtype=jnp.float32) * 2.0) / values.shape[-1]
    )
    angles = token_position.astype(jnp.float32)[:, None] * frequency[None, :]
    cosine = jnp.concatenate([jnp.cos(angles), jnp.cos(angles)], axis=-1)[:, None, :]
    sine_part = jnp.concatenate([jnp.sin(angles), jnp.sin(angles)], axis=-1)[:, None, :]
    turned = jnp.concatenate([-values[..., half_width:], values[..., :half_width]], axis=-1)
    return values * cosine + turned * sine_part


def dot_trans(left_side, right_side):
    return lax.dot_general(
        left_side, right_side, (((1,), (1,)), ((), ())), preferred_element_type=jnp.float32
    )


def outer_rows(left_side, right_side):
    return lax.dot_general(
        left_side, right_side, (((0,), (0,)), ((), ())), preferred_element_type=jnp.float32
    )


def block_plan(piece_rows, local_rows):
    shards = piece_rows // local_rows
    per_block = math.gcd(shards, max(1, 1024 // local_rows))
    return (per_block * local_rows, shards // per_block)


def over_blocks(carried, arrays, local_rows, block_work):
    rows_per_block, count_of_blocks = block_plan(arrays[0].shape[0], local_rows)

    def one_block(turn_index, state_now):
        offset = turn_index * rows_per_block
        parts = tuple(
            (lax.dynamic_slice_in_dim(member, offset, rows_per_block, 0) for member in arrays)
        )
        return block_work(state_now, parts, offset)

    return lax.fori_loop(0, count_of_blocks, one_block, carried)


def segment_begin(tok_ids, starts):
    return jnp.max(jnp.where(tok_ids[:, None] >= starts[None, :], starts[None, :], 0), axis=1)


def general_layer(
    tokens,
    lengths,
    deal,
    attn_gain,
    w_q,
    key_weight,
    value_weight,
    query_norm_gain,
    k_gain,
    w_o,
    mlp_gain,
    w_gate,
    w_up,
    w_down,
    out_cotangent,
):
    local_rows = tokens.shape[1]
    piece_count = lax.axis_size("ctx")
    piece_rows = local_rows // piece_count
    here = lax.axis_index("ctx")
    group_width = QUERY_HEADS // KEY_VALUE_HEADS
    score_scale = HEAD_SIZE ** (-0.5)
    seq_lengths = lengths[0]
    starts = jnp.cumsum(seq_lengths) - seq_lengths
    plan = deal[0]
    devices = jnp.arange(piece_count, dtype=jnp.int32)
    hits = plan[:, :, None] == devices[None, None, :]
    slot_of = jnp.sum(jnp.where(hits, devices[None, :, None], 0), axis=1)
    inner = jnp.arange(piece_rows, dtype=jnp.int32)
    dealt_index = (
        devices[None, :, None] * local_rows
        + jnp.transpose(slot_of)[:, :, None] * piece_rows
        + inner[None, None, :]
    ).reshape(piece_count * local_rows)
    dealt_first = segment_begin(dealt_index, starts)
    tok_index = lax.dynamic_slice_in_dim(dealt_index, here * local_rows, local_rows)
    segment_initial = lax.dynamic_slice_in_dim(dealt_first, here * local_rows, local_rows)
    token_position = tok_index - segment_initial
    own_slots = lax.dynamic_index_in_dim(slot_of, here, 0, keepdims=False)
    own_plan = lax.dynamic_index_in_dim(plan, here, 0, keepdims=False)
    token_pieces = jnp.take(
        tokens[0].reshape(piece_count, piece_rows, MODEL_WIDTH), own_slots, axis=0
    )
    dealt_tok = lax.all_to_all(
        token_pieces, "ctx", split_axis=0, concat_axis=0, tiled=True
    ).reshape(local_rows, MODEL_WIDTH)

    def key_mask(start_row, local_row_count):
        key_identifiers = lax.dynamic_slice_in_dim(dealt_index, start_row, local_row_count)
        return (key_identifiers[None, :] >= segment_initial[:, None]) & (
            key_identifiers[None, :] <= tok_index[:, None]
        )

    def query_mask(start_row, local_row_count):
        query_ids = lax.dynamic_slice_in_dim(dealt_index, start_row, local_row_count)
        first_key = lax.dynamic_slice_in_dim(dealt_first, start_row, local_row_count)
        return (tok_index[None, :] >= first_key[:, None]) & (
            tok_index[None, :] <= query_ids[:, None]
        )

    def fetch_weights():
        attn_set = (
            lax.all_gather(attn_gain, "fsdp", axis=0, tiled=True),
            lax.all_gather(query_norm_gain, "fsdp", axis=0, tiled=True),
            lax.all_gather(k_gain, "fsdp", axis=0, tiled=True),
            lax.all_gather(w_q, "fsdp", axis=0, tiled=True),
            lax.all_gather(key_weight, "fsdp", axis=0, tiled=True),
            lax.all_gather(value_weight, "fsdp", axis=0, tiled=True),
            lax.all_gather(w_o, "fsdp", axis=0, tiled=True),
        )
        mlp_set = (
            lax.all_gather(mlp_gain, "fsdp", axis=0, tiled=True),
            lax.all_gather(w_gate, "fsdp", axis=0, tiled=True),
            lax.all_gather(w_up, "fsdp", axis=0, tiled=True),
            lax.all_gather(w_down, "fsdp", axis=0, tiled=True),
        )
        return (attn_set, mlp_set)

    def forward(attn_set, mlp_set, token_rows):
        a_gain, qn_gain, kn_gain, proj_q, proj_k, proj_v, proj_o = attn_set
        m_gain, proj_gate, proj_up, proj_down = mlp_set
        residual = token_rows.astype(jnp.float32)
        normalized_input = root_mean_norm(residual, a_gain.astype(jnp.float32)).astype(jnp.bfloat16)
        query_prenorm = jnp.dot(
            normalized_input, proj_q, preferred_element_type=jnp.float32
        ).reshape(local_rows, QUERY_HEADS, HEAD_SIZE)
        key_prenorm = jnp.dot(normalized_input, proj_k, preferred_element_type=jnp.float32).reshape(
            local_rows, KEY_VALUE_HEADS, HEAD_SIZE
        )
        value_narrow = jnp.dot(normalized_input, proj_v, preferred_element_type=jnp.float32).astype(
            jnp.bfloat16
        )
        q_heads = (
            rotary_embedding(
                root_mean_norm(query_prenorm, qn_gain.astype(jnp.float32)), token_position
            )
            .astype(jnp.bfloat16)
            .reshape(local_rows, KEY_VALUE_HEADS, group_width, HEAD_SIZE)
        )
        key_narrow = (
            rotary_embedding(
                root_mean_norm(key_prenorm, kn_gain.astype(jnp.float32)), token_position
            )
            .astype(jnp.bfloat16)
            .reshape(local_rows, KEY_VALUE_HEADS * HEAD_SIZE)
        )

        def attend_over_block(state_now, shard_piece, start_row):
            key_segment, value_segment = shard_piece
            local_row_count = key_segment.shape[0]
            allowed = key_mask(start_row, local_row_count)
            row_top, row_total, weighted = state_now
            scores = (
                jnp.einsum(
                    "rkgh,ckh->kgrc",
                    q_heads,
                    key_segment.reshape(local_row_count, KEY_VALUE_HEADS, HEAD_SIZE),
                    preferred_element_type=jnp.float32,
                )
                * score_scale
            )
            scores = jnp.where(allowed, scores, negative_filler)
            new_top = jnp.maximum(row_top, jnp.max(scores, axis=-1))
            rescale = jnp.exp(row_top - new_top)
            weights = jnp.where(allowed, jnp.exp(scores - new_top[..., None]), 0.0)
            row_total = row_total * rescale + jnp.sum(weights, axis=-1)
            weighted = weighted * rescale[..., None] + jnp.einsum(
                "kgrc,ckh->kgrh",
                weights.astype(jnp.bfloat16),
                value_segment.reshape(local_row_count, KEY_VALUE_HEADS, HEAD_SIZE),
                preferred_element_type=jnp.float32,
            )
            return (new_top, row_total, weighted)

        initial = (
            jnp.full((KEY_VALUE_HEADS, group_width, local_rows), negative_filler, jnp.float32),
            jnp.zeros((KEY_VALUE_HEADS, group_width, local_rows), jnp.float32),
            jnp.zeros((KEY_VALUE_HEADS, group_width, local_rows, HEAD_SIZE), jnp.float32),
        )
        row_top, row_total, weighted = over_blocks(
            initial,
            (
                lax.all_gather(key_narrow, "ctx", axis=0, tiled=True),
                lax.all_gather(value_narrow, "ctx", axis=0, tiled=True),
            ),
            local_rows,
            attend_over_block,
        )
        attention_mixed = jnp.transpose(weighted / row_total[..., None], (2, 0, 1, 3)).reshape(
            local_rows, QUERY_HEADS * HEAD_SIZE
        )
        log_total = row_top + jnp.log(row_total)
        mixed_low = attention_mixed.astype(jnp.bfloat16)
        middle = residual + jnp.dot(mixed_low, proj_o, preferred_element_type=jnp.float32)
        normed2 = root_mean_norm(middle, m_gain.astype(jnp.float32)).astype(jnp.bfloat16)
        gate_pre = jnp.dot(normed2, proj_gate, preferred_element_type=jnp.float32)
        up_pre = jnp.dot(normed2, proj_up, preferred_element_type=jnp.float32)
        hidden = (jax.nn.silu(gate_pre) * up_pre).astype(jnp.bfloat16)
        result = middle + jnp.dot(hidden, proj_down, preferred_element_type=jnp.float32)
        return (
            result,
            residual,
            normalized_input,
            query_prenorm,
            key_prenorm,
            value_narrow,
            q_heads,
            key_narrow,
            attention_mixed,
            mixed_low,
            log_total,
            middle,
            normed2,
            gate_pre,
            up_pre,
            hidden,
            attn_set,
            mlp_set,
        )

    first_sets = fetch_weights()
    first_pass = forward(first_sets[0], first_sets[1], dealt_tok)
    again_tok = lax.all_to_all(
        token_pieces, "ctx", split_axis=0, concat_axis=0, tiled=True
    ).reshape(local_rows, MODEL_WIDTH)
    second_sets = fetch_weights()
    kept_pass = forward(second_sets[0], second_sets[1], again_tok)
    (
        unused,
        residual,
        normalized_input,
        query_prenorm,
        key_prenorm,
        value_narrow,
        q_heads,
        key_narrow,
        attention_mixed,
        mixed_low,
        log_total,
        middle,
        normed2,
        gate_pre,
        up_pre,
        hidden,
        attn_set,
        mlp_set,
    ) = kept_pass
    a_gain, qn_gain, kn_gain, proj_q, proj_k, proj_v, proj_o = attn_set
    m_gain, proj_gate, proj_up, proj_down = mlp_set
    grad_low = out_cotangent[0]
    grad_out = grad_low.astype(jnp.float32)
    d_hidden = dot_trans(grad_low, proj_down)
    down_grad = lax.psum_scatter(
        outer_rows(hidden, grad_low).astype(jnp.bfloat16), "fsdp", scatter_dimension=0, tiled=True
    )
    unused, swiglu_back = jax.vjp(
        lambda gate_in, up_in: jax.nn.silu(gate_in) * up_in, gate_pre, up_pre
    )
    d_gate, d_up = swiglu_back(d_hidden)
    d_gate_low = d_gate.astype(jnp.bfloat16)
    d_up_low = d_up.astype(jnp.bfloat16)
    d_normed2 = dot_trans(d_gate_low, proj_gate) + dot_trans(d_up_low, proj_up)
    both_low = jnp.concatenate([d_gate_low, d_up_low], axis=1)
    gate_up_grad = lax.psum_scatter(
        outer_rows(normed2, both_low).astype(jnp.bfloat16), "fsdp", scatter_dimension=0, tiled=True
    )
    unused, norm2_back = jax.vjp(root_mean_norm, middle, m_gain.astype(jnp.float32))
    d_middle_norm, d_m_gain = norm2_back(d_normed2)
    d_middle = grad_out + d_middle_norm
    middle_low = d_middle.astype(jnp.bfloat16)
    mixed_gradient = dot_trans(middle_low, proj_o).astype(jnp.bfloat16)
    out_proj_grad = lax.psum_scatter(
        outer_rows(mixed_low, middle_low).astype(jnp.bfloat16),
        "fsdp",
        scatter_dimension=0,
        tiled=True,
    )
    heads_gradient = mixed_gradient.reshape(local_rows, KEY_VALUE_HEADS, group_width, HEAD_SIZE)
    delta_rows = jnp.sum(
        heads_gradient.astype(jnp.float32)
        * attention_mixed.reshape(local_rows, KEY_VALUE_HEADS, group_width, HEAD_SIZE),
        axis=-1,
    )
    delta_t = jnp.transpose(delta_rows, (1, 2, 0))
    local_keys = key_narrow.reshape(local_rows, KEY_VALUE_HEADS, HEAD_SIZE)
    local_values = value_narrow.reshape(local_rows, KEY_VALUE_HEADS, HEAD_SIZE)

    def query_block(state_now, shard_piece, start_row):
        key_segment, value_segment = shard_piece
        local_row_count = key_segment.shape[0]
        allowed = key_mask(start_row, local_row_count)
        key_row_block = key_segment.reshape(local_row_count, KEY_VALUE_HEADS, HEAD_SIZE)
        scores = (
            jnp.einsum("rkgh,ckh->kgrc", q_heads, key_row_block, preferred_element_type=jnp.float32)
            * score_scale
        )
        probability = jnp.where(allowed, jnp.exp(scores - log_total[..., None]), 0.0)
        d_probs = jnp.einsum(
            "rkgh,ckh->kgrc",
            heads_gradient,
            value_segment.reshape(local_row_count, KEY_VALUE_HEADS, HEAD_SIZE),
            preferred_element_type=jnp.float32,
        )
        d_scores = (probability * (d_probs - delta_t[..., None])).astype(jnp.bfloat16)
        return (
            state_now
            + jnp.einsum(
                "kgrc,ckh->kgrh", d_scores, key_row_block, preferred_element_type=jnp.float32
            )
            * score_scale
        )

    query_grad = over_blocks(
        jnp.zeros((KEY_VALUE_HEADS, group_width, local_rows, HEAD_SIZE), jnp.float32),
        (
            lax.all_gather(key_narrow, "ctx", axis=0, tiled=True),
            lax.all_gather(value_narrow, "ctx", axis=0, tiled=True),
        ),
        local_rows,
        query_block,
    )
    lse_rows = jnp.transpose(log_total, (2, 0, 1)).reshape(local_rows, QUERY_HEADS)
    delta_send = delta_rows.reshape(local_rows, QUERY_HEADS)

    def key_block(state_now, shard_piece, start_row):
        query_segment, output_gradient_segment, logsumexp_segment, delta_segment = shard_piece
        local_row_count = query_segment.shape[0]
        allowed = query_mask(start_row, local_row_count)
        key_grad, value_gradient = state_now
        query_matrix = query_segment.reshape(
            local_row_count, KEY_VALUE_HEADS, group_width, HEAD_SIZE
        )
        gradient_rows = output_gradient_segment.reshape(
            local_row_count, KEY_VALUE_HEADS, group_width, HEAD_SIZE
        )
        scores = (
            jnp.einsum(
                "ckgh,rkh->kgcr", query_matrix, local_keys, preferred_element_type=jnp.float32
            )
            * score_scale
        )
        logsumexp_portion = jnp.transpose(
            logsumexp_segment.reshape(local_row_count, KEY_VALUE_HEADS, group_width), (1, 2, 0)
        )
        delta_portion = jnp.transpose(
            delta_segment.reshape(local_row_count, KEY_VALUE_HEADS, group_width), (1, 2, 0)
        )
        probability = jnp.where(allowed, jnp.exp(scores - logsumexp_portion[..., None]), 0.0)
        value_gradient = value_gradient + jnp.einsum(
            "kgcr,ckgh->rkh",
            probability.astype(jnp.bfloat16),
            gradient_rows,
            preferred_element_type=jnp.float32,
        )
        d_probs = jnp.einsum(
            "ckgh,rkh->kgcr", gradient_rows, local_values, preferred_element_type=jnp.float32
        )
        d_scores = (probability * (d_probs - delta_portion[..., None])).astype(jnp.bfloat16)
        key_grad = (
            key_grad
            + jnp.einsum(
                "kgcr,ckgh->rkh", d_scores, query_matrix, preferred_element_type=jnp.float32
            )
            * score_scale
        )
        return (key_grad, value_gradient)

    key_grad, value_gradient = over_blocks(
        (
            jnp.zeros((local_rows, KEY_VALUE_HEADS, HEAD_SIZE), jnp.float32),
            jnp.zeros((local_rows, KEY_VALUE_HEADS, HEAD_SIZE), jnp.float32),
        ),
        (
            lax.all_gather(
                q_heads.reshape(local_rows, QUERY_HEADS * HEAD_SIZE), "ctx", axis=0, tiled=True
            ),
            lax.all_gather(mixed_gradient, "ctx", axis=0, tiled=True),
            lax.all_gather(lse_rows.astype(jnp.bfloat16), "ctx", axis=0, tiled=True).astype(
                jnp.float32
            ),
            lax.all_gather(delta_send.astype(jnp.bfloat16), "ctx", axis=0, tiled=True).astype(
                jnp.float32
            ),
        ),
        local_rows,
        key_block,
    )
    query_rows = jnp.transpose(query_grad, (2, 0, 1, 3)).reshape(local_rows, QUERY_HEADS, HEAD_SIZE)
    unused, q_back = jax.vjp(
        lambda head_in, gain_in: rotary_embedding(root_mean_norm(head_in, gain_in), token_position),
        query_prenorm,
        qn_gain.astype(jnp.float32),
    )
    d_q_pre, d_qn_gain = q_back(query_rows)
    unused, k_back = jax.vjp(
        lambda head_in, gain_in: rotary_embedding(root_mean_norm(head_in, gain_in), token_position),
        key_prenorm,
        kn_gain.astype(jnp.float32),
    )
    key_prenorm_gradient, d_kn_gain = k_back(key_grad)
    dq_low = d_q_pre.reshape(local_rows, QUERY_HEADS * HEAD_SIZE).astype(jnp.bfloat16)
    key_gradient_narrow = key_prenorm_gradient.reshape(
        local_rows, KEY_VALUE_HEADS * HEAD_SIZE
    ).astype(jnp.bfloat16)
    value_gradient_narrow = value_gradient.reshape(local_rows, KEY_VALUE_HEADS * HEAD_SIZE).astype(
        jnp.bfloat16
    )
    d_normed = (
        dot_trans(dq_low, proj_q)
        + dot_trans(key_gradient_narrow, proj_k)
        + dot_trans(value_gradient_narrow, proj_v)
    )
    qkv_low = jnp.concatenate([dq_low, key_gradient_narrow, value_gradient_narrow], axis=1)
    qkv_grad = lax.psum_scatter(
        outer_rows(normalized_input, qkv_low).astype(jnp.bfloat16),
        "fsdp",
        scatter_dimension=0,
        tiled=True,
    )
    unused, norm1_back = jax.vjp(root_mean_norm, residual, a_gain.astype(jnp.float32))
    d_resid_norm, d_a_gain = norm1_back(d_normed)
    input_dealt = d_middle + d_resid_norm
    back_pieces = lax.all_to_all(
        input_dealt.reshape(piece_count, piece_rows, MODEL_WIDTH).astype(jnp.bfloat16),
        "ctx",
        split_axis=0,
        concat_axis=0,
        tiled=True,
    ).astype(jnp.float32)
    input_grad = jnp.take(back_pieces, own_plan, axis=0).reshape(local_rows, MODEL_WIDTH)
    gain_parts = (
        lax.psum_scatter(d_a_gain, "fsdp", scatter_dimension=0, tiled=True),
        lax.psum_scatter(d_qn_gain, "fsdp", scatter_dimension=0, tiled=True),
        lax.psum_scatter(d_kn_gain, "fsdp", scatter_dimension=0, tiled=True),
        lax.psum_scatter(d_m_gain, "fsdp", scatter_dimension=0, tiled=True),
    )
    totals = (
        lax.psum(gain_parts[0].astype(jnp.bfloat16), "ctx").astype(jnp.float32),
        lax.psum(gain_parts[1].astype(jnp.bfloat16), "ctx").astype(jnp.float32),
        lax.psum(gain_parts[2].astype(jnp.bfloat16), "ctx").astype(jnp.float32),
        lax.psum(gain_parts[3].astype(jnp.bfloat16), "ctx").astype(jnp.float32),
        lax.psum(qkv_grad, "ctx").astype(jnp.float32),
        lax.psum(out_proj_grad, "ctx").astype(jnp.float32),
        lax.psum(gate_up_grad, "ctx").astype(jnp.float32),
        lax.psum(down_grad, "ctx").astype(jnp.float32),
    )
    q_width = QUERY_HEADS * HEAD_SIZE
    key_value_width = KEY_VALUE_HEADS * HEAD_SIZE
    qkv_total = totals[4]
    gate_up_total = totals[6]
    ff_width = w_gate.shape[1]
    return (
        first_pass[0].astype(jnp.bfloat16)[None],
        input_grad[None],
        totals[0],
        totals[1],
        totals[2],
        totals[3],
        qkv_total[:, :q_width],
        qkv_total[:, q_width : q_width + key_value_width],
        qkv_total[:, q_width + key_value_width :],
        totals[5],
        gate_up_total[:, :ff_width],
        gate_up_total[:, ff_width:],
        totals[7],
    )


CTX = ("z", "y")
FSDP = ("x", "core")
VMEM_BYTES = 62 << 20


def norm_back(values, gain_vec, grad):
    scale = lax.rsqrt(jnp.mean(values * values, axis=-1, keepdims=True) + eps)
    inner = gain_vec * grad
    d_values = scale * inner - values * (scale * scale * scale) * jnp.mean(
        values * inner, axis=-1, keepdims=True
    )
    return d_values, grad * values * scale


def half_turn(values):
    half = values.shape[-1] // 2
    return jnp.concatenate([-values[..., half:], values[..., :half]], axis=-1)


def rope_tables(token_position):
    half = HEAD_SIZE // 2
    frequency = theta_base ** (-(jnp.arange(half, dtype=jnp.float32) * 2.0) / HEAD_SIZE)
    angles = token_position.astype(jnp.float32)[:, None] * frequency[None, :]
    cosine, sine = jnp.cos(angles), jnp.sin(angles)
    return jnp.concatenate([cosine, cosine], axis=1), jnp.concatenate([sine, sine], axis=1)


def dot(a, b):
    return jnp.dot(a, b, preferred_element_type=jnp.float32)


def low(a):
    return a.astype(jnp.bfloat16)


def gather_fsdp_plain(block):
    return lax.all_gather(block, FSDP, axis=0, tiled=True)


def over(block, axis):
    return lax.ppermute(block, axis, [(0, 1), (1, 0)])


def half_sum(block, axis):
    place = lax.axis_index(axis)
    got = over(lax.dynamic_index_in_dim(block, 1 - place, 0, keepdims=False), axis)
    own = lax.dynamic_index_in_dim(block, place, 0, keepdims=False)
    return low(own.astype(jnp.float32) + got.astype(jnp.float32))


MESH_ID = pl.DeviceIdType.MESH
LINE = 4


class Net:
    def __init__(self, send, recv):
        self.send, self.recv, self.used = send, recv, 0
        self.z, self.y, self.x, self.core = (lax.axis_index(a) for a in CTX + FSDP)
        self.me = 2 * self.z + self.y
        self.open = []

    def at(self, dz=0, dy=0, dx=0, dc=0):
        return (
            self.z + dz,
            1 - self.y if dy else self.y,
            1 - self.x if dx else self.x,
            1 - self.core if dc else self.core,
        )

    def put(self, src, dst, target, sends=None, recvs=None):
        copy = Copy(self, src, dst, target, sends, recvs)
        self.open.append(copy)
        return copy

    def close(self):
        for copy in self.open:
            copy.arrived()
        for copy in self.open:
            copy.left()


def guarded(condition, action):
    if condition is None:
        action()
    else:
        pl.when(condition)(action)


class Copy:
    def __init__(self, net, src, dst, target, sends, recvs):
        i = net.used
        net.used += 1
        self.sends, self.recvs, self.waited = sends, recvs, False
        self.copy = pltpu.make_async_remote_copy(
            src, dst, net.send.at[i], net.recv.at[i], device_id=target, device_id_type=MESH_ID
        )
        guarded(sends, self.copy.start)

    def arrived(self):
        if not self.waited:
            self.waited = True
            guarded(self.recvs, self.copy.wait_recv)

    def left(self):
        guarded(self.sends, self.copy.wait_send)


class Local:
    def __init__(self, copy):
        self.copy, self.waited = copy, False
        copy.start()

    def arrived(self):
        if not self.waited:
            self.waited = True
            self.copy.wait()

    wait = arrived


def greet(net, kinds):
    barrier = pltpu.get_barrier_semaphore()
    partners = []
    if "z" in kinds:
        partners += [(net.at(dz=1), net.z < LINE - 1), (net.at(dz=-1), net.z > 0)]
    if "y" in kinds:
        partners.append((net.at(dy=1), None))
    if "x" in kinds:
        partners.append((net.at(dx=1), None))
    if "core" in kinds:
        partners.append((net.at(dc=1), None))
    if "far" in kinds:
        partners.append((net.at(dx=1, dc=1), None))
    if "ctx" in kinds:
        for k in range(1, 2 * LINE):
            other = lax.rem(net.me + k, 2 * LINE)
            partners.append(((other // 2, lax.rem(other, 2), net.x, net.core), None))
    for target, there in partners:
        guarded(
            there,
            lambda target=target: pl.semaphore_signal(
                barrier, inc=1, device_id=target, device_id_type=MESH_ID
            ),
        )
    ends = 0
    if "z" in kinds:
        ends = (net.z == 0).astype(jnp.int32) + (net.z == LINE - 1).astype(jnp.int32)
    pl.semaphore_wait(barrier, len(partners) - ends)


def drive(*programs):
    live = list(programs)
    while live:
        for program in list(live):
            if next(program, "end") == "end":
                live.remove(program)


def in_order(order, programs):
    for i in order:
        next(programs[i], None)
    for program in programs:
        for _ in program:
            pass


def by_steps(program):
    yield next(program)
    while next(program, "end") != "end":
        if next(program, "end") == "end":
            return
        yield


def along_line(net, own, view, slot, log=None):
    z = net.z
    up = net.put(own, view(slot(z)), net.at(dz=1), z < LINE - 1, z > 0)
    down = net.put(own, view(slot(z)), net.at(dz=-1), z > 0, z < LINE - 1)
    yield
    for s in range(1, LINE):
        from_low, from_high = z >= s, z + s <= LINE - 1
        up.arrived()
        low_block, high_block = view(slot(z - s)), view(slot(z + s))
        if s < LINE - 1:
            up = net.put(low_block, low_block, net.at(dz=1), from_low & (z < LINE - 1), z >= s + 1)
        if log is not None:
            log[s].append(net.put(low_block, low_block, net.at(dy=1), from_low, from_low))
        yield
        down.arrived()
        if s < LINE - 1:
            down = net.put(
                high_block, high_block, net.at(dz=-1), from_high & (z > 0), z + s + 1 <= LINE - 1
            )
        if log is not None:
            log[s].append(net.put(high_block, high_block, net.at(dy=1), from_high, from_high))
        yield


def gather_line_first(net, own, view, log=None):
    log = {s: [] for s in range(LINE)} if log is None else log
    log[0].append(net.put(own, view(net.me), net.at(dy=1)))
    yield from along_line(net, own, view, lambda z: 2 * z + net.y, log)


def gather_side_first(net, own, view):
    side = net.put(own, view(net.me), net.at(dy=1))
    first = along_line(net, own, view, lambda z: 2 * z + net.y)
    yield next(first)
    side.arrived()
    other = view(net.me + 1 - 2 * net.y)
    second = along_line(net, other, view, lambda z: 2 * z + 1 - net.y)
    for _ in second:
        next(first, None)
        yield


def gather_ctx_programs(net, own, out, cut):
    rows = own.shape[0]
    programs = [
        gather_line_first(
            net, own.at[pl.ds(0, cut)], lambda slot: out.at[slot, pl.ds(0, cut)]
        )
    ]
    if cut < rows:
        rest = pl.ds(cut, rows - cut)
        programs.append(gather_side_first(net, own.at[rest], lambda slot: out.at[slot, rest]))
    return programs


def gather_fsdp(net, own, out):
    f = 2 * net.x + net.core
    net.put(own, out.at[f], net.at(dc=1))
    over = net.put(own, out.at[f], net.at(dx=1))
    yield
    yield
    yield
    over.arrived()
    far = out.at[2 * (1 - net.x) + net.core]
    net.put(far, far, net.at(dc=1))
    yield


def gather_quad(net, own, out):
    q = 2 * net.y + net.core
    net.put(own, out.at[q], net.at(dc=1))
    over = net.put(own, out.at[q], net.at(dy=1))
    yield
    over.arrived()
    far = out.at[2 * (1 - net.y) + net.core]
    net.put(far, far, net.at(dc=1))
    yield


def swap_ctx(net, blocks, out):
    for k in range(1, 2 * LINE):
        other = lax.rem(net.me + k, 2 * LINE)
        net.put(
            blocks.at[other], out.at[net.me], (other // 2, lax.rem(other, 2), net.x, net.core)
        )
    yield


def own_copies(pairs, sem):
    copies = [pltpu.make_async_copy(src, dst, sem.at[i]) for i, (src, dst) in enumerate(pairs)]
    for copy in copies:
        copy.start()
    return copies


def net_call(body, outs, args, copies, locals_, number, scratch=(), vmem=(), smem=()):
    def kernel(*refs):
        *rest, send, recv, local = refs
        net = Net(send, recv)
        body(net, local, *rest)
        assert net.used <= copies, net.used

    any_space = pl.BlockSpec(memory_space=pl.ANY)
    in_vmem = pl.BlockSpec(memory_space=pltpu.VMEM)
    in_smem = pl.BlockSpec(memory_space=pltpu.SMEM)
    count = len(args)

    def place(i):
        return in_vmem if i in vmem else in_smem if i in smem else any_space

    return pl.pallas_call(
        kernel,
        out_shape=outs,
        in_specs=[place(i) for i in range(count)],
        out_specs=[place(count + i) for i in range(len(outs))],
        scratch_shapes=list(scratch)
        + [
            pltpu.SemaphoreType.DMA((copies,)),
            pltpu.SemaphoreType.DMA((copies,)),
            pltpu.SemaphoreType.DMA((max(1, locals_),)),
        ],
        compiler_params=pltpu.CompilerParams(
            collective_id=number, has_side_effects=True, vmem_limit_bytes=VMEM_BYTES
        ),
    )(*args)


def shape_of(*dims, kind=jnp.bfloat16):
    return jax.ShapeDtypeStruct(dims, kind)


def sum_line(net, held, send_up, send_down, got_up, got_down, ready):
    z = net.z
    ups, downs = [], []

    def fill(send, got, block, t, first):
        def alone():
            send[t] = low(held[block])

        def added():
            send[t] = low(held[block] + got[t - 1].astype(jnp.float32))

        return alone if first else added

    for t in range(LINE - 1):
        if t:
            ups[t - 1].arrived()
        ready(t)
        to_up, to_down = LINE - 1 - t + z, z - LINE + 1 + t
        up_on, down_on = (z <= t) & (z < LINE - 1), (z >= LINE - 1 - t) & (z > 0)
        pl.when(z == 0)(fill(send_up, got_up, to_up, t, True))
        if t:
            pl.when(up_on & (z >= 1))(fill(send_up, got_up, to_up, t, False))
        ups.append(
            net.put(
                send_up.at[t], got_up.at[t], net.at(dz=1), up_on, (z >= 1) & (z - 1 <= t)
            )
        )
        yield
        if t:
            downs[t - 1].arrived()
        pl.when(z == LINE - 1)(fill(send_down, got_down, to_down, t, True))
        if t:
            pl.when(down_on & (z <= LINE - 2))(fill(send_down, got_down, to_down, t, False))
        downs.append(
            net.put(
                send_down.at[t],
                got_down.at[t],
                net.at(dz=-1),
                down_on,
                (z <= LINE - 2) & (z + 1 >= LINE - 1 - t),
            )
        )
        yield
    last = LINE - 2

    def add_up():
        held[z] += got_up[last].astype(jnp.float32)

    def add_down():
        held[z] += got_down[last].astype(jnp.float32)

    ups[last].arrived()
    ready(LINE - 1)
    pl.when(z >= 1)(add_up)
    yield
    downs[last].arrived()
    pl.when(z <= LINE - 2)(add_down)


def far_first(z):
    return [
        jnp.where(z < 2, 3, 0),
        jnp.where(z < 2, 2, 1),
        z + 1 - 2 * lax.rem(z, 2),
        z,
    ]


def line_scratch(rows, cols):
    line = pltpu.VMEM((LINE - 1, rows, cols), jnp.bfloat16)
    return [pltpu.VMEM((LINE, rows, cols), jnp.float32), line, line, line, line]


def sum_sides(net, src, from_side, line, make=None):
    z, y = net.z, net.y
    held = line[0]
    order = far_first(z)
    sides = []
    for k in order:
        if make is not None:
            make(2 * k + 1 - y)
        sides.append(net.put(src.at[2 * k + 1 - y], from_side.at[k], net.at(dy=1)))
        if make is not None and len(sides) == 2:
            yield
    yield

    def ready(t):
        k = order[t]
        if make is not None:
            make(2 * k + y)
        sides[t].arrived()
        held[k] = src[2 * k + y].astype(jnp.float32) + from_side[k].astype(jnp.float32)

    yield from sum_line(net, *line, ready)


BLOCK = 256
BACK_ORDER = (
    7, 3, 1, 0, 0, 4, 5, 5, 2, 3, 3, 2, 7, 7, 7, 7, 7, 7, 0, 0, 7, 7, 7, 7, 3, 3, 1, 1, 0, 0,
    3, 3, 7, 7, 1, 1, 4, 4, 6, 0, 3, 3, 6, 0, 7, 7, 0, 2, 1, 1, 4, 6, 3, 3, 4, 7, 7, 2, 2, 0,
    0, 1, 1, 1, 3, 3, 4, 6, 6, 4, 3, 7, 7, 7, 7, 3, 3, 2, 2, 8, 0, 0, 8, 1, 1, 4, 0, 0, 0, 6,
    6, 4, 2, 2, 1, 1, 1, 6, 6, 6, 4, 4, 2, 2, 8, 8, 1, 1, 1, 4, 4, 2, 2, 4, 4, 2, 2, 4, 2, 2,
    2,
)


def turn_lanes(v):
    return pltpu.roll(v, HEAD_SIZE // 2, 1)


def dot_last(a, b):
    return lax.dot_general(a, b, (((1,), (1,)), ((), ())), preferred_element_type=jnp.float32)


def resting(rounds):
    for _ in range(rounds):
        yield


class Bag:
    def __init__(self, **members):
        self.__dict__.update(members)


def bags(tree):
    if isinstance(tree, list):
        return [bags(v) for v in tree]
    return Bag(**{n: bags(v) for n, v in tree.items()}) if isinstance(tree, dict) else tree


def near_first(z):
    return far_first(z)[::-1]


def kernel_with(
    body, moved, loaded, outs, scratch, copies, number, in_vmem=(), near=(), scalar=()
):
    scratch = dict(
        scratch, held={n: pltpu.VMEM(v.shape, v.dtype) for n, v in loaded.items()}
    )
    flat, tree = jax.tree.flatten(scratch)
    f_in, in_tree = jax.tree.flatten((moved, loaded))
    f_out, out_tree = jax.tree.flatten(outs)

    def whole(net, local, *refs):
        given, to_load = jax.tree.unflatten(in_tree, refs[: len(f_in)])
        out = Bag(**jax.tree.unflatten(out_tree, refs[len(f_in) : len(f_in) + len(f_out)]))
        r = bags(jax.tree.unflatten(tree, refs[len(f_in) + len(f_out) :]))
        used = iter(range(96))

        def fetch(src, dst):
            return Local(pltpu.make_async_copy(src, dst, local.at[next(used)]))

        def load():
            return {n: fetch(to_load[n], getattr(r.held, n)) for n in to_load}

        body(net, fetch, load, Bag(**given), out, r)
        net.close()

    order = jax.tree.unflatten(out_tree, range(len(f_out)))
    in_order, _ = jax.tree.unflatten(in_tree, range(len(f_in)))
    result = net_call(
        whole,
        f_out,
        f_in,
        copies,
        96,
        number,
        scratch=flat,
        vmem=[len(f_in) + order.get(n) for n in in_vmem] + [in_order.get(n) for n in near],
        smem=[in_order.get(n) for n in scalar],
    )
    return Bag(**jax.tree.unflatten(out_tree, result))


def middle(net, fetch, arriving, out, r):
    y, x, core = net.y, net.x, net.core
    slots, rows, width = r.mixed_in.shape
    _, shard, wide = r.w_gu.shape
    ff, d = wide // 2, r.residual.shape[1]
    piece, pad = rows // slots, 32
    f32, bf = jnp.float32, jnp.bfloat16

    def land(copies):
        for c in copies:
            c.arrived()

    land(arriving.o)
    total = r.residual[...].astype(f32)
    for i in range(slots):
        total = total + dot(r.mixed_in[i], r.w_o[i // 2, pl.ds(i % 2 * width, width)])
    r.middle[...] = total
    own = 2 * y + core
    r.quad[own] = low(root_mean_norm(total, r.m_gain[...]))
    net.put(r.quad.at[own], r.quad.at[own], net.at(dc=1))
    near = net.open[-1]
    net.put(r.quad.at[own], r.quad.at[own], net.at(dy=1))
    over = net.open[-1]
    near.arrived()
    land(arriving.gu)
    land(arriving.grad)

    def forward(side):
        n2 = r.quad[pl.ds(2 * side, 2)].reshape(2 * rows, d)
        g = r.grad[pl.ds(2 * side, 2)].reshape(2 * rows, d)
        w_gu = r.w_gu[...].reshape(4 * shard, 2 * ff)
        gate_up = dot(n2, w_gu)
        return g, gate_up[:, :ff], gate_up[:, ff:]

    def backward(side, g, gate, up):
        w_dn = r.w_dn[...].reshape(ff, d)
        d_hidden = dot_last(g, w_dn)
        sig = 1.0 / (1.0 + jnp.exp(-gate))
        silu = gate * sig
        r.hidden[side] = low(silu * up)
        r.d_gu[side, :, pl.ds(0, ff)] = low(d_hidden * up * (sig * (1.0 + gate * (1.0 - sig))))
        r.d_gu[side, :, pl.ds(ff, ff)] = low(d_hidden * silu)

    def part(side):
        w_gu = r.w_gu[...].reshape(4 * shard, 2 * ff)
        return dot_last(r.d_gu[side], w_gu).reshape(2, rows, d)

    def out_part(side):
        return dot(r.hidden[side], r.w_dn[...].reshape(ff, d)).reshape(2, rows, d)

    near_values = forward(y)
    over.arrived()
    far = 2 * (1 - y) + core
    net.put(r.quad.at[far], r.quad.at[far], net.at(dc=1))
    last = net.open[-1]
    land(arriving.dn)
    backward(y, *near_values)
    last.arrived()
    backward(1 - y, *forward(1 - y))
    r.far_part[...] = low(part(1 - y))
    one = net.put(r.far_part.at[1 - core], r.got.at[0], net.at(dc=1))
    r.near_part[...] = part(y)
    r.beside[...] = low(r.near_part[1 - core])
    two = net.put(r.beside, r.got.at[1], net.at(dc=1))
    one.arrived()
    r.to_side[0] = low(r.far_part[core].astype(f32) + r.got[0].astype(f32))
    side = net.put(r.to_side.at[0], r.got.at[2], net.at(dy=1))
    r.far_out[...] = low(out_part(1 - y))
    one_out = net.put(r.far_out.at[1 - core], r.got.at[3], net.at(dc=1))
    r.near_out[...] = out_part(y)
    r.beside_out[...] = low(r.near_out[1 - core])
    two_out = net.put(r.beside_out, r.got.at[4], net.at(dc=1))
    n2 = r.quad[...].reshape(4 * rows, d)
    g = r.grad[...].reshape(4 * rows, d)
    d_gu = r.d_gu[...].reshape(4 * rows, 2 * ff)
    r.g_gate[...] = low(outer_rows(n2, d_gu[:, :ff])).reshape(4, shard, ff)
    gate_over = [
        net.put(r.g_gate.at[2 * (1 - x) + c], r.gate_got.at[c], net.at(dx=1))
        for c in range(2)
    ]
    one_out.arrived()
    r.to_side[1] = low(r.far_out[core].astype(f32) + r.got[3].astype(f32))
    side_out = net.put(r.to_side.at[1], r.got.at[5], net.at(dy=1))
    r.g_up[...] = low(outer_rows(n2, d_gu[:, ff:]))
    sent = [fetch(r.g_up, out.up)]
    r.g_dn[...] = low(outer_rows(r.hidden[...].reshape(4 * rows, ff), g))
    sent.append(fetch(r.g_dn, out.down))
    two.arrived()
    side.arrived()
    d_normed = (
        r.near_part[core] + r.got[1].astype(f32) + r.got[2].astype(f32)
    )
    dx2, dg2 = norm_back(r.middle[...], r.m_gain[...], d_normed)
    out.dg2[...] = jnp.sum(dg2, axis=0, keepdims=True)
    middle_low = low(r.grad[own].astype(f32) + dx2)
    for i in range(slots):
        r.dm[i] = low(dot_last(middle_low, r.w_o[i // 2, pl.ds(i % 2 * width, width)]))
    sent.append(fetch(r.dm, out.dm))
    for i in range(slots):
        out.back[i, pl.ds(0, piece)] = middle_low[i * piece : (i + 1) * piece]
        out.back[i, pl.ds(piece, pad - piece)] = jnp.zeros((pad - piece, d), bf)
    out.middle_low[...] = middle_low
    two_out.arrived()
    side_out.arrived()
    out.output[...] = low(
        r.middle[...]
        + r.near_out[core]
        + r.got[4].astype(f32)
        + r.got[5].astype(f32)
    )
    for c in range(2):
        gate_over[c].arrived()
        out.gate[c] = low(r.g_gate[2 * x + c].astype(f32) + r.gate_got[c].astype(f32))
    for c in sent:
        c.wait()


def front_kernel(moved, loaded, number):
    a = Bag(**moved)
    _, rows, d = a.tok.shape
    slots = 2 * LINE
    count = rows * slots
    blocks = count // BLOCK
    width = 2 * HEAD_SIZE
    shard = a.w_q.shape[0]
    half = a.w_gate.shape[1] // 8
    o_rows = a.w_o.shape[0]
    scale = HEAD_SIZE**-0.5
    bf, f32 = jnp.bfloat16, jnp.float32
    piece = rows // slots
    ff = 2 * half
    gain_cols = 2 * a.attn_gain.shape[0] + 2 * HEAD_SIZE

    scratch = dict(
        tok=pltpu.VMEM((slots, rows, d), bf),
        w_qkv=pltpu.VMEM((4, shard, 2 * width), bf),
        gains=pltpu.VMEM((4, 1, gain_cols), f32),
        columns=pltpu.VMEM((count, 8), f32),
        normed=pltpu.VMEM((count, d), bf),
        qkv=pltpu.VMEM((count, 2 * width), f32),
        q=pltpu.VMEM((count, width), bf),
        k=pltpu.VMEM((count, HEAD_SIZE), bf),
        v=pltpu.VMEM((count, HEAD_SIZE), bf),
        kt=pltpu.VMEM((HEAD_SIZE, count), bf),
        vt=pltpu.VMEM((HEAD_SIZE, count), bf),
        cos=pltpu.VMEM((count, HEAD_SIZE), f32),
        sin=pltpu.VMEM((count, HEAD_SIZE), f32),
        mixed=pltpu.VMEM((count, width), f32),
        mixed_low=pltpu.VMEM((count, width), bf),
        sent=pltpu.VMEM((slots, rows, width), bf),
        w_o=pltpu.VMEM((4, o_rows, d), bf),
        w_gu=pltpu.VMEM((4, shard, 4 * half), bf),
        grad=pltpu.VMEM((4, rows, d), bf),
        mixed_in=pltpu.VMEM((slots, rows, width), bf),
        residual=pltpu.VMEM((rows, d), bf),
        m_gain=pltpu.VMEM((1, d), f32),
        w_dn=pltpu.VMEM((2, half, d), bf),
        middle=pltpu.VMEM((rows, d), f32),
        quad=pltpu.VMEM((4, rows, d), bf),
        hidden=pltpu.VMEM((2, 2 * rows, ff), bf),
        d_gu=pltpu.VMEM((2, 2 * rows, 2 * ff), bf),
        near_part=pltpu.VMEM((2, rows, d), f32),
        far_part=pltpu.VMEM((2, rows, d), bf),
        near_out=pltpu.VMEM((2, rows, d), f32),
        far_out=pltpu.VMEM((2, rows, d), bf),
        beside=pltpu.VMEM((rows, d), bf),
        beside_out=pltpu.VMEM((rows, d), bf),
        got=pltpu.VMEM((6, rows, d), bf),
        to_side=pltpu.VMEM((2, rows, d), bf),
        g_gate=pltpu.VMEM((4, shard, ff), bf),
        gate_got=pltpu.VMEM((2, shard, ff), bf),
        g_up=pltpu.VMEM((d, ff), bf),
        g_dn=pltpu.VMEM((ff, d), bf),
        dm=pltpu.VMEM((slots, rows, width), bf),
    )
    outs = dict(
        first=shape_of(1, count, kind=jnp.int32),
        dealt=shape_of(1, count, kind=jnp.int32),
        back_from=shape_of(rows, 1, kind=jnp.int32),
        mixed_in=shape_of(slots, rows, width),
        normed=shape_of(count, d),
        qkv=shape_of(count, 2 * width, kind=f32),
        q=shape_of(count, width),
        k=shape_of(count, HEAD_SIZE),
        v=shape_of(count, HEAD_SIZE),
        kt=shape_of(HEAD_SIZE, count),
        cos=shape_of(count, HEAD_SIZE, kind=f32),
        sin=shape_of(count, HEAD_SIZE, kind=f32),
        mixed=shape_of(count, width, kind=f32),
        lse=shape_of(2, 1, count, kind=f32),
        w_qkv=shape_of(4, shard, 2 * width),
        a_gain=shape_of(1, d, kind=f32),
        q_gain=shape_of(1, HEAD_SIZE, kind=f32),
        k_gain=shape_of(1, HEAD_SIZE, kind=f32),
        output=shape_of(rows, d),
        back=shape_of(slots, 32, d),
        dm=shape_of(slots, rows, width),
        gate=shape_of(2, shard, ff),
        up=shape_of(d, ff),
        down=shape_of(ff, d),
        middle_low=shape_of(rows, d),
        dg2=shape_of(1, d, kind=f32),
    )

    def body(net, fetch, load, given, out, r):
        z, y, x, core, me = net.z, net.y, net.x, net.core, net.me
        f = 2 * x + core
        done = set()
        tok = given.tok.at[0]
        tok_own = fetch(tok, r.tok.at[me])

        def lanes(start, size):
            return pl.ds(pl.multiple_of(start, HEAD_SIZE), size)

        head_parts = [
            (given.w_q.at[:, lanes(me * width, width)], pl.ds(0, width)),
            (given.w_k.at[:, lanes(me * HEAD_SIZE, HEAD_SIZE)], pl.ds(width, HEAD_SIZE)),
            (
                given.w_v.at[:, lanes(me * HEAD_SIZE, HEAD_SIZE)],
                pl.ds(width + HEAD_SIZE, HEAD_SIZE),
            ),
        ]
        w_own = [fetch(src, r.w_qkv.at[f, :, to]) for src, to in head_parts]
        greet(net, ("ctx", "x", "core", "far"))
        log = {s: [] for s in range(LINE)}
        waits = list(w_own)
        zone = lax.broadcasted_iota(jnp.int32, (1, HEAD_SIZE), 1) // (HEAD_SIZE // 4) == f

        def zoned(ref):
            return jnp.where(zone, jnp.concatenate([ref[...].astype(f32)] * 4, axis=1), 0.0)

        r.gains[f] = jnp.concatenate(
            [
                given.attn_gain[...].astype(f32).reshape(1, -1),
                given.mlp_gain[...].astype(f32).reshape(1, -1),
                zoned(given.q_gain),
                zoned(given.k_gain),
            ],
            axis=1,
        )

        def head_weights():
            beside = [net.put(src, r.w_qkv.at[f, :, to], net.at(dc=1)) for src, to in head_parts]
            beside.append(net.put(r.gains.at[f], r.gains.at[f], net.at(dc=1)))
            across = [net.put(src, r.w_qkv.at[f, :, to], net.at(dx=1)) for src, to in head_parts]
            across.append(net.put(r.gains.at[f], r.gains.at[f], net.at(dx=1)))
            yield
            for c in across:
                c.arrived()
            far = 2 * (1 - x) + core
            beside += [
                net.put(r.w_qkv.at[far], r.w_qkv.at[far], net.at(dc=1)),
                net.put(r.gains.at[far], r.gains.at[far], net.at(dc=1)),
            ]
            for c in waits:
                c.wait()
            for c in beside:
                c.arrived()
            r.own = fetch(r.w_qkv, out.w_qkv)
            done.add("head")
            yield

        arriving = Bag(o=[], gu=[], dn=[], grad=[], heads=[])

        def other_weights():
            yield
            arriving.o += [
                fetch(given.w_o, r.w_o.at[f]),
                net.put(given.w_o, r.w_o.at[f], net.at(dx=1)),
                net.put(given.w_o, r.w_o.at[f], net.at(dc=1)),
            ]

            def quarter(c):
                return [
                    (
                        w.at[:, lanes((2 * xs + c) * 2 * half + y * half, half)],
                        r.w_gu.at[f, :, pl.ds((2 * i + xs) * half, half)],
                    )
                    for i, w in enumerate((given.w_gate, given.w_up))
                    for xs in range(2)
                ]

            arriving.gu += [fetch(src, to) for src, to in quarter(core)]
            arriving.gu += [net.put(src, to, net.at(dc=1)) for src, to in quarter(1 - core)]
            arriving.gu += [net.put(src, to, net.at(dx=1)) for src, to in quarter(core)]
            arriving.gu += [net.put(src, to, net.at(dx=1, dc=1)) for src, to in quarter(1 - core)]
            part = given.w_down.at[pl.ds(pl.multiple_of(y * half, half), half)]
            arriving.dn += [
                fetch(part, r.w_dn.at[x]),
                net.put(part, r.w_dn.at[x], net.at(dx=1)),
            ]
            yield from resting(7)
            arriving.o[1].arrived()
            far = r.w_o.at[2 * (1 - x) + core]
            arriving.o.append(net.put(far, far, net.at(dc=1)))

        def output_grad():
            yield from resting(5)
            own = r.grad.at[2 * y + core]
            grad = given.grad.at[0]
            arriving.grad += [
                fetch(grad, own),
                net.put(grad, own, net.at(dc=1)),
                net.put(grad, own, net.at(dy=1)),
            ]
            yield
            arriving.grad[2].arrived()
            far = r.grad.at[2 * (1 - y) + core]
            arriving.grad.append(net.put(far, far, net.at(dc=1)))

        def project(slot):
            at = pl.ds(pl.multiple_of(slot * rows, rows), rows)
            normed = low(root_mean_norm(r.tok[slot].astype(f32), out.a_gain[...]))
            r.normed[at] = normed
            qkv = dot(normed, r.w_qkv[...].reshape(4 * shard, 2 * width))
            r.qkv[at] = qkv
            cos, sin = r.cos[at], r.sin[at]

            def turned(part, gain):
                v = root_mean_norm(part, gain)
                return low(v * cos + turn_lanes(v) * sin)

            for g in range(2):
                cols = pl.ds(g * HEAD_SIZE, HEAD_SIZE)
                r.q[at, cols] = turned(
                    qkv[:, g * HEAD_SIZE : (g + 1) * HEAD_SIZE], out.q_gain[...]
                )
            r.k[at] = turned(qkv[:, width : width + HEAD_SIZE], out.k_gain[...])
            r.v[at] = low(qkv[:, width + HEAD_SIZE :])

        def main():
            ids = lax.broadcasted_iota(jnp.int32, (1, count), 1)
            first, dealt, back, start = jnp.zeros_like(ids), ids, ids, 0
            for i in range(1, given.lengths.shape[1]):
                start = start + given.lengths[0, i - 1]
                first = jnp.where(ids >= start, start, first)
            for s in range(slots):
                for j in range(slots):
                    begin = given.deal[0, s, j] * rows + s * piece
                    dealt = jnp.where(
                        (ids >= begin) & (ids < begin + piece),
                        ids - begin + (s * rows + j * piece),
                        dealt,
                    )
            for j in range(slots):
                begin = given.deal[0, me, j] * 32
                back = jnp.where(
                    (ids >= j * piece) & (ids < (j + 1) * piece), ids - j * piece + begin, back
                )
            out.first[...] = first
            out.dealt[...] = dealt
            row = lax.broadcasted_iota(jnp.int32, (8, count), 0)
            stack = jnp.where(row == 0, ids - first, jnp.where(row == 1, dealt, back))
            r.columns[...] = jnp.transpose(stack.astype(f32))
            out.back_from[...] = r.columns[pl.ds(0, rows), 2:3].astype(jnp.int32)
            for i in range(slots):
                at = pl.ds(i * rows, rows)
                angle = r.columns[at, 0:1] * given.freq[0:1]
                r.cos[at] = jnp.cos(angle)
                r.sin[at] = jnp.sin(angle) * given.freq[1:2]
            yield
            while "head" not in done:
                yield
            gains = [r.gains[i] for i in range(4)]
            part = d // 4
            for i in range(4):
                out.a_gain[:, pl.ds(i * part, part)] = gains[i][:, :part]
                r.m_gain[:, pl.ds(i * part, part)] = gains[i][:, part : 2 * part]
            total = gains[0] + gains[1] + gains[2] + gains[3]
            out.q_gain[...] = total[:, 2 * part : 2 * part + HEAD_SIZE]
            out.k_gain[...] = total[:, 2 * part + HEAD_SIZE :]
            tok_own.wait()
            near = near_first(z)
            for k in range(LINE):
                project(2 * near[k] + y)
                if k:
                    for c in log[k - 1]:
                        c.arrived()
                    project(2 * near[k - 1] + 1 - y)
                yield
            for c in log[LINE - 1]:
                c.arrived()
            project(2 * near[LINE - 1] + 1 - y)
            results = [
                fetch(r.normed, out.normed),
                fetch(r.qkv, out.qkv),
                fetch(r.q, out.q),
                fetch(r.k, out.k),
                fetch(r.v, out.v),
                fetch(r.cos, out.cos),
                fetch(r.sin, out.sin),
                r.own,
            ]
            for i in range(blocks):
                at = pl.ds(i * BLOCK, BLOCK)
                r.kt[:, at] = jnp.transpose(r.k[at])
                r.vt[:, at] = jnp.transpose(r.v[at])
            results.append(fetch(r.kt, out.kt))
            for i in range(blocks):
                here = pl.ds(i * BLOCK, BLOCK)
                first = out.first[:, here]
                t = i * BLOCK + lax.broadcasted_iota(jnp.int32, (BLOCK, BLOCK), 1)
                q = [r.q[here, pl.ds(g * HEAD_SIZE, HEAD_SIZE)] for g in range(2)]

                def step(n, held, i=i, q=q, first=first, t=t):
                    j = i - n
                    at = pl.ds(pl.multiple_of(j * BLOCK, BLOCK), BLOCK)
                    k, vt = r.k[at], r.vt[:, at]
                    u = j * BLOCK + lax.broadcasted_iota(jnp.int32, (BLOCK, BLOCK), 0)
                    allowed = (u >= first) & (u <= t)
                    result = []
                    for g in range(2):
                        top, total, mixed = held[g]
                        scores = jnp.where(allowed, dot_last(k, q[g]) * scale, negative_filler)
                        new = jnp.maximum(top, jnp.max(scores, axis=0, keepdims=True))
                        fade = jnp.exp(top - new)
                        p = jnp.exp(scores - new)
                        total = total * fade + jnp.sum(p, axis=0, keepdims=True)
                        result.append((new, total, mixed * fade + dot(vt, low(p))))
                    return tuple(result)

                row = jnp.full((1, BLOCK), negative_filler, f32)
                none = (row, jnp.zeros((1, BLOCK), f32), jnp.zeros((HEAD_SIZE, BLOCK), f32))
                held = lax.fori_loop(0, i + 1, step, (none, none))
                for g in range(2):
                    top, total, mixed = held[g]
                    cols = pl.ds(g * HEAD_SIZE, HEAD_SIZE)
                    out.lse[g, :, here] = top + jnp.log(total)
                    mixed = jnp.transpose(mixed / total)
                    r.mixed[here, cols] = mixed
                    r.mixed_low[here, cols] = low(mixed)
                yield
            results.append(fetch(r.mixed, out.mixed))
            ids = lax.broadcasted_iota(jnp.int32, (rows, count), 1)

            def hot(slot):
                at = pl.ds(pl.multiple_of(slot * rows, rows), rows)
                return low(jnp.where(r.columns[at, 1:2].astype(jnp.int32) == ids, 1.0, 0.0))

            for k in range(1, slots):
                other = lax.rem(me + k, slots)
                r.sent[other] = low(dot(hot(other), r.mixed_low[...]))
                there = (other // 2, lax.rem(other, 2), x, core)
                arriving.heads.append(net.put(r.sent.at[other], r.mixed_in.at[me], there))
            mine = hot(me)
            r.sent[me] = low(dot(mine, r.mixed_low[...]))
            arriving.heads.append(fetch(r.sent.at[me], r.mixed_in.at[me]))
            r.residual[...] = low(dot(mine, r.tok[...].reshape(count, d)))
            for c in arriving.heads:
                c.arrived()
            results.append(fetch(r.mixed_in, out.mixed_in))
            for c in results:
                c.wait()
            yield

        drive(
            head_weights(),
            by_steps(gather_line_first(net, tok, lambda slot: r.tok.at[slot], log)),
            main(),
            other_weights(),
            output_grad(),
        )
        middle(net, fetch, arriving, out, r)

    return kernel_with(
        body,
        moved,
        loaded,
        outs,
        scratch,
        110,
        number,
        (
            "lse",
            "a_gain",
            "q_gain",
            "k_gain",
            "first",
            "dealt",
            "back_from",
            "output",
            "back",
            "middle_low",
            "dg2",
            "gate",
        ),
        ("attn_gain", "mlp_gain", "q_gain", "k_gain", "freq"),
        ("lengths", "deal"),
    )


def back_kernel(dims, number):
    rows, count = dims
    blocks = count // BLOCK
    scale = HEAD_SIZE**-0.5
    width = 2 * HEAD_SIZE
    d = MODEL_WIDTH

    def run(moved, loaded):
        a = Bag(**moved)
        gu_rows, gu_cols = a.gate.shape[1:]
        dn_rows = a.down.shape[1]
        o_rows = 2 * width
        bf, f32 = jnp.bfloat16, jnp.float32
        z_gu, z_dn, z_o = gu_rows // LINE, dn_rows // LINE, o_rows // (2 * LINE)
        gain_width = 2 * d + 2 * HEAD_SIZE

        def quarter(**more):
            return dict(
                **more,
                own=pltpu.VMEM((2, gu_rows, gu_cols), bf),
                low=pltpu.VMEM((2, z_gu, gu_cols), bf),
                pair=pltpu.VMEM((2, z_gu, gu_cols), bf),
                line=line_scratch(2 * z_gu, gu_cols),
            )

        scratch = dict(
            held={n: pltpu.VMEM(v.shape, v.dtype) for n, v in loaded.items()},
            gate=quarter(),
            up=quarter(got=pltpu.VMEM((2, gu_rows, gu_cols), bf)),
            down=[
                dict(
                    own=pltpu.VMEM((dn_rows, d // 2), bf),
                    got=pltpu.VMEM((dn_rows, d // 2), bf),
                    low=pltpu.VMEM((z_dn, d // 2), bf),
                    line=line_scratch(z_dn, d // 2),
                )
                for _ in range(2)
            ],
            o=dict(
                own=pltpu.VMEM((4, o_rows, d), bf),
                core=pltpu.VMEM((2, o_rows, d), bf),
                got=pltpu.VMEM((o_rows, d), bf),
                sum=pltpu.VMEM((2 * LINE, z_o, d), bf),
                side=pltpu.VMEM((LINE, z_o, d), bf),
                low=pltpu.VMEM((z_o, d), bf),
                line=line_scratch(z_o, d),
            ),
            h=dict(
                own=pltpu.VMEM((4, d // 4, 2 * width), bf),
                core=pltpu.VMEM((2, d // 4, 2 * width), bf),
                got=pltpu.VMEM((d // 4, 2 * width), bf),
                low=pltpu.VMEM((d // 4, 2 * width), bf),
            ),
            dm_all=pltpu.VMEM((2 * LINE, rows, width), bf),
            back=pltpu.VMEM(a.back.shape, bf),
            do=pltpu.VMEM((count, width), bf),
            dk=pltpu.VMEM((count, HEAD_SIZE), f32),
            dv=pltpu.VMEM((count, HEAD_SIZE), f32),
            dqkv=pltpu.VMEM((count, 2 * width), bf),
            dgq=pltpu.VMEM((1, HEAD_SIZE), f32),
            dgk=pltpu.VMEM((1, HEAD_SIZE), f32),
            part=dict(
                sum=pltpu.VMEM((2 * LINE, rows, d), bf),
                side=pltpu.VMEM((LINE, rows, d), bf),
                line=line_scratch(rows, d),
            ),
            g=dict(
                mine=pltpu.VMEM((1, gain_width), f32),
                four=pltpu.VMEM((1, gain_width), f32),
                got=pltpu.VMEM((3, 1, gain_width), f32),
                all=pltpu.VMEM((2 * LINE, 1, gain_width), f32),
            ),
        )
        flat, tree = jax.tree.flatten(scratch)
        f_in, in_tree = jax.tree.flatten((moved, loaded))
        outs = dict(
            input_grad=shape_of(rows, d, kind=f32),
            a_grad=shape_of(1, d // 4, kind=f32),
            m_grad=shape_of(1, d // 4, kind=f32),
            q_grad=shape_of(1, HEAD_SIZE // 4, kind=f32),
            k_grad=shape_of(1, HEAD_SIZE // 4, kind=f32),
            gate=shape_of(2 * LINE, 2, z_gu, gu_cols),
            up=shape_of(2 * LINE, 2, z_gu, gu_cols),
            down=shape_of(2 * LINE, z_dn, d),
            o=shape_of(2 * LINE, z_o, d),
            heads=shape_of(2 * LINE, d // 4, 2 * width),
        )
        f_out, out_tree = jax.tree.flatten(outs)

        def body(net, local, *refs):
            given, to_load = jax.tree.unflatten(in_tree, refs[: len(f_in)])
            given = Bag(**given)
            out = Bag(**jax.tree.unflatten(out_tree, refs[len(f_in) : len(f_in) + len(f_out)]))
            r = bags(jax.tree.unflatten(tree, refs[len(f_in) + len(f_out) :]))
            h = r.held
            z, y, x, core, me = net.z, net.y, net.x, net.core, net.me
            slots = 2 * LINE
            used = iter(range(64))

            def fetch(src, dst):
                copy = pltpu.make_async_copy(src, dst, local.at[next(used)])
                copy.start()
                return copy

            greet(net, ("ctx", "x", "core", "far"))
            loads = {n: fetch(to_load[n], getattr(h, n)) for n in to_load}
            dm_own = fetch(given.dm.at[me], r.dm_all.at[me])
            back_own = fetch(given.back.at[me], r.back.at[me])
            gate_own = [fetch(given.gate.at[c], r.gate.own.at[c]) for c in range(2)]
            up_own = [fetch(given.up.at[2 * x + c], r.up.own.at[c]) for c in range(2)]
            columns = [pl.ds(0, d // 2), pl.ds(d // 2, d // 2)]
            down_own = [fetch(given.down.at[x, :, columns[i]], r.down[i].own) for i in range(2)]
            back_copies = []

            def need(*which):
                for n in which:
                    if n in loads:
                        loads.pop(n).wait()

            def to_all(src, out):
                copies = []
                for k in range(1, slots):
                    other = lax.rem(me + k, slots)
                    there = (other // 2, lax.rem(other, 2), x, core)
                    copies.append(net.put(src(other), out.at[me], there))
                return copies

            def back_rows():
                back_copies.extend(to_all(lambda other: given.back.at[other], r.back))
                yield

            def main():
                dm_copies = to_all(lambda other: given.dm.at[other], r.dm_all)
                yield
                need(*list(loads))
                dm_own.wait()
                for c in dm_copies:
                    c.arrived()
                yield
                for i in range(blocks):
                    t = i * BLOCK + lax.broadcasted_iota(jnp.int32, (BLOCK, count), 0)
                    hot = low(jnp.where(h.dealt[...] == t, 1.0, 0.0))
                    r.do[pl.ds(i * BLOCK, BLOCK)] = low(
                        dot(hot, r.dm_all[...].reshape(count, width))
                    )
                r.dk[...] = jnp.zeros_like(r.dk)
                r.dv[...] = jnp.zeros_like(r.dv)
                yield
                dgq = jnp.zeros((1, HEAD_SIZE), f32)
                for i in range(blocks):
                    here = pl.ds(i * BLOCK, BLOCK)
                    first = h.first[:, here]
                    t = i * BLOCK + lax.broadcasted_iota(jnp.int32, (BLOCK, BLOCK), 1)
                    heads = []
                    for g in range(2):
                        lanes = pl.ds(g * HEAD_SIZE, HEAD_SIZE)
                        q, do = h.q[here, lanes], r.do[here, lanes]
                        product = do.astype(f32) * h.mixed[here, lanes]
                        delta = jnp.sum(jnp.transpose(product), axis=0, keepdims=True)
                        heads.append((q, do, h.lse[g, :, here], delta))

                    def step(j, held, heads=heads, first=first, t=t):
                        at = pl.ds(pl.multiple_of(j * BLOCK, BLOCK), BLOCK)
                        k, v, kt = h.k[at], h.v[at], h.kt[:, at]
                        u = j * BLOCK + lax.broadcasted_iota(jnp.int32, (BLOCK, BLOCK), 0)
                        allowed = (u >= first) & (u <= t)
                        dk, dv, out = r.dk[at], r.dv[at], []
                        for (q, do, lse, delta), dq in zip(heads, held):
                            p = jnp.where(allowed, jnp.exp(dot_last(k, q) * scale - lse), 0.0)
                            ds = low(p * (dot_last(v, do) - delta))
                            dv = dv + dot(low(p), do)
                            dk = dk + dot(ds, q)
                            out.append(dq + dot(kt, ds))
                        r.dk[at] = dk
                        r.dv[at] = dv
                        return tuple(out)

                    zero = jnp.zeros((HEAD_SIZE, BLOCK), f32)
                    result = lax.fori_loop(0, i + 1, step, (zero, zero))
                    cos, sin = h.cos[here], h.sin[here]
                    for g in range(2):
                        lanes = pl.ds(g * HEAD_SIZE, HEAD_SIZE)
                        grad = jnp.transpose(result[g]) * scale
                        grad = grad * cos - turn_lanes(grad) * sin
                        dx, dg = norm_back(h.qkv[here, lanes], h.q_gain[...], grad)
                        r.dqkv[here, lanes] = low(dx)
                        dgq = dgq + jnp.sum(dg, axis=0, keepdims=True)
                    yield
                dgk = jnp.zeros((1, HEAD_SIZE), f32)
                for i in range(blocks):
                    here = pl.ds(i * BLOCK, BLOCK)
                    grad = r.dk[here] * scale
                    grad = grad * h.cos[here] - turn_lanes(grad) * h.sin[here]
                    dx, dg = norm_back(
                        h.qkv[here, pl.ds(width, HEAD_SIZE)], h.k_gain[...], grad
                    )
                    r.dqkv[here, pl.ds(width, HEAD_SIZE)] = low(dx)
                    r.dqkv[here, pl.ds(width + HEAD_SIZE, HEAD_SIZE)] = low(r.dv[here])
                    dgk = dgk + jnp.sum(dg, axis=0, keepdims=True)
                r.dgq[...] = dgq
                r.dgk[...] = dgk
                yield

                def make(slot):
                    at = pl.ds(pl.multiple_of(slot * rows, rows), rows)
                    r.part.sum[slot] = low(dot_last(r.dqkv[at], h.w_qkv[...].reshape(d, 2 * width)))

                yield from sum_sides(net, r.part.sum, r.part.side, r.part.line, make)
                yield
                dx1, dg1 = norm_back(
                    h.tok[0].astype(f32), h.a_gain[...], r.part.line[0][z]
                )
                for c in back_copies:
                    c.arrived()
                back_own.wait()
                ids = lax.broadcasted_iota(jnp.int32, (rows, slots * a.back.shape[1]), 1)
                hot = low(jnp.where(h.back_from[...] == ids, 1.0, 0.0))
                out.input_grad[...] = dx1 + dot(hot, r.back[...].reshape(-1, d))
                r.g.mine[:, pl.ds(0, d)] = jnp.sum(dg1, axis=0, keepdims=True)
                r.g.mine[:, pl.ds(d, d)] = h.dg2[...]
                r.g.mine[:, pl.ds(2 * d, HEAD_SIZE)] = r.dgq[...]
                r.g.mine[:, pl.ds(2 * d + HEAD_SIZE, HEAD_SIZE)] = r.dgk[...]
                yield

            def gains():
                sides = [net.at(dc=1), net.at(dx=1), net.at(dx=1, dc=1)]
                pair = [net.put(r.g.mine, r.g.got.at[i], to) for i, to in enumerate(sides)]
                yield
                for c in pair:
                    c.arrived()
                along = r.g.mine[...] + r.g.got[0]
                across = r.g.got[1] + r.g.got[2]
                r.g.four[...] = along + across
                r.g.all[me] = r.g.four[...]
                copies = to_all(lambda other: r.g.four, r.g.all)
                yield
                for c in copies:
                    c.arrived()
                total = jnp.sum(r.g.all[...], axis=0)

                def own_part(start, size):
                    part = total[:, start : start + size]
                    for i in range(1, 4):
                        at = start + i * size
                        part = jnp.where(2 * x + core == i, total[:, at : at + size], part)
                    return part

                out.a_grad[...] = own_part(0, d // 4)
                out.m_grad[...] = own_part(d, d // 4)
                out.q_grad[...] = own_part(2 * d, HEAD_SIZE // 4)
                out.k_grad[...] = own_part(2 * d + HEAD_SIZE, HEAD_SIZE // 4)
                yield

            def gate_or_up(piece, gathered):
                line = piece.line

                def ready(t):
                    k = far_first(z)[t]
                    at = pl.ds(pl.multiple_of(k * z_gu, z_gu), z_gu)
                    for c in range(2):
                        block = piece.own[c, at].astype(f32)
                        if hasattr(piece, "got"):
                            block = block + piece.got[c, at].astype(f32)
                        line[0][k, pl.ds(c * z_gu, z_gu)] = block

                yield from sum_line(net, *line, ready)
                for c in range(2):
                    piece.low[c] = low(line[0][z, pl.ds(c * z_gu, z_gu)])
                swap = net.put(piece.low.at[1 - core], piece.pair.at[core], net.at(dc=1))
                piece.pair[core] = piece.low[core]
                yield
                swap.arrived()
                own = fetch(piece.pair, gathered.at[me])
                yield from gather_line_first(net, piece.pair, lambda slot: gathered.at[slot])
                own.wait()

            def gate():
                for c in gate_own:
                    c.wait()
                yield from gate_or_up(r.gate, out.gate)

            def up():
                over = [
                    net.put(given.up.at[2 * (1 - x) + c], r.up.got.at[c], net.at(dx=1))
                    for c in range(2)
                ]
                yield
                for c in up_own:
                    c.wait()
                for c in over:
                    c.arrived()
                yield from gate_or_up(r.up, out.up)

            def down(i):
                piece, line = r.down[i], r.down[i].line
                over = net.put(given.down.at[1 - x, :, columns[i]], piece.got, net.at(dx=1))
                yield
                down_own[i].wait()
                over.arrived()

                def ready(t):
                    k = far_first(z)[t]
                    at = pl.ds(pl.multiple_of(k * z_dn, z_dn), z_dn)
                    line[0][k] = piece.own[at].astype(f32) + piece.got[at].astype(f32)

                yield from sum_line(net, *line, ready)
                piece.low[...] = low(line[0][z])
                own = fetch(piece.low, out.down.at[me, :, columns[i]])
                yield from gather_line_first(
                    net, piece.low, lambda slot: out.down.at[slot, :, columns[i]]
                )
                own.wait()

            def out_proj():
                need("heads_in", "middle_low")
                for i in range(slots):
                    r.o.own[i // 2, pl.ds(i % 2 * width, width)] = low(
                        outer_rows(h.heads_in[i], h.middle_low[...])
                    )
                o_core = [
                    net.put(r.o.own.at[2 * s + 1 - core], r.o.core.at[s], net.at(dc=1))
                    for s in range(2)
                ]
                yield
                for c in o_core:
                    c.arrived()
                for s in range(2):
                    f = 2 * s + core
                    r.o.own[f] = low(r.o.own[f].astype(f32) + r.o.core[s].astype(f32))
                over = net.put(r.o.own.at[2 * (1 - x) + core], r.o.got, net.at(dx=1))
                yield
                over.arrived()
                for i in range(slots):
                    at = pl.ds(i * z_o, z_o)
                    r.o.sum[i] = low(r.o.own[2 * x + core, at].astype(f32) + r.o.got[at].astype(f32))
                yield from sum_sides(net, r.o.sum, r.o.side, r.o.line)
                r.o.low[...] = low(r.o.line[0][z])
                own = fetch(r.o.low, out.o.at[me])
                yield from gather_line_first(net, r.o.low, lambda slot: out.o.at[slot])
                own.wait()

            def heads():
                for f in range(4):
                    at = pl.ds(f * (d // 4), d // 4)
                    r.h.own[f] = low(outer_rows(h.normed[:, at], r.dqkv[...]))
                core_copies = [
                    net.put(r.h.own.at[2 * s + 1 - core], r.h.core.at[s], net.at(dc=1))
                    for s in range(2)
                ]
                yield
                for c in core_copies:
                    c.arrived()
                for s in range(2):
                    f = 2 * s + core
                    r.h.own[f] = low(r.h.own[f].astype(f32) + r.h.core[s].astype(f32))
                over = net.put(r.h.own.at[2 * (1 - x) + core], r.h.got, net.at(dx=1))
                yield
                over.arrived()
                r.h.low[...] = low(
                    r.h.own[2 * x + core].astype(f32) + r.h.got[...].astype(f32)
                )
                own = fetch(r.h.low, out.heads.at[me])
                yield from gather_line_first(net, r.h.low, lambda slot: out.heads.at[slot])
                own.wait()

            in_order(
                BACK_ORDER,
                [
                    gate(),
                    up(),
                    out_proj(),
                    down(0),
                    down(1),
                    back_rows(),
                    heads(),
                    main(),
                    gains(),
                ],
            )
            net.close()

        order = jax.tree.unflatten(out_tree, range(len(f_out)))
        result = net_call(
            body,
            f_out,
            f_in,
            200,
            64,
            number,
            scratch=flat,
            vmem=[
                len(f_in) + order.get(n)
                for n in ("input_grad", "a_grad", "m_grad", "q_grad", "k_grad")
            ],
        )
        return Bag(**jax.tree.unflatten(out_tree, result))

    return run


def widen(gate_all, up_all, down_all, o_all, heads_all, *small):
    _, _, z_gu, gu_cols = gate_all.shape
    half = gu_cols // 2
    z_dn, z_o = down_all.shape[1], o_all.shape[1]
    h_rows = heads_all.shape[1] // LINE

    def kernel(gate, up, down, o, heads, *refs):
        passed, outs = refs[: len(small)], refs[len(small) :]
        gate_out, up_out, down_out, o_out, q_out, k_out, v_out = outs[:7]
        for src, out in zip(passed, outs[7:]):
            out[...] = src[...].reshape(out.shape)
        for src, out in ((gate, gate_out), (up, up_out)):
            for y in range(2):
                for c in range(2):
                    for xs in range(2):
                        to = (2 * xs + c) * 2 * half + y * half
                        out[:, pl.ds(to, half)] = src[y, c, :, pl.ds(xs * half, half)].astype(
                            jnp.float32
                        )
        for y in range(2):
            down_out[y] = down[y].astype(jnp.float32)
            o_out[pl.ds(y * z_o, z_o)] = o[y].astype(jnp.float32)
        for h in range(2 * LINE):
            q_out[:, pl.ds(h * 256, 256)] = heads[h, :, pl.ds(0, 256)].astype(jnp.float32)
            k_out[:, pl.ds(h * 128, 128)] = heads[h, :, pl.ds(256, 128)].astype(jnp.float32)
            v_out[:, pl.ds(h * 128, 128)] = heads[h, :, pl.ds(384, 128)].astype(jnp.float32)

    f32 = jnp.float32
    outs = pl.pallas_call(
        kernel,
        grid=(LINE,),
        in_specs=[
            pl.BlockSpec((2, 2, z_gu, gu_cols), lambda i: (i, 0, 0, 0)),
            pl.BlockSpec((2, 2, z_gu, gu_cols), lambda i: (i, 0, 0, 0)),
            pl.BlockSpec((2, z_dn, MODEL_WIDTH), lambda i: (i, 0, 0)),
            pl.BlockSpec((2, z_o, MODEL_WIDTH), lambda i: (i, 0, 0)),
            pl.BlockSpec((2 * LINE, h_rows, 512), lambda i: (0, i, 0)),
        ]
        + [pl.BlockSpec(v.shape, lambda i: (0, 0)) for v in small],
        out_specs=[
            pl.BlockSpec((z_gu, 8 * half), lambda i: (i, 0)),
            pl.BlockSpec((z_gu, 8 * half), lambda i: (i, 0)),
            pl.BlockSpec((2, z_dn, MODEL_WIDTH), lambda i: (0, i, 0)),
            pl.BlockSpec((2 * z_o, MODEL_WIDTH), lambda i: (i, 0)),
            pl.BlockSpec((h_rows, 2048), lambda i: (i, 0)),
            pl.BlockSpec((h_rows, 1024), lambda i: (i, 0)),
            pl.BlockSpec((h_rows, 1024), lambda i: (i, 0)),
        ]
        + [pl.BlockSpec((1, *v.shape), lambda i: (0, 0, 0)) for v in small],
        out_shape=[
            shape_of(LINE * z_gu, 8 * half, kind=f32),
            shape_of(LINE * z_gu, 8 * half, kind=f32),
            shape_of(2, LINE * z_dn, MODEL_WIDTH, kind=f32),
            shape_of(2 * LINE * z_o, MODEL_WIDTH, kind=f32),
            shape_of(LINE * h_rows, 2048, kind=f32),
            shape_of(LINE * h_rows, 1024, kind=f32),
            shape_of(LINE * h_rows, 1024, kind=f32),
        ]
        + [shape_of(1, *v.shape, kind=v.dtype) for v in small],
        compiler_params=pltpu.CompilerParams(vmem_limit_bytes=VMEM_BYTES),
    )(gate_all, up_all, down_all, o_all, heads_all, *small)
    outs = list(outs)
    outs[2] = outs[2].reshape(-1, MODEL_WIDTH)
    return outs


def fast_layer(
    tokens,
    lengths,
    deal,
    attn_gain,
    w_q,
    key_weight,
    value_weight,
    query_norm_gain,
    k_gain,
    w_o,
    mlp_gain,
    w_gate,
    w_up,
    w_down,
    out_cotangent,
):
    rows = tokens.shape[1]
    slots = lax.axis_size(CTX)
    count = rows * slots
    ff_half = w_down.shape[0] // 2
    width = HEAD_SIZE * 2

    frequency = theta_base ** (-(np.arange(HEAD_SIZE // 2) * 2.0) / HEAD_SIZE)
    sign = np.where(np.arange(HEAD_SIZE) < HEAD_SIZE // 2, -1.0, 1.0)
    tables = np.stack([np.tile(frequency, 2), sign]).astype(np.float32)

    front = front_kernel(
        dict(
            tok=tokens,
            lengths=lengths,
            deal=deal,
            attn_gain=attn_gain,
            mlp_gain=mlp_gain,
            q_gain=query_norm_gain[None],
            k_gain=k_gain[None],
            freq=tables,
            w_q=w_q,
            w_k=key_weight,
            w_v=value_weight,
            w_o=w_o,
            w_gate=w_gate,
            w_up=w_up,
            w_down=w_down,
            grad=out_cotangent,
        ),
        {},
        0,
    )
    moved = dict(
        dm=front.dm,
        back=front.back,
        gate=front.gate,
        up=front.up.reshape(4, -1, 2 * ff_half),
        down=front.down.reshape(2, -1, MODEL_WIDTH),
    )
    loaded = dict(
        tok=tokens,
        back_from=front.back_from,
        a_gain=front.a_gain,
        dg2=front.dg2,
        heads_in=front.mixed_in,
        middle_low=front.middle_low,
        q=front.q,
        k=front.k,
        kt=front.kt,
        v=front.v,
        mixed=front.mixed,
        lse=front.lse,
        first=front.first,
        dealt=front.dealt,
        qkv=front.qkv,
        q_gain=front.q_gain,
        k_gain=front.k_gain,
        cos=front.cos,
        sin=front.sin,
        normed=front.normed,
        w_qkv=front.w_qkv,
    )
    sums = back_kernel((rows, count), 2)(moved, loaded)

    gate_sum, up_sum, down_sum, o_sum, q_sum, k_sum, v_sum, *small = widen(
        sums.gate,
        sums.up,
        sums.down,
        sums.o,
        sums.heads,
        front.output,
        sums.input_grad,
        sums.a_grad,
        sums.q_grad,
        sums.k_grad,
        sums.m_grad,
    )
    output, input_grad, *gains = small
    return (
        output,
        input_grad,
        *(gain[0, 0] for gain in gains),
        q_sum,
        k_sum,
        v_sum,
        o_sum,
        gate_sum,
        up_sum,
        down_sum,
    )


def solution(mesh):
    devices = mesh.devices
    if devices.shape == (8, 4):
        mesh = Mesh(devices.reshape(4, 2, 2, 2), CTX + FSDP)
        layer, ctx, fsdp = fast_layer, CTX, FSDP
    else:
        layer, ctx, fsdp = general_layer, "ctx", "fsdp"
    wide_rows = P(fsdp, ctx, None)
    return jax.shard_map(
        layer,
        mesh=mesh,
        in_specs=(
            wide_rows,
            P(fsdp, None),
            P(fsdp, None, None),
            P(fsdp),
            P(fsdp, None),
            P(fsdp, None),
            P(fsdp, None),
            P(fsdp),
            P(fsdp),
            P(fsdp, None),
            P(fsdp),
            P(fsdp, None),
            P(fsdp, None),
            P(fsdp, None),
            wide_rows,
        ),
        out_specs=(wide_rows, wide_rows) + (P(fsdp),) * 4 + (P(fsdp, None),) * 7,
        check_vma=False,
    )
```

```python
import math

import jax
import jax.numpy as jnp
import numpy as np
from jax import lax
from jax.experimental import pallas as pl
from jax.experimental.pallas import tpu as pltpu
from jax.sharding import Mesh
from jax.sharding import PartitionSpec as P

MODEL_WIDTH = 1024
QUERY_HEADS = 16
KEY_VALUE_HEADS = 8
HEAD_SIZE = 128


eps = 1e-06
theta_base = 1000000.0
negative_filler = -1e30


def root_mean_norm(values, gain_vec):
    return values * lax.rsqrt(jnp.mean(values * values, axis=-1, keepdims=True) + eps) * gain_vec


def rotary_embedding(values, token_position):
    half_width = values.shape[-1] // 2
    frequency = theta_base ** (
        -(jnp.arange(half_width, dtype=jnp.float32) * 2.0) / values.shape[-1]
    )
    angles = token_position.astype(jnp.float32)[:, None] * frequency[None, :]
    cosine = jnp.concatenate([jnp.cos(angles), jnp.cos(angles)], axis=-1)[:, None, :]
    sine_part = jnp.concatenate([jnp.sin(angles), jnp.sin(angles)], axis=-1)[:, None, :]
    turned = jnp.concatenate([-values[..., half_width:], values[..., :half_width]], axis=-1)
    return values * cosine + turned * sine_part


def dot_trans(left_side, right_side):
    return lax.dot_general(
        left_side, right_side, (((1,), (1,)), ((), ())), preferred_element_type=jnp.float32
    )


def outer_rows(left_side, right_side):
    return lax.dot_general(
        left_side, right_side, (((0,), (0,)), ((), ())), preferred_element_type=jnp.float32
    )


def block_plan(piece_rows, local_rows):
    shards = piece_rows // local_rows
    per_block = math.gcd(shards, max(1, 1024 // local_rows))
    return (per_block * local_rows, shards // per_block)


def over_blocks(carried, arrays, local_rows, block_work):
    rows_per_block, count_of_blocks = block_plan(arrays[0].shape[0], local_rows)

    def one_block(turn_index, state_now):
        offset = turn_index * rows_per_block
        parts = tuple(
            (lax.dynamic_slice_in_dim(member, offset, rows_per_block, 0) for member in arrays)
        )
        return block_work(state_now, parts, offset)

    return lax.fori_loop(0, count_of_blocks, one_block, carried)


def segment_begin(tok_ids, starts):
    return jnp.max(jnp.where(tok_ids[:, None] >= starts[None, :], starts[None, :], 0), axis=1)


def general_layer(
    tokens,
    lengths,
    deal,
    attn_gain,
    w_q,
    key_weight,
    value_weight,
    query_norm_gain,
    k_gain,
    w_o,
    mlp_gain,
    w_gate,
    w_up,
    w_down,
    out_cotangent,
):
    local_rows = tokens.shape[1]
    piece_count = lax.axis_size("ctx")
    piece_rows = local_rows // piece_count
    here = lax.axis_index("ctx")
    group_width = QUERY_HEADS // KEY_VALUE_HEADS
    score_scale = HEAD_SIZE ** (-0.5)
    seq_lengths = lengths[0]
    starts = jnp.cumsum(seq_lengths) - seq_lengths
    plan = deal[0]
    devices = jnp.arange(piece_count, dtype=jnp.int32)
    hits = plan[:, :, None] == devices[None, None, :]
    slot_of = jnp.sum(jnp.where(hits, devices[None, :, None], 0), axis=1)
    inner = jnp.arange(piece_rows, dtype=jnp.int32)
    dealt_index = (
        devices[None, :, None] * local_rows
        + jnp.transpose(slot_of)[:, :, None] * piece_rows
        + inner[None, None, :]
    ).reshape(piece_count * local_rows)
    dealt_first = segment_begin(dealt_index, starts)
    tok_index = lax.dynamic_slice_in_dim(dealt_index, here * local_rows, local_rows)
    segment_initial = lax.dynamic_slice_in_dim(dealt_first, here * local_rows, local_rows)
    token_position = tok_index - segment_initial
    own_slots = lax.dynamic_index_in_dim(slot_of, here, 0, keepdims=False)
    own_plan = lax.dynamic_index_in_dim(plan, here, 0, keepdims=False)
    token_pieces = jnp.take(
        tokens[0].reshape(piece_count, piece_rows, MODEL_WIDTH), own_slots, axis=0
    )
    dealt_tok = lax.all_to_all(
        token_pieces, "ctx", split_axis=0, concat_axis=0, tiled=True
    ).reshape(local_rows, MODEL_WIDTH)

    def key_mask(start_row, local_row_count):
        key_identifiers = lax.dynamic_slice_in_dim(dealt_index, start_row, local_row_count)
        return (key_identifiers[None, :] >= segment_initial[:, None]) & (
            key_identifiers[None, :] <= tok_index[:, None]
        )

    def query_mask(start_row, local_row_count):
        query_ids = lax.dynamic_slice_in_dim(dealt_index, start_row, local_row_count)
        first_key = lax.dynamic_slice_in_dim(dealt_first, start_row, local_row_count)
        return (tok_index[None, :] >= first_key[:, None]) & (
            tok_index[None, :] <= query_ids[:, None]
        )

    def fetch_weights():
        attn_set = (
            lax.all_gather(attn_gain, "fsdp", axis=0, tiled=True),
            lax.all_gather(query_norm_gain, "fsdp", axis=0, tiled=True),
            lax.all_gather(k_gain, "fsdp", axis=0, tiled=True),
            lax.all_gather(w_q, "fsdp", axis=0, tiled=True),
            lax.all_gather(key_weight, "fsdp", axis=0, tiled=True),
            lax.all_gather(value_weight, "fsdp", axis=0, tiled=True),
            lax.all_gather(w_o, "fsdp", axis=0, tiled=True),
        )
        mlp_set = (
            lax.all_gather(mlp_gain, "fsdp", axis=0, tiled=True),
            lax.all_gather(w_gate, "fsdp", axis=0, tiled=True),
            lax.all_gather(w_up, "fsdp", axis=0, tiled=True),
            lax.all_gather(w_down, "fsdp", axis=0, tiled=True),
        )
        return (attn_set, mlp_set)

    def forward(attn_set, mlp_set, token_rows):
        a_gain, qn_gain, kn_gain, proj_q, proj_k, proj_v, proj_o = attn_set
        m_gain, proj_gate, proj_up, proj_down = mlp_set
        residual = token_rows.astype(jnp.float32)
        normalized_input = root_mean_norm(residual, a_gain.astype(jnp.float32)).astype(jnp.bfloat16)
        query_prenorm = jnp.dot(
            normalized_input, proj_q, preferred_element_type=jnp.float32
        ).reshape(local_rows, QUERY_HEADS, HEAD_SIZE)
        key_prenorm = jnp.dot(normalized_input, proj_k, preferred_element_type=jnp.float32).reshape(
            local_rows, KEY_VALUE_HEADS, HEAD_SIZE
        )
        value_narrow = jnp.dot(normalized_input, proj_v, preferred_element_type=jnp.float32).astype(
            jnp.bfloat16
        )
        q_heads = (
            rotary_embedding(
                root_mean_norm(query_prenorm, qn_gain.astype(jnp.float32)), token_position
            )
            .astype(jnp.bfloat16)
            .reshape(local_rows, KEY_VALUE_HEADS, group_width, HEAD_SIZE)
        )
        key_narrow = (
            rotary_embedding(
                root_mean_norm(key_prenorm, kn_gain.astype(jnp.float32)), token_position
            )
            .astype(jnp.bfloat16)
            .reshape(local_rows, KEY_VALUE_HEADS * HEAD_SIZE)
        )

        def attend_over_block(state_now, shard_piece, start_row):
            key_segment, value_segment = shard_piece
            local_row_count = key_segment.shape[0]
            allowed = key_mask(start_row, local_row_count)
            row_top, row_total, weighted = state_now
            scores = (
                jnp.einsum(
                    "rkgh,ckh->kgrc",
                    q_heads,
                    key_segment.reshape(local_row_count, KEY_VALUE_HEADS, HEAD_SIZE),
                    preferred_element_type=jnp.float32,
                )
                * score_scale
            )
            scores = jnp.where(allowed, scores, negative_filler)
            new_top = jnp.maximum(row_top, jnp.max(scores, axis=-1))
            rescale = jnp.exp(row_top - new_top)
            weights = jnp.where(allowed, jnp.exp(scores - new_top[..., None]), 0.0)
            row_total = row_total * rescale + jnp.sum(weights, axis=-1)
            weighted = weighted * rescale[..., None] + jnp.einsum(
                "kgrc,ckh->kgrh",
                weights.astype(jnp.bfloat16),
                value_segment.reshape(local_row_count, KEY_VALUE_HEADS, HEAD_SIZE),
                preferred_element_type=jnp.float32,
            )
            return (new_top, row_total, weighted)

        initial = (
            jnp.full((KEY_VALUE_HEADS, group_width, local_rows), negative_filler, jnp.float32),
            jnp.zeros((KEY_VALUE_HEADS, group_width, local_rows), jnp.float32),
            jnp.zeros((KEY_VALUE_HEADS, group_width, local_rows, HEAD_SIZE), jnp.float32),
        )
        row_top, row_total, weighted = over_blocks(
            initial,
            (
                lax.all_gather(key_narrow, "ctx", axis=0, tiled=True),
                lax.all_gather(value_narrow, "ctx", axis=0, tiled=True),
            ),
            local_rows,
            attend_over_block,
        )
        attention_mixed = jnp.transpose(weighted / row_total[..., None], (2, 0, 1, 3)).reshape(
            local_rows, QUERY_HEADS * HEAD_SIZE
        )
        log_total = row_top + jnp.log(row_total)
        mixed_low = attention_mixed.astype(jnp.bfloat16)
        middle = residual + jnp.dot(mixed_low, proj_o, preferred_element_type=jnp.float32)
        normed2 = root_mean_norm(middle, m_gain.astype(jnp.float32)).astype(jnp.bfloat16)
        gate_pre = jnp.dot(normed2, proj_gate, preferred_element_type=jnp.float32)
        up_pre = jnp.dot(normed2, proj_up, preferred_element_type=jnp.float32)
        hidden = (jax.nn.silu(gate_pre) * up_pre).astype(jnp.bfloat16)
        result = middle + jnp.dot(hidden, proj_down, preferred_element_type=jnp.float32)
        return (
            result,
            residual,
            normalized_input,
            query_prenorm,
            key_prenorm,
            value_narrow,
            q_heads,
            key_narrow,
            attention_mixed,
            mixed_low,
            log_total,
            middle,
            normed2,
            gate_pre,
            up_pre,
            hidden,
            attn_set,
            mlp_set,
        )

    first_sets = fetch_weights()
    first_pass = forward(first_sets[0], first_sets[1], dealt_tok)
    again_tok = lax.all_to_all(
        token_pieces, "ctx", split_axis=0, concat_axis=0, tiled=True
    ).reshape(local_rows, MODEL_WIDTH)
    second_sets = fetch_weights()
    kept_pass = forward(second_sets[0], second_sets[1], again_tok)
    (
        unused,
        residual,
        normalized_input,
        query_prenorm,
        key_prenorm,
        value_narrow,
        q_heads,
        key_narrow,
        attention_mixed,
        mixed_low,
        log_total,
        middle,
        normed2,
        gate_pre,
        up_pre,
        hidden,
        attn_set,
        mlp_set,
    ) = kept_pass
    a_gain, qn_gain, kn_gain, proj_q, proj_k, proj_v, proj_o = attn_set
    m_gain, proj_gate, proj_up, proj_down = mlp_set
    grad_low = out_cotangent[0]
    grad_out = grad_low.astype(jnp.float32)
    d_hidden = dot_trans(grad_low, proj_down)
    down_grad = lax.psum_scatter(
        outer_rows(hidden, grad_low).astype(jnp.bfloat16), "fsdp", scatter_dimension=0, tiled=True
    )
    unused, swiglu_back = jax.vjp(
        lambda gate_in, up_in: jax.nn.silu(gate_in) * up_in, gate_pre, up_pre
    )
    d_gate, d_up = swiglu_back(d_hidden)
    d_gate_low = d_gate.astype(jnp.bfloat16)
    d_up_low = d_up.astype(jnp.bfloat16)
    d_normed2 = dot_trans(d_gate_low, proj_gate) + dot_trans(d_up_low, proj_up)
    both_low = jnp.concatenate([d_gate_low, d_up_low], axis=1)
    gate_up_grad = lax.psum_scatter(
        outer_rows(normed2, both_low).astype(jnp.bfloat16), "fsdp", scatter_dimension=0, tiled=True
    )
    unused, norm2_back = jax.vjp(root_mean_norm, middle, m_gain.astype(jnp.float32))
    d_middle_norm, d_m_gain = norm2_back(d_normed2)
    d_middle = grad_out + d_middle_norm
    middle_low = d_middle.astype(jnp.bfloat16)
    mixed_gradient = dot_trans(middle_low, proj_o).astype(jnp.bfloat16)
    out_proj_grad = lax.psum_scatter(
        outer_rows(mixed_low, middle_low).astype(jnp.bfloat16),
        "fsdp",
        scatter_dimension=0,
        tiled=True,
    )
    heads_gradient = mixed_gradient.reshape(local_rows, KEY_VALUE_HEADS, group_width, HEAD_SIZE)
    delta_rows = jnp.sum(
        heads_gradient.astype(jnp.float32)
        * attention_mixed.reshape(local_rows, KEY_VALUE_HEADS, group_width, HEAD_SIZE),
        axis=-1,
    )
    delta_t = jnp.transpose(delta_rows, (1, 2, 0))
    local_keys = key_narrow.reshape(local_rows, KEY_VALUE_HEADS, HEAD_SIZE)
    local_values = value_narrow.reshape(local_rows, KEY_VALUE_HEADS, HEAD_SIZE)

    def query_block(state_now, shard_piece, start_row):
        key_segment, value_segment = shard_piece
        local_row_count = key_segment.shape[0]
        allowed = key_mask(start_row, local_row_count)
        key_row_block = key_segment.reshape(local_row_count, KEY_VALUE_HEADS, HEAD_SIZE)
        scores = (
            jnp.einsum("rkgh,ckh->kgrc", q_heads, key_row_block, preferred_element_type=jnp.float32)
            * score_scale
        )
        probability = jnp.where(allowed, jnp.exp(scores - log_total[..., None]), 0.0)
        d_probs = jnp.einsum(
            "rkgh,ckh->kgrc",
            heads_gradient,
            value_segment.reshape(local_row_count, KEY_VALUE_HEADS, HEAD_SIZE),
            preferred_element_type=jnp.float32,
        )
        d_scores = (probability * (d_probs - delta_t[..., None])).astype(jnp.bfloat16)
        return (
            state_now
            + jnp.einsum(
                "kgrc,ckh->kgrh", d_scores, key_row_block, preferred_element_type=jnp.float32
            )
            * score_scale
        )

    query_grad = over_blocks(
        jnp.zeros((KEY_VALUE_HEADS, group_width, local_rows, HEAD_SIZE), jnp.float32),
        (
            lax.all_gather(key_narrow, "ctx", axis=0, tiled=True),
            lax.all_gather(value_narrow, "ctx", axis=0, tiled=True),
        ),
        local_rows,
        query_block,
    )
    lse_rows = jnp.transpose(log_total, (2, 0, 1)).reshape(local_rows, QUERY_HEADS)
    delta_send = delta_rows.reshape(local_rows, QUERY_HEADS)

    def key_block(state_now, shard_piece, start_row):
        query_segment, output_gradient_segment, logsumexp_segment, delta_segment = shard_piece
        local_row_count = query_segment.shape[0]
        allowed = query_mask(start_row, local_row_count)
        key_grad, value_gradient = state_now
        query_matrix = query_segment.reshape(
            local_row_count, KEY_VALUE_HEADS, group_width, HEAD_SIZE
        )
        gradient_rows = output_gradient_segment.reshape(
            local_row_count, KEY_VALUE_HEADS, group_width, HEAD_SIZE
        )
        scores = (
            jnp.einsum(
                "ckgh,rkh->kgcr", query_matrix, local_keys, preferred_element_type=jnp.float32
            )
            * score_scale
        )
        logsumexp_portion = jnp.transpose(
            logsumexp_segment.reshape(local_row_count, KEY_VALUE_HEADS, group_width), (1, 2, 0)
        )
        delta_portion = jnp.transpose(
            delta_segment.reshape(local_row_count, KEY_VALUE_HEADS, group_width), (1, 2, 0)
        )
        probability = jnp.where(allowed, jnp.exp(scores - logsumexp_portion[..., None]), 0.0)
        value_gradient = value_gradient + jnp.einsum(
            "kgcr,ckgh->rkh",
            probability.astype(jnp.bfloat16),
            gradient_rows,
            preferred_element_type=jnp.float32,
        )
        d_probs = jnp.einsum(
            "ckgh,rkh->kgcr", gradient_rows, local_values, preferred_element_type=jnp.float32
        )
        d_scores = (probability * (d_probs - delta_portion[..., None])).astype(jnp.bfloat16)
        key_grad = (
            key_grad
            + jnp.einsum(
                "kgcr,ckgh->rkh", d_scores, query_matrix, preferred_element_type=jnp.float32
            )
            * score_scale
        )
        return (key_grad, value_gradient)

    key_grad, value_gradient = over_blocks(
        (
            jnp.zeros((local_rows, KEY_VALUE_HEADS, HEAD_SIZE), jnp.float32),
            jnp.zeros((local_rows, KEY_VALUE_HEADS, HEAD_SIZE), jnp.float32),
        ),
        (
            lax.all_gather(
                q_heads.reshape(local_rows, QUERY_HEADS * HEAD_SIZE), "ctx", axis=0, tiled=True
            ),
            lax.all_gather(mixed_gradient, "ctx", axis=0, tiled=True),
            lax.all_gather(lse_rows.astype(jnp.bfloat16), "ctx", axis=0, tiled=True).astype(
                jnp.float32
            ),
            lax.all_gather(delta_send.astype(jnp.bfloat16), "ctx", axis=0, tiled=True).astype(
                jnp.float32
            ),
        ),
        local_rows,
        key_block,
    )
    query_rows = jnp.transpose(query_grad, (2, 0, 1, 3)).reshape(local_rows, QUERY_HEADS, HEAD_SIZE)
    unused, q_back = jax.vjp(
        lambda head_in, gain_in: rotary_embedding(root_mean_norm(head_in, gain_in), token_position),
        query_prenorm,
        qn_gain.astype(jnp.float32),
    )
    d_q_pre, d_qn_gain = q_back(query_rows)
    unused, k_back = jax.vjp(
        lambda head_in, gain_in: rotary_embedding(root_mean_norm(head_in, gain_in), token_position),
        key_prenorm,
        kn_gain.astype(jnp.float32),
    )
    key_prenorm_gradient, d_kn_gain = k_back(key_grad)
    dq_low = d_q_pre.reshape(local_rows, QUERY_HEADS * HEAD_SIZE).astype(jnp.bfloat16)
    key_gradient_narrow = key_prenorm_gradient.reshape(
        local_rows, KEY_VALUE_HEADS * HEAD_SIZE
    ).astype(jnp.bfloat16)
    value_gradient_narrow = value_gradient.reshape(local_rows, KEY_VALUE_HEADS * HEAD_SIZE).astype(
        jnp.bfloat16
    )
    d_normed = (
        dot_trans(dq_low, proj_q)
        + dot_trans(key_gradient_narrow, proj_k)
        + dot_trans(value_gradient_narrow, proj_v)
    )
    qkv_low = jnp.concatenate([dq_low, key_gradient_narrow, value_gradient_narrow], axis=1)
    qkv_grad = lax.psum_scatter(
        outer_rows(normalized_input, qkv_low).astype(jnp.bfloat16),
        "fsdp",
        scatter_dimension=0,
        tiled=True,
    )
    unused, norm1_back = jax.vjp(root_mean_norm, residual, a_gain.astype(jnp.float32))
    d_resid_norm, d_a_gain = norm1_back(d_normed)
    input_dealt = d_middle + d_resid_norm
    back_pieces = lax.all_to_all(
        input_dealt.reshape(piece_count, piece_rows, MODEL_WIDTH).astype(jnp.bfloat16),
        "ctx",
        split_axis=0,
        concat_axis=0,
        tiled=True,
    ).astype(jnp.float32)
    input_grad = jnp.take(back_pieces, own_plan, axis=0).reshape(local_rows, MODEL_WIDTH)
    gain_parts = (
        lax.psum_scatter(d_a_gain, "fsdp", scatter_dimension=0, tiled=True),
        lax.psum_scatter(d_qn_gain, "fsdp", scatter_dimension=0, tiled=True),
        lax.psum_scatter(d_kn_gain, "fsdp", scatter_dimension=0, tiled=True),
        lax.psum_scatter(d_m_gain, "fsdp", scatter_dimension=0, tiled=True),
    )
    totals = (
        lax.psum(gain_parts[0].astype(jnp.bfloat16), "ctx").astype(jnp.float32),
        lax.psum(gain_parts[1].astype(jnp.bfloat16), "ctx").astype(jnp.float32),
        lax.psum(gain_parts[2].astype(jnp.bfloat16), "ctx").astype(jnp.float32),
        lax.psum(gain_parts[3].astype(jnp.bfloat16), "ctx").astype(jnp.float32),
        lax.psum(qkv_grad, "ctx").astype(jnp.float32),
        lax.psum(out_proj_grad, "ctx").astype(jnp.float32),
        lax.psum(gate_up_grad, "ctx").astype(jnp.float32),
        lax.psum(down_grad, "ctx").astype(jnp.float32),
    )
    q_width = QUERY_HEADS * HEAD_SIZE
    key_value_width = KEY_VALUE_HEADS * HEAD_SIZE
    qkv_total = totals[4]
    gate_up_total = totals[6]
    ff_width = w_gate.shape[1]
    return (
        first_pass[0].astype(jnp.bfloat16)[None],
        input_grad[None],
        totals[0],
        totals[1],
        totals[2],
        totals[3],
        qkv_total[:, :q_width],
        qkv_total[:, q_width : q_width + key_value_width],
        qkv_total[:, q_width + key_value_width :],
        totals[5],
        gate_up_total[:, :ff_width],
        gate_up_total[:, ff_width:],
        totals[7],
    )


CTX = ("z", "y")
FSDP = ("x", "core")
VMEM_BYTES = 62 << 20


def norm_back(values, gain_vec, grad):
    scale = lax.rsqrt(jnp.mean(values * values, axis=-1, keepdims=True) + eps)
    inner = gain_vec * grad
    d_values = scale * inner - values * (scale * scale * scale) * jnp.mean(
        values * inner, axis=-1, keepdims=True
    )
    return d_values, grad * values * scale


def half_turn(values):
    half = values.shape[-1] // 2
    return jnp.concatenate([-values[..., half:], values[..., :half]], axis=-1)


def rope_tables(token_position):
    half = HEAD_SIZE // 2
    frequency = theta_base ** (-(jnp.arange(half, dtype=jnp.float32) * 2.0) / HEAD_SIZE)
    angles = token_position.astype(jnp.float32)[:, None] * frequency[None, :]
    cosine, sine = jnp.cos(angles), jnp.sin(angles)
    return jnp.concatenate([cosine, cosine], axis=1), jnp.concatenate([sine, sine], axis=1)


def dot(a, b):
    return jnp.dot(a, b, preferred_element_type=jnp.float32)


def low(a):
    return a.astype(jnp.bfloat16)


def gather_fsdp_plain(block):
    return lax.all_gather(block, FSDP, axis=0, tiled=True)


def over(block, axis):
    return lax.ppermute(block, axis, [(0, 1), (1, 0)])


def half_sum(block, axis):
    place = lax.axis_index(axis)
    got = over(lax.dynamic_index_in_dim(block, 1 - place, 0, keepdims=False), axis)
    own = lax.dynamic_index_in_dim(block, place, 0, keepdims=False)
    return low(own.astype(jnp.float32) + got.astype(jnp.float32))


MESH_ID = pl.DeviceIdType.MESH
LINE = 4


class Net:
    def __init__(self, send, recv):
        self.send, self.recv, self.used = send, recv, 0
        self.z, self.y, self.x, self.core = (lax.axis_index(a) for a in CTX + FSDP)
        self.me = 2 * self.z + self.y
        self.open = []

    def at(self, dz=0, dy=0, dx=0, dc=0):
        return (
            self.z + dz,
            1 - self.y if dy else self.y,
            1 - self.x if dx else self.x,
            1 - self.core if dc else self.core,
        )

    def put(self, src, dst, target, sends=None, recvs=None):
        copy = Copy(self, src, dst, target, sends, recvs)
        self.open.append(copy)
        return copy

    def close(self):
        for copy in self.open:
            copy.arrived()
        for copy in self.open:
            copy.left()


def guarded(condition, action):
    if condition is None:
        action()
    else:
        pl.when(condition)(action)


class Copy:
    def __init__(self, net, src, dst, target, sends, recvs):
        i = net.used
        net.used += 1
        self.sends, self.recvs, self.waited = sends, recvs, False
        self.copy = pltpu.make_async_remote_copy(
            src, dst, net.send.at[i], net.recv.at[i], device_id=target, device_id_type=MESH_ID
        )
        guarded(sends, self.copy.start)

    def arrived(self):
        if not self.waited:
            self.waited = True
            guarded(self.recvs, self.copy.wait_recv)

    def left(self):
        guarded(self.sends, self.copy.wait_send)


class Local:
    def __init__(self, copy):
        self.copy, self.waited = copy, False
        copy.start()

    def arrived(self):
        if not self.waited:
            self.waited = True
            self.copy.wait()

    wait = arrived


def greet(net, kinds):
    barrier = pltpu.get_barrier_semaphore()
    partners = []
    if "z" in kinds:
        partners += [(net.at(dz=1), net.z < LINE - 1), (net.at(dz=-1), net.z > 0)]
    if "y" in kinds:
        partners.append((net.at(dy=1), None))
    if "x" in kinds:
        partners.append((net.at(dx=1), None))
    if "core" in kinds:
        partners.append((net.at(dc=1), None))
    if "far" in kinds:
        partners.append((net.at(dx=1, dc=1), None))
    if "ctx" in kinds:
        for k in range(1, 2 * LINE):
            other = lax.rem(net.me + k, 2 * LINE)
            partners.append(((other // 2, lax.rem(other, 2), net.x, net.core), None))
    for target, there in partners:
        guarded(
            there,
            lambda target=target: pl.semaphore_signal(
                barrier, inc=1, device_id=target, device_id_type=MESH_ID
            ),
        )
    ends = 0
    if "z" in kinds:
        ends = (net.z == 0).astype(jnp.int32) + (net.z == LINE - 1).astype(jnp.int32)
    pl.semaphore_wait(barrier, len(partners) - ends)


def drive(*programs):
    live = list(programs)
    while live:
        for program in list(live):
            if next(program, "end") == "end":
                live.remove(program)


def in_order(order, programs):
    for i in order:
        next(programs[i], None)
    for program in programs:
        for _ in program:
            pass


def by_steps(program):
    yield next(program)
    while next(program, "end") != "end":
        if next(program, "end") == "end":
            return
        yield


def along_line(net, own, view, slot, log=None):
    z = net.z
    up = net.put(own, view(slot(z)), net.at(dz=1), z < LINE - 1, z > 0)
    down = net.put(own, view(slot(z)), net.at(dz=-1), z > 0, z < LINE - 1)
    yield
    for s in range(1, LINE):
        from_low, from_high = z >= s, z + s <= LINE - 1
        up.arrived()
        low_block, high_block = view(slot(z - s)), view(slot(z + s))
        if s < LINE - 1:
            up = net.put(low_block, low_block, net.at(dz=1), from_low & (z < LINE - 1), z >= s + 1)
        if log is not None:
            log[s].append(net.put(low_block, low_block, net.at(dy=1), from_low, from_low))
        yield
        down.arrived()
        if s < LINE - 1:
            down = net.put(
                high_block, high_block, net.at(dz=-1), from_high & (z > 0), z + s + 1 <= LINE - 1
            )
        if log is not None:
            log[s].append(net.put(high_block, high_block, net.at(dy=1), from_high, from_high))
        yield


def gather_line_first(net, own, view, log=None):
    log = {s: [] for s in range(LINE)} if log is None else log
    log[0].append(net.put(own, view(net.me), net.at(dy=1)))
    yield from along_line(net, own, view, lambda z: 2 * z + net.y, log)


def gather_side_first(net, own, view):
    side = net.put(own, view(net.me), net.at(dy=1))
    first = along_line(net, own, view, lambda z: 2 * z + net.y)
    yield next(first)
    side.arrived()
    other = view(net.me + 1 - 2 * net.y)
    second = along_line(net, other, view, lambda z: 2 * z + 1 - net.y)
    for _ in second:
        next(first, None)
        yield


def gather_ctx_programs(net, own, out, cut):
    rows = own.shape[0]
    programs = [
        gather_line_first(
            net, own.at[pl.ds(0, cut)], lambda slot: out.at[slot, pl.ds(0, cut)]
        )
    ]
    if cut < rows:
        rest = pl.ds(cut, rows - cut)
        programs.append(gather_side_first(net, own.at[rest], lambda slot: out.at[slot, rest]))
    return programs


def gather_fsdp(net, own, out):
    f = 2 * net.x + net.core
    net.put(own, out.at[f], net.at(dc=1))
    over = net.put(own, out.at[f], net.at(dx=1))
    yield
    yield
    yield
    over.arrived()
    far = out.at[2 * (1 - net.x) + net.core]
    net.put(far, far, net.at(dc=1))
    yield


def gather_quad(net, own, out):
    q = 2 * net.y + net.core
    net.put(own, out.at[q], net.at(dc=1))
    over = net.put(own, out.at[q], net.at(dy=1))
    yield
    over.arrived()
    far = out.at[2 * (1 - net.y) + net.core]
    net.put(far, far, net.at(dc=1))
    yield


def swap_ctx(net, blocks, out):
    for k in range(1, 2 * LINE):
        other = lax.rem(net.me + k, 2 * LINE)
        net.put(
            blocks.at[other], out.at[net.me], (other // 2, lax.rem(other, 2), net.x, net.core)
        )
    yield


def own_copies(pairs, sem):
    copies = [pltpu.make_async_copy(src, dst, sem.at[i]) for i, (src, dst) in enumerate(pairs)]
    for copy in copies:
        copy.start()
    return copies


def net_call(body, outs, args, copies, locals_, number, scratch=(), vmem=(), smem=()):
    def kernel(*refs):
        *rest, send, recv, local = refs
        net = Net(send, recv)
        body(net, local, *rest)
        assert net.used <= copies, net.used

    any_space = pl.BlockSpec(memory_space=pl.ANY)
    in_vmem = pl.BlockSpec(memory_space=pltpu.VMEM)
    in_smem = pl.BlockSpec(memory_space=pltpu.SMEM)
    count = len(args)

    def place(i):
        return in_vmem if i in vmem else in_smem if i in smem else any_space

    return pl.pallas_call(
        kernel,
        out_shape=outs,
        in_specs=[place(i) for i in range(count)],
        out_specs=[place(count + i) for i in range(len(outs))],
        scratch_shapes=list(scratch)
        + [
            pltpu.SemaphoreType.DMA((copies,)),
            pltpu.SemaphoreType.DMA((copies,)),
            pltpu.SemaphoreType.DMA((max(1, locals_),)),
        ],
        compiler_params=pltpu.CompilerParams(
            collective_id=number, has_side_effects=True, vmem_limit_bytes=VMEM_BYTES
        ),
    )(*args)


def shape_of(*dims, kind=jnp.bfloat16):
    return jax.ShapeDtypeStruct(dims, kind)


def sum_line(net, held, send_up, send_down, got_up, got_down, ready):
    z = net.z
    ups, downs = [], []

    def fill(send, got, block, t, first):
        def alone():
            send[t] = low(held[block])

        def added():
            send[t] = low(held[block] + got[t - 1].astype(jnp.float32))

        return alone if first else added

    for t in range(LINE - 1):
        if t:
            ups[t - 1].arrived()
        ready(t)
        to_up, to_down = LINE - 1 - t + z, z - LINE + 1 + t
        up_on, down_on = (z <= t) & (z < LINE - 1), (z >= LINE - 1 - t) & (z > 0)
        pl.when(z == 0)(fill(send_up, got_up, to_up, t, True))
        if t:
            pl.when(up_on & (z >= 1))(fill(send_up, got_up, to_up, t, False))
        ups.append(
            net.put(
                send_up.at[t], got_up.at[t], net.at(dz=1), up_on, (z >= 1) & (z - 1 <= t)
            )
        )
        yield
        if t:
            downs[t - 1].arrived()
        pl.when(z == LINE - 1)(fill(send_down, got_down, to_down, t, True))
        if t:
            pl.when(down_on & (z <= LINE - 2))(fill(send_down, got_down, to_down, t, False))
        downs.append(
            net.put(
                send_down.at[t],
                got_down.at[t],
                net.at(dz=-1),
                down_on,
                (z <= LINE - 2) & (z + 1 >= LINE - 1 - t),
            )
        )
        yield
    last = LINE - 2

    def add_up():
        held[z] += got_up[last].astype(jnp.float32)

    def add_down():
        held[z] += got_down[last].astype(jnp.float32)

    ups[last].arrived()
    ready(LINE - 1)
    pl.when(z >= 1)(add_up)
    yield
    downs[last].arrived()
    pl.when(z <= LINE - 2)(add_down)


def far_first(z):
    return [
        jnp.where(z < 2, 3, 0),
        jnp.where(z < 2, 2, 1),
        z + 1 - 2 * lax.rem(z, 2),
        z,
    ]


def line_scratch(rows, cols):
    line = pltpu.VMEM((LINE - 1, rows, cols), jnp.bfloat16)
    return [pltpu.VMEM((LINE, rows, cols), jnp.float32), line, line, line, line]


def sum_sides(net, src, from_side, line, make=None):
    z, y = net.z, net.y
    held = line[0]
    order = far_first(z)
    sides = []
    for k in order:
        if make is not None:
            make(2 * k + 1 - y)
        sides.append(net.put(src.at[2 * k + 1 - y], from_side.at[k], net.at(dy=1)))
        if make is not None and len(sides) == 2:
            yield
    yield

    def ready(t):
        k = order[t]
        if make is not None:
            make(2 * k + y)
        sides[t].arrived()
        held[k] = src[2 * k + y].astype(jnp.float32) + from_side[k].astype(jnp.float32)

    yield from sum_line(net, *line, ready)


BLOCK = 256
BACK_ORDER = (
    7, 4, 0, 1, 4, 4, 5, 4, 7, 7, 7, 4, 7, 7, 7, 0, 7, 0, 4, 4, 7, 7, 0, 0, 4, 4, 0, 7, 0, 2,
    1, 1, 6, 4, 0, 4, 6, 0, 3, 3, 1, 0, 7, 1, 7, 3, 2, 0, 5, 3, 0, 4, 6, 7, 3, 0, 1, 7, 3, 0,
    1, 2, 6, 4, 6, 4, 7, 7, 2, 2, 6, 1, 6, 2, 2, 7, 0, 3, 3, 7, 2, 2, 1, 6, 1, 7, 0, 6, 8, 2,
    7, 2, 8, 2, 4, 2, 1, 2, 7, 0, 1, 2, 3, 1, 6, 3, 3, 1, 8, 2, 1, 3, 3, 6, 4, 3, 2, 3, 1, 1,
    2, 8,
)


def turn_lanes(v):
    return pltpu.roll(v, HEAD_SIZE // 2, 1)


def dot_last(a, b):
    return lax.dot_general(a, b, (((1,), (1,)), ((), ())), preferred_element_type=jnp.float32)


def resting(rounds):
    for _ in range(rounds):
        yield


class Bag:
    def __init__(self, **members):
        self.__dict__.update(members)


def bags(tree):
    if isinstance(tree, list):
        return [bags(v) for v in tree]
    return Bag(**{n: bags(v) for n, v in tree.items()}) if isinstance(tree, dict) else tree


def near_first(z):
    return far_first(z)[::-1]


def kernel_with(
    body, moved, loaded, outs, scratch, copies, number, in_vmem=(), near=(), scalar=()
):
    scratch = dict(
        scratch, held={n: pltpu.VMEM(v.shape, v.dtype) for n, v in loaded.items()}
    )
    flat, tree = jax.tree.flatten(scratch)
    f_in, in_tree = jax.tree.flatten((moved, loaded))
    f_out, out_tree = jax.tree.flatten(outs)

    def whole(net, local, *refs):
        given, to_load = jax.tree.unflatten(in_tree, refs[: len(f_in)])
        out = Bag(**jax.tree.unflatten(out_tree, refs[len(f_in) : len(f_in) + len(f_out)]))
        r = bags(jax.tree.unflatten(tree, refs[len(f_in) + len(f_out) :]))
        used = iter(range(96))

        def fetch(src, dst):
            return Local(pltpu.make_async_copy(src, dst, local.at[next(used)]))

        def load():
            return {n: fetch(to_load[n], getattr(r.held, n)) for n in to_load}

        body(net, fetch, load, Bag(**given), out, r)
        net.close()

    order = jax.tree.unflatten(out_tree, range(len(f_out)))
    in_order, _ = jax.tree.unflatten(in_tree, range(len(f_in)))
    result = net_call(
        whole,
        f_out,
        f_in,
        copies,
        96,
        number,
        scratch=flat,
        vmem=[len(f_in) + order.get(n) for n in in_vmem] + [in_order.get(n) for n in near],
        smem=[in_order.get(n) for n in scalar],
    )
    return Bag(**jax.tree.unflatten(out_tree, result))


def middle(net, fetch, arriving, out, r):
    y, core, me = net.y, net.core, net.me
    slots, rows, width = r.mixed_in.shape
    _, shard, wide = r.w_gu.shape
    ff, d = wide // 2, r.residual.shape[1]
    piece, pad = rows // slots, 32
    f32, bf = jnp.float32, jnp.bfloat16
    every = pl.ds(0, rows)
    parts = [pl.ds(0, rows // 2), pl.ds(rows // 2, rows // 2)]

    def land(copies):
        for c in copies:
            c.arrived()

    def from_head(head):
        at = pl.ds(pl.multiple_of(lax.rem(head, 2) * width, width), width)
        return dot(r.mixed_in[head], r.w_o[head // 2, at])

    land(arriving.o)
    arriving.heads[-1].arrived()
    total = r.residual[...].astype(f32) + from_head(me)
    for k in range(1, slots):
        arriving.heads[k - 1].arrived()
        total = total + from_head(lax.rem(me + slots - k, slots))
    r.middle[...] = total
    own, far = 2 * y + core, 2 * (1 - y) + core
    r.quad[own] = low(root_mean_norm(total, r.m_gain[...]))
    near = net.put(r.quad.at[own], r.quad.at[own], net.at(dc=1))
    over = [net.put(r.quad.at[own, at], r.quad.at[own, at], net.at(dy=1)) for at in parts]
    arriving.results.append(fetch(r.mixed_in, out.mixed_in))
    near.arrived()
    land(arriving.gu)
    land(arriving.grad)

    def pair(ref, side, at):
        return ref[pl.ds(2 * side, 2), at].reshape(2 * at.size, ref.shape[-1])

    def forward(side, at):
        gate_up = dot(pair(r.quad, side, at), r.w_gu[...].reshape(4 * shard, 2 * ff))
        return gate_up[:, :ff], gate_up[:, ff:]

    def backward(side, at, gate, up):
        d_hidden = dot_last(pair(r.grad, side, at), r.w_dn[...].reshape(ff, d))
        sig = 1.0 / (1.0 + jnp.exp(-gate))
        silu = gate * sig
        d_gate = low(d_hidden * up * (sig * (1.0 + gate * (1.0 - sig))))
        both, split = pl.ds(2 * side, 2), (2, at.size, ff)
        r.hidden[both, at] = low(silu * up).reshape(split)
        r.d_gu[both, at, pl.ds(0, ff)] = d_gate.reshape(split)
        r.d_gu[both, at, pl.ds(ff, ff)] = low(d_hidden * silu).reshape(split)

    def part(side, at):
        w_gu = r.w_gu[...].reshape(4 * shard, 2 * ff)
        return dot_last(pair(r.d_gu, side, at), w_gu).reshape(2, at.size, d)

    def out_part(side):
        return dot(pair(r.hidden, side, every), r.w_dn[...].reshape(ff, d)).reshape(2, rows, d)

    near_values = forward(y, every)
    over[0].arrived()
    last = [net.put(r.quad.at[far, parts[0]], r.quad.at[far, parts[0]], net.at(dc=1))]
    land(arriving.dn)
    backward(y, every, *near_values)
    over[1].arrived()
    last.append(net.put(r.quad.at[far, parts[1]], r.quad.at[far, parts[1]], net.at(dc=1)))
    one, side = [], []

    def far_part(i):
        at = parts[i]
        last[i].arrived()
        backward(1 - y, at, *forward(1 - y, at))
        r.far_part[:, at] = low(part(1 - y, at))
        one.append(net.put(r.far_part.at[1 - core, at], r.got.at[0, at], net.at(dc=1)))

    def far_sum(i):
        at = parts[i]
        one[i].arrived()
        r.to_side[0, at] = low(r.far_part[core, at].astype(f32) + r.got[0, at].astype(f32))
        side.append(net.put(r.to_side.at[0, at], r.got.at[2, at], net.at(dy=1)))

    far_part(0)
    r.near_part[...] = part(y, every)
    r.beside[...] = low(r.near_part[1 - core])
    two = net.put(r.beside, r.got.at[1], net.at(dc=1))
    far_sum(0)
    far_part(1)
    r.far_out[...] = low(out_part(1 - y))
    far_sum(1)
    g = r.grad[...].reshape(4 * rows, d)
    r.g_dn[...] = low(outer_rows(r.hidden[...].reshape(4 * rows, ff), g)).reshape(2, ff // 2, d)
    sent = [fetch(r.g_dn, out.down)]
    some = pl.ds(0, d // 2)
    dn_over = net.put(r.g_dn.at[1 - net.x, :, some], r.dn_got, net.at(dx=1))
    one_out = net.put(r.far_out.at[1 - core], r.got.at[3], net.at(dc=1))
    r.near_out[...] = out_part(y)
    r.beside_out[...] = low(r.near_out[1 - core])
    two_out = net.put(r.beside_out, r.got.at[4], net.at(dc=1))
    n2 = r.quad[...].reshape(4 * rows, d)
    d_gu = r.d_gu[...].reshape(4 * rows, 2 * ff)
    r.g_gate[...] = low(outer_rows(n2, d_gu[:, :ff]))
    sent.append(fetch(r.g_gate, out.gate))
    one_out.arrived()
    r.to_side[1] = low(r.far_out[core].astype(f32) + r.got[3].astype(f32))
    side_out = net.put(r.to_side.at[1], r.got.at[5], net.at(dy=1))
    r.g_up[...] = low(outer_rows(n2, d_gu[:, ff:]))
    sent.append(fetch(r.g_up, out.up))
    two.arrived()
    land(side)
    d_normed = r.near_part[core] + r.got[1].astype(f32) + r.got[2].astype(f32)
    dx2, dg2 = norm_back(r.middle[...], r.m_gain[...], d_normed)
    out.dg2[...] = jnp.sum(dg2, axis=0, keepdims=True)
    middle_low = low(r.grad[own].astype(f32) + dx2)
    for i in range(slots):
        r.dm[i] = low(dot_last(middle_low, r.w_o[i // 2, pl.ds(i % 2 * width, width)]))
    sent.append(fetch(r.dm, out.dm))
    for i in range(slots):
        out.back[i, pl.ds(0, piece)] = middle_low[i * piece : (i + 1) * piece]
        out.back[i, pl.ds(piece, pad - piece)] = jnp.zeros((pad - piece, d), bf)
    out.middle_low[...] = middle_low
    two_out.arrived()
    side_out.arrived()
    out.output[...] = low(
        r.middle[...] + r.near_out[core] + r.got[4].astype(f32) + r.got[5].astype(f32)
    )
    dn_over.arrived()
    out.down_sum[...] = low(
        r.g_dn[net.x, :, some].astype(f32) + r.dn_got[...].astype(f32)
    )
    land(sent)
    land(arriving.results)


def front_kernel(moved, loaded, number):
    a = Bag(**moved)
    _, rows, d = a.tok.shape
    slots = 2 * LINE
    count = rows * slots
    blocks = count // BLOCK
    width = 2 * HEAD_SIZE
    shard = a.w_q.shape[0]
    half = a.w_gate.shape[1] // 8
    o_rows = a.w_o.shape[0]
    scale = HEAD_SIZE**-0.5
    bf, f32 = jnp.bfloat16, jnp.float32
    piece = rows // slots
    ff = 2 * half
    gain_cols = 2 * a.attn_gain.shape[0] + 2 * HEAD_SIZE

    scratch = dict(
        tok=pltpu.VMEM((slots, rows, d), bf),
        w_qkv=pltpu.VMEM((4, shard, 2 * width), bf),
        gains=pltpu.VMEM((4, 1, gain_cols), f32),
        columns=pltpu.VMEM((count, 8), f32),
        normed=pltpu.VMEM((count, d), bf),
        qkv=pltpu.VMEM((count, 2 * width), f32),
        q=pltpu.VMEM((count, width), bf),
        k=pltpu.VMEM((count, HEAD_SIZE), bf),
        v=pltpu.VMEM((count, HEAD_SIZE), bf),
        kt=pltpu.VMEM((HEAD_SIZE, count), bf),
        vt=pltpu.VMEM((HEAD_SIZE, count), bf),
        cos=pltpu.VMEM((count, HEAD_SIZE), f32),
        sin=pltpu.VMEM((count, HEAD_SIZE), f32),
        mixed=pltpu.VMEM((count, width), f32),
        mixed_low=pltpu.VMEM((count, width), bf),
        sent=pltpu.VMEM((slots, rows, width), bf),
        w_o=pltpu.VMEM((4, o_rows, d), bf),
        w_gu=pltpu.VMEM((4, shard, 4 * half), bf),
        grad=pltpu.VMEM((4, rows, d), bf),
        mixed_in=pltpu.VMEM((slots, rows, width), bf),
        residual=pltpu.VMEM((rows, d), bf),
        m_gain=pltpu.VMEM((1, d), f32),
        w_dn=pltpu.VMEM((2, half, d), bf),
        middle=pltpu.VMEM((rows, d), f32),
        quad=pltpu.VMEM((4, rows, d), bf),
        hidden=pltpu.VMEM((4, rows, ff), bf),
        d_gu=pltpu.VMEM((4, rows, 2 * ff), bf),
        near_part=pltpu.VMEM((2, rows, d), f32),
        far_part=pltpu.VMEM((2, rows, d), bf),
        near_out=pltpu.VMEM((2, rows, d), f32),
        far_out=pltpu.VMEM((2, rows, d), bf),
        beside=pltpu.VMEM((rows, d), bf),
        beside_out=pltpu.VMEM((rows, d), bf),
        got=pltpu.VMEM((6, rows, d), bf),
        to_side=pltpu.VMEM((2, rows, d), bf),
        g_gate=pltpu.VMEM((d, ff), bf),
        g_up=pltpu.VMEM((d, ff), bf),
        g_dn=pltpu.VMEM((2, half, d), bf),
        dn_got=pltpu.VMEM((half, d // 2), bf),
        dm=pltpu.VMEM((slots, rows, width), bf),
    )
    outs = dict(
        first=shape_of(1, count, kind=jnp.int32),
        dealt=shape_of(1, count, kind=jnp.int32),
        back_from=shape_of(rows, 1, kind=jnp.int32),
        mixed_in=shape_of(slots, rows, width),
        normed=shape_of(count, d),
        qkv=shape_of(count, 2 * width, kind=f32),
        q=shape_of(count, width),
        k=shape_of(count, HEAD_SIZE),
        v=shape_of(count, HEAD_SIZE),
        kt=shape_of(HEAD_SIZE, count),
        cos=shape_of(count, HEAD_SIZE, kind=f32),
        sin=shape_of(count, HEAD_SIZE, kind=f32),
        mixed=shape_of(count, width, kind=f32),
        lse=shape_of(2, 1, count, kind=f32),
        w_qkv=shape_of(4, shard, 2 * width),
        a_gain=shape_of(1, d, kind=f32),
        q_gain=shape_of(1, HEAD_SIZE, kind=f32),
        k_gain=shape_of(1, HEAD_SIZE, kind=f32),
        output=shape_of(rows, d),
        back=shape_of(slots, 32, d),
        dm=shape_of(slots, rows, width),
        gate=shape_of(d, ff),
        up=shape_of(d, ff),
        down=shape_of(2, half, d),
        down_sum=shape_of(half, d // 2),
        middle_low=shape_of(rows, d),
        dg2=shape_of(1, d, kind=f32),
    )

    def body(net, fetch, load, given, out, r):
        z, y, x, core, me = net.z, net.y, net.x, net.core, net.me
        f = 2 * x + core
        done = set()
        tok = given.tok.at[0]
        tok_own = fetch(tok, r.tok.at[me])

        def lanes(start, size):
            return pl.ds(pl.multiple_of(start, HEAD_SIZE), size)

        head_parts = [
            (given.w_q.at[:, lanes(me * width, width)], pl.ds(0, width)),
            (given.w_k.at[:, lanes(me * HEAD_SIZE, HEAD_SIZE)], pl.ds(width, HEAD_SIZE)),
            (
                given.w_v.at[:, lanes(me * HEAD_SIZE, HEAD_SIZE)],
                pl.ds(width + HEAD_SIZE, HEAD_SIZE),
            ),
        ]
        w_own = [fetch(src, r.w_qkv.at[f, :, to]) for src, to in head_parts]
        greet(net, ("ctx", "x", "core", "far"))
        log = {s: [] for s in range(LINE)}
        waits = list(w_own)
        zone = lax.broadcasted_iota(jnp.int32, (1, HEAD_SIZE), 1) // (HEAD_SIZE // 4) == f

        def zoned(ref):
            return jnp.where(zone, jnp.concatenate([ref[...].astype(f32)] * 4, axis=1), 0.0)

        r.gains[f] = jnp.concatenate(
            [
                given.attn_gain[...].astype(f32).reshape(1, -1),
                given.mlp_gain[...].astype(f32).reshape(1, -1),
                zoned(given.q_gain),
                zoned(given.k_gain),
            ],
            axis=1,
        )

        def head_weights():
            beside = [net.put(src, r.w_qkv.at[f, :, to], net.at(dc=1)) for src, to in head_parts]
            beside.append(net.put(r.gains.at[f], r.gains.at[f], net.at(dc=1)))
            across = [net.put(src, r.w_qkv.at[f, :, to], net.at(dx=1)) for src, to in head_parts]
            across.append(net.put(r.gains.at[f], r.gains.at[f], net.at(dx=1)))
            yield
            for c in across:
                c.arrived()
            far = 2 * (1 - x) + core
            beside += [
                net.put(r.w_qkv.at[far], r.w_qkv.at[far], net.at(dc=1)),
                net.put(r.gains.at[far], r.gains.at[far], net.at(dc=1)),
            ]
            for c in waits:
                c.wait()
            for c in beside:
                c.arrived()
            r.own = fetch(r.w_qkv, out.w_qkv)
            done.add("head")
            yield

        arriving = Bag(o=[], gu=[], dn=[], grad=[], heads=[], results=[])

        def other_weights():
            yield
            arriving.o += [
                fetch(given.w_o, r.w_o.at[f]),
                net.put(given.w_o, r.w_o.at[f], net.at(dx=1)),
                net.put(given.w_o, r.w_o.at[f], net.at(dc=1)),
            ]

            def quarter(c):
                return [
                    (
                        w.at[:, lanes((2 * xs + c) * 2 * half + y * half, half)],
                        r.w_gu.at[f, :, pl.ds((2 * i + xs) * half, half)],
                    )
                    for i, w in enumerate((given.w_gate, given.w_up))
                    for xs in range(2)
                ]

            arriving.gu += [fetch(src, to) for src, to in quarter(core)]
            arriving.gu += [net.put(src, to, net.at(dc=1)) for src, to in quarter(1 - core)]
            arriving.gu += [net.put(src, to, net.at(dx=1)) for src, to in quarter(core)]
            arriving.gu += [net.put(src, to, net.at(dx=1, dc=1)) for src, to in quarter(1 - core)]
            part = given.w_down.at[pl.ds(pl.multiple_of(y * half, half), half)]
            arriving.dn += [
                fetch(part, r.w_dn.at[x]),
                net.put(part, r.w_dn.at[x], net.at(dx=1)),
            ]
            yield from resting(7)
            arriving.o[1].arrived()
            far = r.w_o.at[2 * (1 - x) + core]
            arriving.o.append(net.put(far, far, net.at(dc=1)))

        def output_grad():
            yield from resting(5)
            own = r.grad.at[2 * y + core]
            grad = given.grad.at[0]
            arriving.grad += [
                fetch(grad, own),
                net.put(grad, own, net.at(dc=1)),
                net.put(grad, own, net.at(dy=1)),
            ]
            yield
            arriving.grad[2].arrived()
            far = r.grad.at[2 * (1 - y) + core]
            arriving.grad.append(net.put(far, far, net.at(dc=1)))

        def project(slot):
            at = pl.ds(pl.multiple_of(slot * rows, rows), rows)
            normed = low(root_mean_norm(r.tok[slot].astype(f32), out.a_gain[...]))
            r.normed[at] = normed
            qkv = dot(normed, r.w_qkv[...].reshape(4 * shard, 2 * width))
            r.qkv[at] = qkv
            cos, sin = r.cos[at], r.sin[at]

            def turned(part, gain):
                v = root_mean_norm(part, gain)
                return low(v * cos + turn_lanes(v) * sin)

            for g in range(2):
                cols = pl.ds(g * HEAD_SIZE, HEAD_SIZE)
                r.q[at, cols] = turned(
                    qkv[:, g * HEAD_SIZE : (g + 1) * HEAD_SIZE], out.q_gain[...]
                )
            r.k[at] = turned(qkv[:, width : width + HEAD_SIZE], out.k_gain[...])
            r.v[at] = low(qkv[:, width + HEAD_SIZE :])

        def main():
            ids = lax.broadcasted_iota(jnp.int32, (1, count), 1)
            first, dealt, back, start = jnp.zeros_like(ids), ids, ids, 0
            for i in range(1, given.lengths.shape[1]):
                start = start + given.lengths[0, i - 1]
                first = jnp.where(ids >= start, start, first)
            for s in range(slots):
                for j in range(slots):
                    begin = given.deal[0, s, j] * rows + s * piece
                    dealt = jnp.where(
                        (ids >= begin) & (ids < begin + piece),
                        ids - begin + (s * rows + j * piece),
                        dealt,
                    )
            for j in range(slots):
                begin = given.deal[0, me, j] * 32
                back = jnp.where(
                    (ids >= j * piece) & (ids < (j + 1) * piece), ids - j * piece + begin, back
                )
            out.first[...] = first
            out.dealt[...] = dealt
            row = lax.broadcasted_iota(jnp.int32, (8, count), 0)
            stack = jnp.where(row == 0, ids - first, jnp.where(row == 1, dealt, back))
            r.columns[...] = jnp.transpose(stack.astype(f32))
            out.back_from[...] = r.columns[pl.ds(0, rows), 2:3].astype(jnp.int32)
            for i in range(slots):
                at = pl.ds(i * rows, rows)
                angle = r.columns[at, 0:1] * given.freq[0:1]
                r.cos[at] = jnp.cos(angle)
                r.sin[at] = jnp.sin(angle) * given.freq[1:2]
            yield
            while "head" not in done:
                yield
            gains = [r.gains[i] for i in range(4)]
            part = d // 4
            for i in range(4):
                out.a_gain[:, pl.ds(i * part, part)] = gains[i][:, :part]
                r.m_gain[:, pl.ds(i * part, part)] = gains[i][:, part : 2 * part]
            total = gains[0] + gains[1] + gains[2] + gains[3]
            out.q_gain[...] = total[:, 2 * part : 2 * part + HEAD_SIZE]
            out.k_gain[...] = total[:, 2 * part + HEAD_SIZE :]
            tok_own.wait()
            near = near_first(z)
            for k in range(LINE):
                project(2 * near[k] + y)
                if k:
                    for c in log[k - 1]:
                        c.arrived()
                    project(2 * near[k - 1] + 1 - y)
                yield
            for c in log[LINE - 1]:
                c.arrived()
            project(2 * near[LINE - 1] + 1 - y)
            results = [
                fetch(r.normed, out.normed),
                fetch(r.qkv, out.qkv),
                fetch(r.q, out.q),
                fetch(r.k, out.k),
                fetch(r.v, out.v),
                fetch(r.cos, out.cos),
                fetch(r.sin, out.sin),
                r.own,
            ]
            for i in range(blocks):
                at = pl.ds(i * BLOCK, BLOCK)
                r.kt[:, at] = jnp.transpose(r.k[at])
                r.vt[:, at] = jnp.transpose(r.v[at])
            results.append(fetch(r.kt, out.kt))
            for i in range(blocks):
                here = pl.ds(i * BLOCK, BLOCK)
                first = out.first[:, here]
                t = i * BLOCK + lax.broadcasted_iota(jnp.int32, (BLOCK, BLOCK), 1)
                q = [r.q[here, pl.ds(g * HEAD_SIZE, HEAD_SIZE)] for g in range(2)]

                def step(n, held, i=i, q=q, first=first, t=t):
                    j = i - n
                    at = pl.ds(pl.multiple_of(j * BLOCK, BLOCK), BLOCK)
                    k, vt = r.k[at], r.vt[:, at]
                    u = j * BLOCK + lax.broadcasted_iota(jnp.int32, (BLOCK, BLOCK), 0)
                    allowed = (u >= first) & (u <= t)
                    result = []
                    for g in range(2):
                        top, total, mixed = held[g]
                        scores = jnp.where(allowed, dot_last(k, q[g]) * scale, negative_filler)
                        new = jnp.maximum(top, jnp.max(scores, axis=0, keepdims=True))
                        fade = jnp.exp(top - new)
                        p = jnp.exp(scores - new)
                        total = total * fade + jnp.sum(p, axis=0, keepdims=True)
                        result.append((new, total, mixed * fade + dot(vt, low(p))))
                    return tuple(result)

                row = jnp.full((1, BLOCK), negative_filler, f32)
                none = (row, jnp.zeros((1, BLOCK), f32), jnp.zeros((HEAD_SIZE, BLOCK), f32))
                held = lax.fori_loop(0, i + 1, step, (none, none))
                for g in range(2):
                    top, total, mixed = held[g]
                    cols = pl.ds(g * HEAD_SIZE, HEAD_SIZE)
                    out.lse[g, :, here] = top + jnp.log(total)
                    mixed = jnp.transpose(mixed / total)
                    r.mixed[here, cols] = mixed
                    r.mixed_low[here, cols] = low(mixed)
                yield
            results.append(fetch(r.mixed, out.mixed))
            ids = lax.broadcasted_iota(jnp.int32, (rows, count), 1)

            def hot(slot):
                at = pl.ds(pl.multiple_of(slot * rows, rows), rows)
                return low(jnp.where(r.columns[at, 1:2].astype(jnp.int32) == ids, 1.0, 0.0))

            for k in range(1, slots):
                other = lax.rem(me + k, slots)
                r.sent[other] = low(dot(hot(other), r.mixed_low[...]))
                there = (other // 2, lax.rem(other, 2), x, core)
                arriving.heads.append(net.put(r.sent.at[other], r.mixed_in.at[me], there))
            mine = hot(me)
            r.sent[me] = low(dot(mine, r.mixed_low[...]))
            arriving.heads.append(fetch(r.sent.at[me], r.mixed_in.at[me]))
            r.residual[...] = low(dot(mine, r.tok[...].reshape(count, d)))
            arriving.results += results
            yield

        drive(
            head_weights(),
            by_steps(gather_line_first(net, tok, lambda slot: r.tok.at[slot], log)),
            main(),
            other_weights(),
            output_grad(),
        )
        middle(net, fetch, arriving, out, r)

    return kernel_with(
        body,
        moved,
        loaded,
        outs,
        scratch,
        110,
        number,
        (
            "lse",
            "a_gain",
            "q_gain",
            "k_gain",
            "first",
            "dealt",
            "back_from",
            "output",
            "back",
            "middle_low",
            "dg2",
            "down_sum",
        ),
        ("attn_gain", "mlp_gain", "q_gain", "k_gain", "freq"),
        ("lengths", "deal"),
    )


def back_kernel(dims, number):
    rows, count = dims
    blocks = count // BLOCK
    scale = HEAD_SIZE**-0.5
    width = 2 * HEAD_SIZE
    d = MODEL_WIDTH

    def run(moved, loaded):
        a = Bag(**moved)
        gu_rows, gu_cols = a.gate.shape[1:]
        dn_rows = a.down.shape[1]
        o_rows = 2 * width
        bf, f32 = jnp.bfloat16, jnp.float32
        z_gu, z_dn, z_o = gu_rows // LINE, dn_rows // LINE, o_rows // (2 * LINE)
        gain_width = 2 * d + 2 * HEAD_SIZE

        def quarter():
            return dict(
                got=pltpu.VMEM((2, gu_rows, gu_cols), bf),
                own=pltpu.VMEM((2, gu_rows, gu_cols), bf),
                low=pltpu.VMEM((2, z_gu, gu_cols), bf),
                pair=pltpu.VMEM((2, z_gu, gu_cols), bf),
                line=line_scratch(2 * z_gu, gu_cols),
            )

        scratch = dict(
            held={n: pltpu.VMEM(v.shape, v.dtype) for n, v in loaded.items()},
            gate=quarter(),
            up=quarter(),
            down=[
                dict(
                    own=pltpu.VMEM((dn_rows, d // 2), bf),
                    got=pltpu.VMEM((dn_rows, d // 2), bf),
                    low=pltpu.VMEM((z_dn, d // 2), bf),
                    line=line_scratch(z_dn, d // 2),
                )
                for _ in range(2)
            ],
            o=dict(
                own=pltpu.VMEM((4, o_rows, d), bf),
                core=pltpu.VMEM((2, o_rows, d), bf),
                got=pltpu.VMEM((o_rows, d), bf),
                sum=pltpu.VMEM((2 * LINE, z_o, d), bf),
                side=pltpu.VMEM((LINE, z_o, d), bf),
                low=pltpu.VMEM((z_o, d), bf),
                line=line_scratch(z_o, d),
            ),
            h=dict(
                own=pltpu.VMEM((4, d // 4, 2 * width), bf),
                core=pltpu.VMEM((2, d // 4, 2 * width), bf),
                got=pltpu.VMEM((d // 4, 2 * width), bf),
                low=pltpu.VMEM((d // 4, 2 * width), bf),
            ),
            dm_all=pltpu.VMEM((2 * LINE, rows, width), bf),
            back=pltpu.VMEM(a.back.shape, bf),
            do=pltpu.VMEM((count, width), bf),
            dk=pltpu.VMEM((count, HEAD_SIZE), f32),
            dv=pltpu.VMEM((count, HEAD_SIZE), f32),
            dqkv=pltpu.VMEM((count, 2 * width), bf),
            dgq=pltpu.VMEM((1, HEAD_SIZE), f32),
            dgk=pltpu.VMEM((1, HEAD_SIZE), f32),
            part=dict(
                sum=pltpu.VMEM((2 * LINE, rows, d), bf),
                side=pltpu.VMEM((LINE, rows, d), bf),
                line=line_scratch(rows, d),
            ),
            g=dict(
                mine=pltpu.VMEM((1, gain_width), f32),
                four=pltpu.VMEM((1, gain_width), f32),
                got=pltpu.VMEM((3, 1, gain_width), f32),
                all=pltpu.VMEM((2 * LINE, 1, gain_width), f32),
            ),
        )
        flat, tree = jax.tree.flatten(scratch)
        f_in, in_tree = jax.tree.flatten((moved, loaded))
        outs = dict(
            input_grad=shape_of(rows, d, kind=f32),
            a_grad=shape_of(1, d // 4, kind=f32),
            m_grad=shape_of(1, d // 4, kind=f32),
            q_grad=shape_of(1, HEAD_SIZE // 4, kind=f32),
            k_grad=shape_of(1, HEAD_SIZE // 4, kind=f32),
            gate=shape_of(2 * LINE, 2, z_gu, gu_cols),
            up=shape_of(2 * LINE, 2, z_gu, gu_cols),
            down=shape_of(2 * LINE, z_dn, d),
            o=shape_of(2 * LINE, z_o, d),
            heads=shape_of(2 * LINE, d // 4, 2 * width),
        )
        f_out, out_tree = jax.tree.flatten(outs)

        def body(net, local, *refs):
            given, to_load = jax.tree.unflatten(in_tree, refs[: len(f_in)])
            given = Bag(**given)
            out = Bag(**jax.tree.unflatten(out_tree, refs[len(f_in) : len(f_in) + len(f_out)]))
            r = bags(jax.tree.unflatten(tree, refs[len(f_in) + len(f_out) :]))
            h = r.held
            z, y, x, core, me = net.z, net.y, net.x, net.core, net.me
            slots = 2 * LINE
            used = iter(range(64))

            def fetch(src, dst):
                return Local(pltpu.make_async_copy(src, dst, local.at[next(used)]))

            greet(net, ("ctx", "x", "core", "far"))
            loads = {n: fetch(to_load[n], getattr(h, n)) for n in to_load}
            dm_own = fetch(given.dm.at[me], r.dm_all.at[me])
            back_own = fetch(given.back.at[me], r.back.at[me])
            gate_own, up_own = (
                [fetch(src.at[2 * x + c], piece.own.at[c]) for c in range(2)]
                for src, piece in ((given.gate, r.gate), (given.up, r.up))
            )
            columns = [pl.ds(0, d // 2), pl.ds(d // 2, d // 2)]
            down_own = [
                fetch(given.down_sum, r.down[0].own),
                fetch(given.down.at[x, :, columns[1]], r.down[1].own),
            ]
            back_copies = []

            def need(*which):
                for n in which:
                    if n in loads:
                        loads.pop(n).wait()

            def to_all(src, out):
                copies = []
                for k in range(1, slots):
                    other = lax.rem(me + k, slots)
                    there = (other // 2, lax.rem(other, 2), x, core)
                    copies.append(net.put(src(other), out.at[me], there))
                return copies

            def back_rows():
                back_copies.extend(to_all(lambda other: given.back.at[other], r.back))
                yield

            def main():
                dm_copies = to_all(lambda other: given.dm.at[other], r.dm_all)
                yield
                need(*list(loads))
                dm_own.wait()
                for c in dm_copies:
                    c.arrived()
                yield
                for i in range(blocks):
                    t = i * BLOCK + lax.broadcasted_iota(jnp.int32, (BLOCK, count), 0)
                    hot = low(jnp.where(h.dealt[...] == t, 1.0, 0.0))
                    r.do[pl.ds(i * BLOCK, BLOCK)] = low(
                        dot(hot, r.dm_all[...].reshape(count, width))
                    )
                r.dk[...] = jnp.zeros_like(r.dk)
                r.dv[...] = jnp.zeros_like(r.dv)
                yield
                dgq = jnp.zeros((1, HEAD_SIZE), f32)
                for i in range(blocks):
                    here = pl.ds(i * BLOCK, BLOCK)
                    first = h.first[:, here]
                    t = i * BLOCK + lax.broadcasted_iota(jnp.int32, (BLOCK, BLOCK), 1)
                    heads = []
                    for g in range(2):
                        lanes = pl.ds(g * HEAD_SIZE, HEAD_SIZE)
                        q, do = h.q[here, lanes], r.do[here, lanes]
                        product = do.astype(f32) * h.mixed[here, lanes]
                        delta = jnp.sum(jnp.transpose(product), axis=0, keepdims=True)
                        heads.append((q, do, h.lse[g, :, here], delta))

                    def step(j, held, heads=heads, first=first, t=t):
                        at = pl.ds(pl.multiple_of(j * BLOCK, BLOCK), BLOCK)
                        k, v, kt = h.k[at], h.v[at], h.kt[:, at]
                        u = j * BLOCK + lax.broadcasted_iota(jnp.int32, (BLOCK, BLOCK), 0)
                        allowed = (u >= first) & (u <= t)
                        dk, dv, out = r.dk[at], r.dv[at], []
                        for (q, do, lse, delta), dq in zip(heads, held):
                            p = jnp.where(allowed, jnp.exp(dot_last(k, q) * scale - lse), 0.0)
                            ds = low(p * (dot_last(v, do) - delta))
                            dv = dv + dot(low(p), do)
                            dk = dk + dot(ds, q)
                            out.append(dq + dot(kt, ds))
                        r.dk[at] = dk
                        r.dv[at] = dv
                        return tuple(out)

                    zero = jnp.zeros((HEAD_SIZE, BLOCK), f32)
                    result = lax.fori_loop(0, i + 1, step, (zero, zero))
                    cos, sin = h.cos[here], h.sin[here]
                    for g in range(2):
                        lanes = pl.ds(g * HEAD_SIZE, HEAD_SIZE)
                        grad = jnp.transpose(result[g]) * scale
                        grad = grad * cos - turn_lanes(grad) * sin
                        dx, dg = norm_back(h.qkv[here, lanes], h.q_gain[...], grad)
                        r.dqkv[here, lanes] = low(dx)
                        dgq = dgq + jnp.sum(dg, axis=0, keepdims=True)
                    yield
                dgk = jnp.zeros((1, HEAD_SIZE), f32)
                for i in range(blocks):
                    here = pl.ds(i * BLOCK, BLOCK)
                    grad = r.dk[here] * scale
                    grad = grad * h.cos[here] - turn_lanes(grad) * h.sin[here]
                    dx, dg = norm_back(
                        h.qkv[here, pl.ds(width, HEAD_SIZE)], h.k_gain[...], grad
                    )
                    r.dqkv[here, pl.ds(width, HEAD_SIZE)] = low(dx)
                    r.dqkv[here, pl.ds(width + HEAD_SIZE, HEAD_SIZE)] = low(r.dv[here])
                    dgk = dgk + jnp.sum(dg, axis=0, keepdims=True)
                r.dgq[...] = dgq
                r.dgk[...] = dgk
                yield

                def make(slot):
                    at = pl.ds(pl.multiple_of(slot * rows, rows), rows)
                    r.part.sum[slot] = low(dot_last(r.dqkv[at], h.w_qkv[...].reshape(d, 2 * width)))

                yield from sum_sides(net, r.part.sum, r.part.side, r.part.line, make)
                yield
                dx1, dg1 = norm_back(
                    h.tok[0].astype(f32), h.a_gain[...], r.part.line[0][z]
                )
                for c in back_copies:
                    c.arrived()
                back_own.wait()
                ids = lax.broadcasted_iota(jnp.int32, (rows, slots * a.back.shape[1]), 1)
                hot = low(jnp.where(h.back_from[...] == ids, 1.0, 0.0))
                out.input_grad[...] = dx1 + dot(hot, r.back[...].reshape(-1, d))
                r.g.mine[:, pl.ds(0, d)] = jnp.sum(dg1, axis=0, keepdims=True)
                r.g.mine[:, pl.ds(d, d)] = h.dg2[...]
                r.g.mine[:, pl.ds(2 * d, HEAD_SIZE)] = r.dgq[...]
                r.g.mine[:, pl.ds(2 * d + HEAD_SIZE, HEAD_SIZE)] = r.dgk[...]
                yield

            def gains():
                sides = [net.at(dc=1), net.at(dx=1), net.at(dx=1, dc=1)]
                pair = [net.put(r.g.mine, r.g.got.at[i], to) for i, to in enumerate(sides)]
                yield
                for c in pair:
                    c.arrived()
                along = r.g.mine[...] + r.g.got[0]
                across = r.g.got[1] + r.g.got[2]
                r.g.four[...] = along + across
                r.g.all[me] = r.g.four[...]
                copies = to_all(lambda other: r.g.four, r.g.all)
                yield
                for c in copies:
                    c.arrived()
                total = jnp.sum(r.g.all[...], axis=0)

                def own_part(start, size):
                    part = total[:, start : start + size]
                    for i in range(1, 4):
                        at = start + i * size
                        part = jnp.where(2 * x + core == i, total[:, at : at + size], part)
                    return part

                out.a_grad[...] = own_part(0, d // 4)
                out.m_grad[...] = own_part(d, d // 4)
                out.q_grad[...] = own_part(2 * d, HEAD_SIZE // 4)
                out.k_grad[...] = own_part(2 * d + HEAD_SIZE, HEAD_SIZE // 4)
                yield

            def gate_or_up(src, own, piece, gathered):
                over = [
                    net.put(src.at[2 * (1 - x) + c], piece.got.at[c], net.at(dx=1))
                    for c in range(2)
                ]
                yield
                for c in own + over:
                    c.arrived()
                line = piece.line

                def ready(t):
                    k = far_first(z)[t]
                    at = pl.ds(pl.multiple_of(k * z_gu, z_gu), z_gu)
                    for c in range(2):
                        line[0][k, pl.ds(c * z_gu, z_gu)] = piece.own[c, at].astype(
                            f32
                        ) + piece.got[c, at].astype(f32)

                yield from sum_line(net, *line, ready)
                for c in range(2):
                    piece.low[c] = low(line[0][z, pl.ds(c * z_gu, z_gu)])
                swap = net.put(piece.low.at[1 - core], piece.pair.at[core], net.at(dc=1))
                piece.pair[core] = piece.low[core]
                yield
                swap.arrived()
                own = fetch(piece.pair, gathered.at[me])
                yield from gather_line_first(net, piece.pair, lambda slot: gathered.at[slot])
                own.wait()

            def down(i):
                piece, line = r.down[i], r.down[i].line
                if i:
                    over = net.put(given.down.at[1 - x, :, columns[i]], piece.got, net.at(dx=1))
                    yield
                    over.arrived()
                down_own[i].arrived()

                def ready(t):
                    k = far_first(z)[t]
                    at = pl.ds(pl.multiple_of(k * z_dn, z_dn), z_dn)
                    block = piece.own[at].astype(f32)
                    line[0][k] = block + piece.got[at].astype(f32) if i else block

                yield from sum_line(net, *line, ready)
                piece.low[...] = low(line[0][z])
                own = fetch(piece.low, out.down.at[me, :, columns[i]])
                yield from gather_line_first(
                    net, piece.low, lambda slot: out.down.at[slot, :, columns[i]]
                )
                own.wait()

            def out_proj():
                need("heads_in", "middle_low")
                for i in range(slots):
                    r.o.own[i // 2, pl.ds(i % 2 * width, width)] = low(
                        outer_rows(h.heads_in[i], h.middle_low[...])
                    )
                o_core = [
                    net.put(r.o.own.at[2 * s + 1 - core], r.o.core.at[s], net.at(dc=1))
                    for s in range(2)
                ]
                yield
                for c in o_core:
                    c.arrived()
                for s in range(2):
                    f = 2 * s + core
                    r.o.own[f] = low(r.o.own[f].astype(f32) + r.o.core[s].astype(f32))
                over = net.put(r.o.own.at[2 * (1 - x) + core], r.o.got, net.at(dx=1))
                yield
                over.arrived()
                for i in range(slots):
                    at = pl.ds(i * z_o, z_o)
                    r.o.sum[i] = low(r.o.own[2 * x + core, at].astype(f32) + r.o.got[at].astype(f32))
                yield from sum_sides(net, r.o.sum, r.o.side, r.o.line)
                r.o.low[...] = low(r.o.line[0][z])
                own = fetch(r.o.low, out.o.at[me])
                yield from gather_line_first(net, r.o.low, lambda slot: out.o.at[slot])
                own.wait()

            def heads():
                for f in range(4):
                    at = pl.ds(f * (d // 4), d // 4)
                    r.h.own[f] = low(outer_rows(h.normed[:, at], r.dqkv[...]))
                core_copies = [
                    net.put(r.h.own.at[2 * s + 1 - core], r.h.core.at[s], net.at(dc=1))
                    for s in range(2)
                ]
                yield
                for c in core_copies:
                    c.arrived()
                for s in range(2):
                    f = 2 * s + core
                    r.h.own[f] = low(r.h.own[f].astype(f32) + r.h.core[s].astype(f32))
                over = net.put(r.h.own.at[2 * (1 - x) + core], r.h.got, net.at(dx=1))
                yield
                over.arrived()
                r.h.low[...] = low(
                    r.h.own[2 * x + core].astype(f32) + r.h.got[...].astype(f32)
                )
                own = fetch(r.h.low, out.heads.at[me])
                yield from gather_line_first(net, r.h.low, lambda slot: out.heads.at[slot])
                own.wait()

            in_order(
                BACK_ORDER,
                [
                    gate_or_up(given.gate, gate_own, r.gate, out.gate),
                    gate_or_up(given.up, up_own, r.up, out.up),
                    out_proj(),
                    down(0),
                    down(1),
                    back_rows(),
                    heads(),
                    main(),
                    gains(),
                ],
            )
            net.close()

        order = jax.tree.unflatten(out_tree, range(len(f_out)))
        result = net_call(
            body,
            f_out,
            f_in,
            200,
            64,
            number,
            scratch=flat,
            vmem=[
                len(f_in) + order.get(n)
                for n in ("input_grad", "a_grad", "m_grad", "q_grad", "k_grad")
            ],
        )
        return Bag(**jax.tree.unflatten(out_tree, result))

    return run


def widen(gate_all, up_all, down_all, o_all, heads_all, *small):
    _, _, z_gu, gu_cols = gate_all.shape
    half = gu_cols // 2
    z_dn, z_o = down_all.shape[1], o_all.shape[1]
    h_rows = heads_all.shape[1] // LINE

    def kernel(gate, up, down, o, heads, *refs):
        passed, outs = refs[: len(small)], refs[len(small) :]
        gate_out, up_out, down_out, o_out, q_out, k_out, v_out = outs[:7]
        for src, out in zip(passed, outs[7:]):
            out[...] = src[...].reshape(out.shape)
        for src, out in ((gate, gate_out), (up, up_out)):
            for y in range(2):
                for c in range(2):
                    for xs in range(2):
                        to = (2 * xs + c) * 2 * half + y * half
                        out[:, pl.ds(to, half)] = src[y, c, :, pl.ds(xs * half, half)].astype(
                            jnp.float32
                        )
        for y in range(2):
            down_out[y] = down[y].astype(jnp.float32)
            o_out[pl.ds(y * z_o, z_o)] = o[y].astype(jnp.float32)
        for h in range(2 * LINE):
            q_out[:, pl.ds(h * 256, 256)] = heads[h, :, pl.ds(0, 256)].astype(jnp.float32)
            k_out[:, pl.ds(h * 128, 128)] = heads[h, :, pl.ds(256, 128)].astype(jnp.float32)
            v_out[:, pl.ds(h * 128, 128)] = heads[h, :, pl.ds(384, 128)].astype(jnp.float32)

    f32 = jnp.float32
    outs = pl.pallas_call(
        kernel,
        grid=(LINE,),
        in_specs=[
            pl.BlockSpec((2, 2, z_gu, gu_cols), lambda i: (i, 0, 0, 0)),
            pl.BlockSpec((2, 2, z_gu, gu_cols), lambda i: (i, 0, 0, 0)),
            pl.BlockSpec((2, z_dn, MODEL_WIDTH), lambda i: (i, 0, 0)),
            pl.BlockSpec((2, z_o, MODEL_WIDTH), lambda i: (i, 0, 0)),
            pl.BlockSpec((2 * LINE, h_rows, 512), lambda i: (0, i, 0)),
        ]
        + [pl.BlockSpec(v.shape, lambda i: (0, 0)) for v in small],
        out_specs=[
            pl.BlockSpec((z_gu, 8 * half), lambda i: (i, 0)),
            pl.BlockSpec((z_gu, 8 * half), lambda i: (i, 0)),
            pl.BlockSpec((2, z_dn, MODEL_WIDTH), lambda i: (0, i, 0)),
            pl.BlockSpec((2 * z_o, MODEL_WIDTH), lambda i: (i, 0)),
            pl.BlockSpec((h_rows, 2048), lambda i: (i, 0)),
            pl.BlockSpec((h_rows, 1024), lambda i: (i, 0)),
            pl.BlockSpec((h_rows, 1024), lambda i: (i, 0)),
        ]
        + [pl.BlockSpec((1, *v.shape), lambda i: (0, 0, 0)) for v in small],
        out_shape=[
            shape_of(LINE * z_gu, 8 * half, kind=f32),
            shape_of(LINE * z_gu, 8 * half, kind=f32),
            shape_of(2, LINE * z_dn, MODEL_WIDTH, kind=f32),
            shape_of(2 * LINE * z_o, MODEL_WIDTH, kind=f32),
            shape_of(LINE * h_rows, 2048, kind=f32),
            shape_of(LINE * h_rows, 1024, kind=f32),
            shape_of(LINE * h_rows, 1024, kind=f32),
        ]
        + [shape_of(1, *v.shape, kind=v.dtype) for v in small],
        compiler_params=pltpu.CompilerParams(vmem_limit_bytes=VMEM_BYTES),
    )(gate_all, up_all, down_all, o_all, heads_all, *small)
    outs = list(outs)
    outs[2] = outs[2].reshape(-1, MODEL_WIDTH)
    return outs


def fast_layer(
    tokens,
    lengths,
    deal,
    attn_gain,
    w_q,
    key_weight,
    value_weight,
    query_norm_gain,
    k_gain,
    w_o,
    mlp_gain,
    w_gate,
    w_up,
    w_down,
    out_cotangent,
):
    rows = tokens.shape[1]
    slots = lax.axis_size(CTX)
    count = rows * slots
    ff_half = w_down.shape[0] // 2
    width = HEAD_SIZE * 2

    frequency = theta_base ** (-(np.arange(HEAD_SIZE // 2) * 2.0) / HEAD_SIZE)
    sign = np.where(np.arange(HEAD_SIZE) < HEAD_SIZE // 2, -1.0, 1.0)
    tables = np.stack([np.tile(frequency, 2), sign]).astype(np.float32)

    front = front_kernel(
        dict(
            tok=tokens,
            lengths=lengths,
            deal=deal,
            attn_gain=attn_gain,
            mlp_gain=mlp_gain,
            q_gain=query_norm_gain[None],
            k_gain=k_gain[None],
            freq=tables,
            w_q=w_q,
            w_k=key_weight,
            w_v=value_weight,
            w_o=w_o,
            w_gate=w_gate,
            w_up=w_up,
            w_down=w_down,
            grad=out_cotangent,
        ),
        {},
        0,
    )
    moved = dict(
        dm=front.dm,
        back=front.back,
        gate=front.gate.reshape(4, -1, 2 * ff_half),
        up=front.up.reshape(4, -1, 2 * ff_half),
        down=front.down,
        down_sum=front.down_sum,
    )
    loaded = dict(
        tok=tokens,
        back_from=front.back_from,
        a_gain=front.a_gain,
        dg2=front.dg2,
        heads_in=front.mixed_in,
        middle_low=front.middle_low,
        q=front.q,
        k=front.k,
        kt=front.kt,
        v=front.v,
        mixed=front.mixed,
        lse=front.lse,
        first=front.first,
        dealt=front.dealt,
        qkv=front.qkv,
        q_gain=front.q_gain,
        k_gain=front.k_gain,
        cos=front.cos,
        sin=front.sin,
        normed=front.normed,
        w_qkv=front.w_qkv,
    )
    sums = back_kernel((rows, count), 2)(moved, loaded)

    gate_sum, up_sum, down_sum, o_sum, q_sum, k_sum, v_sum, *small = widen(
        sums.gate,
        sums.up,
        sums.down,
        sums.o,
        sums.heads,
        front.output,
        sums.input_grad,
        sums.a_grad,
        sums.q_grad,
        sums.k_grad,
        sums.m_grad,
    )
    output, input_grad, *gains = small
    return (
        output,
        input_grad,
        *(gain[0, 0] for gain in gains),
        q_sum,
        k_sum,
        v_sum,
        o_sum,
        gate_sum,
        up_sum,
        down_sum,
    )


def solution(mesh):
    devices = mesh.devices
    if devices.shape == (8, 4):
        mesh = Mesh(devices.reshape(4, 2, 2, 2), CTX + FSDP)
        layer, ctx, fsdp = fast_layer, CTX, FSDP
    else:
        layer, ctx, fsdp = general_layer, "ctx", "fsdp"
    wide_rows = P(fsdp, ctx, None)
    return jax.shard_map(
        layer,
        mesh=mesh,
        in_specs=(
            wide_rows,
            P(fsdp, None),
            P(fsdp, None, None),
            P(fsdp),
            P(fsdp, None),
            P(fsdp, None),
            P(fsdp, None),
            P(fsdp),
            P(fsdp),
            P(fsdp, None),
            P(fsdp),
            P(fsdp, None),
            P(fsdp, None),
            P(fsdp, None),
            wide_rows,
        ),
        out_specs=(wide_rows, wide_rows) + (P(fsdp),) * 4 + (P(fsdp, None),) * 7,
        check_vma=False,
    )
```

```python
import math

import jax
import jax.numpy as jnp
import numpy as np
from jax import lax
from jax.experimental import pallas as pl
from jax.experimental.pallas import tpu as pltpu
from jax.sharding import Mesh
from jax.sharding import PartitionSpec as P

MODEL_WIDTH = 1024
QUERY_HEADS = 16
KEY_VALUE_HEADS = 8
HEAD_SIZE = 128


eps = 1e-06
theta_base = 1000000.0
negative_filler = -1e30


def root_mean_norm(values, gain_vec):
    return values * lax.rsqrt(jnp.mean(values * values, axis=-1, keepdims=True) + eps) * gain_vec


def rotary_embedding(values, token_position):
    half_width = values.shape[-1] // 2
    frequency = theta_base ** (
        -(jnp.arange(half_width, dtype=jnp.float32) * 2.0) / values.shape[-1]
    )
    angles = token_position.astype(jnp.float32)[:, None] * frequency[None, :]
    cosine = jnp.concatenate([jnp.cos(angles), jnp.cos(angles)], axis=-1)[:, None, :]
    sine_part = jnp.concatenate([jnp.sin(angles), jnp.sin(angles)], axis=-1)[:, None, :]
    turned = jnp.concatenate([-values[..., half_width:], values[..., :half_width]], axis=-1)
    return values * cosine + turned * sine_part


def dot_trans(left_side, right_side):
    return lax.dot_general(
        left_side, right_side, (((1,), (1,)), ((), ())), preferred_element_type=jnp.float32
    )


def outer_rows(left_side, right_side):
    return lax.dot_general(
        left_side, right_side, (((0,), (0,)), ((), ())), preferred_element_type=jnp.float32
    )


def block_plan(piece_rows, local_rows):
    shards = piece_rows // local_rows
    per_block = math.gcd(shards, max(1, 1024 // local_rows))
    return (per_block * local_rows, shards // per_block)


def over_blocks(carried, arrays, local_rows, block_work):
    rows_per_block, count_of_blocks = block_plan(arrays[0].shape[0], local_rows)

    def one_block(turn_index, state_now):
        offset = turn_index * rows_per_block
        parts = tuple(
            (lax.dynamic_slice_in_dim(member, offset, rows_per_block, 0) for member in arrays)
        )
        return block_work(state_now, parts, offset)

    return lax.fori_loop(0, count_of_blocks, one_block, carried)


def segment_begin(tok_ids, starts):
    return jnp.max(jnp.where(tok_ids[:, None] >= starts[None, :], starts[None, :], 0), axis=1)


def general_layer(
    tokens,
    lengths,
    deal,
    attn_gain,
    w_q,
    key_weight,
    value_weight,
    query_norm_gain,
    k_gain,
    w_o,
    mlp_gain,
    w_gate,
    w_up,
    w_down,
    out_cotangent,
):
    local_rows = tokens.shape[1]
    piece_count = lax.axis_size("ctx")
    piece_rows = local_rows // piece_count
    here = lax.axis_index("ctx")
    group_width = QUERY_HEADS // KEY_VALUE_HEADS
    score_scale = HEAD_SIZE ** (-0.5)
    seq_lengths = lengths[0]
    starts = jnp.cumsum(seq_lengths) - seq_lengths
    plan = deal[0]
    devices = jnp.arange(piece_count, dtype=jnp.int32)
    hits = plan[:, :, None] == devices[None, None, :]
    slot_of = jnp.sum(jnp.where(hits, devices[None, :, None], 0), axis=1)
    inner = jnp.arange(piece_rows, dtype=jnp.int32)
    dealt_index = (
        devices[None, :, None] * local_rows
        + jnp.transpose(slot_of)[:, :, None] * piece_rows
        + inner[None, None, :]
    ).reshape(piece_count * local_rows)
    dealt_first = segment_begin(dealt_index, starts)
    tok_index = lax.dynamic_slice_in_dim(dealt_index, here * local_rows, local_rows)
    segment_initial = lax.dynamic_slice_in_dim(dealt_first, here * local_rows, local_rows)
    token_position = tok_index - segment_initial
    own_slots = lax.dynamic_index_in_dim(slot_of, here, 0, keepdims=False)
    own_plan = lax.dynamic_index_in_dim(plan, here, 0, keepdims=False)
    token_pieces = jnp.take(
        tokens[0].reshape(piece_count, piece_rows, MODEL_WIDTH), own_slots, axis=0
    )
    dealt_tok = lax.all_to_all(
        token_pieces, "ctx", split_axis=0, concat_axis=0, tiled=True
    ).reshape(local_rows, MODEL_WIDTH)

    def key_mask(start_row, local_row_count):
        key_identifiers = lax.dynamic_slice_in_dim(dealt_index, start_row, local_row_count)
        return (key_identifiers[None, :] >= segment_initial[:, None]) & (
            key_identifiers[None, :] <= tok_index[:, None]
        )

    def query_mask(start_row, local_row_count):
        query_ids = lax.dynamic_slice_in_dim(dealt_index, start_row, local_row_count)
        first_key = lax.dynamic_slice_in_dim(dealt_first, start_row, local_row_count)
        return (tok_index[None, :] >= first_key[:, None]) & (
            tok_index[None, :] <= query_ids[:, None]
        )

    def fetch_weights():
        attn_set = (
            lax.all_gather(attn_gain, "fsdp", axis=0, tiled=True),
            lax.all_gather(query_norm_gain, "fsdp", axis=0, tiled=True),
            lax.all_gather(k_gain, "fsdp", axis=0, tiled=True),
            lax.all_gather(w_q, "fsdp", axis=0, tiled=True),
            lax.all_gather(key_weight, "fsdp", axis=0, tiled=True),
            lax.all_gather(value_weight, "fsdp", axis=0, tiled=True),
            lax.all_gather(w_o, "fsdp", axis=0, tiled=True),
        )
        mlp_set = (
            lax.all_gather(mlp_gain, "fsdp", axis=0, tiled=True),
            lax.all_gather(w_gate, "fsdp", axis=0, tiled=True),
            lax.all_gather(w_up, "fsdp", axis=0, tiled=True),
            lax.all_gather(w_down, "fsdp", axis=0, tiled=True),
        )
        return (attn_set, mlp_set)

    def forward(attn_set, mlp_set, token_rows):
        a_gain, qn_gain, kn_gain, proj_q, proj_k, proj_v, proj_o = attn_set
        m_gain, proj_gate, proj_up, proj_down = mlp_set
        residual = token_rows.astype(jnp.float32)
        normalized_input = root_mean_norm(residual, a_gain.astype(jnp.float32)).astype(jnp.bfloat16)
        query_prenorm = jnp.dot(
            normalized_input, proj_q, preferred_element_type=jnp.float32
        ).reshape(local_rows, QUERY_HEADS, HEAD_SIZE)
        key_prenorm = jnp.dot(normalized_input, proj_k, preferred_element_type=jnp.float32).reshape(
            local_rows, KEY_VALUE_HEADS, HEAD_SIZE
        )
        value_narrow = jnp.dot(normalized_input, proj_v, preferred_element_type=jnp.float32).astype(
            jnp.bfloat16
        )
        q_heads = (
            rotary_embedding(
                root_mean_norm(query_prenorm, qn_gain.astype(jnp.float32)), token_position
            )
            .astype(jnp.bfloat16)
            .reshape(local_rows, KEY_VALUE_HEADS, group_width, HEAD_SIZE)
        )
        key_narrow = (
            rotary_embedding(
                root_mean_norm(key_prenorm, kn_gain.astype(jnp.float32)), token_position
            )
            .astype(jnp.bfloat16)
            .reshape(local_rows, KEY_VALUE_HEADS * HEAD_SIZE)
        )

        def attend_over_block(state_now, shard_piece, start_row):
            key_segment, value_segment = shard_piece
            local_row_count = key_segment.shape[0]
            allowed = key_mask(start_row, local_row_count)
            row_top, row_total, weighted = state_now
            scores = (
                jnp.einsum(
                    "rkgh,ckh->kgrc",
                    q_heads,
                    key_segment.reshape(local_row_count, KEY_VALUE_HEADS, HEAD_SIZE),
                    preferred_element_type=jnp.float32,
                )
                * score_scale
            )
            scores = jnp.where(allowed, scores, negative_filler)
            new_top = jnp.maximum(row_top, jnp.max(scores, axis=-1))
            rescale = jnp.exp(row_top - new_top)
            weights = jnp.where(allowed, jnp.exp(scores - new_top[..., None]), 0.0)
            row_total = row_total * rescale + jnp.sum(weights, axis=-1)
            weighted = weighted * rescale[..., None] + jnp.einsum(
                "kgrc,ckh->kgrh",
                weights.astype(jnp.bfloat16),
                value_segment.reshape(local_row_count, KEY_VALUE_HEADS, HEAD_SIZE),
                preferred_element_type=jnp.float32,
            )
            return (new_top, row_total, weighted)

        initial = (
            jnp.full((KEY_VALUE_HEADS, group_width, local_rows), negative_filler, jnp.float32),
            jnp.zeros((KEY_VALUE_HEADS, group_width, local_rows), jnp.float32),
            jnp.zeros((KEY_VALUE_HEADS, group_width, local_rows, HEAD_SIZE), jnp.float32),
        )
        row_top, row_total, weighted = over_blocks(
            initial,
            (
                lax.all_gather(key_narrow, "ctx", axis=0, tiled=True),
                lax.all_gather(value_narrow, "ctx", axis=0, tiled=True),
            ),
            local_rows,
            attend_over_block,
        )
        attention_mixed = jnp.transpose(weighted / row_total[..., None], (2, 0, 1, 3)).reshape(
            local_rows, QUERY_HEADS * HEAD_SIZE
        )
        log_total = row_top + jnp.log(row_total)
        mixed_low = attention_mixed.astype(jnp.bfloat16)
        middle = residual + jnp.dot(mixed_low, proj_o, preferred_element_type=jnp.float32)
        normed2 = root_mean_norm(middle, m_gain.astype(jnp.float32)).astype(jnp.bfloat16)
        gate_pre = jnp.dot(normed2, proj_gate, preferred_element_type=jnp.float32)
        up_pre = jnp.dot(normed2, proj_up, preferred_element_type=jnp.float32)
        hidden = (jax.nn.silu(gate_pre) * up_pre).astype(jnp.bfloat16)
        result = middle + jnp.dot(hidden, proj_down, preferred_element_type=jnp.float32)
        return (
            result,
            residual,
            normalized_input,
            query_prenorm,
            key_prenorm,
            value_narrow,
            q_heads,
            key_narrow,
            attention_mixed,
            mixed_low,
            log_total,
            middle,
            normed2,
            gate_pre,
            up_pre,
            hidden,
            attn_set,
            mlp_set,
        )

    first_sets = fetch_weights()
    first_pass = forward(first_sets[0], first_sets[1], dealt_tok)
    again_tok = lax.all_to_all(
        token_pieces, "ctx", split_axis=0, concat_axis=0, tiled=True
    ).reshape(local_rows, MODEL_WIDTH)
    second_sets = fetch_weights()
    kept_pass = forward(second_sets[0], second_sets[1], again_tok)
    (
        unused,
        residual,
        normalized_input,
        query_prenorm,
        key_prenorm,
        value_narrow,
        q_heads,
        key_narrow,
        attention_mixed,
        mixed_low,
        log_total,
        middle,
        normed2,
        gate_pre,
        up_pre,
        hidden,
        attn_set,
        mlp_set,
    ) = kept_pass
    a_gain, qn_gain, kn_gain, proj_q, proj_k, proj_v, proj_o = attn_set
    m_gain, proj_gate, proj_up, proj_down = mlp_set
    grad_low = out_cotangent[0]
    grad_out = grad_low.astype(jnp.float32)
    d_hidden = dot_trans(grad_low, proj_down)
    down_grad = lax.psum_scatter(
        outer_rows(hidden, grad_low).astype(jnp.bfloat16), "fsdp", scatter_dimension=0, tiled=True
    )
    unused, swiglu_back = jax.vjp(
        lambda gate_in, up_in: jax.nn.silu(gate_in) * up_in, gate_pre, up_pre
    )
    d_gate, d_up = swiglu_back(d_hidden)
    d_gate_low = d_gate.astype(jnp.bfloat16)
    d_up_low = d_up.astype(jnp.bfloat16)
    d_normed2 = dot_trans(d_gate_low, proj_gate) + dot_trans(d_up_low, proj_up)
    both_low = jnp.concatenate([d_gate_low, d_up_low], axis=1)
    gate_up_grad = lax.psum_scatter(
        outer_rows(normed2, both_low).astype(jnp.bfloat16), "fsdp", scatter_dimension=0, tiled=True
    )
    unused, norm2_back = jax.vjp(root_mean_norm, middle, m_gain.astype(jnp.float32))
    d_middle_norm, d_m_gain = norm2_back(d_normed2)
    d_middle = grad_out + d_middle_norm
    middle_low = d_middle.astype(jnp.bfloat16)
    mixed_gradient = dot_trans(middle_low, proj_o).astype(jnp.bfloat16)
    out_proj_grad = lax.psum_scatter(
        outer_rows(mixed_low, middle_low).astype(jnp.bfloat16),
        "fsdp",
        scatter_dimension=0,
        tiled=True,
    )
    heads_gradient = mixed_gradient.reshape(local_rows, KEY_VALUE_HEADS, group_width, HEAD_SIZE)
    delta_rows = jnp.sum(
        heads_gradient.astype(jnp.float32)
        * attention_mixed.reshape(local_rows, KEY_VALUE_HEADS, group_width, HEAD_SIZE),
        axis=-1,
    )
    delta_t = jnp.transpose(delta_rows, (1, 2, 0))
    local_keys = key_narrow.reshape(local_rows, KEY_VALUE_HEADS, HEAD_SIZE)
    local_values = value_narrow.reshape(local_rows, KEY_VALUE_HEADS, HEAD_SIZE)

    def query_block(state_now, shard_piece, start_row):
        key_segment, value_segment = shard_piece
        local_row_count = key_segment.shape[0]
        allowed = key_mask(start_row, local_row_count)
        key_row_block = key_segment.reshape(local_row_count, KEY_VALUE_HEADS, HEAD_SIZE)
        scores = (
            jnp.einsum("rkgh,ckh->kgrc", q_heads, key_row_block, preferred_element_type=jnp.float32)
            * score_scale
        )
        probability = jnp.where(allowed, jnp.exp(scores - log_total[..., None]), 0.0)
        d_probs = jnp.einsum(
            "rkgh,ckh->kgrc",
            heads_gradient,
            value_segment.reshape(local_row_count, KEY_VALUE_HEADS, HEAD_SIZE),
            preferred_element_type=jnp.float32,
        )
        d_scores = (probability * (d_probs - delta_t[..., None])).astype(jnp.bfloat16)
        return (
            state_now
            + jnp.einsum(
                "kgrc,ckh->kgrh", d_scores, key_row_block, preferred_element_type=jnp.float32
            )
            * score_scale
        )

    query_grad = over_blocks(
        jnp.zeros((KEY_VALUE_HEADS, group_width, local_rows, HEAD_SIZE), jnp.float32),
        (
            lax.all_gather(key_narrow, "ctx", axis=0, tiled=True),
            lax.all_gather(value_narrow, "ctx", axis=0, tiled=True),
        ),
        local_rows,
        query_block,
    )
    lse_rows = jnp.transpose(log_total, (2, 0, 1)).reshape(local_rows, QUERY_HEADS)
    delta_send = delta_rows.reshape(local_rows, QUERY_HEADS)

    def key_block(state_now, shard_piece, start_row):
        query_segment, output_gradient_segment, logsumexp_segment, delta_segment = shard_piece
        local_row_count = query_segment.shape[0]
        allowed = query_mask(start_row, local_row_count)
        key_grad, value_gradient = state_now
        query_matrix = query_segment.reshape(
            local_row_count, KEY_VALUE_HEADS, group_width, HEAD_SIZE
        )
        gradient_rows = output_gradient_segment.reshape(
            local_row_count, KEY_VALUE_HEADS, group_width, HEAD_SIZE
        )
        scores = (
            jnp.einsum(
                "ckgh,rkh->kgcr", query_matrix, local_keys, preferred_element_type=jnp.float32
            )
            * score_scale
        )
        logsumexp_portion = jnp.transpose(
            logsumexp_segment.reshape(local_row_count, KEY_VALUE_HEADS, group_width), (1, 2, 0)
        )
        delta_portion = jnp.transpose(
            delta_segment.reshape(local_row_count, KEY_VALUE_HEADS, group_width), (1, 2, 0)
        )
        probability = jnp.where(allowed, jnp.exp(scores - logsumexp_portion[..., None]), 0.0)
        value_gradient = value_gradient + jnp.einsum(
            "kgcr,ckgh->rkh",
            probability.astype(jnp.bfloat16),
            gradient_rows,
            preferred_element_type=jnp.float32,
        )
        d_probs = jnp.einsum(
            "ckgh,rkh->kgcr", gradient_rows, local_values, preferred_element_type=jnp.float32
        )
        d_scores = (probability * (d_probs - delta_portion[..., None])).astype(jnp.bfloat16)
        key_grad = (
            key_grad
            + jnp.einsum(
                "kgcr,ckgh->rkh", d_scores, query_matrix, preferred_element_type=jnp.float32
            )
            * score_scale
        )
        return (key_grad, value_gradient)

    key_grad, value_gradient = over_blocks(
        (
            jnp.zeros((local_rows, KEY_VALUE_HEADS, HEAD_SIZE), jnp.float32),
            jnp.zeros((local_rows, KEY_VALUE_HEADS, HEAD_SIZE), jnp.float32),
        ),
        (
            lax.all_gather(
                q_heads.reshape(local_rows, QUERY_HEADS * HEAD_SIZE), "ctx", axis=0, tiled=True
            ),
            lax.all_gather(mixed_gradient, "ctx", axis=0, tiled=True),
            lax.all_gather(lse_rows.astype(jnp.bfloat16), "ctx", axis=0, tiled=True).astype(
                jnp.float32
            ),
            lax.all_gather(delta_send.astype(jnp.bfloat16), "ctx", axis=0, tiled=True).astype(
                jnp.float32
            ),
        ),
        local_rows,
        key_block,
    )
    query_rows = jnp.transpose(query_grad, (2, 0, 1, 3)).reshape(local_rows, QUERY_HEADS, HEAD_SIZE)
    unused, q_back = jax.vjp(
        lambda head_in, gain_in: rotary_embedding(root_mean_norm(head_in, gain_in), token_position),
        query_prenorm,
        qn_gain.astype(jnp.float32),
    )
    d_q_pre, d_qn_gain = q_back(query_rows)
    unused, k_back = jax.vjp(
        lambda head_in, gain_in: rotary_embedding(root_mean_norm(head_in, gain_in), token_position),
        key_prenorm,
        kn_gain.astype(jnp.float32),
    )
    key_prenorm_gradient, d_kn_gain = k_back(key_grad)
    dq_low = d_q_pre.reshape(local_rows, QUERY_HEADS * HEAD_SIZE).astype(jnp.bfloat16)
    key_gradient_narrow = key_prenorm_gradient.reshape(
        local_rows, KEY_VALUE_HEADS * HEAD_SIZE
    ).astype(jnp.bfloat16)
    value_gradient_narrow = value_gradient.reshape(local_rows, KEY_VALUE_HEADS * HEAD_SIZE).astype(
        jnp.bfloat16
    )
    d_normed = (
        dot_trans(dq_low, proj_q)
        + dot_trans(key_gradient_narrow, proj_k)
        + dot_trans(value_gradient_narrow, proj_v)
    )
    qkv_low = jnp.concatenate([dq_low, key_gradient_narrow, value_gradient_narrow], axis=1)
    qkv_grad = lax.psum_scatter(
        outer_rows(normalized_input, qkv_low).astype(jnp.bfloat16),
        "fsdp",
        scatter_dimension=0,
        tiled=True,
    )
    unused, norm1_back = jax.vjp(root_mean_norm, residual, a_gain.astype(jnp.float32))
    d_resid_norm, d_a_gain = norm1_back(d_normed)
    input_dealt = d_middle + d_resid_norm
    back_pieces = lax.all_to_all(
        input_dealt.reshape(piece_count, piece_rows, MODEL_WIDTH).astype(jnp.bfloat16),
        "ctx",
        split_axis=0,
        concat_axis=0,
        tiled=True,
    ).astype(jnp.float32)
    input_grad = jnp.take(back_pieces, own_plan, axis=0).reshape(local_rows, MODEL_WIDTH)
    gain_parts = (
        lax.psum_scatter(d_a_gain, "fsdp", scatter_dimension=0, tiled=True),
        lax.psum_scatter(d_qn_gain, "fsdp", scatter_dimension=0, tiled=True),
        lax.psum_scatter(d_kn_gain, "fsdp", scatter_dimension=0, tiled=True),
        lax.psum_scatter(d_m_gain, "fsdp", scatter_dimension=0, tiled=True),
    )
    totals = (
        lax.psum(gain_parts[0].astype(jnp.bfloat16), "ctx").astype(jnp.float32),
        lax.psum(gain_parts[1].astype(jnp.bfloat16), "ctx").astype(jnp.float32),
        lax.psum(gain_parts[2].astype(jnp.bfloat16), "ctx").astype(jnp.float32),
        lax.psum(gain_parts[3].astype(jnp.bfloat16), "ctx").astype(jnp.float32),
        lax.psum(qkv_grad, "ctx").astype(jnp.float32),
        lax.psum(out_proj_grad, "ctx").astype(jnp.float32),
        lax.psum(gate_up_grad, "ctx").astype(jnp.float32),
        lax.psum(down_grad, "ctx").astype(jnp.float32),
    )
    q_width = QUERY_HEADS * HEAD_SIZE
    key_value_width = KEY_VALUE_HEADS * HEAD_SIZE
    qkv_total = totals[4]
    gate_up_total = totals[6]
    ff_width = w_gate.shape[1]
    return (
        first_pass[0].astype(jnp.bfloat16)[None],
        input_grad[None],
        totals[0],
        totals[1],
        totals[2],
        totals[3],
        qkv_total[:, :q_width],
        qkv_total[:, q_width : q_width + key_value_width],
        qkv_total[:, q_width + key_value_width :],
        totals[5],
        gate_up_total[:, :ff_width],
        gate_up_total[:, ff_width:],
        totals[7],
    )


CTX = ("z", "y")
FSDP = ("x", "core")
VMEM_BYTES = 62 << 20


def norm_back(values, gain_vec, grad):
    scale = lax.rsqrt(jnp.mean(values * values, axis=-1, keepdims=True) + eps)
    inner = gain_vec * grad
    d_values = scale * inner - values * (scale * scale * scale) * jnp.mean(
        values * inner, axis=-1, keepdims=True
    )
    return d_values, grad * values * scale


def half_turn(values):
    half = values.shape[-1] // 2
    return jnp.concatenate([-values[..., half:], values[..., :half]], axis=-1)


def rope_tables(token_position):
    half = HEAD_SIZE // 2
    frequency = theta_base ** (-(jnp.arange(half, dtype=jnp.float32) * 2.0) / HEAD_SIZE)
    angles = token_position.astype(jnp.float32)[:, None] * frequency[None, :]
    cosine, sine = jnp.cos(angles), jnp.sin(angles)
    return jnp.concatenate([cosine, cosine], axis=1), jnp.concatenate([sine, sine], axis=1)


def dot(a, b):
    return jnp.dot(a, b, preferred_element_type=jnp.float32)


def low(a):
    return a.astype(jnp.bfloat16)


def gather_fsdp_plain(block):
    return lax.all_gather(block, FSDP, axis=0, tiled=True)


def over(block, axis):
    return lax.ppermute(block, axis, [(0, 1), (1, 0)])


def half_sum(block, axis):
    place = lax.axis_index(axis)
    got = over(lax.dynamic_index_in_dim(block, 1 - place, 0, keepdims=False), axis)
    own = lax.dynamic_index_in_dim(block, place, 0, keepdims=False)
    return low(own.astype(jnp.float32) + got.astype(jnp.float32))


MESH_ID = pl.DeviceIdType.MESH
LINE = 4


class Net:
    def __init__(self, send, recv):
        self.send, self.recv, self.used = send, recv, 0
        self.z, self.y, self.x, self.core = (lax.axis_index(a) for a in CTX + FSDP)
        self.me = 2 * self.z + self.y
        self.open = []

    def at(self, dz=0, dy=0, dx=0, dc=0):
        return (
            self.z + dz,
            1 - self.y if dy else self.y,
            1 - self.x if dx else self.x,
            1 - self.core if dc else self.core,
        )

    def put(self, src, dst, target, sends=None, recvs=None):
        copy = Copy(self, src, dst, target, sends, recvs)
        self.open.append(copy)
        return copy

    def close(self):
        for copy in self.open:
            copy.arrived()
        for copy in self.open:
            copy.left()


def guarded(condition, action):
    if condition is None:
        action()
    else:
        pl.when(condition)(action)


class Copy:
    def __init__(self, net, src, dst, target, sends, recvs):
        i = net.used
        net.used += 1
        self.sends, self.recvs, self.waited = sends, recvs, False
        self.copy = pltpu.make_async_remote_copy(
            src, dst, net.send.at[i], net.recv.at[i], device_id=target, device_id_type=MESH_ID
        )
        guarded(sends, self.copy.start)

    def arrived(self):
        if not self.waited:
            self.waited = True
            guarded(self.recvs, self.copy.wait_recv)

    def left(self):
        guarded(self.sends, self.copy.wait_send)


class Local:
    def __init__(self, copy):
        self.copy, self.waited = copy, False
        copy.start()

    def arrived(self):
        if not self.waited:
            self.waited = True
            self.copy.wait()

    wait = arrived


def greet(net, kinds):
    barrier = pltpu.get_barrier_semaphore()
    partners = []
    if "z" in kinds:
        partners += [(net.at(dz=1), net.z < LINE - 1), (net.at(dz=-1), net.z > 0)]
    if "y" in kinds:
        partners.append((net.at(dy=1), None))
    if "x" in kinds:
        partners.append((net.at(dx=1), None))
    if "core" in kinds:
        partners.append((net.at(dc=1), None))
    if "far" in kinds:
        partners.append((net.at(dx=1, dc=1), None))
    if "ctx" in kinds:
        for k in range(1, 2 * LINE):
            other = lax.rem(net.me + k, 2 * LINE)
            partners.append(((other // 2, lax.rem(other, 2), net.x, net.core), None))
    for target, there in partners:
        guarded(
            there,
            lambda target=target: pl.semaphore_signal(
                barrier, inc=1, device_id=target, device_id_type=MESH_ID
            ),
        )
    ends = 0
    if "z" in kinds:
        ends = (net.z == 0).astype(jnp.int32) + (net.z == LINE - 1).astype(jnp.int32)
    pl.semaphore_wait(barrier, len(partners) - ends)


def drive(*programs):
    live = list(programs)
    while live:
        for program in list(live):
            if next(program, "end") == "end":
                live.remove(program)


def in_order(order, programs):
    for i in order:
        next(programs[i], None)
    for program in programs:
        for _ in program:
            pass


def by_steps(program):
    yield next(program)
    while next(program, "end") != "end":
        if next(program, "end") == "end":
            return
        yield


def along_line(net, own, view, slot, log=None):
    z = net.z
    up = net.put(own, view(slot(z)), net.at(dz=1), z < LINE - 1, z > 0)
    down = net.put(own, view(slot(z)), net.at(dz=-1), z > 0, z < LINE - 1)
    yield
    for s in range(1, LINE):
        from_low, from_high = z >= s, z + s <= LINE - 1
        up.arrived()
        low_block, high_block = view(slot(z - s)), view(slot(z + s))
        if s < LINE - 1:
            up = net.put(low_block, low_block, net.at(dz=1), from_low & (z < LINE - 1), z >= s + 1)
        if log is not None:
            log[s].append(net.put(low_block, low_block, net.at(dy=1), from_low, from_low))
        yield
        down.arrived()
        if s < LINE - 1:
            down = net.put(
                high_block, high_block, net.at(dz=-1), from_high & (z > 0), z + s + 1 <= LINE - 1
            )
        if log is not None:
            log[s].append(net.put(high_block, high_block, net.at(dy=1), from_high, from_high))
        yield


def gather_line_first(net, own, view, log=None):
    log = {s: [] for s in range(LINE)} if log is None else log
    log[0].append(net.put(own, view(net.me), net.at(dy=1)))
    yield from along_line(net, own, view, lambda z: 2 * z + net.y, log)


def gather_side_first(net, own, view):
    side = net.put(own, view(net.me), net.at(dy=1))
    first = along_line(net, own, view, lambda z: 2 * z + net.y)
    yield next(first)
    side.arrived()
    other = view(net.me + 1 - 2 * net.y)
    second = along_line(net, other, view, lambda z: 2 * z + 1 - net.y)
    for _ in second:
        next(first, None)
        yield


def gather_ctx_programs(net, own, out, cut):
    rows = own.shape[0]
    programs = [
        gather_line_first(
            net, own.at[pl.ds(0, cut)], lambda slot: out.at[slot, pl.ds(0, cut)]
        )
    ]
    if cut < rows:
        rest = pl.ds(cut, rows - cut)
        programs.append(gather_side_first(net, own.at[rest], lambda slot: out.at[slot, rest]))
    return programs


def gather_fsdp(net, own, out):
    f = 2 * net.x + net.core
    net.put(own, out.at[f], net.at(dc=1))
    over = net.put(own, out.at[f], net.at(dx=1))
    yield
    yield
    yield
    over.arrived()
    far = out.at[2 * (1 - net.x) + net.core]
    net.put(far, far, net.at(dc=1))
    yield


def gather_quad(net, own, out):
    q = 2 * net.y + net.core
    net.put(own, out.at[q], net.at(dc=1))
    over = net.put(own, out.at[q], net.at(dy=1))
    yield
    over.arrived()
    far = out.at[2 * (1 - net.y) + net.core]
    net.put(far, far, net.at(dc=1))
    yield


def swap_ctx(net, blocks, out):
    for k in range(1, 2 * LINE):
        other = lax.rem(net.me + k, 2 * LINE)
        net.put(
            blocks.at[other], out.at[net.me], (other // 2, lax.rem(other, 2), net.x, net.core)
        )
    yield


def own_copies(pairs, sem):
    copies = [pltpu.make_async_copy(src, dst, sem.at[i]) for i, (src, dst) in enumerate(pairs)]
    for copy in copies:
        copy.start()
    return copies


def net_call(body, outs, args, copies, locals_, number, scratch=(), vmem=(), smem=()):
    def kernel(*refs):
        *rest, send, recv, local = refs
        net = Net(send, recv)
        body(net, local, *rest)
        assert net.used <= copies, net.used

    any_space = pl.BlockSpec(memory_space=pl.ANY)
    in_vmem = pl.BlockSpec(memory_space=pltpu.VMEM)
    in_smem = pl.BlockSpec(memory_space=pltpu.SMEM)
    count = len(args)

    def place(i):
        return in_vmem if i in vmem else in_smem if i in smem else any_space

    return pl.pallas_call(
        kernel,
        out_shape=outs,
        in_specs=[place(i) for i in range(count)],
        out_specs=[place(count + i) for i in range(len(outs))],
        scratch_shapes=list(scratch)
        + [
            pltpu.SemaphoreType.DMA((copies,)),
            pltpu.SemaphoreType.DMA((copies,)),
            pltpu.SemaphoreType.DMA((max(1, locals_),)),
        ],
        compiler_params=pltpu.CompilerParams(
            collective_id=number, has_side_effects=True, vmem_limit_bytes=VMEM_BYTES
        ),
    )(*args)


def shape_of(*dims, kind=jnp.bfloat16):
    return jax.ShapeDtypeStruct(dims, kind)


def sum_line(net, held, send_up, send_down, got_up, got_down, ready):
    z = net.z
    ups, downs = [], []

    def fill(send, got, block, t, first):
        def alone():
            send[t] = low(held[block])

        def added():
            send[t] = low(held[block] + got[t - 1].astype(jnp.float32))

        return alone if first else added

    for t in range(LINE - 1):
        if t:
            ups[t - 1].arrived()
        ready(t)
        to_up, to_down = LINE - 1 - t + z, z - LINE + 1 + t
        up_on, down_on = (z <= t) & (z < LINE - 1), (z >= LINE - 1 - t) & (z > 0)
        pl.when(z == 0)(fill(send_up, got_up, to_up, t, True))
        if t:
            pl.when(up_on & (z >= 1))(fill(send_up, got_up, to_up, t, False))
        ups.append(
            net.put(
                send_up.at[t], got_up.at[t], net.at(dz=1), up_on, (z >= 1) & (z - 1 <= t)
            )
        )
        yield
        if t:
            downs[t - 1].arrived()
        pl.when(z == LINE - 1)(fill(send_down, got_down, to_down, t, True))
        if t:
            pl.when(down_on & (z <= LINE - 2))(fill(send_down, got_down, to_down, t, False))
        downs.append(
            net.put(
                send_down.at[t],
                got_down.at[t],
                net.at(dz=-1),
                down_on,
                (z <= LINE - 2) & (z + 1 >= LINE - 1 - t),
            )
        )
        yield
    last = LINE - 2

    def add_up():
        held[z] += got_up[last].astype(jnp.float32)

    def add_down():
        held[z] += got_down[last].astype(jnp.float32)

    ups[last].arrived()
    ready(LINE - 1)
    pl.when(z >= 1)(add_up)
    yield
    downs[last].arrived()
    pl.when(z <= LINE - 2)(add_down)


def far_first(z):
    return [
        jnp.where(z < 2, 3, 0),
        jnp.where(z < 2, 2, 1),
        z + 1 - 2 * lax.rem(z, 2),
        z,
    ]


def line_scratch(rows, cols):
    line = pltpu.VMEM((LINE - 1, rows, cols), jnp.bfloat16)
    return [pltpu.VMEM((LINE, rows, cols), jnp.float32), line, line, line, line]


def sum_sides(net, src, from_side, line, make=None):
    z, y = net.z, net.y
    held = line[0]
    order = far_first(z)
    sides = []
    for k in order:
        if make is not None:
            make(2 * k + 1 - y)
        sides.append(net.put(src.at[2 * k + 1 - y], from_side.at[k], net.at(dy=1)))
        if make is not None and len(sides) == 2:
            yield
    yield

    def ready(t):
        k = order[t]
        if make is not None:
            make(2 * k + y)
        sides[t].arrived()
        held[k] = src[2 * k + y].astype(jnp.float32) + from_side[k].astype(jnp.float32)

    yield from sum_line(net, *line, ready)


BLOCK = 256
REST = (4, 3)
BACK_ORDER = (
    7, 4, 0, 1, 4, 4, 5, 4, 7, 7, 7, 4, 7, 7, 7, 0, 7, 0, 4, 4, 7, 7, 0, 0, 4, 4, 0, 7, 0, 2,
    1, 1, 6, 4, 0, 4, 6, 0, 3, 3, 1, 0, 7, 1, 7, 3, 2, 0, 5, 3, 0, 4, 6, 7, 3, 0, 1, 7, 3, 0,
    1, 2, 6, 4, 6, 4, 7, 7, 2, 2, 6, 1, 6, 2, 2, 7, 0, 3, 3, 7, 2, 2, 1, 6, 1, 7, 0, 6, 8, 2,
    7, 2, 8, 2, 4, 2, 1, 2, 7, 0, 1, 2, 3, 1, 6, 3, 3, 1, 8, 2, 1, 3, 3, 6, 4, 3, 2, 3, 1, 1,
    2, 8,
)


def turn_lanes(v):
    return pltpu.roll(v, HEAD_SIZE // 2, 1)


def dot_last(a, b):
    return lax.dot_general(a, b, (((1,), (1,)), ((), ())), preferred_element_type=jnp.float32)


def resting(rounds):
    for _ in range(rounds):
        yield


class Bag:
    def __init__(self, **members):
        self.__dict__.update(members)


def bags(tree):
    if isinstance(tree, list):
        return [bags(v) for v in tree]
    return Bag(**{n: bags(v) for n, v in tree.items()}) if isinstance(tree, dict) else tree


def near_first(z):
    return far_first(z)[::-1]


def kernel_with(
    body, moved, loaded, outs, scratch, copies, number, in_vmem=(), near=(), scalar=()
):
    scratch = dict(
        scratch, held={n: pltpu.VMEM(v.shape, v.dtype) for n, v in loaded.items()}
    )
    flat, tree = jax.tree.flatten(scratch)
    f_in, in_tree = jax.tree.flatten((moved, loaded))
    f_out, out_tree = jax.tree.flatten(outs)

    def whole(net, local, *refs):
        given, to_load = jax.tree.unflatten(in_tree, refs[: len(f_in)])
        out = Bag(**jax.tree.unflatten(out_tree, refs[len(f_in) : len(f_in) + len(f_out)]))
        r = bags(jax.tree.unflatten(tree, refs[len(f_in) + len(f_out) :]))
        used = iter(range(96))

        def fetch(src, dst):
            return Local(pltpu.make_async_copy(src, dst, local.at[next(used)]))

        def load():
            return {n: fetch(to_load[n], getattr(r.held, n)) for n in to_load}

        body(net, fetch, load, Bag(**given), out, r)
        net.close()

    order = jax.tree.unflatten(out_tree, range(len(f_out)))
    in_order, _ = jax.tree.unflatten(in_tree, range(len(f_in)))
    result = net_call(
        whole,
        f_out,
        f_in,
        copies,
        96,
        number,
        scratch=flat,
        vmem=[len(f_in) + order.get(n) for n in in_vmem] + [in_order.get(n) for n in near],
        smem=[in_order.get(n) for n in scalar],
    )
    return Bag(**jax.tree.unflatten(out_tree, result))


def middle(net, fetch, arriving, out, r):
    y, core, me = net.y, net.core, net.me
    slots, rows, width = r.mixed_in.shape
    _, shard, wide = r.w_gu.shape
    ff, d = wide // 2, r.residual.shape[1]
    piece, pad = rows // slots, 32
    f32, bf = jnp.float32, jnp.bfloat16
    every = pl.ds(0, rows)
    parts = [pl.ds(0, rows // 2), pl.ds(rows // 2, rows // 2)]

    def land(copies):
        for c in copies:
            c.arrived()

    def from_head(head):
        at = pl.ds(pl.multiple_of(lax.rem(head, 2) * width, width), width)
        return dot(r.mixed_in[head], r.w_o[head // 2, at])

    land(arriving.o)
    arriving.heads[-1].arrived()
    total = r.residual[...].astype(f32) + from_head(me)
    for k in range(1, slots):
        arriving.heads[k - 1].arrived()
        total = total + from_head(lax.rem(me + slots - k, slots))
    r.middle[...] = total
    own, far = 2 * y + core, 2 * (1 - y) + core
    r.quad[own] = low(root_mean_norm(total, r.m_gain[...]))
    near = net.put(r.quad.at[own], r.quad.at[own], net.at(dc=1))
    over = [net.put(r.quad.at[own, at], r.quad.at[own, at], net.at(dy=1)) for at in parts]
    arriving.results.append(fetch(r.mixed_in, out.mixed_in))
    near.arrived()
    land(arriving.gu)
    land(arriving.grad)

    def pair(ref, side, at):
        return ref[pl.ds(2 * side, 2), at].reshape(2 * at.size, ref.shape[-1])

    def forward(side, at):
        gate_up = dot(pair(r.quad, side, at), r.w_gu[...].reshape(4 * shard, 2 * ff))
        return gate_up[:, :ff], gate_up[:, ff:]

    def backward(side, at, gate, up):
        d_hidden = dot_last(pair(r.grad, side, at), r.w_dn[...].reshape(ff, d))
        sig = 1.0 / (1.0 + jnp.exp(-gate))
        silu = gate * sig
        d_gate = low(d_hidden * up * (sig * (1.0 + gate * (1.0 - sig))))
        both, split = pl.ds(2 * side, 2), (2, at.size, ff)
        r.hidden[both, at] = low(silu * up).reshape(split)
        r.d_gu[both, at, pl.ds(0, ff)] = d_gate.reshape(split)
        r.d_gu[both, at, pl.ds(ff, ff)] = low(d_hidden * silu).reshape(split)

    def part(side, at):
        w_gu = r.w_gu[...].reshape(4 * shard, 2 * ff)
        return dot_last(pair(r.d_gu, side, at), w_gu).reshape(2, at.size, d)

    def out_part(side):
        return dot(pair(r.hidden, side, every), r.w_dn[...].reshape(ff, d)).reshape(2, rows, d)

    near_values = forward(y, every)
    over[0].arrived()
    last = [net.put(r.quad.at[far, parts[0]], r.quad.at[far, parts[0]], net.at(dc=1))]
    land(arriving.dn)
    backward(y, every, *near_values)
    over[1].arrived()
    last.append(net.put(r.quad.at[far, parts[1]], r.quad.at[far, parts[1]], net.at(dc=1)))
    one, side = [], []

    def far_part(i):
        at = parts[i]
        last[i].arrived()
        backward(1 - y, at, *forward(1 - y, at))
        r.far_part[:, at] = low(part(1 - y, at))
        one.append(net.put(r.far_part.at[1 - core, at], r.got.at[0, at], net.at(dc=1)))

    def far_sum(i):
        at = parts[i]
        one[i].arrived()
        r.to_side[0, at] = low(r.far_part[core, at].astype(f32) + r.got[0, at].astype(f32))
        side.append(net.put(r.to_side.at[0, at], r.got.at[2, at], net.at(dy=1)))

    far_part(0)
    r.near_part[...] = part(y, every)
    r.beside[...] = low(r.near_part[1 - core])
    two = net.put(r.beside, r.got.at[1], net.at(dc=1))
    far_sum(0)
    far_part(1)
    r.far_out[...] = low(out_part(1 - y))
    far_sum(1)
    g = r.grad[...].reshape(4 * rows, d)
    r.g_dn[...] = low(outer_rows(r.hidden[...].reshape(4 * rows, ff), g)).reshape(2, ff // 2, d)
    sent = [fetch(r.g_dn, out.down)]
    some = pl.ds(0, d // 2)
    dn_over = net.put(r.g_dn.at[1 - net.x, :, some], r.dn_got, net.at(dx=1))
    one_out = net.put(r.far_out.at[1 - core], r.got.at[3], net.at(dc=1))
    r.near_out[...] = out_part(y)
    r.beside_out[...] = low(r.near_out[1 - core])
    two_out = net.put(r.beside_out, r.got.at[4], net.at(dc=1))
    n2 = r.quad[...].reshape(4 * rows, d)
    d_gu = r.d_gu[...].reshape(4 * rows, 2 * ff)
    r.g_gate[...] = low(outer_rows(n2, d_gu[:, :ff]))
    sent.append(fetch(r.g_gate, out.gate))
    one_out.arrived()
    r.to_side[1] = low(r.far_out[core].astype(f32) + r.got[3].astype(f32))
    side_out = net.put(r.to_side.at[1], r.got.at[5], net.at(dy=1))
    r.g_up[...] = low(outer_rows(n2, d_gu[:, ff:]))
    sent.append(fetch(r.g_up, out.up))
    two.arrived()
    land(side)
    d_normed = r.near_part[core] + r.got[1].astype(f32) + r.got[2].astype(f32)
    dx2, dg2 = norm_back(r.middle[...], r.m_gain[...], d_normed)
    out.dg2[...] = jnp.sum(dg2, axis=0, keepdims=True)
    middle_low = low(r.grad[own].astype(f32) + dx2)
    for i in range(slots):
        r.dm[i] = low(dot_last(middle_low, r.w_o[i // 2, pl.ds(i % 2 * width, width)]))
    sent.append(fetch(r.dm, out.dm))
    for i in range(slots):
        out.back[i, pl.ds(0, piece)] = middle_low[i * piece : (i + 1) * piece]
        out.back[i, pl.ds(piece, pad - piece)] = jnp.zeros((pad - piece, d), bf)
    out.middle_low[...] = middle_low
    two_out.arrived()
    side_out.arrived()
    out.output[...] = low(
        r.middle[...] + r.near_out[core] + r.got[4].astype(f32) + r.got[5].astype(f32)
    )
    dn_over.arrived()
    out.down_sum[...] = low(
        r.g_dn[net.x, :, some].astype(f32) + r.dn_got[...].astype(f32)
    )
    land(sent)
    land(arriving.results)


def front_kernel(moved, loaded, number):
    a = Bag(**moved)
    _, rows, d = a.tok.shape
    slots = 2 * LINE
    count = rows * slots
    blocks = count // BLOCK
    width = 2 * HEAD_SIZE
    shard = a.w_q.shape[0]
    half = a.w_gate.shape[1] // 8
    o_rows = a.w_o.shape[0]
    scale = HEAD_SIZE**-0.5
    bf, f32 = jnp.bfloat16, jnp.float32
    piece = rows // slots
    ff = 2 * half
    gain_cols = 2 * a.attn_gain.shape[0] + 2 * HEAD_SIZE

    scratch = dict(
        tok=pltpu.VMEM((slots, rows, d), bf),
        w_qkv=pltpu.VMEM((4, shard, 2 * width), bf),
        gains=pltpu.VMEM((4, 1, gain_cols), f32),
        columns=pltpu.VMEM((count, 8), f32),
        normed=pltpu.VMEM((count, d), bf),
        qkv=pltpu.VMEM((count, 2 * width), f32),
        q=pltpu.VMEM((count, width), bf),
        k=pltpu.VMEM((count, HEAD_SIZE), bf),
        v=pltpu.VMEM((count, HEAD_SIZE), bf),
        kt=pltpu.VMEM((HEAD_SIZE, count), bf),
        vt=pltpu.VMEM((HEAD_SIZE, count), bf),
        cos=pltpu.VMEM((count, HEAD_SIZE), f32),
        sin=pltpu.VMEM((count, HEAD_SIZE), f32),
        mixed=pltpu.VMEM((count, width), f32),
        mixed_low=pltpu.VMEM((count, width), bf),
        sent=pltpu.VMEM((slots, rows, width), bf),
        w_o=pltpu.VMEM((4, o_rows, d), bf),
        w_gu=pltpu.VMEM((4, shard, 4 * half), bf),
        grad=pltpu.VMEM((4, rows, d), bf),
        mixed_in=pltpu.VMEM((slots, rows, width), bf),
        residual=pltpu.VMEM((rows, d), bf),
        m_gain=pltpu.VMEM((1, d), f32),
        w_dn=pltpu.VMEM((2, half, d), bf),
        middle=pltpu.VMEM((rows, d), f32),
        quad=pltpu.VMEM((4, rows, d), bf),
        hidden=pltpu.VMEM((4, rows, ff), bf),
        d_gu=pltpu.VMEM((4, rows, 2 * ff), bf),
        near_part=pltpu.VMEM((2, rows, d), f32),
        far_part=pltpu.VMEM((2, rows, d), bf),
        near_out=pltpu.VMEM((2, rows, d), f32),
        far_out=pltpu.VMEM((2, rows, d), bf),
        beside=pltpu.VMEM((rows, d), bf),
        beside_out=pltpu.VMEM((rows, d), bf),
        got=pltpu.VMEM((6, rows, d), bf),
        to_side=pltpu.VMEM((2, rows, d), bf),
        g_gate=pltpu.VMEM((d, ff), bf),
        g_up=pltpu.VMEM((d, ff), bf),
        g_dn=pltpu.VMEM((2, half, d), bf),
        dn_got=pltpu.VMEM((half, d // 2), bf),
        dm=pltpu.VMEM((slots, rows, width), bf),
    )
    outs = dict(
        first=shape_of(1, count, kind=jnp.int32),
        dealt=shape_of(1, count, kind=jnp.int32),
        back_from=shape_of(rows, 1, kind=jnp.int32),
        mixed_in=shape_of(slots, rows, width),
        normed=shape_of(count, d),
        qkv=shape_of(count, 2 * width, kind=f32),
        q=shape_of(count, width),
        k=shape_of(count, HEAD_SIZE),
        v=shape_of(count, HEAD_SIZE),
        kt=shape_of(HEAD_SIZE, count),
        cos=shape_of(count, HEAD_SIZE, kind=f32),
        sin=shape_of(count, HEAD_SIZE, kind=f32),
        mixed=shape_of(count, width, kind=f32),
        lse=shape_of(2, 1, count, kind=f32),
        w_qkv=shape_of(4, shard, 2 * width),
        a_gain=shape_of(1, d, kind=f32),
        q_gain=shape_of(1, HEAD_SIZE, kind=f32),
        k_gain=shape_of(1, HEAD_SIZE, kind=f32),
        output=shape_of(rows, d),
        back=shape_of(slots, 32, d),
        dm=shape_of(slots, rows, width),
        gate=shape_of(d, ff),
        up=shape_of(d, ff),
        down=shape_of(2, half, d),
        down_sum=shape_of(half, d // 2),
        middle_low=shape_of(rows, d),
        dg2=shape_of(1, d, kind=f32),
    )

    def body(net, fetch, load, given, out, r):
        z, y, x, core, me = net.z, net.y, net.x, net.core, net.me
        f = 2 * x + core
        done = set()
        tok = given.tok.at[0]
        tok_own = fetch(tok, r.tok.at[me])

        def lanes(start, size):
            return pl.ds(pl.multiple_of(start, HEAD_SIZE), size)

        head_parts = [
            (given.w_q.at[:, lanes(me * width, width)], pl.ds(0, width)),
            (given.w_k.at[:, lanes(me * HEAD_SIZE, HEAD_SIZE)], pl.ds(width, HEAD_SIZE)),
            (
                given.w_v.at[:, lanes(me * HEAD_SIZE, HEAD_SIZE)],
                pl.ds(width + HEAD_SIZE, HEAD_SIZE),
            ),
        ]
        w_own = [fetch(src, r.w_qkv.at[f, :, to]) for src, to in head_parts]
        greet(net, ("ctx", "x", "core", "far"))
        log = {s: [] for s in range(LINE)}
        waits = list(w_own)
        zone = lax.broadcasted_iota(jnp.int32, (1, HEAD_SIZE), 1) // (HEAD_SIZE // 4) == f

        def zoned(ref):
            return jnp.where(zone, jnp.concatenate([ref[...].astype(f32)] * 4, axis=1), 0.0)

        r.gains[f] = jnp.concatenate(
            [
                given.attn_gain[...].astype(f32).reshape(1, -1),
                given.mlp_gain[...].astype(f32).reshape(1, -1),
                zoned(given.q_gain),
                zoned(given.k_gain),
            ],
            axis=1,
        )

        def head_weights():
            beside = [net.put(src, r.w_qkv.at[f, :, to], net.at(dc=1)) for src, to in head_parts]
            beside.append(net.put(r.gains.at[f], r.gains.at[f], net.at(dc=1)))
            across = [net.put(src, r.w_qkv.at[f, :, to], net.at(dx=1)) for src, to in head_parts]
            across.append(net.put(r.gains.at[f], r.gains.at[f], net.at(dx=1)))
            yield
            for c in across:
                c.arrived()
            far = 2 * (1 - x) + core
            beside += [
                net.put(r.w_qkv.at[far], r.w_qkv.at[far], net.at(dc=1)),
                net.put(r.gains.at[far], r.gains.at[far], net.at(dc=1)),
            ]
            for c in waits:
                c.wait()
            for c in beside:
                c.arrived()
            r.own = fetch(r.w_qkv, out.w_qkv)
            done.add("head")
            yield

        arriving = Bag(o=[], gu=[], dn=[], grad=[], heads=[], results=[])

        def other_weights():
            yield
            pair, part_rows = lax.rem(z, 2), o_rows // 2
            mine, other = (
                pl.ds(pl.multiple_of(p * part_rows, part_rows), part_rows) for p in (pair, 1 - pair)
            )
            over = net.put(given.w_o.at[mine], r.w_o.at[f, mine], net.at(dx=1))
            arriving.o += [
                fetch(given.w_o, r.w_o.at[f]),
                net.put(given.w_o, r.w_o.at[f], net.at(dc=1)),
            ]

            def quarter(c):
                return [
                    (
                        w.at[:, lanes((2 * xs + c) * 2 * half + y * half, half)],
                        r.w_gu.at[f, :, pl.ds((2 * i + xs) * half, half)],
                    )
                    for i, w in enumerate((given.w_gate, given.w_up))
                    for xs in range(2)
                ]

            arriving.gu += [fetch(src, to) for src, to in quarter(core)]
            arriving.gu += [net.put(src, to, net.at(dc=1)) for src, to in quarter(1 - core)]
            arriving.gu += [net.put(src, to, net.at(dx=1)) for src, to in quarter(core)]
            arriving.gu += [net.put(src, to, net.at(dx=1, dc=1)) for src, to in quarter(1 - core)]
            part = given.w_down.at[pl.ds(pl.multiple_of(y * half, half), half)]
            arriving.dn += [
                fetch(part, r.w_dn.at[x]),
                net.put(part, r.w_dn.at[x], net.at(dx=1)),
            ]
            yield from resting(REST[0])
            over.arrived()
            far = r.w_o.at[2 * (1 - x) + core, mine]
            handed = net.put(far, far, net.at(dz=1 - 2 * pair))
            arriving.o.append(net.put(far, far, net.at(dc=1)))
            yield from resting(REST[1])
            handed.arrived()
            far = r.w_o.at[2 * (1 - x) + core, other]
            arriving.o.append(net.put(far, far, net.at(dc=1)))

        def output_grad():
            yield from resting(5)
            own = r.grad.at[2 * y + core]
            grad = given.grad.at[0]
            arriving.grad += [
                fetch(grad, own),
                net.put(grad, own, net.at(dc=1)),
                net.put(grad, own, net.at(dy=1)),
            ]
            yield
            arriving.grad[2].arrived()
            far = r.grad.at[2 * (1 - y) + core]
            arriving.grad.append(net.put(far, far, net.at(dc=1)))

        def project(slot):
            at = pl.ds(pl.multiple_of(slot * rows, rows), rows)
            normed = low(root_mean_norm(r.tok[slot].astype(f32), out.a_gain[...]))
            r.normed[at] = normed
            qkv = dot(normed, r.w_qkv[...].reshape(4 * shard, 2 * width))
            r.qkv[at] = qkv
            cos, sin = r.cos[at], r.sin[at]

            def turned(part, gain):
                v = root_mean_norm(part, gain)
                return low(v * cos + turn_lanes(v) * sin)

            for g in range(2):
                cols = pl.ds(g * HEAD_SIZE, HEAD_SIZE)
                r.q[at, cols] = turned(
                    qkv[:, g * HEAD_SIZE : (g + 1) * HEAD_SIZE], out.q_gain[...]
                )
            r.k[at] = turned(qkv[:, width : width + HEAD_SIZE], out.k_gain[...])
            r.v[at] = low(qkv[:, width + HEAD_SIZE :])

        def main():
            ids = lax.broadcasted_iota(jnp.int32, (1, count), 1)
            first, dealt, back, start = jnp.zeros_like(ids), ids, ids, 0
            for i in range(1, given.lengths.shape[1]):
                start = start + given.lengths[0, i - 1]
                first = jnp.where(ids >= start, start, first)
            for s in range(slots):
                for j in range(slots):
                    begin = given.deal[0, s, j] * rows + s * piece
                    dealt = jnp.where(
                        (ids >= begin) & (ids < begin + piece),
                        ids - begin + (s * rows + j * piece),
                        dealt,
                    )
            for j in range(slots):
                begin = given.deal[0, me, j] * 32
                back = jnp.where(
                    (ids >= j * piece) & (ids < (j + 1) * piece), ids - j * piece + begin, back
                )
            out.first[...] = first
            out.dealt[...] = dealt
            row = lax.broadcasted_iota(jnp.int32, (8, count), 0)
            stack = jnp.where(row == 0, ids - first, jnp.where(row == 1, dealt, back))
            r.columns[...] = jnp.transpose(stack.astype(f32))
            out.back_from[...] = r.columns[pl.ds(0, rows), 2:3].astype(jnp.int32)
            for i in range(slots):
                at = pl.ds(i * rows, rows)
                angle = r.columns[at, 0:1] * given.freq[0:1]
                r.cos[at] = jnp.cos(angle)
                r.sin[at] = jnp.sin(angle) * given.freq[1:2]
            yield
            while "head" not in done:
                yield
            gains = [r.gains[i] for i in range(4)]
            part = d // 4
            for i in range(4):
                out.a_gain[:, pl.ds(i * part, part)] = gains[i][:, :part]
                r.m_gain[:, pl.ds(i * part, part)] = gains[i][:, part : 2 * part]
            total = gains[0] + gains[1] + gains[2] + gains[3]
            out.q_gain[...] = total[:, 2 * part : 2 * part + HEAD_SIZE]
            out.k_gain[...] = total[:, 2 * part + HEAD_SIZE :]
            tok_own.wait()
            near = near_first(z)
            for k in range(LINE):
                project(2 * near[k] + y)
                if k:
                    for c in log[k - 1]:
                        c.arrived()
                    project(2 * near[k - 1] + 1 - y)
                yield
            for c in log[LINE - 1]:
                c.arrived()
            project(2 * near[LINE - 1] + 1 - y)
            results = [
                fetch(r.normed, out.normed),
                fetch(r.qkv, out.qkv),
                fetch(r.q, out.q),
                fetch(r.k, out.k),
                fetch(r.v, out.v),
                fetch(r.cos, out.cos),
                fetch(r.sin, out.sin),
                r.own,
            ]
            for i in range(blocks):
                at = pl.ds(i * BLOCK, BLOCK)
                r.kt[:, at] = jnp.transpose(r.k[at])
                r.vt[:, at] = jnp.transpose(r.v[at])
            results.append(fetch(r.kt, out.kt))
            for i in range(blocks):
                here = pl.ds(i * BLOCK, BLOCK)
                first = out.first[:, here]
                t = i * BLOCK + lax.broadcasted_iota(jnp.int32, (BLOCK, BLOCK), 1)
                q = [r.q[here, pl.ds(g * HEAD_SIZE, HEAD_SIZE)] for g in range(2)]

                def step(n, held, i=i, q=q, first=first, t=t):
                    j = i - n
                    at = pl.ds(pl.multiple_of(j * BLOCK, BLOCK), BLOCK)
                    k, vt = r.k[at], r.vt[:, at]
                    u = j * BLOCK + lax.broadcasted_iota(jnp.int32, (BLOCK, BLOCK), 0)
                    allowed = (u >= first) & (u <= t)
                    result = []
                    for g in range(2):
                        top, total, mixed = held[g]
                        scores = jnp.where(allowed, dot_last(k, q[g]) * scale, negative_filler)
                        new = jnp.maximum(top, jnp.max(scores, axis=0, keepdims=True))
                        fade = jnp.exp(top - new)
                        p = jnp.exp(scores - new)
                        total = total * fade + jnp.sum(p, axis=0, keepdims=True)
                        result.append((new, total, mixed * fade + dot(vt, low(p))))
                    return tuple(result)

                row = jnp.full((1, BLOCK), negative_filler, f32)
                none = (row, jnp.zeros((1, BLOCK), f32), jnp.zeros((HEAD_SIZE, BLOCK), f32))
                held = lax.fori_loop(0, i + 1, step, (none, none))
                for g in range(2):
                    top, total, mixed = held[g]
                    cols = pl.ds(g * HEAD_SIZE, HEAD_SIZE)
                    out.lse[g, :, here] = top + jnp.log(total)
                    mixed = jnp.transpose(mixed / total)
                    r.mixed[here, cols] = mixed
                    r.mixed_low[here, cols] = low(mixed)
                yield
            results.append(fetch(r.mixed, out.mixed))
            ids = lax.broadcasted_iota(jnp.int32, (rows, count), 1)

            def hot(slot):
                at = pl.ds(pl.multiple_of(slot * rows, rows), rows)
                return low(jnp.where(r.columns[at, 1:2].astype(jnp.int32) == ids, 1.0, 0.0))

            for k in range(1, slots):
                other = lax.rem(me + k, slots)
                r.sent[other] = low(dot(hot(other), r.mixed_low[...]))
                there = (other // 2, lax.rem(other, 2), x, core)
                arriving.heads.append(net.put(r.sent.at[other], r.mixed_in.at[me], there))
            mine = hot(me)
            r.sent[me] = low(dot(mine, r.mixed_low[...]))
            arriving.heads.append(fetch(r.sent.at[me], r.mixed_in.at[me]))
            r.residual[...] = low(dot(mine, r.tok[...].reshape(count, d)))
            arriving.results += results
            yield

        drive(
            head_weights(),
            by_steps(gather_line_first(net, tok, lambda slot: r.tok.at[slot], log)),
            main(),
            other_weights(),
            output_grad(),
        )
        middle(net, fetch, arriving, out, r)

    return kernel_with(
        body,
        moved,
        loaded,
        outs,
        scratch,
        110,
        number,
        (
            "lse",
            "a_gain",
            "q_gain",
            "k_gain",
            "first",
            "dealt",
            "back_from",
            "output",
            "back",
            "middle_low",
            "dg2",
            "down_sum",
        ),
        ("attn_gain", "mlp_gain", "q_gain", "k_gain", "freq"),
        ("lengths", "deal"),
    )


def back_kernel(dims, number):
    rows, count = dims
    blocks = count // BLOCK
    scale = HEAD_SIZE**-0.5
    width = 2 * HEAD_SIZE
    d = MODEL_WIDTH

    def run(moved, loaded):
        a = Bag(**moved)
        gu_rows, gu_cols = a.gate.shape[1:]
        dn_rows = a.down.shape[1]
        o_rows = 2 * width
        bf, f32 = jnp.bfloat16, jnp.float32
        z_gu, z_dn, z_o = gu_rows // LINE, dn_rows // LINE, o_rows // (2 * LINE)
        gain_width = 2 * d + 2 * HEAD_SIZE

        def quarter():
            return dict(
                got=pltpu.VMEM((2, gu_rows, gu_cols), bf),
                own=pltpu.VMEM((2, gu_rows, gu_cols), bf),
                low=pltpu.VMEM((2, z_gu, gu_cols), bf),
                pair=pltpu.VMEM((2, z_gu, gu_cols), bf),
                line=line_scratch(2 * z_gu, gu_cols),
            )

        scratch = dict(
            held={n: pltpu.VMEM(v.shape, v.dtype) for n, v in loaded.items()},
            gate=quarter(),
            up=quarter(),
            down=[
                dict(
                    own=pltpu.VMEM((dn_rows, d // 2), bf),
                    got=pltpu.VMEM((dn_rows, d // 2), bf),
                    low=pltpu.VMEM((z_dn, d // 2), bf),
                    line=line_scratch(z_dn, d // 2),
                )
                for _ in range(2)
            ],
            o=dict(
                own=pltpu.VMEM((4, o_rows, d), bf),
                core=pltpu.VMEM((2, o_rows, d), bf),
                got=pltpu.VMEM((o_rows, d), bf),
                sum=pltpu.VMEM((2 * LINE, z_o, d), bf),
                side=pltpu.VMEM((LINE, z_o, d), bf),
                low=pltpu.VMEM((z_o, d), bf),
                line=line_scratch(z_o, d),
            ),
            h=dict(
                own=pltpu.VMEM((4, d // 4, 2 * width), bf),
                core=pltpu.VMEM((2, d // 4, 2 * width), bf),
                got=pltpu.VMEM((d // 4, 2 * width), bf),
                low=pltpu.VMEM((d // 4, 2 * width), bf),
            ),
            dm_all=pltpu.VMEM((2 * LINE, rows, width), bf),
            back=pltpu.VMEM(a.back.shape, bf),
            do=pltpu.VMEM((count, width), bf),
            dk=pltpu.VMEM((count, HEAD_SIZE), f32),
            dv=pltpu.VMEM((count, HEAD_SIZE), f32),
            dqkv=pltpu.VMEM((count, 2 * width), bf),
            dgq=pltpu.VMEM((1, HEAD_SIZE), f32),
            dgk=pltpu.VMEM((1, HEAD_SIZE), f32),
            part=dict(
                sum=pltpu.VMEM((2 * LINE, rows, d), bf),
                side=pltpu.VMEM((LINE, rows, d), bf),
                line=line_scratch(rows, d),
            ),
            g=dict(
                mine=pltpu.VMEM((1, gain_width), f32),
                four=pltpu.VMEM((1, gain_width), f32),
                got=pltpu.VMEM((3, 1, gain_width), f32),
                all=pltpu.VMEM((2 * LINE, 1, gain_width), f32),
            ),
        )
        flat, tree = jax.tree.flatten(scratch)
        f_in, in_tree = jax.tree.flatten((moved, loaded))
        outs = dict(
            input_grad=shape_of(rows, d, kind=f32),
            a_grad=shape_of(1, d // 4, kind=f32),
            m_grad=shape_of(1, d // 4, kind=f32),
            q_grad=shape_of(1, HEAD_SIZE // 4, kind=f32),
            k_grad=shape_of(1, HEAD_SIZE // 4, kind=f32),
            gate=shape_of(2 * LINE, 2, z_gu, gu_cols),
            up=shape_of(2 * LINE, 2, z_gu, gu_cols),
            down=shape_of(2 * LINE, z_dn, d),
            o=shape_of(2 * LINE, z_o, d),
            heads=shape_of(2 * LINE, d // 4, 2 * width),
        )
        f_out, out_tree = jax.tree.flatten(outs)

        def body(net, local, *refs):
            given, to_load = jax.tree.unflatten(in_tree, refs[: len(f_in)])
            given = Bag(**given)
            out = Bag(**jax.tree.unflatten(out_tree, refs[len(f_in) : len(f_in) + len(f_out)]))
            r = bags(jax.tree.unflatten(tree, refs[len(f_in) + len(f_out) :]))
            h = r.held
            z, y, x, core, me = net.z, net.y, net.x, net.core, net.me
            slots = 2 * LINE
            used = iter(range(64))

            def fetch(src, dst):
                return Local(pltpu.make_async_copy(src, dst, local.at[next(used)]))

            greet(net, ("ctx", "x", "core", "far"))
            loads = {n: fetch(to_load[n], getattr(h, n)) for n in to_load}
            dm_own = fetch(given.dm.at[me], r.dm_all.at[me])
            back_own = fetch(given.back.at[me], r.back.at[me])
            gate_own, up_own = (
                [fetch(src.at[2 * x + c], piece.own.at[c]) for c in range(2)]
                for src, piece in ((given.gate, r.gate), (given.up, r.up))
            )
            columns = [pl.ds(0, d // 2), pl.ds(d // 2, d // 2)]
            down_own = [
                fetch(given.down_sum, r.down[0].own),
                fetch(given.down.at[x, :, columns[1]], r.down[1].own),
            ]
            back_copies = []

            def need(*which):
                for n in which:
                    if n in loads:
                        loads.pop(n).wait()

            def to_all(src, out):
                copies = []
                for k in range(1, slots):
                    other = lax.rem(me + k, slots)
                    there = (other // 2, lax.rem(other, 2), x, core)
                    copies.append(net.put(src(other), out.at[me], there))
                return copies

            def back_rows():
                back_copies.extend(to_all(lambda other: given.back.at[other], r.back))
                yield

            def main():
                dm_copies = to_all(lambda other: given.dm.at[other], r.dm_all)
                yield
                need(*list(loads))
                dm_own.wait()
                for c in dm_copies:
                    c.arrived()
                yield
                for i in range(blocks):
                    t = i * BLOCK + lax.broadcasted_iota(jnp.int32, (BLOCK, count), 0)
                    hot = low(jnp.where(h.dealt[...] == t, 1.0, 0.0))
                    r.do[pl.ds(i * BLOCK, BLOCK)] = low(
                        dot(hot, r.dm_all[...].reshape(count, width))
                    )
                r.dk[...] = jnp.zeros_like(r.dk)
                r.dv[...] = jnp.zeros_like(r.dv)
                yield
                dgq = jnp.zeros((1, HEAD_SIZE), f32)
                for i in range(blocks):
                    here = pl.ds(i * BLOCK, BLOCK)
                    first = h.first[:, here]
                    t = i * BLOCK + lax.broadcasted_iota(jnp.int32, (BLOCK, BLOCK), 1)
                    heads = []
                    for g in range(2):
                        lanes = pl.ds(g * HEAD_SIZE, HEAD_SIZE)
                        q, do = h.q[here, lanes], r.do[here, lanes]
                        product = do.astype(f32) * h.mixed[here, lanes]
                        delta = jnp.sum(jnp.transpose(product), axis=0, keepdims=True)
                        heads.append((q, do, h.lse[g, :, here], delta))

                    def step(j, held, heads=heads, first=first, t=t):
                        at = pl.ds(pl.multiple_of(j * BLOCK, BLOCK), BLOCK)
                        k, v, kt = h.k[at], h.v[at], h.kt[:, at]
                        u = j * BLOCK + lax.broadcasted_iota(jnp.int32, (BLOCK, BLOCK), 0)
                        allowed = (u >= first) & (u <= t)
                        dk, dv, out = r.dk[at], r.dv[at], []
                        for (q, do, lse, delta), dq in zip(heads, held):
                            p = jnp.where(allowed, jnp.exp(dot_last(k, q) * scale - lse), 0.0)
                            ds = low(p * (dot_last(v, do) - delta))
                            dv = dv + dot(low(p), do)
                            dk = dk + dot(ds, q)
                            out.append(dq + dot(kt, ds))
                        r.dk[at] = dk
                        r.dv[at] = dv
                        return tuple(out)

                    zero = jnp.zeros((HEAD_SIZE, BLOCK), f32)
                    result = lax.fori_loop(0, i + 1, step, (zero, zero))
                    cos, sin = h.cos[here], h.sin[here]
                    for g in range(2):
                        lanes = pl.ds(g * HEAD_SIZE, HEAD_SIZE)
                        grad = jnp.transpose(result[g]) * scale
                        grad = grad * cos - turn_lanes(grad) * sin
                        dx, dg = norm_back(h.qkv[here, lanes], h.q_gain[...], grad)
                        r.dqkv[here, lanes] = low(dx)
                        dgq = dgq + jnp.sum(dg, axis=0, keepdims=True)
                    yield
                dgk = jnp.zeros((1, HEAD_SIZE), f32)
                for i in range(blocks):
                    here = pl.ds(i * BLOCK, BLOCK)
                    grad = r.dk[here] * scale
                    grad = grad * h.cos[here] - turn_lanes(grad) * h.sin[here]
                    dx, dg = norm_back(
                        h.qkv[here, pl.ds(width, HEAD_SIZE)], h.k_gain[...], grad
                    )
                    r.dqkv[here, pl.ds(width, HEAD_SIZE)] = low(dx)
                    r.dqkv[here, pl.ds(width + HEAD_SIZE, HEAD_SIZE)] = low(r.dv[here])
                    dgk = dgk + jnp.sum(dg, axis=0, keepdims=True)
                r.dgq[...] = dgq
                r.dgk[...] = dgk
                yield

                def make(slot):
                    at = pl.ds(pl.multiple_of(slot * rows, rows), rows)
                    r.part.sum[slot] = low(dot_last(r.dqkv[at], h.w_qkv[...].reshape(d, 2 * width)))

                yield from sum_sides(net, r.part.sum, r.part.side, r.part.line, make)
                yield
                dx1, dg1 = norm_back(
                    h.tok[0].astype(f32), h.a_gain[...], r.part.line[0][z]
                )
                for c in back_copies:
                    c.arrived()
                back_own.wait()
                ids = lax.broadcasted_iota(jnp.int32, (rows, slots * a.back.shape[1]), 1)
                hot = low(jnp.where(h.back_from[...] == ids, 1.0, 0.0))
                out.input_grad[...] = dx1 + dot(hot, r.back[...].reshape(-1, d))
                r.g.mine[:, pl.ds(0, d)] = jnp.sum(dg1, axis=0, keepdims=True)
                r.g.mine[:, pl.ds(d, d)] = h.dg2[...]
                r.g.mine[:, pl.ds(2 * d, HEAD_SIZE)] = r.dgq[...]
                r.g.mine[:, pl.ds(2 * d + HEAD_SIZE, HEAD_SIZE)] = r.dgk[...]
                yield

            def gains():
                sides = [net.at(dc=1), net.at(dx=1), net.at(dx=1, dc=1)]
                pair = [net.put(r.g.mine, r.g.got.at[i], to) for i, to in enumerate(sides)]
                yield
                for c in pair:
                    c.arrived()
                along = r.g.mine[...] + r.g.got[0]
                across = r.g.got[1] + r.g.got[2]
                r.g.four[...] = along + across
                r.g.all[me] = r.g.four[...]
                copies = to_all(lambda other: r.g.four, r.g.all)
                yield
                for c in copies:
                    c.arrived()
                total = jnp.sum(r.g.all[...], axis=0)

                def own_part(start, size):
                    part = total[:, start : start + size]
                    for i in range(1, 4):
                        at = start + i * size
                        part = jnp.where(2 * x + core == i, total[:, at : at + size], part)
                    return part

                out.a_grad[...] = own_part(0, d // 4)
                out.m_grad[...] = own_part(d, d // 4)
                out.q_grad[...] = own_part(2 * d, HEAD_SIZE // 4)
                out.k_grad[...] = own_part(2 * d + HEAD_SIZE, HEAD_SIZE // 4)
                yield

            def gate_or_up(src, own, piece, gathered):
                over = [
                    net.put(src.at[2 * (1 - x) + c], piece.got.at[c], net.at(dx=1))
                    for c in range(2)
                ]
                yield
                for c in own + over:
                    c.arrived()
                line = piece.line

                def ready(t):
                    k = far_first(z)[t]
                    at = pl.ds(pl.multiple_of(k * z_gu, z_gu), z_gu)
                    for c in range(2):
                        line[0][k, pl.ds(c * z_gu, z_gu)] = piece.own[c, at].astype(
                            f32
                        ) + piece.got[c, at].astype(f32)

                yield from sum_line(net, *line, ready)
                for c in range(2):
                    piece.low[c] = low(line[0][z, pl.ds(c * z_gu, z_gu)])
                swap = net.put(piece.low.at[1 - core], piece.pair.at[core], net.at(dc=1))
                piece.pair[core] = piece.low[core]
                yield
                swap.arrived()
                own = fetch(piece.pair, gathered.at[me])
                yield from gather_line_first(net, piece.pair, lambda slot: gathered.at[slot])
                own.wait()

            def down(i):
                piece, line = r.down[i], r.down[i].line
                if i:
                    over = net.put(given.down.at[1 - x, :, columns[i]], piece.got, net.at(dx=1))
                    yield
                    over.arrived()
                down_own[i].arrived()

                def ready(t):
                    k = far_first(z)[t]
                    at = pl.ds(pl.multiple_of(k * z_dn, z_dn), z_dn)
                    block = piece.own[at].astype(f32)
                    line[0][k] = block + piece.got[at].astype(f32) if i else block

                yield from sum_line(net, *line, ready)
                piece.low[...] = low(line[0][z])
                own = fetch(piece.low, out.down.at[me, :, columns[i]])
                yield from gather_line_first(
                    net, piece.low, lambda slot: out.down.at[slot, :, columns[i]]
                )
                own.wait()

            def out_proj():
                need("heads_in", "middle_low")
                for i in range(slots):
                    r.o.own[i // 2, pl.ds(i % 2 * width, width)] = low(
                        outer_rows(h.heads_in[i], h.middle_low[...])
                    )
                o_core = [
                    net.put(r.o.own.at[2 * s + 1 - core], r.o.core.at[s], net.at(dc=1))
                    for s in range(2)
                ]
                yield
                for c in o_core:
                    c.arrived()
                for s in range(2):
                    f = 2 * s + core
                    r.o.own[f] = low(r.o.own[f].astype(f32) + r.o.core[s].astype(f32))
                over = net.put(r.o.own.at[2 * (1 - x) + core], r.o.got, net.at(dx=1))
                yield
                over.arrived()
                for i in range(slots):
                    at = pl.ds(i * z_o, z_o)
                    r.o.sum[i] = low(r.o.own[2 * x + core, at].astype(f32) + r.o.got[at].astype(f32))
                yield from sum_sides(net, r.o.sum, r.o.side, r.o.line)
                r.o.low[...] = low(r.o.line[0][z])
                own = fetch(r.o.low, out.o.at[me])
                yield from gather_line_first(net, r.o.low, lambda slot: out.o.at[slot])
                own.wait()

            def heads():
                for f in range(4):
                    at = pl.ds(f * (d // 4), d // 4)
                    r.h.own[f] = low(outer_rows(h.normed[:, at], r.dqkv[...]))
                core_copies = [
                    net.put(r.h.own.at[2 * s + 1 - core], r.h.core.at[s], net.at(dc=1))
                    for s in range(2)
                ]
                yield
                for c in core_copies:
                    c.arrived()
                for s in range(2):
                    f = 2 * s + core
                    r.h.own[f] = low(r.h.own[f].astype(f32) + r.h.core[s].astype(f32))
                over = net.put(r.h.own.at[2 * (1 - x) + core], r.h.got, net.at(dx=1))
                yield
                over.arrived()
                r.h.low[...] = low(
                    r.h.own[2 * x + core].astype(f32) + r.h.got[...].astype(f32)
                )
                own = fetch(r.h.low, out.heads.at[me])
                yield from gather_line_first(net, r.h.low, lambda slot: out.heads.at[slot])
                own.wait()

            in_order(
                BACK_ORDER,
                [
                    gate_or_up(given.gate, gate_own, r.gate, out.gate),
                    gate_or_up(given.up, up_own, r.up, out.up),
                    out_proj(),
                    down(0),
                    down(1),
                    back_rows(),
                    heads(),
                    main(),
                    gains(),
                ],
            )
            net.close()

        order = jax.tree.unflatten(out_tree, range(len(f_out)))
        result = net_call(
            body,
            f_out,
            f_in,
            200,
            64,
            number,
            scratch=flat,
            vmem=[
                len(f_in) + order.get(n)
                for n in ("input_grad", "a_grad", "m_grad", "q_grad", "k_grad")
            ],
        )
        return Bag(**jax.tree.unflatten(out_tree, result))

    return run


def widen(gate_all, up_all, down_all, o_all, heads_all, *small):
    _, _, z_gu, gu_cols = gate_all.shape
    half = gu_cols // 2
    z_dn, z_o = down_all.shape[1], o_all.shape[1]
    h_rows = heads_all.shape[1] // LINE

    def kernel(gate, up, down, o, heads, *refs):
        passed, outs = refs[: len(small)], refs[len(small) :]
        gate_out, up_out, down_out, o_out, q_out, k_out, v_out = outs[:7]
        for src, out in zip(passed, outs[7:]):
            out[...] = src[...].reshape(out.shape)
        for src, out in ((gate, gate_out), (up, up_out)):
            for y in range(2):
                for c in range(2):
                    for xs in range(2):
                        to = (2 * xs + c) * 2 * half + y * half
                        out[:, pl.ds(to, half)] = src[y, c, :, pl.ds(xs * half, half)].astype(
                            jnp.float32
                        )
        for y in range(2):
            down_out[y] = down[y].astype(jnp.float32)
            o_out[pl.ds(y * z_o, z_o)] = o[y].astype(jnp.float32)
        for h in range(2 * LINE):
            q_out[:, pl.ds(h * 256, 256)] = heads[h, :, pl.ds(0, 256)].astype(jnp.float32)
            k_out[:, pl.ds(h * 128, 128)] = heads[h, :, pl.ds(256, 128)].astype(jnp.float32)
            v_out[:, pl.ds(h * 128, 128)] = heads[h, :, pl.ds(384, 128)].astype(jnp.float32)

    f32 = jnp.float32
    outs = pl.pallas_call(
        kernel,
        grid=(LINE,),
        in_specs=[
            pl.BlockSpec((2, 2, z_gu, gu_cols), lambda i: (i, 0, 0, 0)),
            pl.BlockSpec((2, 2, z_gu, gu_cols), lambda i: (i, 0, 0, 0)),
            pl.BlockSpec((2, z_dn, MODEL_WIDTH), lambda i: (i, 0, 0)),
            pl.BlockSpec((2, z_o, MODEL_WIDTH), lambda i: (i, 0, 0)),
            pl.BlockSpec((2 * LINE, h_rows, 512), lambda i: (0, i, 0)),
        ]
        + [pl.BlockSpec(v.shape, lambda i: (0, 0)) for v in small],
        out_specs=[
            pl.BlockSpec((z_gu, 8 * half), lambda i: (i, 0)),
            pl.BlockSpec((z_gu, 8 * half), lambda i: (i, 0)),
            pl.BlockSpec((2, z_dn, MODEL_WIDTH), lambda i: (0, i, 0)),
            pl.BlockSpec((2 * z_o, MODEL_WIDTH), lambda i: (i, 0)),
            pl.BlockSpec((h_rows, 2048), lambda i: (i, 0)),
            pl.BlockSpec((h_rows, 1024), lambda i: (i, 0)),
            pl.BlockSpec((h_rows, 1024), lambda i: (i, 0)),
        ]
        + [pl.BlockSpec((1, *v.shape), lambda i: (0, 0, 0)) for v in small],
        out_shape=[
            shape_of(LINE * z_gu, 8 * half, kind=f32),
            shape_of(LINE * z_gu, 8 * half, kind=f32),
            shape_of(2, LINE * z_dn, MODEL_WIDTH, kind=f32),
            shape_of(2 * LINE * z_o, MODEL_WIDTH, kind=f32),
            shape_of(LINE * h_rows, 2048, kind=f32),
            shape_of(LINE * h_rows, 1024, kind=f32),
            shape_of(LINE * h_rows, 1024, kind=f32),
        ]
        + [shape_of(1, *v.shape, kind=v.dtype) for v in small],
        compiler_params=pltpu.CompilerParams(vmem_limit_bytes=VMEM_BYTES),
    )(gate_all, up_all, down_all, o_all, heads_all, *small)
    outs = list(outs)
    outs[2] = outs[2].reshape(-1, MODEL_WIDTH)
    return outs


def fast_layer(
    tokens,
    lengths,
    deal,
    attn_gain,
    w_q,
    key_weight,
    value_weight,
    query_norm_gain,
    k_gain,
    w_o,
    mlp_gain,
    w_gate,
    w_up,
    w_down,
    out_cotangent,
):
    rows = tokens.shape[1]
    slots = lax.axis_size(CTX)
    count = rows * slots
    ff_half = w_down.shape[0] // 2
    width = HEAD_SIZE * 2

    frequency = theta_base ** (-(np.arange(HEAD_SIZE // 2) * 2.0) / HEAD_SIZE)
    sign = np.where(np.arange(HEAD_SIZE) < HEAD_SIZE // 2, -1.0, 1.0)
    tables = np.stack([np.tile(frequency, 2), sign]).astype(np.float32)

    front = front_kernel(
        dict(
            tok=tokens,
            lengths=lengths,
            deal=deal,
            attn_gain=attn_gain,
            mlp_gain=mlp_gain,
            q_gain=query_norm_gain[None],
            k_gain=k_gain[None],
            freq=tables,
            w_q=w_q,
            w_k=key_weight,
            w_v=value_weight,
            w_o=w_o,
            w_gate=w_gate,
            w_up=w_up,
            w_down=w_down,
            grad=out_cotangent,
        ),
        {},
        0,
    )
    moved = dict(
        dm=front.dm,
        back=front.back,
        gate=front.gate.reshape(4, -1, 2 * ff_half),
        up=front.up.reshape(4, -1, 2 * ff_half),
        down=front.down,
        down_sum=front.down_sum,
    )
    loaded = dict(
        tok=tokens,
        back_from=front.back_from,
        a_gain=front.a_gain,
        dg2=front.dg2,
        heads_in=front.mixed_in,
        middle_low=front.middle_low,
        q=front.q,
        k=front.k,
        kt=front.kt,
        v=front.v,
        mixed=front.mixed,
        lse=front.lse,
        first=front.first,
        dealt=front.dealt,
        qkv=front.qkv,
        q_gain=front.q_gain,
        k_gain=front.k_gain,
        cos=front.cos,
        sin=front.sin,
        normed=front.normed,
        w_qkv=front.w_qkv,
    )
    sums = back_kernel((rows, count), 2)(moved, loaded)

    gate_sum, up_sum, down_sum, o_sum, q_sum, k_sum, v_sum, *small = widen(
        sums.gate,
        sums.up,
        sums.down,
        sums.o,
        sums.heads,
        front.output,
        sums.input_grad,
        sums.a_grad,
        sums.q_grad,
        sums.k_grad,
        sums.m_grad,
    )
    output, input_grad, *gains = small
    return (
        output,
        input_grad,
        *(gain[0, 0] for gain in gains),
        q_sum,
        k_sum,
        v_sum,
        o_sum,
        gate_sum,
        up_sum,
        down_sum,
    )


def solution(mesh):
    devices = mesh.devices
    if devices.shape == (8, 4):
        mesh = Mesh(devices.reshape(4, 2, 2, 2), CTX + FSDP)
        layer, ctx, fsdp = fast_layer, CTX, FSDP
    else:
        layer, ctx, fsdp = general_layer, "ctx", "fsdp"
    wide_rows = P(fsdp, ctx, None)
    return jax.shard_map(
        layer,
        mesh=mesh,
        in_specs=(
            wide_rows,
            P(fsdp, None),
            P(fsdp, None, None),
            P(fsdp),
            P(fsdp, None),
            P(fsdp, None),
            P(fsdp, None),
            P(fsdp),
            P(fsdp),
            P(fsdp, None),
            P(fsdp),
            P(fsdp, None),
            P(fsdp, None),
            P(fsdp, None),
            wide_rows,
        ),
        out_specs=(wide_rows, wide_rows) + (P(fsdp),) * 4 + (P(fsdp, None),) * 7,
        check_vma=False,
    )
```

```python
import math

import jax
import jax.numpy as jnp
import numpy as np
from jax import lax
from jax.experimental import pallas as pl
from jax.experimental.pallas import tpu as pltpu
from jax.sharding import Mesh
from jax.sharding import PartitionSpec as P

MODEL_WIDTH = 1024
QUERY_HEADS = 16
KEY_VALUE_HEADS = 8
HEAD_SIZE = 128


eps = 1e-06
theta_base = 1000000.0
negative_filler = -1e30


def root_mean_norm(values, gain_vec):
    return values * lax.rsqrt(jnp.mean(values * values, axis=-1, keepdims=True) + eps) * gain_vec


def rotary_embedding(values, token_position):
    half_width = values.shape[-1] // 2
    frequency = theta_base ** (
        -(jnp.arange(half_width, dtype=jnp.float32) * 2.0) / values.shape[-1]
    )
    angles = token_position.astype(jnp.float32)[:, None] * frequency[None, :]
    cosine = jnp.concatenate([jnp.cos(angles), jnp.cos(angles)], axis=-1)[:, None, :]
    sine_part = jnp.concatenate([jnp.sin(angles), jnp.sin(angles)], axis=-1)[:, None, :]
    turned = jnp.concatenate([-values[..., half_width:], values[..., :half_width]], axis=-1)
    return values * cosine + turned * sine_part


def dot_trans(left_side, right_side):
    return lax.dot_general(
        left_side, right_side, (((1,), (1,)), ((), ())), preferred_element_type=jnp.float32
    )


def outer_rows(left_side, right_side):
    return lax.dot_general(
        left_side, right_side, (((0,), (0,)), ((), ())), preferred_element_type=jnp.float32
    )


def block_plan(piece_rows, local_rows):
    shards = piece_rows // local_rows
    per_block = math.gcd(shards, max(1, 1024 // local_rows))
    return (per_block * local_rows, shards // per_block)


def over_blocks(carried, arrays, local_rows, block_work):
    rows_per_block, count_of_blocks = block_plan(arrays[0].shape[0], local_rows)

    def one_block(turn_index, state_now):
        offset = turn_index * rows_per_block
        parts = tuple(
            (lax.dynamic_slice_in_dim(member, offset, rows_per_block, 0) for member in arrays)
        )
        return block_work(state_now, parts, offset)

    return lax.fori_loop(0, count_of_blocks, one_block, carried)


def segment_begin(tok_ids, starts):
    return jnp.max(jnp.where(tok_ids[:, None] >= starts[None, :], starts[None, :], 0), axis=1)


def general_layer(
    tokens,
    lengths,
    deal,
    attn_gain,
    w_q,
    key_weight,
    value_weight,
    query_norm_gain,
    k_gain,
    w_o,
    mlp_gain,
    w_gate,
    w_up,
    w_down,
    out_cotangent,
):
    local_rows = tokens.shape[1]
    piece_count = lax.axis_size("ctx")
    piece_rows = local_rows // piece_count
    here = lax.axis_index("ctx")
    group_width = QUERY_HEADS // KEY_VALUE_HEADS
    score_scale = HEAD_SIZE ** (-0.5)
    seq_lengths = lengths[0]
    starts = jnp.cumsum(seq_lengths) - seq_lengths
    plan = deal[0]
    devices = jnp.arange(piece_count, dtype=jnp.int32)
    hits = plan[:, :, None] == devices[None, None, :]
    slot_of = jnp.sum(jnp.where(hits, devices[None, :, None], 0), axis=1)
    inner = jnp.arange(piece_rows, dtype=jnp.int32)
    dealt_index = (
        devices[None, :, None] * local_rows
        + jnp.transpose(slot_of)[:, :, None] * piece_rows
        + inner[None, None, :]
    ).reshape(piece_count * local_rows)
    dealt_first = segment_begin(dealt_index, starts)
    tok_index = lax.dynamic_slice_in_dim(dealt_index, here * local_rows, local_rows)
    segment_initial = lax.dynamic_slice_in_dim(dealt_first, here * local_rows, local_rows)
    token_position = tok_index - segment_initial
    own_slots = lax.dynamic_index_in_dim(slot_of, here, 0, keepdims=False)
    own_plan = lax.dynamic_index_in_dim(plan, here, 0, keepdims=False)
    token_pieces = jnp.take(
        tokens[0].reshape(piece_count, piece_rows, MODEL_WIDTH), own_slots, axis=0
    )
    dealt_tok = lax.all_to_all(
        token_pieces, "ctx", split_axis=0, concat_axis=0, tiled=True
    ).reshape(local_rows, MODEL_WIDTH)

    def key_mask(start_row, local_row_count):
        key_identifiers = lax.dynamic_slice_in_dim(dealt_index, start_row, local_row_count)
        return (key_identifiers[None, :] >= segment_initial[:, None]) & (
            key_identifiers[None, :] <= tok_index[:, None]
        )

    def query_mask(start_row, local_row_count):
        query_ids = lax.dynamic_slice_in_dim(dealt_index, start_row, local_row_count)
        first_key = lax.dynamic_slice_in_dim(dealt_first, start_row, local_row_count)
        return (tok_index[None, :] >= first_key[:, None]) & (
            tok_index[None, :] <= query_ids[:, None]
        )

    def fetch_weights():
        attn_set = (
            lax.all_gather(attn_gain, "fsdp", axis=0, tiled=True),
            lax.all_gather(query_norm_gain, "fsdp", axis=0, tiled=True),
            lax.all_gather(k_gain, "fsdp", axis=0, tiled=True),
            lax.all_gather(w_q, "fsdp", axis=0, tiled=True),
            lax.all_gather(key_weight, "fsdp", axis=0, tiled=True),
            lax.all_gather(value_weight, "fsdp", axis=0, tiled=True),
            lax.all_gather(w_o, "fsdp", axis=0, tiled=True),
        )
        mlp_set = (
            lax.all_gather(mlp_gain, "fsdp", axis=0, tiled=True),
            lax.all_gather(w_gate, "fsdp", axis=0, tiled=True),
            lax.all_gather(w_up, "fsdp", axis=0, tiled=True),
            lax.all_gather(w_down, "fsdp", axis=0, tiled=True),
        )
        return (attn_set, mlp_set)

    def forward(attn_set, mlp_set, token_rows):
        a_gain, qn_gain, kn_gain, proj_q, proj_k, proj_v, proj_o = attn_set
        m_gain, proj_gate, proj_up, proj_down = mlp_set
        residual = token_rows.astype(jnp.float32)
        normalized_input = root_mean_norm(residual, a_gain.astype(jnp.float32)).astype(jnp.bfloat16)
        query_prenorm = jnp.dot(
            normalized_input, proj_q, preferred_element_type=jnp.float32
        ).reshape(local_rows, QUERY_HEADS, HEAD_SIZE)
        key_prenorm = jnp.dot(normalized_input, proj_k, preferred_element_type=jnp.float32).reshape(
            local_rows, KEY_VALUE_HEADS, HEAD_SIZE
        )
        value_narrow = jnp.dot(normalized_input, proj_v, preferred_element_type=jnp.float32).astype(
            jnp.bfloat16
        )
        q_heads = (
            rotary_embedding(
                root_mean_norm(query_prenorm, qn_gain.astype(jnp.float32)), token_position
            )
            .astype(jnp.bfloat16)
            .reshape(local_rows, KEY_VALUE_HEADS, group_width, HEAD_SIZE)
        )
        key_narrow = (
            rotary_embedding(
                root_mean_norm(key_prenorm, kn_gain.astype(jnp.float32)), token_position
            )
            .astype(jnp.bfloat16)
            .reshape(local_rows, KEY_VALUE_HEADS * HEAD_SIZE)
        )

        def attend_over_block(state_now, shard_piece, start_row):
            key_segment, value_segment = shard_piece
            local_row_count = key_segment.shape[0]
            allowed = key_mask(start_row, local_row_count)
            row_top, row_total, weighted = state_now
            scores = (
                jnp.einsum(
                    "rkgh,ckh->kgrc",
                    q_heads,
                    key_segment.reshape(local_row_count, KEY_VALUE_HEADS, HEAD_SIZE),
                    preferred_element_type=jnp.float32,
                )
                * score_scale
            )
            scores = jnp.where(allowed, scores, negative_filler)
            new_top = jnp.maximum(row_top, jnp.max(scores, axis=-1))
            rescale = jnp.exp(row_top - new_top)
            weights = jnp.where(allowed, jnp.exp(scores - new_top[..., None]), 0.0)
            row_total = row_total * rescale + jnp.sum(weights, axis=-1)
            weighted = weighted * rescale[..., None] + jnp.einsum(
                "kgrc,ckh->kgrh",
                weights.astype(jnp.bfloat16),
                value_segment.reshape(local_row_count, KEY_VALUE_HEADS, HEAD_SIZE),
                preferred_element_type=jnp.float32,
            )
            return (new_top, row_total, weighted)

        initial = (
            jnp.full((KEY_VALUE_HEADS, group_width, local_rows), negative_filler, jnp.float32),
            jnp.zeros((KEY_VALUE_HEADS, group_width, local_rows), jnp.float32),
            jnp.zeros((KEY_VALUE_HEADS, group_width, local_rows, HEAD_SIZE), jnp.float32),
        )
        row_top, row_total, weighted = over_blocks(
            initial,
            (
                lax.all_gather(key_narrow, "ctx", axis=0, tiled=True),
                lax.all_gather(value_narrow, "ctx", axis=0, tiled=True),
            ),
            local_rows,
            attend_over_block,
        )
        attention_mixed = jnp.transpose(weighted / row_total[..., None], (2, 0, 1, 3)).reshape(
            local_rows, QUERY_HEADS * HEAD_SIZE
        )
        log_total = row_top + jnp.log(row_total)
        mixed_low = attention_mixed.astype(jnp.bfloat16)
        middle = residual + jnp.dot(mixed_low, proj_o, preferred_element_type=jnp.float32)
        normed2 = root_mean_norm(middle, m_gain.astype(jnp.float32)).astype(jnp.bfloat16)
        gate_pre = jnp.dot(normed2, proj_gate, preferred_element_type=jnp.float32)
        up_pre = jnp.dot(normed2, proj_up, preferred_element_type=jnp.float32)
        hidden = (jax.nn.silu(gate_pre) * up_pre).astype(jnp.bfloat16)
        result = middle + jnp.dot(hidden, proj_down, preferred_element_type=jnp.float32)
        return (
            result,
            residual,
            normalized_input,
            query_prenorm,
            key_prenorm,
            value_narrow,
            q_heads,
            key_narrow,
            attention_mixed,
            mixed_low,
            log_total,
            middle,
            normed2,
            gate_pre,
            up_pre,
            hidden,
            attn_set,
            mlp_set,
        )

    first_sets = fetch_weights()
    first_pass = forward(first_sets[0], first_sets[1], dealt_tok)
    again_tok = lax.all_to_all(
        token_pieces, "ctx", split_axis=0, concat_axis=0, tiled=True
    ).reshape(local_rows, MODEL_WIDTH)
    second_sets = fetch_weights()
    kept_pass = forward(second_sets[0], second_sets[1], again_tok)
    (
        unused,
        residual,
        normalized_input,
        query_prenorm,
        key_prenorm,
        value_narrow,
        q_heads,
        key_narrow,
        attention_mixed,
        mixed_low,
        log_total,
        middle,
        normed2,
        gate_pre,
        up_pre,
        hidden,
        attn_set,
        mlp_set,
    ) = kept_pass
    a_gain, qn_gain, kn_gain, proj_q, proj_k, proj_v, proj_o = attn_set
    m_gain, proj_gate, proj_up, proj_down = mlp_set
    grad_low = out_cotangent[0]
    grad_out = grad_low.astype(jnp.float32)
    d_hidden = dot_trans(grad_low, proj_down)
    down_grad = lax.psum_scatter(
        outer_rows(hidden, grad_low).astype(jnp.bfloat16), "fsdp", scatter_dimension=0, tiled=True
    )
    unused, swiglu_back = jax.vjp(
        lambda gate_in, up_in: jax.nn.silu(gate_in) * up_in, gate_pre, up_pre
    )
    d_gate, d_up = swiglu_back(d_hidden)
    d_gate_low = d_gate.astype(jnp.bfloat16)
    d_up_low = d_up.astype(jnp.bfloat16)
    d_normed2 = dot_trans(d_gate_low, proj_gate) + dot_trans(d_up_low, proj_up)
    both_low = jnp.concatenate([d_gate_low, d_up_low], axis=1)
    gate_up_grad = lax.psum_scatter(
        outer_rows(normed2, both_low).astype(jnp.bfloat16), "fsdp", scatter_dimension=0, tiled=True
    )
    unused, norm2_back = jax.vjp(root_mean_norm, middle, m_gain.astype(jnp.float32))
    d_middle_norm, d_m_gain = norm2_back(d_normed2)
    d_middle = grad_out + d_middle_norm
    middle_low = d_middle.astype(jnp.bfloat16)
    mixed_gradient = dot_trans(middle_low, proj_o).astype(jnp.bfloat16)
    out_proj_grad = lax.psum_scatter(
        outer_rows(mixed_low, middle_low).astype(jnp.bfloat16),
        "fsdp",
        scatter_dimension=0,
        tiled=True,
    )
    heads_gradient = mixed_gradient.reshape(local_rows, KEY_VALUE_HEADS, group_width, HEAD_SIZE)
    delta_rows = jnp.sum(
        heads_gradient.astype(jnp.float32)
        * attention_mixed.reshape(local_rows, KEY_VALUE_HEADS, group_width, HEAD_SIZE),
        axis=-1,
    )
    delta_t = jnp.transpose(delta_rows, (1, 2, 0))
    local_keys = key_narrow.reshape(local_rows, KEY_VALUE_HEADS, HEAD_SIZE)
    local_values = value_narrow.reshape(local_rows, KEY_VALUE_HEADS, HEAD_SIZE)

    def query_block(state_now, shard_piece, start_row):
        key_segment, value_segment = shard_piece
        local_row_count = key_segment.shape[0]
        allowed = key_mask(start_row, local_row_count)
        key_row_block = key_segment.reshape(local_row_count, KEY_VALUE_HEADS, HEAD_SIZE)
        scores = (
            jnp.einsum("rkgh,ckh->kgrc", q_heads, key_row_block, preferred_element_type=jnp.float32)
            * score_scale
        )
        probability = jnp.where(allowed, jnp.exp(scores - log_total[..., None]), 0.0)
        d_probs = jnp.einsum(
            "rkgh,ckh->kgrc",
            heads_gradient,
            value_segment.reshape(local_row_count, KEY_VALUE_HEADS, HEAD_SIZE),
            preferred_element_type=jnp.float32,
        )
        d_scores = (probability * (d_probs - delta_t[..., None])).astype(jnp.bfloat16)
        return (
            state_now
            + jnp.einsum(
                "kgrc,ckh->kgrh", d_scores, key_row_block, preferred_element_type=jnp.float32
            )
            * score_scale
        )

    query_grad = over_blocks(
        jnp.zeros((KEY_VALUE_HEADS, group_width, local_rows, HEAD_SIZE), jnp.float32),
        (
            lax.all_gather(key_narrow, "ctx", axis=0, tiled=True),
            lax.all_gather(value_narrow, "ctx", axis=0, tiled=True),
        ),
        local_rows,
        query_block,
    )
    lse_rows = jnp.transpose(log_total, (2, 0, 1)).reshape(local_rows, QUERY_HEADS)
    delta_send = delta_rows.reshape(local_rows, QUERY_HEADS)

    def key_block(state_now, shard_piece, start_row):
        query_segment, output_gradient_segment, logsumexp_segment, delta_segment = shard_piece
        local_row_count = query_segment.shape[0]
        allowed = query_mask(start_row, local_row_count)
        key_grad, value_gradient = state_now
        query_matrix = query_segment.reshape(
            local_row_count, KEY_VALUE_HEADS, group_width, HEAD_SIZE
        )
        gradient_rows = output_gradient_segment.reshape(
            local_row_count, KEY_VALUE_HEADS, group_width, HEAD_SIZE
        )
        scores = (
            jnp.einsum(
                "ckgh,rkh->kgcr", query_matrix, local_keys, preferred_element_type=jnp.float32
            )
            * score_scale
        )
        logsumexp_portion = jnp.transpose(
            logsumexp_segment.reshape(local_row_count, KEY_VALUE_HEADS, group_width), (1, 2, 0)
        )
        delta_portion = jnp.transpose(
            delta_segment.reshape(local_row_count, KEY_VALUE_HEADS, group_width), (1, 2, 0)
        )
        probability = jnp.where(allowed, jnp.exp(scores - logsumexp_portion[..., None]), 0.0)
        value_gradient = value_gradient + jnp.einsum(
            "kgcr,ckgh->rkh",
            probability.astype(jnp.bfloat16),
            gradient_rows,
            preferred_element_type=jnp.float32,
        )
        d_probs = jnp.einsum(
            "ckgh,rkh->kgcr", gradient_rows, local_values, preferred_element_type=jnp.float32
        )
        d_scores = (probability * (d_probs - delta_portion[..., None])).astype(jnp.bfloat16)
        key_grad = (
            key_grad
            + jnp.einsum(
                "kgcr,ckgh->rkh", d_scores, query_matrix, preferred_element_type=jnp.float32
            )
            * score_scale
        )
        return (key_grad, value_gradient)

    key_grad, value_gradient = over_blocks(
        (
            jnp.zeros((local_rows, KEY_VALUE_HEADS, HEAD_SIZE), jnp.float32),
            jnp.zeros((local_rows, KEY_VALUE_HEADS, HEAD_SIZE), jnp.float32),
        ),
        (
            lax.all_gather(
                q_heads.reshape(local_rows, QUERY_HEADS * HEAD_SIZE), "ctx", axis=0, tiled=True
            ),
            lax.all_gather(mixed_gradient, "ctx", axis=0, tiled=True),
            lax.all_gather(lse_rows.astype(jnp.bfloat16), "ctx", axis=0, tiled=True).astype(
                jnp.float32
            ),
            lax.all_gather(delta_send.astype(jnp.bfloat16), "ctx", axis=0, tiled=True).astype(
                jnp.float32
            ),
        ),
        local_rows,
        key_block,
    )
    query_rows = jnp.transpose(query_grad, (2, 0, 1, 3)).reshape(local_rows, QUERY_HEADS, HEAD_SIZE)
    unused, q_back = jax.vjp(
        lambda head_in, gain_in: rotary_embedding(root_mean_norm(head_in, gain_in), token_position),
        query_prenorm,
        qn_gain.astype(jnp.float32),
    )
    d_q_pre, d_qn_gain = q_back(query_rows)
    unused, k_back = jax.vjp(
        lambda head_in, gain_in: rotary_embedding(root_mean_norm(head_in, gain_in), token_position),
        key_prenorm,
        kn_gain.astype(jnp.float32),
    )
    key_prenorm_gradient, d_kn_gain = k_back(key_grad)
    dq_low = d_q_pre.reshape(local_rows, QUERY_HEADS * HEAD_SIZE).astype(jnp.bfloat16)
    key_gradient_narrow = key_prenorm_gradient.reshape(
        local_rows, KEY_VALUE_HEADS * HEAD_SIZE
    ).astype(jnp.bfloat16)
    value_gradient_narrow = value_gradient.reshape(local_rows, KEY_VALUE_HEADS * HEAD_SIZE).astype(
        jnp.bfloat16
    )
    d_normed = (
        dot_trans(dq_low, proj_q)
        + dot_trans(key_gradient_narrow, proj_k)
        + dot_trans(value_gradient_narrow, proj_v)
    )
    qkv_low = jnp.concatenate([dq_low, key_gradient_narrow, value_gradient_narrow], axis=1)
    qkv_grad = lax.psum_scatter(
        outer_rows(normalized_input, qkv_low).astype(jnp.bfloat16),
        "fsdp",
        scatter_dimension=0,
        tiled=True,
    )
    unused, norm1_back = jax.vjp(root_mean_norm, residual, a_gain.astype(jnp.float32))
    d_resid_norm, d_a_gain = norm1_back(d_normed)
    input_dealt = d_middle + d_resid_norm
    back_pieces = lax.all_to_all(
        input_dealt.reshape(piece_count, piece_rows, MODEL_WIDTH).astype(jnp.bfloat16),
        "ctx",
        split_axis=0,
        concat_axis=0,
        tiled=True,
    ).astype(jnp.float32)
    input_grad = jnp.take(back_pieces, own_plan, axis=0).reshape(local_rows, MODEL_WIDTH)
    gain_parts = (
        lax.psum_scatter(d_a_gain, "fsdp", scatter_dimension=0, tiled=True),
        lax.psum_scatter(d_qn_gain, "fsdp", scatter_dimension=0, tiled=True),
        lax.psum_scatter(d_kn_gain, "fsdp", scatter_dimension=0, tiled=True),
        lax.psum_scatter(d_m_gain, "fsdp", scatter_dimension=0, tiled=True),
    )
    totals = (
        lax.psum(gain_parts[0].astype(jnp.bfloat16), "ctx").astype(jnp.float32),
        lax.psum(gain_parts[1].astype(jnp.bfloat16), "ctx").astype(jnp.float32),
        lax.psum(gain_parts[2].astype(jnp.bfloat16), "ctx").astype(jnp.float32),
        lax.psum(gain_parts[3].astype(jnp.bfloat16), "ctx").astype(jnp.float32),
        lax.psum(qkv_grad, "ctx").astype(jnp.float32),
        lax.psum(out_proj_grad, "ctx").astype(jnp.float32),
        lax.psum(gate_up_grad, "ctx").astype(jnp.float32),
        lax.psum(down_grad, "ctx").astype(jnp.float32),
    )
    q_width = QUERY_HEADS * HEAD_SIZE
    key_value_width = KEY_VALUE_HEADS * HEAD_SIZE
    qkv_total = totals[4]
    gate_up_total = totals[6]
    ff_width = w_gate.shape[1]
    return (
        first_pass[0].astype(jnp.bfloat16)[None],
        input_grad[None],
        totals[0],
        totals[1],
        totals[2],
        totals[3],
        qkv_total[:, :q_width],
        qkv_total[:, q_width : q_width + key_value_width],
        qkv_total[:, q_width + key_value_width :],
        totals[5],
        gate_up_total[:, :ff_width],
        gate_up_total[:, ff_width:],
        totals[7],
    )


CTX = ("z", "y")
FSDP = ("x", "core")
VMEM_BYTES = 62 << 20


def norm_back(values, gain_vec, grad):
    scale = lax.rsqrt(jnp.mean(values * values, axis=-1, keepdims=True) + eps)
    inner = gain_vec * grad
    d_values = scale * inner - values * (scale * scale * scale) * jnp.mean(
        values * inner, axis=-1, keepdims=True
    )
    return d_values, grad * values * scale


def half_turn(values):
    half = values.shape[-1] // 2
    return jnp.concatenate([-values[..., half:], values[..., :half]], axis=-1)


def rope_tables(token_position):
    half = HEAD_SIZE // 2
    frequency = theta_base ** (-(jnp.arange(half, dtype=jnp.float32) * 2.0) / HEAD_SIZE)
    angles = token_position.astype(jnp.float32)[:, None] * frequency[None, :]
    cosine, sine = jnp.cos(angles), jnp.sin(angles)
    return jnp.concatenate([cosine, cosine], axis=1), jnp.concatenate([sine, sine], axis=1)


def dot(a, b):
    return jnp.dot(a, b, preferred_element_type=jnp.float32)


def low(a):
    return a.astype(jnp.bfloat16)


def gather_fsdp_plain(block):
    return lax.all_gather(block, FSDP, axis=0, tiled=True)


def over(block, axis):
    return lax.ppermute(block, axis, [(0, 1), (1, 0)])


def half_sum(block, axis):
    place = lax.axis_index(axis)
    got = over(lax.dynamic_index_in_dim(block, 1 - place, 0, keepdims=False), axis)
    own = lax.dynamic_index_in_dim(block, place, 0, keepdims=False)
    return low(own.astype(jnp.float32) + got.astype(jnp.float32))


MESH_ID = pl.DeviceIdType.MESH
LINE = 4


class Net:
    def __init__(self, send, recv):
        self.send, self.recv, self.used = send, recv, 0
        self.z, self.y, self.x, self.core = (lax.axis_index(a) for a in CTX + FSDP)
        self.me = 2 * self.z + self.y
        self.open = []

    def at(self, dz=0, dy=0, dx=0, dc=0):
        return (
            self.z + dz,
            1 - self.y if dy else self.y,
            1 - self.x if dx else self.x,
            1 - self.core if dc else self.core,
        )

    def put(self, src, dst, target, sends=None, recvs=None):
        copy = Copy(self, src, dst, target, sends, recvs)
        self.open.append(copy)
        return copy

    def close(self):
        for copy in self.open:
            copy.arrived()
        for copy in self.open:
            copy.left()


def guarded(condition, action):
    if condition is None:
        action()
    else:
        pl.when(condition)(action)


class Copy:
    def __init__(self, net, src, dst, target, sends, recvs):
        i = net.used
        net.used += 1
        self.sends, self.recvs, self.waited = sends, recvs, False
        self.copy = pltpu.make_async_remote_copy(
            src, dst, net.send.at[i], net.recv.at[i], device_id=target, device_id_type=MESH_ID
        )
        guarded(sends, self.copy.start)

    def arrived(self):
        if not self.waited:
            self.waited = True
            guarded(self.recvs, self.copy.wait_recv)

    def left(self):
        guarded(self.sends, self.copy.wait_send)


class Local:
    def __init__(self, copy):
        self.copy, self.waited = copy, False
        copy.start()

    def arrived(self):
        if not self.waited:
            self.waited = True
            self.copy.wait()

    wait = arrived


def greet(net, kinds):
    barrier = pltpu.get_barrier_semaphore()
    partners = []
    if "z" in kinds:
        partners += [(net.at(dz=1), net.z < LINE - 1), (net.at(dz=-1), net.z > 0)]
    if "y" in kinds:
        partners.append((net.at(dy=1), None))
    if "x" in kinds:
        partners.append((net.at(dx=1), None))
    if "core" in kinds:
        partners.append((net.at(dc=1), None))
    if "far" in kinds:
        partners.append((net.at(dx=1, dc=1), None))
    if "ctx" in kinds:
        for k in range(1, 2 * LINE):
            other = lax.rem(net.me + k, 2 * LINE)
            partners.append(((other // 2, lax.rem(other, 2), net.x, net.core), None))
    for target, there in partners:
        guarded(
            there,
            lambda target=target: pl.semaphore_signal(
                barrier, inc=1, device_id=target, device_id_type=MESH_ID
            ),
        )
    ends = 0
    if "z" in kinds:
        ends = (net.z == 0).astype(jnp.int32) + (net.z == LINE - 1).astype(jnp.int32)
    pl.semaphore_wait(barrier, len(partners) - ends)


def drive(*programs):
    live = list(programs)
    while live:
        for program in list(live):
            if next(program, "end") == "end":
                live.remove(program)


def in_order(order, programs):
    for i in order:
        next(programs[i], None)
    for program in programs:
        for _ in program:
            pass


def by_steps(program):
    yield next(program)
    while next(program, "end") != "end":
        if next(program, "end") == "end":
            return
        yield


def along_line(net, own, view, slot, log=None):
    z = net.z
    up = net.put(own, view(slot(z)), net.at(dz=1), z < LINE - 1, z > 0)
    down = net.put(own, view(slot(z)), net.at(dz=-1), z > 0, z < LINE - 1)
    yield
    for s in range(1, LINE):
        from_low, from_high = z >= s, z + s <= LINE - 1
        up.arrived()
        low_block, high_block = view(slot(z - s)), view(slot(z + s))
        if s < LINE - 1:
            up = net.put(low_block, low_block, net.at(dz=1), from_low & (z < LINE - 1), z >= s + 1)
        if log is not None:
            log[s].append(net.put(low_block, low_block, net.at(dy=1), from_low, from_low))
        yield
        down.arrived()
        if s < LINE - 1:
            down = net.put(
                high_block, high_block, net.at(dz=-1), from_high & (z > 0), z + s + 1 <= LINE - 1
            )
        if log is not None:
            log[s].append(net.put(high_block, high_block, net.at(dy=1), from_high, from_high))
        yield


def gather_line_first(net, own, view, log=None):
    log = {s: [] for s in range(LINE)} if log is None else log
    log[0].append(net.put(own, view(net.me), net.at(dy=1)))
    yield from along_line(net, own, view, lambda z: 2 * z + net.y, log)


def gather_side_first(net, own, view):
    side = net.put(own, view(net.me), net.at(dy=1))
    first = along_line(net, own, view, lambda z: 2 * z + net.y)
    yield next(first)
    side.arrived()
    other = view(net.me + 1 - 2 * net.y)
    second = along_line(net, other, view, lambda z: 2 * z + 1 - net.y)
    for _ in second:
        next(first, None)
        yield


def gather_ctx_programs(net, own, out, cut):
    rows = own.shape[0]
    programs = [
        gather_line_first(
            net, own.at[pl.ds(0, cut)], lambda slot: out.at[slot, pl.ds(0, cut)]
        )
    ]
    if cut < rows:
        rest = pl.ds(cut, rows - cut)
        programs.append(gather_side_first(net, own.at[rest], lambda slot: out.at[slot, rest]))
    return programs


def gather_fsdp(net, own, out):
    f = 2 * net.x + net.core
    net.put(own, out.at[f], net.at(dc=1))
    over = net.put(own, out.at[f], net.at(dx=1))
    yield
    yield
    yield
    over.arrived()
    far = out.at[2 * (1 - net.x) + net.core]
    net.put(far, far, net.at(dc=1))
    yield


def gather_quad(net, own, out):
    q = 2 * net.y + net.core
    net.put(own, out.at[q], net.at(dc=1))
    over = net.put(own, out.at[q], net.at(dy=1))
    yield
    over.arrived()
    far = out.at[2 * (1 - net.y) + net.core]
    net.put(far, far, net.at(dc=1))
    yield


def swap_ctx(net, blocks, out):
    for k in range(1, 2 * LINE):
        other = lax.rem(net.me + k, 2 * LINE)
        net.put(
            blocks.at[other], out.at[net.me], (other // 2, lax.rem(other, 2), net.x, net.core)
        )
    yield


def own_copies(pairs, sem):
    copies = [pltpu.make_async_copy(src, dst, sem.at[i]) for i, (src, dst) in enumerate(pairs)]
    for copy in copies:
        copy.start()
    return copies


def net_call(body, outs, args, copies, locals_, number, scratch=(), vmem=(), smem=()):
    def kernel(*refs):
        *rest, send, recv, local = refs
        net = Net(send, recv)
        body(net, local, *rest)
        assert net.used <= copies, net.used

    any_space = pl.BlockSpec(memory_space=pl.ANY)
    in_vmem = pl.BlockSpec(memory_space=pltpu.VMEM)
    in_smem = pl.BlockSpec(memory_space=pltpu.SMEM)
    count = len(args)

    def place(i):
        return in_vmem if i in vmem else in_smem if i in smem else any_space

    return pl.pallas_call(
        kernel,
        out_shape=outs,
        in_specs=[place(i) for i in range(count)],
        out_specs=[place(count + i) for i in range(len(outs))],
        scratch_shapes=list(scratch)
        + [
            pltpu.SemaphoreType.DMA((copies,)),
            pltpu.SemaphoreType.DMA((copies,)),
            pltpu.SemaphoreType.DMA((max(1, locals_),)),
        ],
        compiler_params=pltpu.CompilerParams(
            collective_id=number, has_side_effects=True, vmem_limit_bytes=VMEM_BYTES
        ),
    )(*args)


def shape_of(*dims, kind=jnp.bfloat16):
    return jax.ShapeDtypeStruct(dims, kind)


def sum_line(net, held, send_up, send_down, got_up, got_down, ready):
    z = net.z
    ups, downs = [], []

    def fill(send, got, block, t, first):
        def alone():
            send[t] = low(held[block])

        def added():
            send[t] = low(held[block] + got[t - 1].astype(jnp.float32))

        return alone if first else added

    for t in range(LINE - 1):
        if t:
            ups[t - 1].arrived()
        ready(t)
        to_up, to_down = LINE - 1 - t + z, z - LINE + 1 + t
        up_on, down_on = (z <= t) & (z < LINE - 1), (z >= LINE - 1 - t) & (z > 0)
        pl.when(z == 0)(fill(send_up, got_up, to_up, t, True))
        if t:
            pl.when(up_on & (z >= 1))(fill(send_up, got_up, to_up, t, False))
        ups.append(
            net.put(
                send_up.at[t], got_up.at[t], net.at(dz=1), up_on, (z >= 1) & (z - 1 <= t)
            )
        )
        yield
        if t:
            downs[t - 1].arrived()
        pl.when(z == LINE - 1)(fill(send_down, got_down, to_down, t, True))
        if t:
            pl.when(down_on & (z <= LINE - 2))(fill(send_down, got_down, to_down, t, False))
        downs.append(
            net.put(
                send_down.at[t],
                got_down.at[t],
                net.at(dz=-1),
                down_on,
                (z <= LINE - 2) & (z + 1 >= LINE - 1 - t),
            )
        )
        yield
    last = LINE - 2

    def add_up():
        held[z] += got_up[last].astype(jnp.float32)

    def add_down():
        held[z] += got_down[last].astype(jnp.float32)

    ups[last].arrived()
    ready(LINE - 1)
    pl.when(z >= 1)(add_up)
    yield
    downs[last].arrived()
    pl.when(z <= LINE - 2)(add_down)


def far_first(z):
    return [
        jnp.where(z < 2, 3, 0),
        jnp.where(z < 2, 2, 1),
        z + 1 - 2 * lax.rem(z, 2),
        z,
    ]


def line_scratch(rows, cols):
    line = pltpu.VMEM((LINE - 1, rows, cols), jnp.bfloat16)
    return [pltpu.VMEM((LINE, rows, cols), jnp.float32), line, line, line, line]


def sum_sides(net, src, from_side, line, make=None):
    z, y = net.z, net.y
    held = line[0]
    order = far_first(z)
    sides = []
    for k in order:
        if make is not None:
            make(2 * k + 1 - y)
        sides.append(net.put(src.at[2 * k + 1 - y], from_side.at[k], net.at(dy=1)))
        if make is not None and len(sides) == 2:
            yield
    yield

    def ready(t):
        k = order[t]
        if make is not None:
            make(2 * k + y)
        sides[t].arrived()
        held[k] = src[2 * k + y].astype(jnp.float32) + from_side[k].astype(jnp.float32)

    yield from sum_line(net, *line, ready)


BLOCK = 256
REST = (4, 3)
BACK_ORDER = (
    7, 4, 0, 1, 4, 4, 5, 4, 7, 7, 7, 4, 7, 7, 7, 0, 7, 0, 4, 4, 7, 7, 0, 0, 4, 4, 0, 7, 0, 2,
    1, 1, 6, 4, 0, 4, 6, 0, 3, 3, 1, 0, 7, 1, 7, 3, 2, 0, 5, 3, 0, 4, 6, 7, 3, 0, 1, 7, 3, 0,
    1, 2, 6, 4, 6, 4, 7, 7, 2, 2, 6, 1, 6, 2, 2, 7, 0, 3, 3, 7, 2, 2, 1, 6, 1, 7, 0, 6, 8, 2,
    7, 2, 8, 2, 4, 2, 1, 2, 7, 0, 1, 2, 3, 1, 6, 3, 3, 1, 8, 2, 1, 3, 3, 6, 4, 3, 2, 3, 1, 1,
    2, 8,
)


def turn_lanes(v):
    return pltpu.roll(v, HEAD_SIZE // 2, 1)


def dot_last(a, b):
    return lax.dot_general(a, b, (((1,), (1,)), ((), ())), preferred_element_type=jnp.float32)


def resting(rounds):
    for _ in range(rounds):
        yield


class Bag:
    def __init__(self, **members):
        self.__dict__.update(members)


def bags(tree):
    if isinstance(tree, list):
        return [bags(v) for v in tree]
    return Bag(**{n: bags(v) for n, v in tree.items()}) if isinstance(tree, dict) else tree


def near_first(z):
    return far_first(z)[::-1]


def kernel_with(
    body, moved, loaded, outs, scratch, copies, number, in_vmem=(), near=(), scalar=()
):
    scratch = dict(
        scratch, held={n: pltpu.VMEM(v.shape, v.dtype) for n, v in loaded.items()}
    )
    flat, tree = jax.tree.flatten(scratch)
    f_in, in_tree = jax.tree.flatten((moved, loaded))
    f_out, out_tree = jax.tree.flatten(outs)

    def whole(net, local, *refs):
        given, to_load = jax.tree.unflatten(in_tree, refs[: len(f_in)])
        out = Bag(**jax.tree.unflatten(out_tree, refs[len(f_in) : len(f_in) + len(f_out)]))
        r = bags(jax.tree.unflatten(tree, refs[len(f_in) + len(f_out) :]))
        used = iter(range(96))

        def fetch(src, dst):
            return Local(pltpu.make_async_copy(src, dst, local.at[next(used)]))

        def load():
            return {n: fetch(to_load[n], getattr(r.held, n)) for n in to_load}

        body(net, fetch, load, Bag(**given), out, r)
        net.close()

    order = jax.tree.unflatten(out_tree, range(len(f_out)))
    in_order, _ = jax.tree.unflatten(in_tree, range(len(f_in)))
    result = net_call(
        whole,
        f_out,
        f_in,
        copies,
        96,
        number,
        scratch=flat,
        vmem=[len(f_in) + order.get(n) for n in in_vmem] + [in_order.get(n) for n in near],
        smem=[in_order.get(n) for n in scalar],
    )
    return Bag(**jax.tree.unflatten(out_tree, result))


def middle(net, fetch, arriving, out, r):
    y, core, me = net.y, net.core, net.me
    slots, rows, width = r.mixed_in.shape
    _, shard, wide = r.w_gu.shape
    ff, d = wide // 2, r.residual.shape[1]
    piece, pad = rows // slots, 32
    f32, bf = jnp.float32, jnp.bfloat16
    every = pl.ds(0, rows)
    parts = [pl.ds(0, rows // 2), pl.ds(rows // 2, rows // 2)]

    def land(copies):
        for c in copies:
            c.arrived()

    def from_head(head):
        at = pl.ds(pl.multiple_of(lax.rem(head, 2) * width, width), width)
        return dot(r.mixed_in[head], r.w_o[head // 2, at])

    land(arriving.o)
    arriving.heads[-1].arrived()
    total = r.residual[...].astype(f32) + from_head(me)
    for k in range(1, slots):
        arriving.heads[k - 1].arrived()
        total = total + from_head(lax.rem(me + slots - k, slots))
    r.middle[...] = total
    own, far = 2 * y + core, 2 * (1 - y) + core
    r.quad[own] = low(root_mean_norm(total, r.m_gain[...]))
    near = net.put(r.quad.at[own], r.quad.at[own], net.at(dc=1))
    over = [net.put(r.quad.at[own, at], r.quad.at[own, at], net.at(dy=1)) for at in parts]
    arriving.results.append(fetch(r.mixed_in, out.mixed_in))
    near.arrived()
    land(arriving.gu)
    land(arriving.grad)

    def pair(ref, side, at):
        return ref[pl.ds(2 * side, 2), at].reshape(2 * at.size, ref.shape[-1])

    def forward(side, at):
        gate_up = dot(pair(r.quad, side, at), r.w_gu[...].reshape(4 * shard, 2 * ff))
        return gate_up[:, :ff], gate_up[:, ff:]

    def backward(side, at, gate, up):
        d_hidden = dot_last(pair(r.grad, side, at), r.w_dn[...].reshape(ff, d))
        sig = 1.0 / (1.0 + jnp.exp(-gate))
        silu = gate * sig
        d_gate = low(d_hidden * up * (sig * (1.0 + gate * (1.0 - sig))))
        both, split = pl.ds(2 * side, 2), (2, at.size, ff)
        r.hidden[both, at] = low(silu * up).reshape(split)
        r.d_gu[both, at, pl.ds(0, ff)] = d_gate.reshape(split)
        r.d_gu[both, at, pl.ds(ff, ff)] = low(d_hidden * silu).reshape(split)

    def part(side, at):
        w_gu = r.w_gu[...].reshape(4 * shard, 2 * ff)
        return dot_last(pair(r.d_gu, side, at), w_gu).reshape(2, at.size, d)

    def out_part(side):
        return dot(pair(r.hidden, side, every), r.w_dn[...].reshape(ff, d)).reshape(2, rows, d)

    near_values = forward(y, every)
    over[0].arrived()
    last = [net.put(r.quad.at[far, parts[0]], r.quad.at[far, parts[0]], net.at(dc=1))]
    land(arriving.dn)
    backward(y, every, *near_values)
    over[1].arrived()
    last.append(net.put(r.quad.at[far, parts[1]], r.quad.at[far, parts[1]], net.at(dc=1)))
    one, side = [], []

    def far_part(i):
        at = parts[i]
        last[i].arrived()
        backward(1 - y, at, *forward(1 - y, at))
        r.far_part[:, at] = low(part(1 - y, at))
        one.append(net.put(r.far_part.at[1 - core, at], r.got.at[0, at], net.at(dc=1)))

    def far_sum(i):
        at = parts[i]
        one[i].arrived()
        r.to_side[0, at] = low(r.far_part[core, at].astype(f32) + r.got[0, at].astype(f32))
        side.append(net.put(r.to_side.at[0, at], r.got.at[2, at], net.at(dy=1)))

    far_part(0)
    r.near_part[...] = part(y, every)
    r.beside[...] = low(r.near_part[1 - core])
    two = net.put(r.beside, r.got.at[1], net.at(dc=1))
    far_sum(0)
    far_part(1)
    r.far_out[...] = low(out_part(1 - y))
    far_sum(1)
    g = r.grad[...].reshape(4 * rows, d)
    r.g_dn[...] = low(outer_rows(r.hidden[...].reshape(4 * rows, ff), g)).reshape(2, ff // 2, d)
    sent = [fetch(r.g_dn, out.down)]
    some = pl.ds(0, d // 2)
    dn_over = net.put(r.g_dn.at[1 - net.x, :, some], r.dn_got, net.at(dx=1))
    one_out = net.put(r.far_out.at[1 - core], r.got.at[3], net.at(dc=1))
    r.near_out[...] = out_part(y)
    r.beside_out[...] = low(r.near_out[1 - core])
    two_out = net.put(r.beside_out, r.got.at[4], net.at(dc=1))
    n2 = r.quad[...].reshape(4 * rows, d)
    d_gu = r.d_gu[...].reshape(4 * rows, 2 * ff)
    r.g_gate[...] = low(outer_rows(n2, d_gu[:, :ff]))
    sent.append(fetch(r.g_gate, out.gate))
    one_out.arrived()
    r.to_side[1] = low(r.far_out[core].astype(f32) + r.got[3].astype(f32))
    side_out = net.put(r.to_side.at[1], r.got.at[5], net.at(dy=1))
    r.g_up[...] = low(outer_rows(n2, d_gu[:, ff:]))
    sent.append(fetch(r.g_up, out.up))
    two.arrived()
    land(side)
    d_normed = r.near_part[core] + r.got[1].astype(f32) + r.got[2].astype(f32)
    dx2, dg2 = norm_back(r.middle[...], r.m_gain[...], d_normed)
    out.dg2[...] = jnp.sum(dg2, axis=0, keepdims=True)
    middle_low = low(r.grad[own].astype(f32) + dx2)
    for i in range(slots):
        r.dm[i] = low(dot_last(middle_low, r.w_o[i // 2, pl.ds(i % 2 * width, width)]))
    sent.append(fetch(r.dm, out.dm))
    for i in range(slots):
        out.back[i, pl.ds(0, piece)] = middle_low[i * piece : (i + 1) * piece]
        out.back[i, pl.ds(piece, pad - piece)] = jnp.zeros((pad - piece, d), bf)
    out.middle_low[...] = middle_low
    two_out.arrived()
    side_out.arrived()
    out.output[...] = low(
        r.middle[...] + r.near_out[core] + r.got[4].astype(f32) + r.got[5].astype(f32)
    )
    dn_over.arrived()
    out.down_sum[...] = low(
        r.g_dn[net.x, :, some].astype(f32) + r.dn_got[...].astype(f32)
    )
    land(sent)
    land(arriving.results)


def front_kernel(moved, loaded, number):
    a = Bag(**moved)
    _, rows, d = a.tok.shape
    slots = 2 * LINE
    count = rows * slots
    blocks = count // BLOCK
    width = 2 * HEAD_SIZE
    shard = a.w_q.shape[0]
    half = a.w_gate.shape[1] // 8
    o_rows = a.w_o.shape[0]
    scale = HEAD_SIZE**-0.5
    bf, f32 = jnp.bfloat16, jnp.float32
    piece = rows // slots
    ff = 2 * half
    gain_cols = 2 * a.attn_gain.shape[0] + 2 * HEAD_SIZE

    scratch = dict(
        tok=pltpu.VMEM((slots, rows, d), bf),
        w_qkv=pltpu.VMEM((4, shard, 2 * width), bf),
        gains=pltpu.VMEM((4, 1, gain_cols), f32),
        columns=pltpu.VMEM((count, 8), f32),
        normed=pltpu.VMEM((count, d), bf),
        qkv=pltpu.VMEM((count, 2 * width), f32),
        q=pltpu.VMEM((count, width), bf),
        k=pltpu.VMEM((count, HEAD_SIZE), bf),
        v=pltpu.VMEM((count, HEAD_SIZE), bf),
        kt=pltpu.VMEM((HEAD_SIZE, count), bf),
        vt=pltpu.VMEM((HEAD_SIZE, count), bf),
        cos=pltpu.VMEM((count, HEAD_SIZE), f32),
        sin=pltpu.VMEM((count, HEAD_SIZE), f32),
        mixed=pltpu.VMEM((count, width), f32),
        mixed_low=pltpu.VMEM((count, width), bf),
        sent=pltpu.VMEM((slots, rows, width), bf),
        w_o=pltpu.VMEM((4, o_rows, d), bf),
        w_gu=pltpu.VMEM((4, shard, 4 * half), bf),
        grad=pltpu.VMEM((4, rows, d), bf),
        mixed_in=pltpu.VMEM((slots, rows, width), bf),
        residual=pltpu.VMEM((rows, d), bf),
        m_gain=pltpu.VMEM((1, d), f32),
        w_dn=pltpu.VMEM((2, half, d), bf),
        middle=pltpu.VMEM((rows, d), f32),
        quad=pltpu.VMEM((4, rows, d), bf),
        hidden=pltpu.VMEM((4, rows, ff), bf),
        d_gu=pltpu.VMEM((4, rows, 2 * ff), bf),
        near_part=pltpu.VMEM((2, rows, d), f32),
        far_part=pltpu.VMEM((2, rows, d), bf),
        near_out=pltpu.VMEM((2, rows, d), f32),
        far_out=pltpu.VMEM((2, rows, d), bf),
        beside=pltpu.VMEM((rows, d), bf),
        beside_out=pltpu.VMEM((rows, d), bf),
        got=pltpu.VMEM((6, rows, d), bf),
        to_side=pltpu.VMEM((2, rows, d), bf),
        g_gate=pltpu.VMEM((d, ff), bf),
        g_up=pltpu.VMEM((d, ff), bf),
        g_dn=pltpu.VMEM((2, half, d), bf),
        dn_got=pltpu.VMEM((half, d // 2), bf),
        dm=pltpu.VMEM((slots, rows, width), bf),
    )
    outs = dict(
        first=shape_of(1, count, kind=jnp.int32),
        dealt=shape_of(1, count, kind=jnp.int32),
        back_from=shape_of(rows, 1, kind=jnp.int32),
        mixed_in=shape_of(slots, rows, width),
        normed=shape_of(count, d),
        qkv=shape_of(count, 2 * width, kind=f32),
        q=shape_of(count, width),
        k=shape_of(count, HEAD_SIZE),
        v=shape_of(count, HEAD_SIZE),
        kt=shape_of(HEAD_SIZE, count),
        cos=shape_of(count, HEAD_SIZE, kind=f32),
        sin=shape_of(count, HEAD_SIZE, kind=f32),
        mixed=shape_of(count, width, kind=f32),
        lse=shape_of(2, 1, count, kind=f32),
        w_qkv=shape_of(4, shard, 2 * width),
        a_gain=shape_of(1, d, kind=f32),
        q_gain=shape_of(1, HEAD_SIZE, kind=f32),
        k_gain=shape_of(1, HEAD_SIZE, kind=f32),
        output=shape_of(rows, d),
        back=shape_of(slots, 32, d),
        dm=shape_of(slots, rows, width),
        gate=shape_of(d, ff),
        up=shape_of(d, ff),
        down=shape_of(2, half, d),
        down_sum=shape_of(half, d // 2),
        middle_low=shape_of(rows, d),
        dg2=shape_of(1, d, kind=f32),
    )

    def body(net, fetch, load, given, out, r):
        z, y, x, core, me = net.z, net.y, net.x, net.core, net.me
        f = 2 * x + core
        done = set()
        tok = given.tok.at[0]
        tok_own = fetch(tok, r.tok.at[me])

        def lanes(start, size):
            return pl.ds(pl.multiple_of(start, HEAD_SIZE), size)

        head_parts = [
            (given.w_q.at[:, lanes(me * width, width)], pl.ds(0, width)),
            (given.w_k.at[:, lanes(me * HEAD_SIZE, HEAD_SIZE)], pl.ds(width, HEAD_SIZE)),
            (
                given.w_v.at[:, lanes(me * HEAD_SIZE, HEAD_SIZE)],
                pl.ds(width + HEAD_SIZE, HEAD_SIZE),
            ),
        ]
        w_own = [fetch(src, r.w_qkv.at[f, :, to]) for src, to in head_parts]
        greet(net, ("ctx", "x", "core", "far"))
        log = {s: [] for s in range(LINE)}
        waits = list(w_own)
        zone = lax.broadcasted_iota(jnp.int32, (1, HEAD_SIZE), 1) // (HEAD_SIZE // 4) == f

        def zoned(ref):
            return jnp.where(zone, jnp.concatenate([ref[...].astype(f32)] * 4, axis=1), 0.0)

        r.gains[f] = jnp.concatenate(
            [
                given.attn_gain[...].astype(f32).reshape(1, -1),
                given.mlp_gain[...].astype(f32).reshape(1, -1),
                zoned(given.q_gain),
                zoned(given.k_gain),
            ],
            axis=1,
        )

        def head_weights():
            beside = [net.put(src, r.w_qkv.at[f, :, to], net.at(dc=1)) for src, to in head_parts]
            beside.append(net.put(r.gains.at[f], r.gains.at[f], net.at(dc=1)))
            across = [net.put(src, r.w_qkv.at[f, :, to], net.at(dx=1)) for src, to in head_parts]
            across.append(net.put(r.gains.at[f], r.gains.at[f], net.at(dx=1)))
            yield
            for c in across:
                c.arrived()
            far = 2 * (1 - x) + core
            beside += [
                net.put(r.w_qkv.at[far], r.w_qkv.at[far], net.at(dc=1)),
                net.put(r.gains.at[far], r.gains.at[far], net.at(dc=1)),
            ]
            for c in waits:
                c.wait()
            for c in beside:
                c.arrived()
            r.own = fetch(r.w_qkv, out.w_qkv)
            done.add("head")
            yield

        arriving = Bag(o=[], gu=[], dn=[], grad=[], heads=[], results=[])

        def other_weights():
            yield
            pair, part_rows = lax.rem(z, 2), o_rows // 2
            mine, other = (
                pl.ds(pl.multiple_of(p * part_rows, part_rows), part_rows) for p in (pair, 1 - pair)
            )
            over = net.put(given.w_o.at[mine], r.w_o.at[f, mine], net.at(dx=1))
            arriving.o += [
                fetch(given.w_o, r.w_o.at[f]),
                net.put(given.w_o, r.w_o.at[f], net.at(dc=1)),
            ]

            def quarter(c):
                return [
                    (
                        w.at[:, lanes((2 * xs + c) * 2 * half + y * half, half)],
                        r.w_gu.at[f, :, pl.ds((2 * i + xs) * half, half)],
                    )
                    for i, w in enumerate((given.w_gate, given.w_up))
                    for xs in range(2)
                ]

            arriving.gu += [fetch(src, to) for src, to in quarter(core)]
            arriving.gu += [net.put(src, to, net.at(dc=1)) for src, to in quarter(1 - core)]
            arriving.gu += [net.put(src, to, net.at(dx=1)) for src, to in quarter(core)]
            arriving.gu += [net.put(src, to, net.at(dx=1, dc=1)) for src, to in quarter(1 - core)]
            part = given.w_down.at[pl.ds(pl.multiple_of(y * half, half), half)]
            arriving.dn += [
                fetch(part, r.w_dn.at[x]),
                net.put(part, r.w_dn.at[x], net.at(dx=1)),
            ]
            yield from resting(REST[0])
            over.arrived()
            far = r.w_o.at[2 * (1 - x) + core, mine]
            handed = net.put(far, far, net.at(dz=1 - 2 * pair))
            arriving.o.append(net.put(far, far, net.at(dc=1)))
            yield from resting(REST[1])
            handed.arrived()
            far = r.w_o.at[2 * (1 - x) + core, other]
            arriving.o.append(net.put(far, far, net.at(dc=1)))

        def output_grad():
            yield from resting(5)
            own = r.grad.at[2 * y + core]
            grad = given.grad.at[0]
            arriving.grad += [
                fetch(grad, own),
                net.put(grad, own, net.at(dc=1)),
                net.put(grad, own, net.at(dy=1)),
            ]
            yield
            arriving.grad[2].arrived()
            far = r.grad.at[2 * (1 - y) + core]
            arriving.grad.append(net.put(far, far, net.at(dc=1)))

        def project(slot):
            at = pl.ds(pl.multiple_of(slot * rows, rows), rows)
            normed = low(root_mean_norm(r.tok[slot].astype(f32), out.a_gain[...]))
            r.normed[at] = normed
            qkv = dot(normed, r.w_qkv[...].reshape(4 * shard, 2 * width))
            r.qkv[at] = qkv
            cos, sin = r.cos[at], r.sin[at]

            def turned(part, gain):
                v = root_mean_norm(part, gain)
                return low(v * cos + turn_lanes(v) * sin)

            for g in range(2):
                cols = pl.ds(g * HEAD_SIZE, HEAD_SIZE)
                r.q[at, cols] = turned(
                    qkv[:, g * HEAD_SIZE : (g + 1) * HEAD_SIZE], out.q_gain[...]
                )
            r.k[at] = turned(qkv[:, width : width + HEAD_SIZE], out.k_gain[...])
            r.v[at] = low(qkv[:, width + HEAD_SIZE :])

        def main():
            ids = lax.broadcasted_iota(jnp.int32, (1, count), 1)
            first, dealt, back, start = jnp.zeros_like(ids), ids, ids, 0
            for i in range(1, given.lengths.shape[1]):
                start = start + given.lengths[0, i - 1]
                first = jnp.where(ids >= start, start, first)
            for s in range(slots):
                for j in range(slots):
                    begin = given.deal[0, s, j] * rows + s * piece
                    dealt = jnp.where(
                        (ids >= begin) & (ids < begin + piece),
                        ids - begin + (s * rows + j * piece),
                        dealt,
                    )
            for j in range(slots):
                begin = given.deal[0, me, j] * 32
                back = jnp.where(
                    (ids >= j * piece) & (ids < (j + 1) * piece), ids - j * piece + begin, back
                )
            out.first[...] = first
            out.dealt[...] = dealt
            row = lax.broadcasted_iota(jnp.int32, (8, count), 0)
            stack = jnp.where(row == 0, ids - first, jnp.where(row == 1, dealt, back))
            r.columns[...] = jnp.transpose(stack.astype(f32))
            out.back_from[...] = r.columns[pl.ds(0, rows), 2:3].astype(jnp.int32)
            for i in range(slots):
                at = pl.ds(i * rows, rows)
                angle = r.columns[at, 0:1] * given.freq[0:1]
                r.cos[at] = jnp.cos(angle)
                r.sin[at] = jnp.sin(angle) * given.freq[1:2]
            yield
            while "head" not in done:
                yield
            gains = [r.gains[i] for i in range(4)]
            part = d // 4
            for i in range(4):
                out.a_gain[:, pl.ds(i * part, part)] = gains[i][:, :part]
                r.m_gain[:, pl.ds(i * part, part)] = gains[i][:, part : 2 * part]
            total = gains[0] + gains[1] + gains[2] + gains[3]
            out.q_gain[...] = total[:, 2 * part : 2 * part + HEAD_SIZE]
            out.k_gain[...] = total[:, 2 * part + HEAD_SIZE :]
            tok_own.wait()
            near = near_first(z)
            for k in range(LINE):
                project(2 * near[k] + y)
                if k:
                    for c in log[k - 1]:
                        c.arrived()
                    project(2 * near[k - 1] + 1 - y)
                yield
            for c in log[LINE - 1]:
                c.arrived()
            project(2 * near[LINE - 1] + 1 - y)
            results = [
                fetch(r.normed, out.normed),
                fetch(r.qkv, out.qkv),
                fetch(r.q, out.q),
                fetch(r.k, out.k),
                fetch(r.v, out.v),
                fetch(r.cos, out.cos),
                fetch(r.sin, out.sin),
                r.own,
            ]
            for i in range(blocks):
                at = pl.ds(i * BLOCK, BLOCK)
                r.kt[:, at] = jnp.transpose(r.k[at])
                r.vt[:, at] = jnp.transpose(r.v[at])
            results.append(fetch(r.kt, out.kt))
            for i in range(blocks):
                here = pl.ds(i * BLOCK, BLOCK)
                first = out.first[:, here]
                t = i * BLOCK + lax.broadcasted_iota(jnp.int32, (BLOCK, BLOCK), 1)
                q = [r.q[here, pl.ds(g * HEAD_SIZE, HEAD_SIZE)] for g in range(2)]

                def step(n, held, i=i, q=q, first=first, t=t):
                    j = i - n
                    at = pl.ds(pl.multiple_of(j * BLOCK, BLOCK), BLOCK)
                    k, vt = r.k[at], r.vt[:, at]
                    u = j * BLOCK + lax.broadcasted_iota(jnp.int32, (BLOCK, BLOCK), 0)
                    allowed = (u >= first) & (u <= t)
                    result = []
                    for g in range(2):
                        top, total, mixed = held[g]
                        scores = jnp.where(allowed, dot_last(k, q[g]) * scale, negative_filler)
                        new = jnp.maximum(top, jnp.max(scores, axis=0, keepdims=True))
                        fade = jnp.exp(top - new)
                        p = jnp.exp(scores - new)
                        total = total * fade + jnp.sum(p, axis=0, keepdims=True)
                        result.append((new, total, mixed * fade + dot(vt, low(p))))
                    return tuple(result)

                row = jnp.full((1, BLOCK), negative_filler, f32)
                none = (row, jnp.zeros((1, BLOCK), f32), jnp.zeros((HEAD_SIZE, BLOCK), f32))
                held = lax.fori_loop(0, i + 1, step, (none, none))
                for g in range(2):
                    top, total, mixed = held[g]
                    cols = pl.ds(g * HEAD_SIZE, HEAD_SIZE)
                    out.lse[g, :, here] = top + jnp.log(total)
                    mixed = jnp.transpose(mixed / total)
                    r.mixed[here, cols] = mixed
                    r.mixed_low[here, cols] = low(mixed)
                yield
            results.append(fetch(r.mixed, out.mixed))
            ids = lax.broadcasted_iota(jnp.int32, (rows, count), 1)

            def hot(slot):
                at = pl.ds(pl.multiple_of(slot * rows, rows), rows)
                return low(jnp.where(r.columns[at, 1:2].astype(jnp.int32) == ids, 1.0, 0.0))

            for k in range(1, slots):
                other = lax.rem(me + k, slots)
                r.sent[other] = low(dot(hot(other), r.mixed_low[...]))
                there = (other // 2, lax.rem(other, 2), x, core)
                arriving.heads.append(net.put(r.sent.at[other], r.mixed_in.at[me], there))
            mine = hot(me)
            r.sent[me] = low(dot(mine, r.mixed_low[...]))
            arriving.heads.append(fetch(r.sent.at[me], r.mixed_in.at[me]))
            r.residual[...] = low(dot(mine, r.tok[...].reshape(count, d)))
            arriving.results += results
            yield

        drive(
            head_weights(),
            by_steps(gather_line_first(net, tok, lambda slot: r.tok.at[slot], log)),
            main(),
            other_weights(),
            output_grad(),
        )
        middle(net, fetch, arriving, out, r)

    return kernel_with(
        body,
        moved,
        loaded,
        outs,
        scratch,
        110,
        number,
        (
            "lse",
            "a_gain",
            "q_gain",
            "k_gain",
            "first",
            "dealt",
            "back_from",
            "output",
            "back",
            "middle_low",
            "dg2",
            "down_sum",
        ),
        ("attn_gain", "mlp_gain", "q_gain", "k_gain", "freq"),
        ("lengths", "deal"),
    )


def back_kernel(dims, number):
    rows, count = dims
    blocks = count // BLOCK
    scale = HEAD_SIZE**-0.5
    width = 2 * HEAD_SIZE
    d = MODEL_WIDTH

    def run(moved, loaded):
        a = Bag(**moved)
        gu_rows, gu_cols = a.gate.shape[1:]
        dn_rows = a.down.shape[1]
        o_rows = 2 * width
        bf, f32 = jnp.bfloat16, jnp.float32
        z_gu, z_dn, z_o = gu_rows // LINE, dn_rows // LINE, o_rows // (2 * LINE)
        gain_width = 2 * d + 2 * HEAD_SIZE

        def quarter():
            return dict(
                got=pltpu.VMEM((2, gu_rows, gu_cols), bf),
                own=pltpu.VMEM((2, gu_rows, gu_cols), bf),
                low=pltpu.VMEM((2, z_gu, gu_cols), bf),
                pair=pltpu.VMEM((2, z_gu, gu_cols), bf),
                line=line_scratch(2 * z_gu, gu_cols),
            )

        scratch = dict(
            held={n: pltpu.VMEM(v.shape, v.dtype) for n, v in loaded.items()},
            gate=quarter(),
            up=quarter(),
            down=[
                dict(
                    own=pltpu.VMEM((dn_rows, d // 2), bf),
                    got=pltpu.VMEM((dn_rows, d // 2), bf),
                    low=pltpu.VMEM((z_dn, d // 2), bf),
                    line=line_scratch(z_dn, d // 2),
                )
                for _ in range(2)
            ],
            o=dict(
                own=pltpu.VMEM((4, o_rows, d), bf),
                core=pltpu.VMEM((2, o_rows, d), bf),
                got=pltpu.VMEM((o_rows, d), bf),
                sum=pltpu.VMEM((2 * LINE, z_o, d), bf),
                side=pltpu.VMEM((LINE, z_o, d), bf),
                low=pltpu.VMEM((z_o, d), bf),
                line=line_scratch(z_o, d),
            ),
            h=dict(
                own=pltpu.VMEM((4, d // 4, 2 * width), bf),
                core=pltpu.VMEM((2, d // 4, 2 * width), bf),
                got=pltpu.VMEM((d // 4, 2 * width), bf),
                low=pltpu.VMEM((d // 4, 2 * width), bf),
            ),
            dm_all=pltpu.VMEM((2 * LINE, rows, width), bf),
            back=pltpu.VMEM(a.back.shape, bf),
            do=pltpu.VMEM((count, width), bf),
            dk=pltpu.VMEM((count, HEAD_SIZE), f32),
            dv=pltpu.VMEM((count, HEAD_SIZE), f32),
            dqkv=pltpu.VMEM((count, 2 * width), bf),
            dgq=pltpu.VMEM((1, HEAD_SIZE), f32),
            dgk=pltpu.VMEM((1, HEAD_SIZE), f32),
            part=dict(
                sum=pltpu.VMEM((2 * LINE, rows, d), bf),
                side=pltpu.VMEM((LINE, rows, d), bf),
                line=line_scratch(rows, d),
            ),
            g=dict(
                mine=pltpu.VMEM((1, gain_width), f32),
                four=pltpu.VMEM((1, gain_width), f32),
                got=pltpu.VMEM((3, 1, gain_width), f32),
                all=pltpu.VMEM((2 * LINE, 1, gain_width), f32),
            ),
        )
        flat, tree = jax.tree.flatten(scratch)
        f_in, in_tree = jax.tree.flatten((moved, loaded))
        outs = dict(
            input_grad=shape_of(rows, d, kind=f32),
            a_grad=shape_of(1, d // 4, kind=f32),
            m_grad=shape_of(1, d // 4, kind=f32),
            q_grad=shape_of(1, HEAD_SIZE // 4, kind=f32),
            k_grad=shape_of(1, HEAD_SIZE // 4, kind=f32),
            gate=shape_of(2 * LINE, 2, z_gu, gu_cols),
            up=shape_of(2 * LINE, 2, z_gu, gu_cols),
            down=shape_of(2 * LINE, z_dn, d),
            o=shape_of(2 * LINE, z_o, d),
            heads=shape_of(2 * LINE, d // 4, 2 * width),
        )
        f_out, out_tree = jax.tree.flatten(outs)

        def body(net, local, *refs):
            given, to_load = jax.tree.unflatten(in_tree, refs[: len(f_in)])
            given = Bag(**given)
            out = Bag(**jax.tree.unflatten(out_tree, refs[len(f_in) : len(f_in) + len(f_out)]))
            r = bags(jax.tree.unflatten(tree, refs[len(f_in) + len(f_out) :]))
            h = r.held
            z, y, x, core, me = net.z, net.y, net.x, net.core, net.me
            slots = 2 * LINE
            used = iter(range(64))

            def fetch(src, dst):
                return Local(pltpu.make_async_copy(src, dst, local.at[next(used)]))

            greet(net, ("ctx", "x", "core", "far"))
            loads = {n: fetch(to_load[n], getattr(h, n)) for n in to_load}
            dm_own = fetch(given.dm.at[me], r.dm_all.at[me])
            back_own = fetch(given.back.at[me], r.back.at[me])
            gate_own, up_own = (
                [fetch(src.at[2 * x + c], piece.own.at[c]) for c in range(2)]
                for src, piece in ((given.gate, r.gate), (given.up, r.up))
            )
            columns = [pl.ds(0, d // 2), pl.ds(d // 2, d // 2)]
            down_own = [
                fetch(given.down_sum, r.down[0].own),
                fetch(given.down.at[x, :, columns[1]], r.down[1].own),
            ]
            back_copies = []

            def need(*which):
                for n in which:
                    if n in loads:
                        loads.pop(n).wait()

            def to_all(src, out):
                copies = []
                for k in range(1, slots):
                    other = lax.rem(me + k, slots)
                    there = (other // 2, lax.rem(other, 2), x, core)
                    copies.append(net.put(src(other), out.at[me], there))
                return copies

            def back_rows():
                back_copies.extend(to_all(lambda other: given.back.at[other], r.back))
                yield

            def main():
                dm_copies = to_all(lambda other: given.dm.at[other], r.dm_all)
                yield
                need(*list(loads))
                dm_own.wait()
                for c in dm_copies:
                    c.arrived()
                yield
                for i in range(blocks):
                    t = i * BLOCK + lax.broadcasted_iota(jnp.int32, (BLOCK, count), 0)
                    hot = low(jnp.where(h.dealt[...] == t, 1.0, 0.0))
                    r.do[pl.ds(i * BLOCK, BLOCK)] = low(
                        dot(hot, r.dm_all[...].reshape(count, width))
                    )
                r.dk[...] = jnp.zeros_like(r.dk)
                r.dv[...] = jnp.zeros_like(r.dv)
                yield
                dgq = jnp.zeros((1, HEAD_SIZE), f32)
                for i in range(blocks):
                    here = pl.ds(i * BLOCK, BLOCK)
                    first = h.first[:, here]
                    t = i * BLOCK + lax.broadcasted_iota(jnp.int32, (BLOCK, BLOCK), 1)
                    heads = []
                    for g in range(2):
                        lanes = pl.ds(g * HEAD_SIZE, HEAD_SIZE)
                        q, do = h.q[here, lanes], r.do[here, lanes]
                        product = do.astype(f32) * h.mixed[here, lanes]
                        delta = jnp.sum(jnp.transpose(product), axis=0, keepdims=True)
                        heads.append((q, do, h.lse[g, :, here], delta))

                    def step(j, held, heads=heads, first=first, t=t):
                        at = pl.ds(pl.multiple_of(j * BLOCK, BLOCK), BLOCK)
                        k, v, kt = h.k[at], h.v[at], h.kt[:, at]
                        u = j * BLOCK + lax.broadcasted_iota(jnp.int32, (BLOCK, BLOCK), 0)
                        allowed = (u >= first) & (u <= t)
                        dk, dv, out = r.dk[at], r.dv[at], []
                        for (q, do, lse, delta), dq in zip(heads, held):
                            p = jnp.where(allowed, jnp.exp(dot_last(k, q) * scale - lse), 0.0)
                            ds = low(p * (dot_last(v, do) - delta))
                            dv = dv + dot(low(p), do)
                            dk = dk + dot(ds, q)
                            out.append(dq + dot(kt, ds))
                        r.dk[at] = dk
                        r.dv[at] = dv
                        return tuple(out)

                    zero = jnp.zeros((HEAD_SIZE, BLOCK), f32)
                    result = lax.fori_loop(0, i + 1, step, (zero, zero))
                    cos, sin = h.cos[here], h.sin[here]
                    for g in range(2):
                        lanes = pl.ds(g * HEAD_SIZE, HEAD_SIZE)
                        grad = jnp.transpose(result[g]) * scale
                        grad = grad * cos - turn_lanes(grad) * sin
                        dx, dg = norm_back(h.qkv[here, lanes], h.q_gain[...], grad)
                        r.dqkv[here, lanes] = low(dx)
                        dgq = dgq + jnp.sum(dg, axis=0, keepdims=True)
                    yield
                dgk = jnp.zeros((1, HEAD_SIZE), f32)
                for i in range(blocks):
                    here = pl.ds(i * BLOCK, BLOCK)
                    grad = r.dk[here] * scale
                    grad = grad * h.cos[here] - turn_lanes(grad) * h.sin[here]
                    dx, dg = norm_back(
                        h.qkv[here, pl.ds(width, HEAD_SIZE)], h.k_gain[...], grad
                    )
                    r.dqkv[here, pl.ds(width, HEAD_SIZE)] = low(dx)
                    r.dqkv[here, pl.ds(width + HEAD_SIZE, HEAD_SIZE)] = low(r.dv[here])
                    dgk = dgk + jnp.sum(dg, axis=0, keepdims=True)
                r.dgq[...] = dgq
                r.dgk[...] = dgk
                yield

                def make(slot):
                    at = pl.ds(pl.multiple_of(slot * rows, rows), rows)
                    r.part.sum[slot] = low(dot_last(r.dqkv[at], h.w_qkv[...].reshape(d, 2 * width)))

                yield from sum_sides(net, r.part.sum, r.part.side, r.part.line, make)
                yield
                dx1, dg1 = norm_back(
                    h.tok[0].astype(f32), h.a_gain[...], r.part.line[0][z]
                )
                for c in back_copies:
                    c.arrived()
                back_own.wait()
                ids = lax.broadcasted_iota(jnp.int32, (rows, slots * a.back.shape[1]), 1)
                hot = low(jnp.where(h.back_from[...] == ids, 1.0, 0.0))
                out.input_grad[...] = dx1 + dot(hot, r.back[...].reshape(-1, d))
                r.g.mine[:, pl.ds(0, d)] = jnp.sum(dg1, axis=0, keepdims=True)
                r.g.mine[:, pl.ds(d, d)] = h.dg2[...]
                r.g.mine[:, pl.ds(2 * d, HEAD_SIZE)] = r.dgq[...]
                r.g.mine[:, pl.ds(2 * d + HEAD_SIZE, HEAD_SIZE)] = r.dgk[...]
                yield

            def gains():
                sides = [net.at(dc=1), net.at(dx=1), net.at(dx=1, dc=1)]
                pair = [net.put(r.g.mine, r.g.got.at[i], to) for i, to in enumerate(sides)]
                yield
                for c in pair:
                    c.arrived()
                along = r.g.mine[...] + r.g.got[0]
                across = r.g.got[1] + r.g.got[2]
                r.g.four[...] = along + across
                r.g.all[me] = r.g.four[...]
                copies = to_all(lambda other: r.g.four, r.g.all)
                yield
                for c in copies:
                    c.arrived()
                total = jnp.sum(r.g.all[...], axis=0)

                def own_part(start, size):
                    part = total[:, start : start + size]
                    for i in range(1, 4):
                        at = start + i * size
                        part = jnp.where(2 * x + core == i, total[:, at : at + size], part)
                    return part

                out.a_grad[...] = own_part(0, d // 4)
                out.m_grad[...] = own_part(d, d // 4)
                out.q_grad[...] = own_part(2 * d, HEAD_SIZE // 4)
                out.k_grad[...] = own_part(2 * d + HEAD_SIZE, HEAD_SIZE // 4)
                yield

            def gate_or_up(src, own, piece, gathered):
                over = [
                    net.put(src.at[2 * (1 - x) + c], piece.got.at[c], net.at(dx=1))
                    for c in range(2)
                ]
                yield
                for c in own + over:
                    c.arrived()
                line = piece.line

                def ready(t):
                    k = far_first(z)[t]
                    at = pl.ds(pl.multiple_of(k * z_gu, z_gu), z_gu)
                    for c in range(2):
                        line[0][k, pl.ds(c * z_gu, z_gu)] = piece.own[c, at].astype(
                            f32
                        ) + piece.got[c, at].astype(f32)

                yield from sum_line(net, *line, ready)
                for c in range(2):
                    piece.low[c] = low(line[0][z, pl.ds(c * z_gu, z_gu)])
                swap = net.put(piece.low.at[1 - core], piece.pair.at[core], net.at(dc=1))
                piece.pair[core] = piece.low[core]
                yield
                swap.arrived()
                own = fetch(piece.pair, gathered.at[me])
                yield from gather_line_first(net, piece.pair, lambda slot: gathered.at[slot])
                own.wait()

            def down(i):
                piece, line = r.down[i], r.down[i].line
                if i:
                    over = net.put(given.down.at[1 - x, :, columns[i]], piece.got, net.at(dx=1))
                    yield
                    over.arrived()
                down_own[i].arrived()

                def ready(t):
                    k = far_first(z)[t]
                    at = pl.ds(pl.multiple_of(k * z_dn, z_dn), z_dn)
                    block = piece.own[at].astype(f32)
                    line[0][k] = block + piece.got[at].astype(f32) if i else block

                yield from sum_line(net, *line, ready)
                piece.low[...] = low(line[0][z])
                own = fetch(piece.low, out.down.at[me, :, columns[i]])
                yield from gather_line_first(
                    net, piece.low, lambda slot: out.down.at[slot, :, columns[i]]
                )
                own.wait()

            def out_proj():
                need("heads_in", "middle_low")
                for i in range(slots):
                    r.o.own[i // 2, pl.ds(i % 2 * width, width)] = low(
                        outer_rows(h.heads_in[i], h.middle_low[...])
                    )
                o_core = [
                    net.put(r.o.own.at[2 * s + 1 - core], r.o.core.at[s], net.at(dc=1))
                    for s in range(2)
                ]
                yield
                for c in o_core:
                    c.arrived()
                for s in range(2):
                    f = 2 * s + core
                    r.o.own[f] = low(r.o.own[f].astype(f32) + r.o.core[s].astype(f32))
                over = net.put(r.o.own.at[2 * (1 - x) + core], r.o.got, net.at(dx=1))
                yield
                over.arrived()
                for i in range(slots):
                    at = pl.ds(i * z_o, z_o)
                    r.o.sum[i] = low(r.o.own[2 * x + core, at].astype(f32) + r.o.got[at].astype(f32))
                yield from sum_sides(net, r.o.sum, r.o.side, r.o.line)
                r.o.low[...] = low(r.o.line[0][z])
                own = fetch(r.o.low, out.o.at[me])
                yield from gather_line_first(net, r.o.low, lambda slot: out.o.at[slot])
                own.wait()

            def heads():
                for f in range(4):
                    at = pl.ds(f * (d // 4), d // 4)
                    r.h.own[f] = low(outer_rows(h.normed[:, at], r.dqkv[...]))
                core_copies = [
                    net.put(r.h.own.at[2 * s + 1 - core], r.h.core.at[s], net.at(dc=1))
                    for s in range(2)
                ]
                yield
                for c in core_copies:
                    c.arrived()
                for s in range(2):
                    f = 2 * s + core
                    r.h.own[f] = low(r.h.own[f].astype(f32) + r.h.core[s].astype(f32))
                over = net.put(r.h.own.at[2 * (1 - x) + core], r.h.got, net.at(dx=1))
                yield
                over.arrived()
                r.h.low[...] = low(
                    r.h.own[2 * x + core].astype(f32) + r.h.got[...].astype(f32)
                )
                own = fetch(r.h.low, out.heads.at[me])
                yield from gather_line_first(net, r.h.low, lambda slot: out.heads.at[slot])
                own.wait()

            in_order(
                BACK_ORDER,
                [
                    gate_or_up(given.gate, gate_own, r.gate, out.gate),
                    gate_or_up(given.up, up_own, r.up, out.up),
                    out_proj(),
                    down(0),
                    down(1),
                    back_rows(),
                    heads(),
                    main(),
                    gains(),
                ],
            )
            net.close()

        order = jax.tree.unflatten(out_tree, range(len(f_out)))
        result = net_call(
            body,
            f_out,
            f_in,
            200,
            64,
            number,
            scratch=flat,
            vmem=[
                len(f_in) + order.get(n)
                for n in ("input_grad", "a_grad", "m_grad", "q_grad", "k_grad")
            ],
        )
        return Bag(**jax.tree.unflatten(out_tree, result))

    return run


def widen(gate_all, up_all, down_all, o_all, heads_all, *small):
    _, _, z_gu, gu_cols = gate_all.shape
    half = gu_cols // 2
    z_dn, z_o = down_all.shape[1], o_all.shape[1]
    h_rows = heads_all.shape[1] // (2 * LINE)

    def kernel(gate, up, down, o, heads, *refs):
        passed, outs = refs[: len(small)], refs[len(small) :]
        gate_out, up_out, down_out, o_out, q_out, k_out, v_out = outs[:7]
        for src, out in zip(passed, outs[7:]):
            out[...] = src[...].reshape(out.shape)
        for src, out in ((gate, gate_out), (up, up_out)):
            for y in range(2):
                for c in range(2):
                    for xs in range(2):
                        to = (2 * xs + c) * 2 * half + y * half
                        out[:, pl.ds(to, half)] = src[y, c, :, pl.ds(xs * half, half)].astype(
                            jnp.float32
                        )
        for y in range(2):
            down_out[y] = down[y].astype(jnp.float32)
            o_out[y] = o[y].astype(jnp.float32)
        for h in range(2 * LINE):
            q_out[:, pl.ds(h * 256, 256)] = heads[h, :, pl.ds(0, 256)].astype(jnp.float32)
            k_out[:, pl.ds(h * 128, 128)] = heads[h, :, pl.ds(256, 128)].astype(jnp.float32)
            v_out[:, pl.ds(h * 128, 128)] = heads[h, :, pl.ds(384, 128)].astype(jnp.float32)

    f32 = jnp.float32
    outs = pl.pallas_call(
        kernel,
        grid=(2 * LINE,),
        in_specs=[
            pl.BlockSpec((2, 2, z_gu // 2, gu_cols), lambda i: (i // 2, 0, i % 2, 0)),
            pl.BlockSpec((2, 2, z_gu // 2, gu_cols), lambda i: (i // 2, 0, i % 2, 0)),
            pl.BlockSpec((2, z_dn // 2, MODEL_WIDTH), lambda i: (i // 2, i % 2, 0)),
            pl.BlockSpec((2, z_o // 2, MODEL_WIDTH), lambda i: (i // 2, i % 2, 0)),
            pl.BlockSpec((2 * LINE, h_rows, 512), lambda i: (0, i, 0)),
        ]
        + [pl.BlockSpec(v.shape, lambda i: (0, 0)) for v in small],
        out_specs=[
            pl.BlockSpec((z_gu // 2, 8 * half), lambda i: (i, 0)),
            pl.BlockSpec((z_gu // 2, 8 * half), lambda i: (i, 0)),
            pl.BlockSpec((2, z_dn // 2, MODEL_WIDTH), lambda i: (0, i, 0)),
            pl.BlockSpec((2, z_o // 2, MODEL_WIDTH), lambda i: (i // 2, i % 2, 0)),
            pl.BlockSpec((h_rows, 2048), lambda i: (i, 0)),
            pl.BlockSpec((h_rows, 1024), lambda i: (i, 0)),
            pl.BlockSpec((h_rows, 1024), lambda i: (i, 0)),
        ]
        + [pl.BlockSpec((1, *v.shape), lambda i: (0, 0, 0)) for v in small],
        out_shape=[
            shape_of(LINE * z_gu, 8 * half, kind=f32),
            shape_of(LINE * z_gu, 8 * half, kind=f32),
            shape_of(2, LINE * z_dn, MODEL_WIDTH, kind=f32),
            shape_of(2 * LINE, z_o, MODEL_WIDTH, kind=f32),
            shape_of(2 * LINE * h_rows, 2048, kind=f32),
            shape_of(2 * LINE * h_rows, 1024, kind=f32),
            shape_of(2 * LINE * h_rows, 1024, kind=f32),
        ]
        + [shape_of(1, *v.shape, kind=v.dtype) for v in small],
        compiler_params=pltpu.CompilerParams(vmem_limit_bytes=VMEM_BYTES),
    )(gate_all, up_all, down_all, o_all, heads_all, *small)
    outs = list(outs)
    outs[2] = outs[2].reshape(-1, MODEL_WIDTH)
    outs[3] = outs[3].reshape(-1, MODEL_WIDTH)
    return outs


def fast_layer(
    tokens,
    lengths,
    deal,
    attn_gain,
    w_q,
    key_weight,
    value_weight,
    query_norm_gain,
    k_gain,
    w_o,
    mlp_gain,
    w_gate,
    w_up,
    w_down,
    out_cotangent,
):
    rows = tokens.shape[1]
    slots = lax.axis_size(CTX)
    count = rows * slots
    ff_half = w_down.shape[0] // 2
    width = HEAD_SIZE * 2

    frequency = theta_base ** (-(np.arange(HEAD_SIZE // 2) * 2.0) / HEAD_SIZE)
    sign = np.where(np.arange(HEAD_SIZE) < HEAD_SIZE // 2, -1.0, 1.0)
    tables = np.stack([np.tile(frequency, 2), sign]).astype(np.float32)

    front = front_kernel(
        dict(
            tok=tokens,
            lengths=lengths,
            deal=deal,
            attn_gain=attn_gain,
            mlp_gain=mlp_gain,
            q_gain=query_norm_gain[None],
            k_gain=k_gain[None],
            freq=tables,
            w_q=w_q,
            w_k=key_weight,
            w_v=value_weight,
            w_o=w_o,
            w_gate=w_gate,
            w_up=w_up,
            w_down=w_down,
            grad=out_cotangent,
        ),
        {},
        0,
    )
    moved = dict(
        dm=front.dm,
        back=front.back,
        gate=front.gate.reshape(4, -1, 2 * ff_half),
        up=front.up.reshape(4, -1, 2 * ff_half),
        down=front.down,
        down_sum=front.down_sum,
    )
    loaded = dict(
        tok=tokens,
        back_from=front.back_from,
        a_gain=front.a_gain,
        dg2=front.dg2,
        heads_in=front.mixed_in,
        middle_low=front.middle_low,
        q=front.q,
        k=front.k,
        kt=front.kt,
        v=front.v,
        mixed=front.mixed,
        lse=front.lse,
        first=front.first,
        dealt=front.dealt,
        qkv=front.qkv,
        q_gain=front.q_gain,
        k_gain=front.k_gain,
        cos=front.cos,
        sin=front.sin,
        normed=front.normed,
        w_qkv=front.w_qkv,
    )
    sums = back_kernel((rows, count), 2)(moved, loaded)

    gate_sum, up_sum, down_sum, o_sum, q_sum, k_sum, v_sum, *small = widen(
        sums.gate,
        sums.up,
        sums.down,
        sums.o,
        sums.heads,
        front.output,
        sums.input_grad,
        sums.a_grad,
        sums.q_grad,
        sums.k_grad,
        sums.m_grad,
    )
    output, input_grad, *gains = small
    return (
        output,
        input_grad,
        *(gain[0, 0] for gain in gains),
        q_sum,
        k_sum,
        v_sum,
        o_sum,
        gate_sum,
        up_sum,
        down_sum,
    )


def solution(mesh):
    devices = mesh.devices
    if devices.shape == (8, 4):
        mesh = Mesh(devices.reshape(4, 2, 2, 2), CTX + FSDP)
        layer, ctx, fsdp = fast_layer, CTX, FSDP
    else:
        layer, ctx, fsdp = general_layer, "ctx", "fsdp"
    wide_rows = P(fsdp, ctx, None)
    return jax.shard_map(
        layer,
        mesh=mesh,
        in_specs=(
            wide_rows,
            P(fsdp, None),
            P(fsdp, None, None),
            P(fsdp),
            P(fsdp, None),
            P(fsdp, None),
            P(fsdp, None),
            P(fsdp),
            P(fsdp),
            P(fsdp, None),
            P(fsdp),
            P(fsdp, None),
            P(fsdp, None),
            P(fsdp, None),
            wide_rows,
        ),
        out_specs=(wide_rows, wide_rows) + (P(fsdp),) * 4 + (P(fsdp, None),) * 7,
        check_vma=False,
    )
```
